32 devices in a mesh: rows: 8 (over y, x, core), blk: 4 (over z).
Axes of the slice: x: 2, y: 2, z: 4, core: 2. Of those that a mesh axis runs over, the one named last changes fastest.
Arguments:
- image: bfloat16 [4, 8, 96, 512], P('blk', 'rows'), may hold values from -6 to 6
- skip: bfloat16 [4, 16, 192, 512], P('blk', 'rows'), may hold values from -6 to 6
- labels: int32 [4, 16, 192], P('blk', 'rows'), may hold values from 0 to 1
- weight_map: int32 [4, 16, 192], P('blk', 'rows'), may hold values from 2 to 24
- valid: int32 [4, 16, 192], P('blk', 'rows'), may hold values from 0 to 1
- owner: int32 [320], replicated, may hold values from 0 to 319, each once
- master: float32 [4, 320, 128, 128], P('blk', 'rows'), may hold values from -0.0625 to 0.0625
- first_moment: float32 [4, 320, 128, 128], P('blk', 'rows'), may hold values from -0.0014648438 to 0.0014648438
- second_moment: float32 [4, 320, 128, 128], P('blk', 'rows'), may hold values from 8.138021e-10 to 3.2552083e-09
- left_basis: float32 [4, 320, 128, 128], P('blk', 'rows'), may hold values from -1 to 1, as said below
- right_basis: float32 [4, 320, 128, 128], P('blk', 'rows'), may hold values from -1 to 1, as said below
- left_stat: float32 [4, 320, 128, 128], P('blk', 'rows'), as said below
- right_stat: float32 [4, 320, 128, 128], P('blk', 'rows'), as said below
- norm_params: float32 [6144], replicated
- norm_first: float32 [6144], replicated, may hold values from -0.00390625 to 0.00390625
- norm_second: float32 [6144], replicated, may hold values from 8.138021e-09 to 3.2552084e-08
- head_bias: float32 [2], replicated, may hold values from -3 to 3
- bias_first: float32 [2], replicated, may hold values from -0.4375 to 0.4375
- bias_second: float32 [2], replicated, may hold values from 0.0001 to 0.0004
Outputs:
- loss_sum: float32 [], replicated
- valid_count: float32 [], replicated
- new_master: float32 [4, 320, 128, 128], P('blk', 'rows')
- new_copy: bfloat16 [4, 320, 128, 128], P('blk', 'rows')
- new_first: float32 [4, 320, 128, 128], P('blk', 'rows')
- new_second: float32 [4, 320, 128, 128], P('blk', 'rows')
- new_left: float32 [4, 320, 128, 128], P('blk', 'rows')
- new_right: float32 [4, 320, 128, 128], P('blk', 'rows')
- new_left_stat: float32 [4, 320, 128, 128], P('blk', 'rows')
- new_right_stat: float32 [4, 320, 128, 128], P('blk', 'rows')
- new_norm_first: float32 [6144], replicated
- new_norm_second: float32 [6144], replicated
- new_norm: float32 [6144], replicated
- new_bias_first: float32 [2], replicated
- new_bias_second: float32 [2], replicated
- new_bias: float32 [2], replicated
The draws below stay inside these ranges and needn't reach their ends.
Inputs may be any that keep to these rules, and one draw needn't show every extreme that they name: `owner`: the device at index r of rows owns slots r * 40 to (r + 1) * 40 - 1; every block is in one slot. `left_basis`: each block is orthogonal. `right_basis`: each block is orthogonal. `left_stat`: each block is symmetric positive definite. `right_stat`: each block is symmetric positive definite.
All inputs are finite; a program needn't handle non-finite values.
Results may differ from the reference program's by a relative error of at most 0.0034.
The reference program's roundings to bfloat16 on the way count: a program that leaves them out, or rounds other values in their place, can miss the bound.
Values may be sent and summed in bfloat16 or wider, within the bound.
A program may use at most 320 MiB of HBM per device.

```python
import math
import jax
import jax.numpy as jnp
from jax import lax

C0 = 512
C1 = 1024
GROUPS = 32
BS = 128
STEP = 10
W_LO = 96
SHARDS = 4
IMAGES = 4
H_LO = 8
H_HI = 16
W_HI = 192
HI_PIX = 12288
NBLOCKS = 320
NPARAM = 6144


def signed_hadamard(key):
    total = SHARDS * NBLOCKS
    keys = jax.random.split(key, total)
    orders = jax.vmap(lambda single: jax.random.permutation(single, BS))(keys)
    signs = jax.random.randint(jax.random.fold_in(key, 11), (2, total, BS), 0, 2) * 2 - 1
    columns = jnp.arange(BS)
    joined = orders[:, :, None] & columns[None, None, :]
    parity = jnp.zeros_like(joined)
    for bit in range(16):
        parity = parity + (joined >> bit & 1)
    entries = (1 - 2 * (parity % 2)) * signs[0][:, :, None] * signs[1][:, None, :]
    return (entries.astype(jnp.float32) * BS ** (-0.5)).reshape(SHARDS, NBLOCKS, BS, BS)


def stat_matrix(key):
    total = SHARDS * NBLOCKS
    diag_key, noise_key = jax.random.split(key)
    diagonal = jax.random.uniform(diag_key, (total, BS), jnp.float32, 2.0, 8.0)
    noise = jax.random.normal(noise_key, (total, BS, BS), jnp.float32) * (0.8 * BS ** (-0.5))
    symmetric = (noise + jnp.swapaxes(noise, 1, 2)) * 0.5 ** 0.5
    matrix = symmetric + diagonal[:, :, None] * jnp.eye(BS, dtype=jnp.float32)[None]
    return (matrix * (0.0001 * BS / HI_PIX)).reshape(SHARDS, NBLOCKS, BS, BS)


def draw_left_basis(key, part):
    key = jax.random.fold_in(key, 1)
    return signed_hadamard(key)


def draw_right_basis(key, part):
    key = jax.random.fold_in(key, 2)
    return signed_hadamard(key)


def draw_left_stat(key, part):
    key = jax.random.fold_in(key, 3)
    return stat_matrix(key)


def draw_right_stat(key, part):
    key = jax.random.fold_in(key, 4)
    return stat_matrix(key)


def draw_valid(key, part):
    key = jax.random.fold_in(key, 5)
    picks = jax.random.randint(key, (IMAGES, H_HI, W_HI), 0, 1000)
    level = 250 + 500 * jnp.arange(H_HI) // H_HI
    return (picks < level[None, :, None]).astype(jnp.int32)


def draw_norm_params(key, part):
    key = jax.random.fold_in(key, 7)
    noise = jax.random.normal(key, (NPARAM,), jnp.float32)
    index = jnp.arange(NPARAM)
    is_gain = (index < 4 * C1) & (index // C1 % 2 == 0) | (index >= 4 * C1) & (index < 4 * C1 + C0)
    is_head = index >= 4 * C1 + 2 * C0
    scale = jnp.where(is_head, C0 ** (-0.5), 0.3)
    return jnp.where(is_gain, 1.0, 0.0) + noise * scale


def with_ends(values, own_key, least, high):
    spot = [jax.random.randint(jax.random.fold_in(own_key, axis), (), 0, length) for axis, length in enumerate(values.shape)]
    longest = values.shape.index(max(values.shape))
    next_to = spot[:longest] + [(spot[longest] + 1) % values.shape[longest]] + spot[longest + 1:]
    return values.at[tuple(spot)].set(least).at[tuple(next_to)].set(high)


def block_levels(rng, dims, cuts, smallest, high):
    level, own = 1.0, jax.random.fold_in(rng, 6)
    for axis_at, shards_of in cuts:
        heights = jnp.exp(jax.random.uniform(jax.random.fold_in(own, axis_at), (shards_of,), jnp.float32, smallest / len(cuts), high / len(cuts)))
        level = level * jnp.repeat(heights, dims[axis_at] // shards_of).reshape([-1 if axis == axis_at else 1 for axis in range(len(dims))])
    return level


def normal_values(own_key, extent, deviation, most, cuts=(), kind=jnp.bfloat16):
    drawn = jax.random.normal(own_key, extent, jnp.float32) * deviation
    if len(cuts) > 0:
        drawn = block_levels(own_key, extent, cuts, -0.22, 0.18) * drawn
    return jnp.clip(drawn, min=-most, max=most).astype(kind)


def setup_inputs(seed: int = 0) -> dict:
    key_of = jax.random.split(jax.random.key(seed), 20)
    image = normal_values(key_of[0], (IMAGES, H_LO, W_LO, C0), 1.0, 6.0, ((0, 4), (1, 8)))
    skip = normal_values(key_of[1], (IMAGES, H_HI, W_HI, C0), 1.0, 6.0, ((0, 4), (1, 8)))
    labels = with_ends(jax.random.randint(key_of[2], (IMAGES, H_HI, W_HI), 0, 2), jax.random.fold_in(key_of[2], 1), 0, 1).astype(jnp.int32)
    weight_map = with_ends(jax.random.randint(key_of[3], (IMAGES, H_HI, W_HI), 2, 25), jax.random.fold_in(key_of[3], 1), 2, 24).astype(jnp.int32)
    valid = draw_valid(jax.random.fold_in(key_of[19], 71), 0)
    owner = jax.random.permutation(key_of[5], NBLOCKS).astype(jnp.int32)
    master = normal_values(key_of[6], (SHARDS, NBLOCKS, BS, BS), (9 * C1) ** -0.5, 0.0625, ((0, 4), (1, 8)), jnp.float32)
    first_moment = normal_values(key_of[7], (SHARDS, NBLOCKS, BS, BS), (0.011 * HI_PIX ** -0.5), 0.0014648438, ((0, 4), (1, 8)), jnp.float32)
    second_moment = jnp.clip(jnp.exp(math.log(3.2552083251147224e-09) - 1.3862944 * jax.random.uniform(key_of[8], (SHARDS, NBLOCKS, BS, BS), jnp.float32) ** block_levels(key_of[8], (SHARDS, NBLOCKS, BS, BS), ((0, 4), (1, 8)), -0.2, 0.2)), 8.138020812786806e-10, 3.2552083251147224e-09)
    left_basis = draw_left_basis(jax.random.fold_in(key_of[19], 71), 0)
    right_basis = draw_right_basis(jax.random.fold_in(key_of[19], 71), 0)
    left_stat = draw_left_stat(jax.random.fold_in(key_of[19], 71), 0)
    right_stat = draw_right_stat(jax.random.fold_in(key_of[19], 71), 0)
    norm_params = draw_norm_params(jax.random.fold_in(key_of[19], 71), 0)
    norm_first = normal_values(key_of[14], (NPARAM,), (0.03 * HI_PIX ** -0.5), 0.00390625, (), jnp.float32)
    norm_second = jnp.clip(jnp.exp(jax.random.uniform(key_of[15], (NPARAM,), jnp.float32, math.log(8.138020923809108e-09), math.log(3.2552083695236433e-08))), 8.138020923809108e-09, 3.2552083695236433e-08)
    head_bias = normal_values(key_of[16], (2,), 0.3, 3.0, (), jnp.float32)
    bias_first = normal_values(key_of[17], (2,), 0.03, 0.4375, (), jnp.float32)
    bias_second = jnp.clip(jnp.exp(jax.random.uniform(key_of[18], (2,), jnp.float32, math.log(0.0001), math.log(0.0004))), 0.0001, 0.0004)
    return {"image": image, "skip": skip, "labels": labels, "weight_map": weight_map, "valid": valid, "owner": owner, "master": master, "first_moment": first_moment, "second_moment": second_moment, "left_basis": left_basis, "right_basis": right_basis, "left_stat": left_stat, "right_stat": right_stat, "norm_params": norm_params, "norm_first": norm_first, "norm_second": norm_second, "head_bias": head_bias, "bias_first": bias_first, "bias_second": bias_second}


@jax.custom_vjp
def low(v):
    return lax.optimization_barrier(v.astype(jnp.bfloat16)).astype(jnp.float32)

@jax.custom_vjp
def low_back(v):
    return v

def low_keep(v):
    return (low(v), None)

def low_pass(kept, grad):
    return (grad,)

def back_keep(v):
    return (v, None)

def back_low(kept, grad):
    return (low(grad),)
low.defvjp(low_keep, low_pass)
low_back.defvjp(back_keep, back_low)
beta_one = 0.9
beta_two = 0.999
beta_stat = 0.95
adam_eps = 1e-08
norm_eps = 1e-05
soap_rate = 0.008
soap_decay = 0.01
small_rate = 0.4
small_decay = 0.01
highest = lax.Precision.HIGHEST

def assemble(blocks, in_width, out_width, taps):
    out_rows = out_width // SHARDS
    split = blocks.reshape(SHARDS, out_rows // BS, taps, in_width // BS, BS, BS)
    return split.transpose(0, 1, 4, 2, 3, 5).reshape(out_width, taps, in_width)

def disassemble(weight, in_width, out_width, taps):
    out_rows = out_width // SHARDS
    split = weight.reshape(SHARDS, out_rows // BS, BS, taps, in_width // BS, BS)
    return split.transpose(0, 1, 3, 4, 2, 5).reshape(SHARDS, -1, BS, BS)

def conv(values, weight):
    height, width = (values.shape[0], values.shape[1])
    padded = jnp.pad(values, ((1, 1), (1, 1), (0, 0)))
    result = jnp.zeros((height, width, weight.shape[0]), jnp.float32)
    for tap in range(9):
        row_off, col_off = divmod(tap, 3)
        window = padded[row_off:row_off + height, col_off:col_off + width]
        result = result + jnp.einsum('hwc,oc->hwo', window, weight[:, tap, :], precision=highest)
    return result

def upsample(values, weight):
    height, width = (values.shape[0], values.shape[1])
    taps = jnp.einsum('hwc,otc->hwto', values, weight, precision=highest)
    taps = taps.reshape(height, width, 2, 2, weight.shape[0]).transpose(0, 2, 1, 3, 4)
    return taps.reshape(2 * height, 2 * width, weight.shape[0])

def norm_act(values, gain, shift):
    height, width, chans = values.shape
    part = values.reshape(height, width, GROUPS, chans // GROUPS)
    mean = lax.optimization_barrier(jnp.mean(part, axis=(0, 1, 3), keepdims=True))
    variance = lax.optimization_barrier(jnp.mean(part * part, axis=(0, 1, 3), keepdims=True)) - mean * mean
    zhat = ((part - mean) * lax.rsqrt(variance + norm_eps)).reshape(height, width, chans)
    normed = zhat * gain + shift
    return normed * jax.nn.sigmoid(normed)

def image_loss(weights, params, head_low, bias, image, skip, labels, scales):
    marks = (0, C1, 2 * C1, 3 * C1, 4 * C1, 4 * C1 + C0, 4 * C1 + 2 * C0)
    pieces = [params[marks[index]:marks[index + 1]] for index in range(6)]
    act_one = low(norm_act(low_back(conv(image, weights[0])), pieces[0], pieces[1]))
    act_two = low(norm_act(low_back(conv(act_one, weights[1])), pieces[2], pieces[3]))
    upper = low(low_back(upsample(act_two, weights[2])))
    joined = jnp.concatenate([upper, skip], -1)
    act_three = low(norm_act(low_back(conv(joined, weights[3])), pieces[4], pieces[5]))
    logits = jnp.einsum('hwc,ck->hwk', act_three, head_low, precision=highest) + bias
    log_total = jax.nn.logsumexp(logits, -1)
    picked = jnp.take_along_axis(logits, labels[..., None], -1)[..., 0]
    return jnp.sum(scales * (log_total - picked))

def orthonormal(stat, basis):
    product = jnp.matmul(stat, basis, precision=highest)
    gram = jnp.matmul(jnp.swapaxes(product, -1, -2), product, precision=highest)
    factor = jnp.linalg.cholesky(gram)
    order = product.shape[-1]
    flat_factor = factor.reshape(-1, order, order)
    flat_product = product.reshape(-1, order, order)
    solved = jax.vmap(lambda lower, right: jax.scipy.linalg.solve_triangular(lower, right.T, lower=True))(flat_factor, flat_product)
    return jnp.swapaxes(solved, -1, -2).reshape(product.shape)

def soap_update(grads, master, first, second, left, right, left_stat, right_stat):
    rotated = jnp.matmul(jnp.matmul(jnp.swapaxes(left, -1, -2), grads, precision=highest), right, precision=highest)
    first_new = beta_one * first + (1.0 - beta_one) * rotated
    second_new = beta_two * second + (1.0 - beta_two) * rotated * rotated
    direction = first_new / (1.0 - beta_one ** STEP) / (jnp.sqrt(second_new / (1.0 - beta_two ** STEP)) + adam_eps)
    update = jnp.matmul(jnp.matmul(left, direction, precision=highest), jnp.swapaxes(right, -1, -2), precision=highest)
    master_new = master - soap_rate * (update + soap_decay * master)
    left_new_stat = beta_stat * left_stat + (1.0 - beta_stat) * jnp.matmul(grads, jnp.swapaxes(grads, -1, -2), precision=highest)
    right_new_stat = beta_stat * right_stat + (1.0 - beta_stat) * jnp.matmul(jnp.swapaxes(grads, -1, -2), grads, precision=highest)
    return (master_new, first_new, second_new, orthonormal(left_new_stat, left), orthonormal(right_new_stat, right), left_new_stat, right_new_stat)

def adam_small(grads, value, first, second):
    first_new = beta_one * first + (1.0 - beta_one) * grads
    second_new = beta_two * second + (1.0 - beta_two) * grads * grads
    direction = first_new / (1.0 - beta_one ** STEP) / (jnp.sqrt(second_new / (1.0 - beta_two ** STEP)) + adam_eps)
    return (first_new, second_new, value - small_rate * (direction + small_decay * value))

def reference(image, skip, labels, weight_map, valid, owner, master, first_moment, second_moment, left_basis, right_basis, left_stat, right_stat, norm_params, norm_first, norm_second, head_bias, bias_first, bias_second):
    layers = ((C0, C1, 9), (C1, C1, 9), (C1, C0, 4), (2 * C0, C0, 9))
    by_number = master[:, jnp.argsort(owner)]
    weights = []
    offset = 0
    for in_width, out_width, taps in layers:
        number = out_width // SHARDS // BS * taps * (in_width // BS)
        weights.append(assemble(by_number[:, offset:offset + number], in_width, out_width, taps))
        offset = offset + number
    count = jnp.sum(valid.astype(jnp.float32))
    scales = valid.astype(jnp.float32) * weight_map.astype(jnp.float32) * 0.125
    images_float = image.astype(jnp.float32)
    skips_float = skip.astype(jnp.float32)

    def objective(weight_list, params, bias):
        low_weights = [low(weight) for weight in weight_list]
        head_low = low(params[4 * C1 + 2 * C0:].reshape(C0, 2))

        def one_image(total, item):
            return (total + image_loss(low_weights, params, head_low, bias, *item), None)
        total, _ = lax.scan(jax.checkpoint(one_image), jnp.zeros((), jnp.float32), (images_float, skips_float, labels, scales))
        return (total / count, total)
    _, backward, loss_sum = jax.vjp(objective, weights, norm_params, head_bias, has_aux=True)
    grad_weights, grad_params, grad_bias = backward(jnp.ones((), jnp.float32))
    blocks = jnp.concatenate([disassemble(grad_weights[index], *layers[index]) for index in range(4)], 1)
    grads = blocks[:, owner]
    soap = soap_update(grads, master, first_moment, second_moment, left_basis, right_basis, left_stat, right_stat)
    norm_new = adam_small(grad_params, norm_params, norm_first, norm_second)
    bias_new = adam_small(grad_bias, head_bias, bias_first, bias_second)
    return (loss_sum, count, soap[0], soap[0].astype(jnp.bfloat16), soap[1], soap[2], soap[3], soap[4], soap[5], soap[6], norm_new[0], norm_new[1], norm_new[2], bias_new[0], bias_new[1], bias_new[2])
```

```python
from functools import reduce

import jax
import jax.numpy as jnp
from jax import lax
from jax.experimental import pallas as pl
from jax.experimental.pallas import tpu as pltpu
from jax.sharding import PartitionSpec as P

C0 = 512
C1 = 1024
GROUPS = 32
STEP = 10


beta_one = 0.9
beta_two = 0.999
beta_stat = 0.95
adam_eps = 1e-08
norm_eps = 1e-05
soap_rate = 0.008
soap_decay = 0.01
small_rate = 0.4
small_decay = 0.01
highest = lax.Precision.HIGHEST


def padded_2(block, sides, width):
    for axis, dim in sides:
        count = lax.axis_size(axis)
        forward = [(i, i + 1) for i in range(count - 1)]
        backward = [(target, source) for source, target in forward]
        low = lax.ppermute(
            lax.slice_in_dim(block, block.shape[dim] - width, None, axis=dim), axis, forward
        )
        high = lax.ppermute(lax.slice_in_dim(block, 0, width, axis=dim), axis, backward)
        block = jnp.concatenate([low, block, high], axis=dim)
    return block


def from_blocks(blocks, out_rows, taps, in_width):
    order = blocks.shape[-1]
    split = blocks.reshape(out_rows // order, taps, in_width // order, order, order)
    return split.transpose(0, 3, 1, 2, 4).reshape(out_rows, taps, in_width)


def to_blocks(weight, order):
    out_rows, taps, in_width = weight.shape
    split = weight.reshape(out_rows // order, order, taps, in_width // order, order)
    return split.transpose(0, 2, 3, 1, 4).reshape(-1, order, order)


def pad_rows(values):
    padded = padded_2(values, (("rows", 1),), 1)
    return jnp.pad(padded, ((0, 0), (0, 0), (1, 1), (0, 0)))


def tap_views(padded, height, width, flipped):
    views = []
    for row_off in range(3):
        for col_off in range(3):
            first_row = 2 - row_off if flipped else row_off
            first_col = 2 - col_off if flipped else col_off
            window = padded[:, first_row : first_row + height, first_col : first_col + width, :]
            views.append(window.reshape(-1, padded.shape[-1]))
    return views


def make_views(source, height, width, summed):
    if summed:
        return tap_views(source, height, width, False)
    return [source.reshape(-1, source.shape[-1])] * 4


def tap_products(views, piece, summed):
    terms = [
        lax.dot_general(
            views[tap],
            piece[:, tap, :],
            (((1,), (1,)), ((), ())),
            preferred_element_type=jnp.float32,
        )
        for tap in range(len(views))
    ]
    if summed:
        return reduce(lambda left, right: left + right, terms)
    return jnp.stack(terms, 1)


def forward_conv(source, shard, height, width, summed):
    views = make_views(source, height, width, summed)
    return (tap_products(views, shard, summed), views)


def input_grad(grad_views, shard, keep):
    carry = jnp.zeros((grad_views[0].shape[0], keep), jnp.float32)
    for tap in range(len(grad_views)):
        carry = carry + jnp.dot(
            grad_views[tap], shard[:, tap, :keep], preferred_element_type=jnp.float32
        )
    return lax.psum_scatter(carry, "blk", scatter_dimension=1, tiled=True)


def weight_grad(pairs):
    parts = [
        lax.dot_general(
            grad_view, in_view, (((0,), (0,)), ((), ())), preferred_element_type=jnp.float32
        )
        for grad_view, in_view in pairs
    ]
    return jnp.stack(parts, 1)


def backward_conv(grad, views, shard, keep, spatial, need_input):
    chans = grad.shape[-1]
    if spatial:
        flat = grad.reshape(-1, chans)
        pairs = [(flat, view) for view in views]
        grad_views = tap_views(pad_rows(grad), grad.shape[1], grad.shape[2], True)
    else:
        grad_views = [grad[:, tap, :] for tap in range(4)]
        pairs = list(zip(grad_views, views))
    weight_part = weight_grad(pairs)
    if not need_input:
        return (weight_part, None)
    return (weight_part, input_grad(grad_views, shard, keep))


def group_forward(values, gain, shift, total_rows, groups):
    images, height, width, chans = values.shape
    part = values.reshape(images, height, width, groups, chans // groups)
    first_sum = jnp.sum(part, axis=(1, 2, 4))
    second_sum = jnp.sum(part * part, axis=(1, 2, 4))
    first_sum, second_sum = lax.psum((first_sum, second_sum), "rows")
    number = total_rows * width * (chans // groups)
    mean = first_sum / number
    variance = second_sum / number - mean * mean
    inv_scale = lax.rsqrt(variance + norm_eps)[:, None, None, :, None]
    zhat = ((part - mean[:, None, None, :, None]) * inv_scale).reshape(values.shape)
    normed = zhat * gain + shift
    return (normed * jax.nn.sigmoid(normed), (zhat, inv_scale, normed))


def group_backward(grad_act, saved, gain, total_rows, groups):
    zhat, inv_scale, normed = saved
    images, height, width, chans = zhat.shape
    sigmoid_y = jax.nn.sigmoid(normed)
    grad_y = grad_act * sigmoid_y * (1.0 + normed * (1.0 - sigmoid_y))
    gain_grad = jnp.sum(grad_y * zhat, axis=(0, 1, 2))
    shift_grad = jnp.sum(grad_y, axis=(0, 1, 2))
    grad_hat = (grad_y * gain).reshape(images, height, width, groups, chans // groups)
    zpart = zhat.reshape(grad_hat.shape)
    grad_sum = jnp.sum(grad_hat, axis=(1, 2, 4))
    cross_sum = jnp.sum(grad_hat * zpart, axis=(1, 2, 4))
    grad_sum, cross_sum = lax.psum((grad_sum, cross_sum), "rows")
    number = total_rows * width * (chans // groups)
    grad_pre = (
        grad_hat
        - (grad_sum / number)[:, None, None, :, None]
        - zpart * (cross_sum / number)[:, None, None, :, None]
    ) * inv_scale
    return (grad_pre.reshape(zhat.shape).astype(jnp.bfloat16), gain_grad, shift_grad)


LANES = 128


def inverse_factor_kernel(stat_ref, inverse_ref, factor_ref):
    order = stat_ref.shape[0]
    tile = (8, LANES)
    sub = lax.broadcasted_iota(jnp.int32, tile, 0)

    def eliminate(source_ref, base, start, first, count, accs):
        def body(group, accs):
            top = pl.multiple_of(group * 8, 8)
            for unit in range(8):
                value = source_ref[top + unit, pl.ds(start, 8), :]
                accs = tuple(
                    accs[c]
                    - value
                    * jnp.broadcast_to(factor_ref[top + unit, pl.ds(base + c, 1), :], tile)
                    for c in range(8)
                )
            return accs

        return list(lax.fori_loop(first, count, body, tuple(accs)))

    def block(kb, _):
        base = pl.multiple_of(kb * 8, 8)
        accs = [stat_ref[base + c, pl.ds(base, 8), :] for c in range(8)]
        accs = eliminate(factor_ref, base, base, 0, kb, accs)
        scale = []
        coef = {}
        for c in range(8):
            scale.append(jnp.broadcast_to(lax.rsqrt(accs[c][c : c + 1, :]), tile))
            accs[c] = accs[c] * scale[c]
            for d in range(c + 1, 8):
                coef[(c, d)] = jnp.broadcast_to(accs[c][d : d + 1, :], tile)
                accs[d] = accs[d] - accs[c] * coef[(c, d)]
        for c in range(8):
            factor_ref[base + c, pl.ds(base, 8), :] = jnp.where(sub >= c, accs[c], 0.0)

        def finish(accs, target_ref, start):
            accs = list(accs)
            for c in range(8):
                for e in range(c):
                    accs[c] = accs[c] - accs[e] * coef[(e, c)]
                accs[c] = accs[c] * scale[c]
                target_ref[base + c, pl.ds(start, 8), :] = accs[c]

        def below(group, _):
            start = pl.multiple_of(group * 8, 8)
            accs = [stat_ref[base + c, pl.ds(start, 8), :] for c in range(8)]
            finish(eliminate(factor_ref, base, start, 0, kb, accs), factor_ref, start)
            return 0

        def left(group, _):
            start = pl.multiple_of(group * 8, 8)
            accs = [jnp.zeros(tile, jnp.float32) for c in range(8)]
            finish(eliminate(inverse_ref, base, start, group, kb, accs), inverse_ref, start)
            return 0

        def clear(group, _):
            start = pl.multiple_of(group * 8, 8)
            for c in range(8):
                inverse_ref[base + c, pl.ds(start, 8), :] = jnp.zeros(tile, jnp.float32)
            return 0

        lax.fori_loop(kb + 1, order // 8, below, 0)
        lax.fori_loop(0, kb, left, 0)
        finish([jnp.where(sub == c, 1.0, 0.0) for c in range(8)], inverse_ref, base)
        lax.fori_loop(kb + 1, order // 8, clear, 0)
        return 0

    lax.fori_loop(0, order // 8, block, 0)


def inverse_factors(grams):
    count, order = grams.shape[0], grams.shape[-1]
    chunks = -(-count // LANES)
    spare = chunks * LANES - count
    eye = jnp.broadcast_to(jnp.eye(order, dtype=jnp.float32), (spare, order, order))
    lanes = jnp.concatenate([grams, eye], 0).transpose(1, 2, 0)
    block = pl.BlockSpec((order, order, LANES), lambda chunk: (0, 0, chunk))
    result = pl.pallas_call(
        inverse_factor_kernel,
        grid=(chunks,),
        out_shape=jax.ShapeDtypeStruct(lanes.shape, jnp.float32),
        in_specs=[block],
        out_specs=block,
        scratch_shapes=[pltpu.VMEM((order, order, LANES), jnp.float32)],
        compiler_params=pltpu.CompilerParams(vmem_limit_bytes=56 * 2**20),
    )(lanes)
    return result.transpose(2, 0, 1)[:count]


def orthonormal(stats, bases):
    products = [
        jnp.matmul(stat, basis, precision=highest)[0] for stat, basis in zip(stats, bases)
    ]
    grams = [
        jnp.matmul(jnp.swapaxes(product, -1, -2), product, precision=highest)
        for product in products
    ]
    inverses = inverse_factors(jnp.concatenate(grams, 0))
    count = products[0].shape[0]
    return [
        jnp.matmul(product, jnp.swapaxes(inverse, -1, -2), precision=highest)[None]
        for product, inverse in zip(products, (inverses[:count], inverses[count:]))
    ]


def soap_update(grads, master, first, second, left, right, left_stat, right_stat):
    rotated = jnp.matmul(
        jnp.matmul(jnp.swapaxes(left, -1, -2), grads, precision=highest), right, precision=highest
    )
    first_new = beta_one * first + (1.0 - beta_one) * rotated
    second_new = beta_two * second + (1.0 - beta_two) * rotated * rotated
    direction = (
        first_new
        / (1.0 - beta_one**STEP)
        / (jnp.sqrt(second_new / (1.0 - beta_two**STEP)) + adam_eps)
    )
    update = jnp.matmul(
        jnp.matmul(left, direction, precision=highest),
        jnp.swapaxes(right, -1, -2),
        precision=highest,
    )
    master_new = master - soap_rate * (update + soap_decay * master)
    left_new_stat = beta_stat * left_stat + (1.0 - beta_stat) * jnp.matmul(
        grads, jnp.swapaxes(grads, -1, -2), precision=highest
    )
    right_new_stat = beta_stat * right_stat + (1.0 - beta_stat) * jnp.matmul(
        jnp.swapaxes(grads, -1, -2), grads, precision=highest
    )
    left_new, right_new = orthonormal((left_new_stat, right_new_stat), (left, right))
    return (
        master_new,
        first_new,
        second_new,
        left_new,
        right_new,
        left_new_stat,
        right_new_stat,
    )


def adam_small(grads, value, first, second):
    first_new = beta_one * first + (1.0 - beta_one) * grads
    second_new = beta_two * second + (1.0 - beta_two) * grads * grads
    direction = (
        first_new
        / (1.0 - beta_one**STEP)
        / (jnp.sqrt(second_new / (1.0 - beta_two**STEP)) + adam_eps)
    )
    return (first_new, second_new, value - small_rate * (direction + small_decay * value))


def local(
    image,
    skip,
    labels,
    weight_map,
    valid,
    owner,
    master,
    first_moment,
    second_moment,
    left_basis,
    right_basis,
    left_stat,
    right_stat,
    norm_params,
    norm_first,
    norm_second,
    head_bias,
    bias_first,
    bias_second,
):
    shards = lax.axis_size("blk")
    shard = lax.axis_index("blk")
    image, skip, labels, weight_map, valid = [
        lax.all_gather(part, "blk", axis=0, tiled=True)
        for part in (image, skip, labels, weight_map, valid)
    ]
    images, low_rows, low_cols = (image.shape[0], image.shape[1], image.shape[2])
    high_rows, high_cols = (2 * low_rows, 2 * low_cols)
    total_rows = low_rows * lax.axis_size("rows")
    order = master.shape[-1]
    groups = GROUPS // shards
    layers = ((C0, C1, 9), (C1, C1, 9), (C1, C0, 4), (2 * C0, C0, 9))
    copies = lax.all_gather(master.astype(jnp.bfloat16), "rows", axis=1, tiled=True)[0]
    ordered = copies[jnp.argsort(owner)]
    shard_list = []
    offset = 0
    for in_width, out_width, taps in layers:
        out_rows = out_width // shards
        number = out_rows // order * taps * (in_width // order)
        shard_list.append(from_blocks(ordered[offset : offset + number], out_rows, taps, in_width))
        offset = offset + number
    widths = (C1, C1, C1, C1, C0, C0)
    pieces = []
    offset = 0
    for width in widths:
        local_width = width // shards
        pieces.append(
            lax.dynamic_slice_in_dim(norm_params, offset + shard * local_width, local_width)
        )
        offset = offset + width
    head_width = C0 // shards
    head_low = lax.dynamic_slice_in_dim(
        norm_params[offset:].reshape(C0, 2), shard * head_width, head_width
    ).astype(jnp.bfloat16)
    pre_one, views_one = forward_conv(pad_rows(image), shard_list[0], low_rows, low_cols, True)
    act_one, saved_one = group_forward(
        pre_one.reshape(images, low_rows, low_cols, -1), pieces[0], pieces[1], total_rows, groups
    )
    full_one = lax.all_gather(act_one.astype(jnp.bfloat16), "blk", axis=3, tiled=True)
    pre_two, views_two = forward_conv(pad_rows(full_one), shard_list[1], low_rows, low_cols, True)
    act_two, saved_two = group_forward(
        pre_two.reshape(images, low_rows, low_cols, -1), pieces[2], pieces[3], total_rows, groups
    )
    full_two = lax.all_gather(act_two.astype(jnp.bfloat16), "blk", axis=3, tiled=True)
    up_taps, views_up = forward_conv(full_two, shard_list[2], low_rows, low_cols, False)
    upsampled = up_taps.astype(jnp.bfloat16)
    upsampled = upsampled.reshape(images, low_rows, low_cols, 2, 2, -1).transpose(0, 1, 3, 2, 4, 5)
    upsampled = upsampled.reshape(images, high_rows, high_cols, -1)
    upsampled = lax.all_gather(upsampled, "blk", axis=3, tiled=True)
    joined = jnp.concatenate([upsampled, skip], -1)
    pre_three, views_three = forward_conv(
        pad_rows(joined), shard_list[3], high_rows, high_cols, True
    )
    act_three, saved_three = group_forward(
        pre_three.reshape(images, high_rows, high_cols, -1),
        pieces[4],
        pieces[5],
        2 * total_rows,
        groups,
    )
    flat_three = act_three.astype(jnp.bfloat16).reshape(-1, head_width)
    logits = (
        lax.psum(jnp.dot(flat_three, head_low, preferred_element_type=jnp.float32), "blk")
        + head_bias
    )
    targets = (labels.reshape(-1, 1) == jnp.arange(2)[None, :]).astype(jnp.float32)
    valid_flat = valid.reshape(-1).astype(jnp.float32)
    scales = valid_flat * weight_map.reshape(-1).astype(jnp.float32) * 0.125
    valid_count = lax.psum(jnp.sum(valid_flat), "rows")
    largest = jnp.max(logits, -1, keepdims=True)
    log_total = jnp.log(jnp.sum(jnp.exp(logits - largest), -1, keepdims=True)) + largest
    losses = log_total[:, 0] - jnp.sum(logits * targets, -1)
    loss_part = jnp.sum(scales * losses)
    grad_logits = (jnp.exp(logits - log_total) - targets) * (scales / valid_count)[:, None]
    grad_head = jnp.dot(flat_three.astype(jnp.float32).T, grad_logits, precision=highest)
    grad_bias = jnp.sum(grad_logits, 0)
    grad_act = jnp.dot(grad_logits, head_low.astype(jnp.float32).T, precision=highest)
    grad_pre, gain_three, shift_three = group_backward(
        grad_act.reshape(images, high_rows, high_cols, -1),
        saved_three,
        pieces[4],
        2 * total_rows,
        groups,
    )
    grad_four, grad_joined = backward_conv(grad_pre, views_three, shard_list[3], C0, True, True)
    grad_up = grad_joined.astype(jnp.bfloat16).reshape(images, low_rows, 2, low_cols, 2, -1)
    grad_up = grad_up.transpose(0, 1, 3, 2, 4, 5).reshape(-1, 4, grad_up.shape[-1])
    grad_three, grad_act = backward_conv(grad_up, views_up, shard_list[2], C1, False, True)
    grad_pre, gain_two, shift_two = group_backward(
        grad_act.reshape(images, low_rows, low_cols, -1), saved_two, pieces[2], total_rows, groups
    )
    grad_two, grad_act = backward_conv(grad_pre, views_two, shard_list[1], C1, True, True)
    grad_pre, gain_one, shift_one = group_backward(
        grad_act.reshape(images, low_rows, low_cols, -1), saved_one, pieces[0], total_rows, groups
    )
    grad_one, unused = backward_conv(grad_pre, views_one, shard_list[0], C0, True, False)
    blocks = jnp.concatenate(
        [to_blocks(grad, order) for grad in (grad_one, grad_two, grad_three, grad_four)], 0
    )
    grads = lax.psum_scatter(blocks[owner], "rows", scatter_dimension=0, tiled=True)[None]
    small = jnp.concatenate(
        [gain_one, shift_one, gain_two, shift_two, gain_three, shift_three, grad_head.reshape(-1)]
    )
    small, grad_bias, loss_sum = lax.psum((small, grad_bias, loss_part), "rows")
    spread = lax.all_gather(small, "blk", axis=0)
    parts = []
    offset = 0
    for width in widths + (2 * C0,):
        parts.append(spread[:, offset : offset + width // shards].reshape(-1))
        offset = offset + width // shards
    small = jnp.concatenate(parts)
    soap = soap_update(
        grads, master, first_moment, second_moment, left_basis, right_basis, left_stat, right_stat
    )
    norm_new = adam_small(small, norm_params, norm_first, norm_second)
    bias_new = adam_small(grad_bias, head_bias, bias_first, bias_second)
    return (
        loss_sum,
        valid_count,
        soap[0],
        soap[0].astype(jnp.bfloat16),
        soap[1],
        soap[2],
        soap[3],
        soap[4],
        soap[5],
        soap[6],
        norm_new[0],
        norm_new[1],
        norm_new[2],
        bias_new[0],
        bias_new[1],
        bias_new[2],
    )


def solution(mesh):
    placed = (
        P("blk", "rows", None, None),
        P("blk", "rows", None, None),
        P("blk", "rows", None),
        P("blk", "rows", None),
        P("blk", "rows", None),
        P(),
        P("blk", "rows", None, None),
        P("blk", "rows", None, None),
        P("blk", "rows", None, None),
        P("blk", "rows", None, None),
        P("blk", "rows", None, None),
        P("blk", "rows", None, None),
        P("blk", "rows", None, None),
        P(),
        P(),
        P(),
        P(),
        P(),
        P(),
    )
    return jax.shard_map(
        local,
        mesh=mesh,
        in_specs=placed,
        out_specs=(
            P(),
            P(),
            P("blk", "rows", None, None),
            P("blk", "rows", None, None),
            P("blk", "rows", None, None),
            P("blk", "rows", None, None),
            P("blk", "rows", None, None),
            P("blk", "rows", None, None),
            P("blk", "rows", None, None),
            P("blk", "rows", None, None),
            P(),
            P(),
            P(),
            P(),
            P(),
            P(),
        ),
        check_vma=False,
    )
```

```python
import functools

import jax
import jax.numpy as jnp
from jax import lax
from jax.experimental import pallas as pl
from jax.experimental.pallas import tpu as pltpu
from jax.sharding import PartitionSpec as P

C0 = 512
C1 = 1024
GROUPS = 32
STEP = 10


beta_one = 0.9
beta_two = 0.999
beta_stat = 0.95
adam_eps = 1e-08
norm_eps = 1e-05
soap_rate = 0.008
soap_decay = 0.01
small_rate = 0.4
small_decay = 0.01
highest = lax.Precision.HIGHEST


MESH = pl.DeviceIdType.MESH
bf16 = jnp.bfloat16
f32 = jnp.float32
TILE = 128


def dot_nt(left, right):
    return lax.dot_general(left, right, (((1,), (1,)), ((), ())), preferred_element_type=f32)


def dot_nn(left, right):
    return jnp.dot(left, right, preferred_element_type=f32)


def sigmoid(value):
    return 1.0 / (1.0 + jnp.exp(-value))


def block_layers(nb):
    result = []
    first = 0
    for in_width, out_width, taps in ((C0, C1, 9), (C1, C1, 9), (C1, C0, 4), (2 * C0, C0, 9)):
        out = out_width // nb
        result.append((out, in_width, taps, first))
        first = first + out // TILE * taps * (in_width // TILE)
    return result


def step_kernel(
    nr,
    nb,
    cols,
    copies_ref,
    place_ref,
    bias_ref,
    image_ref,
    skip_ref,
    lab_ref,
    wide_ref,
    narrow_ref,
    grad_ref,
    sums_ref,
    x_one,
    x_skip,
    x_lab,
    w_one,
    w_two,
    w_up,
    w_three,
    a_one,
    a_two,
    u_full,
    z_one,
    z_two,
    z_three,
    dy_low,
    dy_high,
    inv_one,
    inv_two,
    inv_three,
    dz_low,
    dz_high,
    shifted_low,
    shifted_high,
    turned_low,
    turned_high,
    dub,
    send_high,
    recv_high,
    send_low,
    recv_low,
    logit,
    reduce_wide,
    reduce_narrow,
    local_sem,
    line_send,
    line_recv,
    halo_send,
    halo_recv,
    red_send,
    red_recv,
    all_send,
    all_recv,
    high_send,
    high_recv,
    edge_send,
    edge_recv,
):
    r = lax.axis_index("rows")
    b = lax.axis_index("blk")
    px = nb * cols
    wide = C1 // nb
    slim = C0 // nb
    taps_high = 3 * slim
    layers = block_layers(nb)

    def remote(src, dst, send, recv, rows, blk):
        return pltpu.make_async_remote_copy(
            src_ref=src,
            dst_ref=dst,
            send_sem=send,
            recv_sem=recv,
            device_id={"rows": rows, "blk": blk},
            device_id_type=MESH,
        )

    def lanes(index, size):
        return pl.ds(pl.multiple_of(index * size, TILE), size)

    def ring(index, count):
        return lax.rem(index + count, count)

    barrier = pltpu.get_barrier_semaphore()

    def greet_rows(step, _):
        pl.semaphore_signal(
            barrier, inc=1, device_id={"rows": ring(r + step, nr), "blk": b}, device_id_type=MESH
        )
        return 0

    lax.fori_loop(1, nr, greet_rows, 0)
    for step in range(1, nb):
        pl.semaphore_signal(
            barrier, inc=1, device_id={"rows": r, "blk": ring(b + step, nb)}, device_id_type=MESH
        )
    pl.semaphore_wait(barrier, nr - 1 + nb - 1)

    class Exchange:
        def __init__(self, number, piece, up=None, down=None):
            self.number, self.piece, self.up, self.down = number, piece, up, down

        def right(self, j):
            return remote(
                self.piece(j),
                self.piece(j),
                line_send.at[self.number, j, 0],
                line_recv.at[self.number, j],
                r,
                ring(b + 1, nb),
            )

        def left(self, j):
            return remote(
                self.piece(j),
                self.piece(j),
                line_send.at[self.number, j, 1],
                line_recv.at[self.number, j],
                r,
                ring(b - 1, nb),
            )

        def higher(self, j):
            src, dst = self.up(j)
            return remote(
                src,
                dst,
                halo_send.at[self.number, j, 0],
                halo_recv.at[self.number, j, 0],
                ring(r + 1, nr),
                b,
            )

        def lower(self, j):
            src, dst = self.down(j)
            return remote(
                src,
                dst,
                halo_send.at[self.number, j, 1],
                halo_recv.at[self.number, j, 1],
                ring(r - 1, nr),
                b,
            )

        def halos(self, j):
            if self.up is None:
                return

            @pl.when(r + 1 < nr)
            def _():
                self.higher(j).start()

            @pl.when(r > 0)
            def _():
                self.lower(j).start()

        def begin(self):
            @pl.when(b + 1 < nb)
            def _():
                self.right(b).start()

            @pl.when(b > 0)
            def _():
                self.left(b).start()

            self.halos(b)

        def hop(self, k):
            @pl.when(b >= k)
            def _():
                self.right(b - k).wait_recv()

                @pl.when(b + 1 < nb)
                def _():
                    self.right(b - k).start()

                self.halos(b - k)

            @pl.when(b + k < nb)
            def _():
                self.left(b + k).wait_recv()

                @pl.when(b > 0)
                def _():
                    self.left(b + k).start()

                self.halos(b + k)

        def hops(self):
            for k in range(1, nb):
                self.hop(k)

        def finish(self):
            for k in range(nb):

                @pl.when((b >= k) & (b + 1 < nb))
                def _():
                    self.right(b - k).wait_send()

                @pl.when((b + k < nb) & (b > 0))
                def _():
                    self.left(b + k).wait_send()

            if self.up is None:
                return
            for j in range(nb):

                @pl.when(r + 1 < nr)
                def _():
                    self.higher(j).wait_send()
                    self.lower(j).wait_recv()

                @pl.when(r > 0)
                def _():
                    self.lower(j).wait_send()
                    self.higher(j).wait_recv()

    def all_reduce(number, buffer):
        def start(step, _):
            remote(
                buffer.at[r],
                buffer.at[r],
                red_send.at[number, step],
                red_recv.at[number, r],
                ring(r + step, nr),
                b,
            ).start()
            return 0

        def wait(step, _):
            source = ring(r + step, nr)
            copy = remote(
                buffer.at[source],
                buffer.at[source],
                red_send.at[number, step],
                red_recv.at[number, source],
                source,
                b,
            )
            copy.wait_recv()
            copy.wait_send()
            return 0

        lax.fori_loop(1, nr, start, 0)
        lax.fori_loop(1, nr, wait, 0)
        return lax.fori_loop(1, nr, lambda k, total: total + buffer[k], buffer[0])

    class Spread:
        def __init__(self, send, recv, source, target):
            self.send, self.recv, self.source, self.target = send, recv, source, target

        def copy(self, step):
            other = ring(b + step, nb)
            return remote(
                self.source(other),
                self.target(b),
                self.send.at[step],
                self.recv.at[b],
                r,
                other,
            )

        def begin(self):
            for step in range(1, nb):
                self.copy(step).start()

        def finish(self):
            for step in range(1, nb):
                other = ring(b + step, nb)
                remote(
                    self.source(other),
                    self.target(other),
                    self.send.at[step],
                    self.recv.at[other],
                    r,
                    other,
                ).wait_recv()
                self.copy(step).wait_send()

    position = lax.rem(lax.broadcasted_iota(jnp.int32, (px, TILE), 0), cols)

    def mask_of(value, column):
        hit = position[:, :1] == column
        return jnp.where(hit, 0.0, value)

    def shift_down(value):
        return mask_of(pltpu.roll(value, 1, 0), 0)

    def shift_up(value):
        return mask_of(pltpu.roll(value, px - 1, 0), cols - 1)

    def group_sum(value, size):
        width = value.shape[-1]
        bits = size.bit_length() - 1
        first = lax.shift_right_logical(lax.broadcasted_iota(jnp.int32, (width, width), 0), bits)
        second = lax.shift_right_logical(lax.broadcasted_iota(jnp.int32, (width, width), 1), bits)
        same = jnp.where(first == second, 1.0, 0.0).astype(f32)
        return jnp.dot(value, same, preferred_element_type=f32, precision=highest)

    def rows_of(image):
        return pl.ds(image * cols, cols)

    def norm_sums(buffer, z_ref):
        for image in range(nb):
            first = 0.0
            second = 0.0
            for part in range(z_ref.shape[0]):
                value = z_ref[part, rows_of(image), :]
                first = first + jnp.sum(value, 0, keepdims=True)
                second = second + jnp.sum(value * value, 0, keepdims=True)
            buffer[r, image : image + 1, :] = first
            buffer[r, nb + image : nb + image + 1, :] = second

    def norm_apply(total, z_ref, inv_ref, gain, shift, size, put):
        width = z_ref.shape[-1]
        number = nr * cols * z_ref.shape[0] * size
        sums = group_sum(total[: 2 * nb], size) / number
        mean = sums[:nb]
        inv = lax.rsqrt(sums[nb:] - mean * mean + norm_eps)
        inv_ref[:nb, :] = inv
        for part in range(z_ref.shape[0]):
            for image in range(nb):
                value = z_ref[part, rows_of(image), :]
                value = (value - mean[image : image + 1]) * inv[image : image + 1]
                z_ref[part, rows_of(image), :] = value
                normed = value * gain + shift
                put(part, image, (normed * sigmoid(normed)).astype(bf16))

    def back_sums(buffer, z_ref, dy_ref, gain, shift, grad_of):
        for image in range(nb):
            first = 0.0
            second = 0.0
            for part in range(z_ref.shape[0]):
                value = z_ref[part, rows_of(image), :]
                normed = value * gain + shift
                gate = sigmoid(normed)
                grad = grad_of(part, image) * gate * (1.0 + normed * (1.0 - gate))
                dy_ref[part, rows_of(image), :] = grad
                first = first + jnp.sum(grad, 0, keepdims=True)
                second = second + jnp.sum(grad * value, 0, keepdims=True)
            buffer[r, image : image + 1, :] = first
            buffer[r, nb + image : nb + image + 1, :] = second

    def back_apply(total, z_ref, dy_ref, inv_ref, gain, size, put):
        number = nr * cols * z_ref.shape[0] * size
        sums = group_sum(total[: 2 * nb] * gain, size) / number
        inv = inv_ref[:nb, :]
        for part in range(z_ref.shape[0]):
            for image in range(nb):
                one = slice(image, image + 1)
                two = slice(nb + image, nb + image + 1)
                value = dy_ref[part, rows_of(image), :] * gain - sums[one]
                value = value - z_ref[part, rows_of(image), :] * sums[two]
                put(part, image, (value * inv[one]).astype(bf16))
        shift_grad = jnp.sum(total[:nb], 0, keepdims=True)
        gain_grad = jnp.sum(total[nb : 2 * nb], 0, keepdims=True)
        return gain_grad, shift_grad

    x_one[1, b] = image_ref[...]
    x_skip[1:3, :, b] = skip_ref[...]
    x_lab[b] = lab_ref[...]
    move_image = Exchange(
        0,
        lambda j: x_one.at[1, j],
        lambda j: (x_one.at[1, j], x_one.at[0, j]),
        lambda j: (x_one.at[1, j], x_one.at[2, j]),
    )
    move_skip = Exchange(
        1,
        lambda j: x_skip.at[pl.ds(1, 2), :, j],
        lambda j: (x_skip.at[2, :, j], x_skip.at[0, :, j]),
        lambda j: (x_skip.at[1, :, j], x_skip.at[3, :, j]),
    )
    move_lab = Exchange(2, lambda j: x_lab.at[j])
    moves = (move_image, move_lab, move_skip)
    for move in moves:
        move.begin()
    stage = pltpu.make_async_copy(copies_ref, grad_ref, local_sem)
    stage.start()

    @pl.when(r == 0)
    def _():
        x_one[0] = jnp.zeros_like(x_one[0])
        x_skip[0] = jnp.zeros_like(x_skip[0])
        a_one[0] = jnp.zeros_like(a_one[0])
        u_full[0] = jnp.zeros_like(u_full[0])
        dz_low[0] = jnp.zeros_like(dz_low[0])
        dz_high[0] = jnp.zeros_like(dz_high[0])

    @pl.when(r == nr - 1)
    def _():
        x_one[2] = jnp.zeros_like(x_one[2])
        x_skip[3] = jnp.zeros_like(x_skip[3])
        a_one[2] = jnp.zeros_like(a_one[2])
        u_full[3] = jnp.zeros_like(u_full[3])
        dz_low[2] = jnp.zeros_like(dz_low[2])
        dz_high[3] = jnp.zeros_like(dz_high[3])

    stage.wait()
    for target, (out, width, taps, first) in zip((w_one, w_two, w_up, w_three), layers):
        across = width // TILE

        def arrange(n, _, target=target, out=out, taps=taps, first=first, across=across):
            ib = lax.rem(n, across)
            t = lax.rem(lax.div(n, across), taps)
            ob = lax.div(n, across * taps)
            target[
                pl.ds(pl.multiple_of(t * out + ob * TILE, TILE), TILE), lanes(ib, TILE)
            ] = grad_ref[place_ref[first + n]]
            return 0

        lax.fori_loop(0, out // TILE * taps * across, arrange, 0)
    for k in range(1, nb):
        for move in moves:
            move.hop(k)
    for move in moves:
        move.finish()

    gain_one, shift_one = wide_ref[0:1, :], wide_ref[1:2, :]
    gain_two, shift_two = wide_ref[2:3, :], wide_ref[3:4, :]
    gain_three, shift_three = narrow_ref[0:1, :], narrow_ref[1:2, :]
    size_low, size_high = C1 // GROUPS, C0 // GROUPS

    def conv_low(z_ref, weight, source):
        def tap(dx):
            total = 0.0
            for dy in range(3):
                first = (3 * dy + dx) * wide
                total = total + dot_nt(source(dy), weight[first : first + wide, :])
            return total

        z_ref[0] = tap(1)
        z_ref[0] += shift_down(tap(0))
        z_ref[0] += shift_up(tap(2))

    conv_low(z_one, w_one, lambda dy: x_one[dy].reshape(px, C0))
    reduce_one, reduce_two = reduce_wide.at[0], reduce_wide.at[1]
    norm_sums(reduce_one, z_one)
    count = 0.0
    for image in range(nb):
        for part in range(4):
            count = count + jnp.sum(x_lab[image, part, 2:3, :], 1, keepdims=True)
    reduce_one[r, 2 * nb : 2 * nb + 1, :] = jnp.broadcast_to(count, (1, wide))
    total = all_reduce(0, reduce_one)
    count = total[2 * nb : 2 * nb + 1, :1]

    def put_one(part, image, value):
        a_one[1, rows_of(image), lanes(b, wide)] = value

    norm_apply(total, z_one, inv_one, gain_one, shift_one, size_low, put_one)
    move = Exchange(
        3,
        lambda j: a_one.at[1, :, lanes(j, wide)],
        lambda j: (a_one.at[1, :, lanes(j, wide)], a_one.at[0, :, lanes(j, wide)]),
        lambda j: (a_one.at[1, :, lanes(j, wide)], a_one.at[2, :, lanes(j, wide)]),
    )
    move.begin()
    move.hops()
    move.finish()
    conv_low(z_two, w_two, lambda dy: a_one[dy])
    norm_sums(reduce_two, z_two)
    total = all_reduce(1, reduce_two)

    def put_two(part, image, value):
        a_two[rows_of(image), lanes(b, wide)] = value

    norm_apply(total, z_two, inv_two, gain_two, shift_two, size_low, put_two)
    move = Exchange(4, lambda j: a_two.at[:, lanes(j, wide)])
    move.begin()
    move.hops()
    move.finish()
    for part in range(4):
        u_full[1 + part // 2, part % 2, :, lanes(b, slim)] = dot_nt(
            a_two[...], w_up[part * slim : (part + 1) * slim, :]
        ).astype(bf16)
    move = Exchange(
        5,
        lambda j: u_full.at[pl.ds(1, 2), :, :, lanes(j, slim)],
        lambda j: (u_full.at[2, :, :, lanes(j, slim)], u_full.at[0, :, :, lanes(j, slim)]),
        lambda j: (u_full.at[1, :, :, lanes(j, slim)], u_full.at[3, :, :, lanes(j, slim)]),
    )
    move.begin()
    move.hops()
    move.finish()
    for e in range(2):
        found = []
        for f in range(2):
            total = 0.0
            for dy in range(3):
                weight = w_three[dy * taps_high : (dy + 1) * taps_high, :]
                total = total + dot_nt(u_full[e + dy, f], weight[:, :C0])
                total = total + dot_nt(x_skip[e + dy, f].reshape(px, C0), weight[:, C0:])
            found.append(total)
        even, odd = found
        z_three[2 * e] = (
            even[:, slim : 2 * slim] + shift_down(odd[:, :slim]) + odd[:, 2 * slim :]
        )
        z_three[2 * e + 1] = (
            odd[:, slim : 2 * slim] + even[:, :slim] + shift_up(even[:, 2 * slim :])
        )
    reduce_three, reduce_four = reduce_narrow.at[0], reduce_narrow.at[1]
    norm_sums(reduce_three, z_three)
    total = all_reduce(2, reduce_three)
    a_three = send_high

    def put_three(part, image, value):
        a_three[part, 0, rows_of(image), :] = value

    norm_apply(total, z_three, inv_three, gain_three, shift_three, size_high, put_three)
    head_low = narrow_ref[8:16, :].astype(bf16)
    head = head_low.astype(f32)
    for part in range(4):
        for image in range(nb):
            logit[b, part * nb + image] = dot_nt(
                head_low, a_three[part, 0, rows_of(image), :]
            )
    spread = Spread(all_send.at[0], all_recv.at[0], lambda other: logit.at[b], lambda j: logit.at[j])
    spread.begin()
    spread.finish()
    loss = jnp.zeros((1, cols), f32)
    bias_grad = [jnp.zeros((1, cols), f32), jnp.zeros((1, cols), f32)]
    head_grad = jnp.zeros((8, slim), f32)
    level = lax.broadcasted_iota(jnp.int32, (8, cols), 0)

    def head_of(part, image):
        tile = logit[0, part * nb + image]
        for j in range(1, nb):
            tile = tile + logit[j, part * nb + image]
        first = tile[0:1, :] + bias_ref[0]
        second = tile[1:2, :] + bias_ref[1]
        scale = x_lab[image, part, 0:1, :]
        label = x_lab[image, part, 1:2, :]
        largest = jnp.maximum(first, second)
        log_total = jnp.log(jnp.exp(first - largest) + jnp.exp(second - largest)) + largest
        picked = first * (1.0 - label) + second * label
        unit = scale / count
        return (
            scale * (log_total - picked),
            (jnp.exp(first - log_total) - (1.0 - label)) * unit,
            (jnp.exp(second - log_total) - label) * unit,
        )

    for part in range(4):
        for image in range(nb):
            cost, first, second = head_of(part, image)
            loss = loss + cost
            bias_grad = [bias_grad[0] + first, bias_grad[1] + second]
            tile = jnp.where(level == 0, first, jnp.where(level == 1, second, 0.0))
            logit[0, part * nb + image] = tile
            head_grad = head_grad + jnp.dot(
                tile,
                a_three[part, 0, rows_of(image), :].astype(f32),
                preferred_element_type=f32,
                precision=highest,
            )

    def grad_three(part, image):
        return lax.dot_general(
            logit[0, part * nb + image],
            head,
            (((0,), (0,)), ((), ())),
            preferred_element_type=f32,
            precision=highest,
        )

    reduce_four[r, 2 * nb : 2 * nb + 8, :] = head_grad
    for row, value in enumerate([loss] + bias_grad):
        reduce_four[r, 2 * nb + 2 + row : 2 * nb + 3 + row, :] = jnp.broadcast_to(
            jnp.sum(value, 1, keepdims=True), (1, slim)
        )
    back_sums(reduce_four, z_three, dy_high, gain_three, shift_three, grad_three)
    total = all_reduce(3, reduce_four)

    def put_high(part, image, value):
        dz_high[1 + part // 2, part % 2, rows_of(image), :] = value

    gain_grad, shift_grad = back_apply(
        total, z_three, dy_high, inv_three, gain_three, size_high, put_high
    )
    sums_ref[b] = jnp.zeros_like(sums_ref[b])
    sums_ref[b, 4:5, :slim] = gain_grad
    sums_ref[b, 4:5, slim : 2 * slim] = shift_grad
    sums_ref[b, 5:6, :slim] = total[2 * nb : 2 * nb + 1]
    sums_ref[b, 5:6, slim : 2 * slim] = total[2 * nb + 1 : 2 * nb + 2]
    for row in range(3):
        sums_ref[b, 6 + row : 7 + row, :slim] = total[2 * nb + 2 + row : 2 * nb + 3 + row]
    sums_ref[b, 9:10, :] = jnp.broadcast_to(count, (1, wide))

    def edges(number, source_up, target_up, source_down, target_down):
        def higher():
            return remote(
                source_up,
                target_up,
                edge_send.at[number, 0],
                edge_recv.at[number, 0],
                ring(r + 1, nr),
                b,
            )

        def lower():
            return remote(
                source_down,
                target_down,
                edge_send.at[number, 1],
                edge_recv.at[number, 1],
                ring(r - 1, nr),
                b,
            )

        def begin():
            @pl.when(r + 1 < nr)
            def _():
                higher().start()

            @pl.when(r > 0)
            def _():
                lower().start()

        def finish():
            @pl.when(r + 1 < nr)
            def _():
                higher().wait_send()
                lower().wait_recv()

            @pl.when(r > 0)
            def _():
                lower().wait_send()
                higher().wait_recv()

        return begin, finish

    def widen_high(row):
        even, odd = dz_high[row, 0], dz_high[row, 1]
        shifted_high[row, 0, :, :slim] = odd
        shifted_high[row, 0, :, slim : 2 * slim] = even
        shifted_high[row, 0, :, 2 * slim :] = shift_down(odd.astype(f32)).astype(bf16)
        shifted_high[row, 1, :, :slim] = shift_up(even.astype(f32)).astype(bf16)
        shifted_high[row, 1, :, slim : 2 * slim] = odd
        shifted_high[row, 1, :, 2 * slim :] = even

    begin, finish = edges(0, dz_high.at[2], dz_high.at[0], dz_high.at[1], dz_high.at[3])
    begin()
    widen_high(1)
    widen_high(2)
    finish()
    widen_high(0)
    widen_high(3)
    spreads = []
    own_high = []
    for part in range(4):
        e, f = part // 2, part % 2
        total = 0.0
        for dy in range(3):
            total = total + dot_nn(
                shifted_high[e + 2 - dy, f], w_three[dy * taps_high : (dy + 1) * taps_high, :C0]
            )
        for j in range(nb):
            send_high[part, j] = total[:, j * slim : (j + 1) * slim].astype(bf16)

            @pl.when(b == j)
            def _():
                dy_high[part] = total[:, j * slim : (j + 1) * slim]

        spread = Spread(
            high_send.at[part],
            high_recv.at[part],
            lambda other, part=part: send_high.at[part, other],
            lambda j, part=part: recv_high.at[part, j],
        )
        spread.begin()
        spreads.append(spread)

    def put_grad(first, across, value, rows, start):
        for row, number in rows:
            for k in range(value.shape[1] // TILE):
                grad_ref[first + number * across + start + k] = value[
                    row : row + TILE, k * TILE : (k + 1) * TILE
                ].astype(bf16)

    out, width, taps, first = layers[3]
    for e in range(2):
        for f in range(2):
            turned_high[e, :, f * px : (f + 1) * px] = shifted_high[1 + e, f].T
    for dy in range(3):
        rows = [(dx * slim, 3 * dy + dx) for dx in range(3)]
        for half, source in enumerate((u_full, x_skip)):
            total = 0.0
            for e in range(2):
                for f in range(2):
                    value = source[e + dy, f].reshape(px, C0)
                    total = total + dot_nn(turned_high[e, :, f * px : (f + 1) * px], value)
            put_grad(first, width // TILE, total, rows, half * (C0 // TILE))
    for part in range(4):
        spreads[part].finish()
        total = dy_high[part]
        for step in range(1, nb):
            total = total + recv_high[part, ring(b + step, nb)].astype(f32)
        dub[:, part * slim : (part + 1) * slim] = total.astype(bf16)

    def input_low(number, product):
        for j in range(nb):
            total = product(j)
            send_low[j] = total.astype(bf16)

            @pl.when(b == j)
            def _():
                dy_low[0] = total

        spread = Spread(
            all_send.at[number],
            all_recv.at[number],
            lambda other: send_low.at[other],
            lambda j: recv_low.at[number - 1, j],
        )
        spread.begin()

        def finish():
            spread.finish()
            total = dy_low[0]
            for step in range(1, nb):
                total = total + recv_low[number - 1, ring(b + step, nb)].astype(f32)
            dy_low[0] = total

        return finish

    finish_sum = input_low(
        1, lambda j: dot_nn(dub[...], w_up[:, j * wide : (j + 1) * wide])
    )
    out, width, taps, first = layers[2]
    turned_low[: 4 * slim, :] = dub[...].T
    for j in range(nb):
        total = dot_nn(turned_low[: 4 * slim, :], a_two[:, j * wide : (j + 1) * wide])
        rows = [(part * slim, part) for part in range(4)]
        put_grad(first, width // TILE, total, rows, j * (wide // TILE))
    finish_sum()

    def back_low(number, z_ref, inv_ref, gain, shift):
        def grad_of(part, image):
            return dy_low[0, rows_of(image), :]

        buffer = reduce_wide.at[number - 2]
        back_sums(buffer, z_ref, dy_low, gain, shift, grad_of)
        total = all_reduce(number, buffer)

        def put(part, image, value):
            dz_low[1, rows_of(image), :] = value

        return back_apply(total, z_ref, dy_low, inv_ref, gain, size_low, put)

    def widen_low(row):
        value = dz_low[row]
        wider = value.astype(f32)
        shifted_low[row, :, :wide] = shift_up(wider).astype(bf16)
        shifted_low[row, :, wide : 2 * wide] = value
        shifted_low[row, :, 2 * wide :] = shift_down(wider).astype(bf16)

    def weight_low(number, source):
        out, width, taps, first = layers[number]
        turned_low[...] = shifted_low[1].T
        chunk = 2 * TILE
        for dy in range(3):
            rows = []
            for dx in range(3):
                for ob in range(wide // TILE):
                    rows.append((dx * wide + ob * TILE, ob * taps + 3 * dy + dx))
            for j in range(width // chunk):
                total = dot_nn(turned_low[...], source(dy, j * chunk, chunk))
                put_grad(first, width // TILE, total, rows, j * (chunk // TILE))

    gain_grad, shift_grad = back_low(4, z_two, inv_two, gain_two, shift_two)
    sums_ref[b, 2:3, :] = gain_grad
    sums_ref[b, 3:4, :] = shift_grad
    begin, finish = edges(1, dz_low.at[1], dz_low.at[0], dz_low.at[1], dz_low.at[2])
    begin()
    widen_low(1)
    finish()
    widen_low(0)
    widen_low(2)

    def product_two(j):
        total = 0.0
        for dy in range(3):
            total = total + dot_nn(
                shifted_low[2 - dy],
                w_two[3 * dy * wide : 3 * (dy + 1) * wide, j * wide : (j + 1) * wide],
            )
        return total

    finish_sum = input_low(2, product_two)
    weight_low(1, lambda dy, start, size: a_one[dy, :, start : start + size])
    finish_sum()
    gain_grad, shift_grad = back_low(5, z_one, inv_one, gain_one, shift_one)
    sums_ref[b, 0:1, :] = gain_grad
    sums_ref[b, 1:2, :] = shift_grad
    spread = Spread(
        all_send.at[3], all_recv.at[3], lambda other: sums_ref.at[b], lambda j: sums_ref.at[j]
    )
    spread.begin()
    widen_low(1)
    weight_low(0, lambda dy, start, size: x_one[dy].reshape(px, C0)[:, start : start + size])
    spread.finish()


def run_step(copies, place, bias, image, skip, lab, wide_rows, narrow_rows):
    nr, nb = lax.axis_size("rows"), lax.axis_size("blk")
    cols = image.shape[0]
    px = nb * cols
    wide, slim = C1 // nb, C0 // nb
    vmem = pl.BlockSpec(memory_space=pltpu.VMEM)
    smem = pl.BlockSpec(memory_space=pltpu.SMEM)
    dma = pltpu.SemaphoreType.DMA
    scratch = [
        pltpu.VMEM((3, nb, cols, C0), bf16),
        pltpu.VMEM((4, 2, nb, cols, C0), bf16),
        pltpu.VMEM((nb, 4, 8, cols), f32),
        pltpu.VMEM((9 * wide, C0), bf16),
        pltpu.VMEM((9 * wide, C1), bf16),
        pltpu.VMEM((4 * slim, C1), bf16),
        pltpu.VMEM((9 * slim, 2 * C0), bf16),
        pltpu.VMEM((3, px, C1), bf16),
        pltpu.VMEM((px, C1), bf16),
        pltpu.VMEM((4, 2, px, C0), bf16),
        pltpu.VMEM((1, px, wide), f32),
        pltpu.VMEM((1, px, wide), f32),
        pltpu.VMEM((4, px, slim), f32),
        pltpu.VMEM((1, px, wide), f32),
        pltpu.VMEM((4, px, slim), f32),
        pltpu.VMEM((8, wide), f32),
        pltpu.VMEM((8, wide), f32),
        pltpu.VMEM((8, slim), f32),
        pltpu.VMEM((3, px, wide), bf16),
        pltpu.VMEM((4, 2, px, slim), bf16),
        pltpu.VMEM((3, px, 3 * wide), bf16),
        pltpu.VMEM((4, 2, px, 3 * slim), bf16),
        pltpu.VMEM((3 * wide, px), bf16),
        pltpu.VMEM((2, 3 * slim, 2 * px), bf16),
        pltpu.VMEM((px, 4 * slim), bf16),
        pltpu.VMEM((4, nb, px, slim), bf16),
        pltpu.VMEM((4, nb, px, slim), bf16),
        pltpu.VMEM((nb, px, wide), bf16),
        pltpu.VMEM((2, nb, px, wide), bf16),
        pltpu.VMEM((nb, 4 * nb, 8, cols), f32),
        pltpu.VMEM((4, nr, 2 * nb + 8, wide), f32),
        pltpu.VMEM((2, nr, 2 * nb + 8, slim), f32),
        dma(()),
        dma((6, nb, 2)),
        dma((6, nb)),
        dma((6, nb, 2)),
        dma((6, nb, 2)),
        dma((6, nr)),
        dma((6, nr)),
        dma((4, nb)),
        dma((4, nb)),
        dma((4, nb)),
        dma((4, nb)),
        dma((2, 2)),
        dma((2, 2)),
    ]
    return pl.pallas_call(
        functools.partial(step_kernel, nr, nb, cols),
        out_shape=(
            jax.ShapeDtypeStruct(copies.shape, bf16),
            jax.ShapeDtypeStruct((nb, 16, wide), f32),
        ),
        in_specs=[pl.BlockSpec(memory_space=pl.ANY), smem, smem, vmem, vmem, vmem, vmem, vmem],
        out_specs=(vmem, vmem),
        scratch_shapes=scratch,
        compiler_params=pltpu.CompilerParams(
            collective_id=0, has_side_effects=True, vmem_limit_bytes=60 * 2**20
        ),
    )(copies, place, bias, image, skip, lab, wide_rows, narrow_rows)


LANES = 128


def inverse_factor_kernel(stat_ref, inverse_ref, factor_ref):
    order = stat_ref.shape[0]
    tile = (8, LANES)
    sub = lax.broadcasted_iota(jnp.int32, tile, 0)

    def eliminate(source_ref, base, start, first, count, accs):
        def body(group, accs):
            top = pl.multiple_of(group * 8, 8)
            for unit in range(8):
                value = source_ref[top + unit, pl.ds(start, 8), :]
                accs = tuple(
                    accs[c]
                    - value
                    * jnp.broadcast_to(factor_ref[top + unit, pl.ds(base + c, 1), :], tile)
                    for c in range(8)
                )
            return accs

        return list(lax.fori_loop(first, count, body, tuple(accs)))

    def block(kb, _):
        base = pl.multiple_of(kb * 8, 8)
        accs = [stat_ref[base + c, pl.ds(base, 8), :] for c in range(8)]
        accs = eliminate(factor_ref, base, base, 0, kb, accs)
        scale = []
        coef = {}
        for c in range(8):
            scale.append(jnp.broadcast_to(lax.rsqrt(accs[c][c : c + 1, :]), tile))
            accs[c] = accs[c] * scale[c]
            for d in range(c + 1, 8):
                coef[(c, d)] = jnp.broadcast_to(accs[c][d : d + 1, :], tile)
                accs[d] = accs[d] - accs[c] * coef[(c, d)]
        for c in range(8):
            factor_ref[base + c, pl.ds(base, 8), :] = jnp.where(sub >= c, accs[c], 0.0)

        def finish(accs, target_ref, start):
            accs = list(accs)
            for c in range(8):
                for e in range(c):
                    accs[c] = accs[c] - accs[e] * coef[(e, c)]
                accs[c] = accs[c] * scale[c]
                target_ref[base + c, pl.ds(start, 8), :] = accs[c]

        def below(group, _):
            start = pl.multiple_of(group * 8, 8)
            accs = [stat_ref[base + c, pl.ds(start, 8), :] for c in range(8)]
            finish(eliminate(factor_ref, base, start, 0, kb, accs), factor_ref, start)
            return 0

        def left(group, _):
            start = pl.multiple_of(group * 8, 8)
            accs = [jnp.zeros(tile, jnp.float32) for c in range(8)]
            finish(eliminate(inverse_ref, base, start, group, kb, accs), inverse_ref, start)
            return 0

        def clear(group, _):
            start = pl.multiple_of(group * 8, 8)
            for c in range(8):
                inverse_ref[base + c, pl.ds(start, 8), :] = jnp.zeros(tile, jnp.float32)
            return 0

        lax.fori_loop(kb + 1, order // 8, below, 0)
        lax.fori_loop(0, kb, left, 0)
        finish([jnp.where(sub == c, 1.0, 0.0) for c in range(8)], inverse_ref, base)
        lax.fori_loop(kb + 1, order // 8, clear, 0)
        return 0

    lax.fori_loop(0, order // 8, block, 0)


def inverse_factors(grams):
    count, order = grams.shape[0], grams.shape[-1]
    chunks = -(-count // LANES)
    spare = chunks * LANES - count
    eye = jnp.broadcast_to(jnp.eye(order, dtype=jnp.float32), (spare, order, order))
    lanes = jnp.concatenate([grams, eye], 0).transpose(1, 2, 0)
    block = pl.BlockSpec((order, order, LANES), lambda chunk: (0, 0, chunk))
    result = pl.pallas_call(
        inverse_factor_kernel,
        grid=(chunks,),
        out_shape=jax.ShapeDtypeStruct(lanes.shape, jnp.float32),
        in_specs=[block],
        out_specs=block,
        scratch_shapes=[pltpu.VMEM((order, order, LANES), jnp.float32)],
        compiler_params=pltpu.CompilerParams(vmem_limit_bytes=56 * 2**20),
    )(lanes)
    return result.transpose(2, 0, 1)[:count]


def orthonormal(stats, bases):
    products = [
        jnp.matmul(stat, basis, precision=highest)[0] for stat, basis in zip(stats, bases)
    ]
    grams = [
        jnp.matmul(jnp.swapaxes(product, -1, -2), product, precision=highest)
        for product in products
    ]
    inverses = inverse_factors(jnp.concatenate(grams, 0))
    count = products[0].shape[0]
    return [
        jnp.matmul(product, jnp.swapaxes(inverse, -1, -2), precision=highest)[None]
        for product, inverse in zip(products, (inverses[:count], inverses[count:]))
    ]


def soap_update(grads, master, first, second, left, right, left_stat, right_stat):
    rotated = jnp.matmul(
        jnp.matmul(jnp.swapaxes(left, -1, -2), grads, precision=highest), right, precision=highest
    )
    first_new = beta_one * first + (1.0 - beta_one) * rotated
    second_new = beta_two * second + (1.0 - beta_two) * rotated * rotated
    direction = (
        first_new
        / (1.0 - beta_one**STEP)
        / (jnp.sqrt(second_new / (1.0 - beta_two**STEP)) + adam_eps)
    )
    update = jnp.matmul(
        jnp.matmul(left, direction, precision=highest),
        jnp.swapaxes(right, -1, -2),
        precision=highest,
    )
    master_new = master - soap_rate * (update + soap_decay * master)
    left_new_stat = beta_stat * left_stat + (1.0 - beta_stat) * jnp.matmul(
        grads, jnp.swapaxes(grads, -1, -2), precision=highest
    )
    right_new_stat = beta_stat * right_stat + (1.0 - beta_stat) * jnp.matmul(
        jnp.swapaxes(grads, -1, -2), grads, precision=highest
    )
    left_new, right_new = orthonormal((left_new_stat, right_new_stat), (left, right))
    return (
        master_new,
        first_new,
        second_new,
        left_new,
        right_new,
        left_new_stat,
        right_new_stat,
    )


def adam_small(grads, value, first, second):
    first_new = beta_one * first + (1.0 - beta_one) * grads
    second_new = beta_two * second + (1.0 - beta_two) * grads * grads
    direction = (
        first_new
        / (1.0 - beta_one**STEP)
        / (jnp.sqrt(second_new / (1.0 - beta_two**STEP)) + adam_eps)
    )
    return (first_new, second_new, value - small_rate * (direction + small_decay * value))


def local(
    image,
    skip,
    labels,
    weight_map,
    valid,
    owner,
    master,
    first_moment,
    second_moment,
    left_basis,
    right_basis,
    left_stat,
    right_stat,
    norm_params,
    norm_first,
    norm_second,
    head_bias,
    bias_first,
    bias_second,
):
    shards = lax.axis_size("blk")
    shard = lax.axis_index("blk")
    cols = image.shape[2]
    copies = lax.all_gather(master.astype(bf16), "rows", axis=1, tiled=True)[0]
    slots = jnp.arange(owner.shape[0])
    place = jnp.sum(jnp.where(owner[None, :] == slots[:, None], slots[None, :], 0), 1)
    widths = (C1, C1, C1, C1, C0, C0)
    rows = []
    offset = 0
    for width in widths:
        part = width // shards
        rows.append(lax.dynamic_slice_in_dim(norm_params, offset + shard * part, part))
        offset = offset + width
    heads = norm_params[offset:].reshape(C0, 2)
    part = C0 // shards
    heads = lax.dynamic_slice_in_dim(heads, shard * part, part).T
    wide_rows = jnp.pad(jnp.stack(rows[:4]), ((0, 4), (0, 0)))
    narrow_rows = jnp.concatenate(
        [jnp.pad(jnp.stack(rows[4:]), ((0, 6), (0, 0))), jnp.pad(heads, ((0, 6), (0, 0)))]
    )
    valid_float = valid.astype(f32)
    scales = valid_float * weight_map.astype(f32) * 0.125
    lab = jnp.stack([scales, labels.astype(f32), valid_float]).reshape(3, 2, cols, 2)
    lab = lab.transpose(1, 3, 0, 2).reshape(4, 3, cols)
    lab = jnp.pad(lab, ((0, 0), (0, 5), (0, 0)))
    skip = skip.reshape(2, cols, 2, C0).transpose(0, 2, 1, 3)
    blocks, sums = run_step(
        copies, place.astype(jnp.int32), head_bias, image[0, 0], skip, lab, wide_rows, narrow_rows
    )
    grads = lax.psum_scatter(
        blocks[owner].astype(f32), "rows", scatter_dimension=0, tiled=True
    )[None]
    loss_sum, valid_count = sums[0, 6, 0], sums[0, 9, 0]
    grad_bias = sums[0, 7:9, 0]
    grad_head = jnp.stack([sums[:, 5, :part].reshape(-1), sums[:, 5, part : 2 * part].reshape(-1)], 1)
    small = jnp.concatenate(
        [sums[:, row].reshape(-1) for row in range(4)]
        + [
            sums[:, 4, :part].reshape(-1),
            sums[:, 4, part : 2 * part].reshape(-1),
            grad_head.reshape(-1),
        ]
    )
    soap = soap_update(
        grads, master, first_moment, second_moment, left_basis, right_basis, left_stat, right_stat
    )
    norm_new = adam_small(small, norm_params, norm_first, norm_second)
    bias_new = adam_small(grad_bias, head_bias, bias_first, bias_second)
    return (
        loss_sum,
        valid_count,
        soap[0],
        soap[0].astype(jnp.bfloat16),
        soap[1],
        soap[2],
        soap[3],
        soap[4],
        soap[5],
        soap[6],
        norm_new[0],
        norm_new[1],
        norm_new[2],
        bias_new[0],
        bias_new[1],
        bias_new[2],
    )


def solution(mesh):
    placed = (
        P("blk", "rows", None, None),
        P("blk", "rows", None, None),
        P("blk", "rows", None),
        P("blk", "rows", None),
        P("blk", "rows", None),
        P(),
        P("blk", "rows", None, None),
        P("blk", "rows", None, None),
        P("blk", "rows", None, None),
        P("blk", "rows", None, None),
        P("blk", "rows", None, None),
        P("blk", "rows", None, None),
        P("blk", "rows", None, None),
        P(),
        P(),
        P(),
        P(),
        P(),
        P(),
    )
    return jax.shard_map(
        local,
        mesh=mesh,
        in_specs=placed,
        out_specs=(
            P(),
            P(),
            P("blk", "rows", None, None),
            P("blk", "rows", None, None),
            P("blk", "rows", None, None),
            P("blk", "rows", None, None),
            P("blk", "rows", None, None),
            P("blk", "rows", None, None),
            P("blk", "rows", None, None),
            P("blk", "rows", None, None),
            P(),
            P(),
            P(),
            P(),
            P(),
            P(),
        ),
        check_vma=False,
    )
```

```python
import functools

import jax
import jax.numpy as jnp
from jax import lax
from jax.experimental import pallas as pl
from jax.experimental.pallas import tpu as pltpu
from jax.sharding import PartitionSpec as P

C0 = 512
C1 = 1024
GROUPS = 32
STEP = 10


beta_one = 0.9
beta_two = 0.999
beta_stat = 0.95
adam_eps = 1e-08
norm_eps = 1e-05
soap_rate = 0.008
soap_decay = 0.01
small_rate = 0.4
small_decay = 0.01
highest = lax.Precision.HIGHEST


MESH = pl.DeviceIdType.MESH
bf16 = jnp.bfloat16
f32 = jnp.float32
TILE = 128


def dot_nt(left, right):
    return lax.dot_general(left, right, (((1,), (1,)), ((), ())), preferred_element_type=f32)


def dot_nn(left, right):
    return jnp.dot(left, right, preferred_element_type=f32)


def sigmoid(value):
    return 1.0 / (1.0 + jnp.exp(-value))


def block_layers(nb):
    result = []
    first = 0
    for in_width, out_width, taps in ((C0, C1, 9), (C1, C1, 9), (C1, C0, 4), (2 * C0, C0, 9)):
        out = out_width // nb
        result.append((out, in_width, taps, first))
        first = first + out // TILE * taps * (in_width // TILE)
    return result


def step_kernel(
    nr,
    nb,
    cols,
    copies_ref,
    place_ref,
    bias_ref,
    image_ref,
    skip_ref,
    lab_ref,
    wide_ref,
    narrow_ref,
    grad_ref,
    sums_ref,
    x_one,
    x_skip,
    x_lab,
    w_one,
    w_two,
    w_up,
    w_three,
    a_one,
    a_two,
    u_full,
    z_one,
    z_two,
    z_three,
    dy_low,
    dy_high,
    inv_one,
    inv_two,
    inv_three,
    dz_low,
    dz_high,
    shifted_low,
    shifted_high,
    turned_low,
    turned_high,
    dub,
    send_high,
    recv_high,
    send_low,
    recv_low,
    logit,
    reduce_wide,
    reduce_narrow,
    local_sem,
    line_send,
    line_recv,
    halo_send,
    halo_recv,
    red_send,
    red_recv,
    all_send,
    all_recv,
    high_send,
    high_recv,
    edge_send,
    edge_recv,
):
    r = lax.axis_index("rows")
    b = lax.axis_index("blk")
    px = nb * cols
    wide = C1 // nb
    slim = C0 // nb
    taps_high = 3 * slim
    layers = block_layers(nb)

    def remote(src, dst, send, recv, rows, blk):
        return pltpu.make_async_remote_copy(
            src_ref=src,
            dst_ref=dst,
            send_sem=send,
            recv_sem=recv,
            device_id={"rows": rows, "blk": blk},
            device_id_type=MESH,
        )

    def lanes(index, size):
        return pl.ds(pl.multiple_of(index * size, TILE), size)

    def ring(index, count):
        return lax.rem(index + count, count)

    barrier = pltpu.get_barrier_semaphore()

    def greet_rows(step, _):
        pl.semaphore_signal(
            barrier, inc=1, device_id={"rows": ring(r + step, nr), "blk": b}, device_id_type=MESH
        )
        return 0

    lax.fori_loop(1, nr, greet_rows, 0)
    for step in range(1, nb):
        pl.semaphore_signal(
            barrier, inc=1, device_id={"rows": r, "blk": ring(b + step, nb)}, device_id_type=MESH
        )
    pl.semaphore_wait(barrier, nr - 1 + nb - 1)

    class Exchange:
        def __init__(self, number, piece, up=None, down=None):
            self.number, self.piece, self.up, self.down = number, piece, up, down

        def right(self, j):
            return remote(
                self.piece(j),
                self.piece(j),
                line_send.at[self.number, j, 0],
                line_recv.at[self.number, j],
                r,
                ring(b + 1, nb),
            )

        def left(self, j):
            return remote(
                self.piece(j),
                self.piece(j),
                line_send.at[self.number, j, 1],
                line_recv.at[self.number, j],
                r,
                ring(b - 1, nb),
            )

        def higher(self, j):
            src, dst = self.up(j)
            return remote(
                src,
                dst,
                halo_send.at[self.number, j, 0],
                halo_recv.at[self.number, j, 0],
                ring(r + 1, nr),
                b,
            )

        def lower(self, j):
            src, dst = self.down(j)
            return remote(
                src,
                dst,
                halo_send.at[self.number, j, 1],
                halo_recv.at[self.number, j, 1],
                ring(r - 1, nr),
                b,
            )

        def halos(self, j):
            if self.up is None:
                return

            @pl.when(r + 1 < nr)
            def _():
                self.higher(j).start()

            @pl.when(r > 0)
            def _():
                self.lower(j).start()

        def begin(self):
            @pl.when(b + 1 < nb)
            def _():
                self.right(b).start()

            @pl.when(b > 0)
            def _():
                self.left(b).start()

            self.halos(b)

        def hop(self, k):
            @pl.when(b >= k)
            def _():
                self.right(b - k).wait_recv()

                @pl.when(b + 1 < nb)
                def _():
                    self.right(b - k).start()

                self.halos(b - k)

            @pl.when(b + k < nb)
            def _():
                self.left(b + k).wait_recv()

                @pl.when(b > 0)
                def _():
                    self.left(b + k).start()

                self.halos(b + k)

        def hops(self):
            for k in range(1, nb):
                self.hop(k)

        def finish(self):
            for k in range(nb):

                @pl.when((b >= k) & (b + 1 < nb))
                def _():
                    self.right(b - k).wait_send()

                @pl.when((b + k < nb) & (b > 0))
                def _():
                    self.left(b + k).wait_send()

            if self.up is None:
                return
            for j in range(nb):

                @pl.when(r + 1 < nr)
                def _():
                    self.higher(j).wait_send()
                    self.lower(j).wait_recv()

                @pl.when(r > 0)
                def _():
                    self.lower(j).wait_send()
                    self.higher(j).wait_recv()

    def all_reduce(number, buffer):
        def start(step, _):
            remote(
                buffer.at[r],
                buffer.at[r],
                red_send.at[number, step],
                red_recv.at[number, r],
                ring(r + step, nr),
                b,
            ).start()
            return 0

        def wait(step, _):
            source = ring(r + step, nr)
            copy = remote(
                buffer.at[source],
                buffer.at[source],
                red_send.at[number, step],
                red_recv.at[number, source],
                source,
                b,
            )
            copy.wait_recv()
            copy.wait_send()
            return 0

        lax.fori_loop(1, nr, start, 0)
        lax.fori_loop(1, nr, wait, 0)
        return lax.fori_loop(1, nr, lambda k, total: total + buffer[k], buffer[0])

    class Spread:
        def __init__(self, send, recv, source, target):
            self.send, self.recv, self.source, self.target = send, recv, source, target

        def copy(self, step):
            other = ring(b + step, nb)
            return remote(
                self.source(other),
                self.target(b),
                self.send.at[step],
                self.recv.at[b],
                r,
                other,
            )

        def begin(self):
            for step in range(1, nb):
                self.copy(step).start()

        def finish(self):
            for step in range(1, nb):
                other = ring(b + step, nb)
                remote(
                    self.source(other),
                    self.target(other),
                    self.send.at[step],
                    self.recv.at[other],
                    r,
                    other,
                ).wait_recv()
                self.copy(step).wait_send()

    position = lax.rem(lax.broadcasted_iota(jnp.int32, (px, TILE), 0), cols)

    def mask_of(value, column):
        hit = position[:, :1] == column
        return jnp.where(hit, 0.0, value)

    def shift_down(value):
        return mask_of(pltpu.roll(value, 1, 0), 0)

    def shift_up(value):
        return mask_of(pltpu.roll(value, px - 1, 0), cols - 1)

    def group_sum(value, size):
        width = value.shape[-1]
        bits = size.bit_length() - 1
        first = lax.shift_right_logical(lax.broadcasted_iota(jnp.int32, (width, width), 0), bits)
        second = lax.shift_right_logical(lax.broadcasted_iota(jnp.int32, (width, width), 1), bits)
        same = jnp.where(first == second, 1.0, 0.0).astype(f32)
        return jnp.dot(value, same, preferred_element_type=f32, precision=highest)

    def rows_of(image):
        return pl.ds(image * cols, cols)

    def norm_sums(buffer, z_ref):
        for image in range(nb):
            first = 0.0
            second = 0.0
            for part in range(z_ref.shape[0]):
                value = z_ref[part, rows_of(image), :]
                first = first + jnp.sum(value, 0, keepdims=True)
                second = second + jnp.sum(value * value, 0, keepdims=True)
            buffer[r, image : image + 1, :] = first
            buffer[r, nb + image : nb + image + 1, :] = second

    def norm_apply(total, z_ref, inv_ref, gain, shift, size, put):
        width = z_ref.shape[-1]
        number = nr * cols * z_ref.shape[0] * size
        sums = group_sum(total[: 2 * nb], size) / number
        mean = sums[:nb]
        inv = lax.rsqrt(sums[nb:] - mean * mean + norm_eps)
        inv_ref[:nb, :] = inv
        for part in range(z_ref.shape[0]):
            for image in range(nb):
                value = z_ref[part, rows_of(image), :]
                value = (value - mean[image : image + 1]) * inv[image : image + 1]
                z_ref[part, rows_of(image), :] = value
                normed = value * gain + shift
                put(part, image, (normed * sigmoid(normed)).astype(bf16))

    def back_sums(buffer, z_ref, dy_ref, gain, shift, grad_of):
        for image in range(nb):
            first = 0.0
            second = 0.0
            for part in range(z_ref.shape[0]):
                value = z_ref[part, rows_of(image), :]
                normed = value * gain + shift
                gate = sigmoid(normed)
                grad = grad_of(part, image) * gate * (1.0 + normed * (1.0 - gate))
                dy_ref[part, rows_of(image), :] = grad
                first = first + jnp.sum(grad, 0, keepdims=True)
                second = second + jnp.sum(grad * value, 0, keepdims=True)
            buffer[r, image : image + 1, :] = first
            buffer[r, nb + image : nb + image + 1, :] = second

    def back_apply(total, z_ref, dy_ref, inv_ref, gain, size, put):
        number = nr * cols * z_ref.shape[0] * size
        sums = group_sum(total[: 2 * nb] * gain, size) / number
        inv = inv_ref[:nb, :]
        for part in range(z_ref.shape[0]):
            for image in range(nb):
                one = slice(image, image + 1)
                two = slice(nb + image, nb + image + 1)
                value = dy_ref[part, rows_of(image), :] * gain - sums[one]
                value = value - z_ref[part, rows_of(image), :] * sums[two]
                put(part, image, (value * inv[one]).astype(bf16))
        shift_grad = jnp.sum(total[:nb], 0, keepdims=True)
        gain_grad = jnp.sum(total[nb : 2 * nb], 0, keepdims=True)
        return gain_grad, shift_grad

    x_one[1, b] = image_ref[...]
    x_skip[1:3, :, b] = skip_ref[...]
    x_lab[b] = lab_ref[...]
    move_image = Exchange(
        0,
        lambda j: x_one.at[1, j],
        lambda j: (x_one.at[1, j], x_one.at[0, j]),
        lambda j: (x_one.at[1, j], x_one.at[2, j]),
    )
    move_skip = Exchange(
        1,
        lambda j: x_skip.at[pl.ds(1, 2), :, j],
        lambda j: (x_skip.at[2, :, j], x_skip.at[0, :, j]),
        lambda j: (x_skip.at[1, :, j], x_skip.at[3, :, j]),
    )
    move_lab = Exchange(2, lambda j: x_lab.at[j])
    moves = (move_image, move_lab, move_skip)
    for move in moves:
        move.begin()
    stage = pltpu.make_async_copy(copies_ref, grad_ref, local_sem)
    stage.start()

    @pl.when(r == 0)
    def _():
        x_one[0] = jnp.zeros_like(x_one[0])
        x_skip[0] = jnp.zeros_like(x_skip[0])
        a_one[0] = jnp.zeros_like(a_one[0])
        u_full[0] = jnp.zeros_like(u_full[0])
        dz_low[0] = jnp.zeros_like(dz_low[0])
        dz_high[0] = jnp.zeros_like(dz_high[0])

    @pl.when(r == nr - 1)
    def _():
        x_one[2] = jnp.zeros_like(x_one[2])
        x_skip[3] = jnp.zeros_like(x_skip[3])
        a_one[2] = jnp.zeros_like(a_one[2])
        u_full[3] = jnp.zeros_like(u_full[3])
        dz_low[2] = jnp.zeros_like(dz_low[2])
        dz_high[3] = jnp.zeros_like(dz_high[3])

    stage.wait()
    for target, (out, width, taps, first) in zip((w_one, w_two, w_up, w_three), layers):
        across = width // TILE

        def arrange(n, _, target=target, out=out, taps=taps, first=first, across=across):
            ib = lax.rem(n, across)
            t = lax.rem(lax.div(n, across), taps)
            ob = lax.div(n, across * taps)
            target[
                pl.ds(pl.multiple_of(t * out + ob * TILE, TILE), TILE), lanes(ib, TILE)
            ] = grad_ref[place_ref[first + n]]
            return 0

        lax.fori_loop(0, out // TILE * taps * across, arrange, 0)
    for k in range(1, nb):
        for move in moves:
            move.hop(k)
    for move in moves:
        move.finish()

    gain_one, shift_one = wide_ref[0:1, :], wide_ref[1:2, :]
    gain_two, shift_two = wide_ref[2:3, :], wide_ref[3:4, :]
    gain_three, shift_three = narrow_ref[0:1, :], narrow_ref[1:2, :]
    size_low, size_high = C1 // GROUPS, C0 // GROUPS

    def conv_low(z_ref, weight, source):
        def tap(dx):
            total = 0.0
            for dy in range(3):
                first = (3 * dy + dx) * wide
                total = total + dot_nt(source(dy), weight[first : first + wide, :])
            return total

        z_ref[0] = tap(1)
        z_ref[0] += shift_down(tap(0))
        z_ref[0] += shift_up(tap(2))

    conv_low(z_one, w_one, lambda dy: x_one[dy].reshape(px, C0))
    reduce_one, reduce_two = reduce_wide.at[0], reduce_wide.at[1]
    norm_sums(reduce_one, z_one)
    count = 0.0
    for image in range(nb):
        for part in range(4):
            count = count + jnp.sum(x_lab[image, part, 2:3, :], 1, keepdims=True)
    reduce_one[r, 2 * nb : 2 * nb + 1, :] = jnp.broadcast_to(count, (1, wide))
    total = all_reduce(0, reduce_one)
    count = total[2 * nb : 2 * nb + 1, :1]

    def put_one(part, image, value):
        a_one[1, rows_of(image), lanes(b, wide)] = value

    norm_apply(total, z_one, inv_one, gain_one, shift_one, size_low, put_one)
    move = Exchange(
        3,
        lambda j: a_one.at[1, :, lanes(j, wide)],
        lambda j: (a_one.at[1, :, lanes(j, wide)], a_one.at[0, :, lanes(j, wide)]),
        lambda j: (a_one.at[1, :, lanes(j, wide)], a_one.at[2, :, lanes(j, wide)]),
    )
    move.begin()
    move.hops()
    move.finish()
    conv_low(z_two, w_two, lambda dy: a_one[dy])
    norm_sums(reduce_two, z_two)
    total = all_reduce(1, reduce_two)

    def put_two(part, image, value):
        a_two[rows_of(image), lanes(b, wide)] = value

    norm_apply(total, z_two, inv_two, gain_two, shift_two, size_low, put_two)
    move = Exchange(4, lambda j: a_two.at[:, lanes(j, wide)])
    move.begin()
    move.hops()
    move.finish()
    for part in range(4):
        u_full[1 + part // 2, part % 2, :, lanes(b, slim)] = dot_nt(
            a_two[...], w_up[part * slim : (part + 1) * slim, :]
        ).astype(bf16)
    move = Exchange(
        5,
        lambda j: u_full.at[pl.ds(1, 2), :, :, lanes(j, slim)],
        lambda j: (u_full.at[2, :, :, lanes(j, slim)], u_full.at[0, :, :, lanes(j, slim)]),
        lambda j: (u_full.at[1, :, :, lanes(j, slim)], u_full.at[3, :, :, lanes(j, slim)]),
    )
    move.begin()
    move.hops()
    move.finish()
    for e in range(2):
        found = []
        for f in range(2):
            total = 0.0
            for dy in range(3):
                weight = w_three[dy * taps_high : (dy + 1) * taps_high, :]
                total = total + dot_nt(u_full[e + dy, f], weight[:, :C0])
                total = total + dot_nt(x_skip[e + dy, f].reshape(px, C0), weight[:, C0:])
            found.append(total)
        even, odd = found
        z_three[2 * e] = (
            even[:, slim : 2 * slim] + shift_down(odd[:, :slim]) + odd[:, 2 * slim :]
        )
        z_three[2 * e + 1] = (
            odd[:, slim : 2 * slim] + even[:, :slim] + shift_up(even[:, 2 * slim :])
        )
    reduce_three, reduce_four = reduce_narrow.at[0], reduce_narrow.at[1]
    norm_sums(reduce_three, z_three)
    total = all_reduce(2, reduce_three)
    a_three = send_high

    def put_three(part, image, value):
        a_three[part, 0, rows_of(image), :] = value

    norm_apply(total, z_three, inv_three, gain_three, shift_three, size_high, put_three)
    head_low = narrow_ref[8:16, :].astype(bf16)
    head = head_low.astype(f32)
    for part in range(4):
        for image in range(nb):
            logit[b, part * nb + image] = dot_nt(
                head_low, a_three[part, 0, rows_of(image), :]
            )
    spread = Spread(all_send.at[0], all_recv.at[0], lambda other: logit.at[b], lambda j: logit.at[j])
    spread.begin()
    spread.finish()
    loss = jnp.zeros((1, cols), f32)
    bias_grad = [jnp.zeros((1, cols), f32), jnp.zeros((1, cols), f32)]
    head_grad = jnp.zeros((8, slim), f32)
    level = lax.broadcasted_iota(jnp.int32, (8, cols), 0)

    def head_of(part, image):
        tile = logit[0, part * nb + image]
        for j in range(1, nb):
            tile = tile + logit[j, part * nb + image]
        first = tile[0:1, :] + bias_ref[0]
        second = tile[1:2, :] + bias_ref[1]
        scale = x_lab[image, part, 0:1, :]
        label = x_lab[image, part, 1:2, :]
        largest = jnp.maximum(first, second)
        log_total = jnp.log(jnp.exp(first - largest) + jnp.exp(second - largest)) + largest
        picked = first * (1.0 - label) + second * label
        unit = scale / count
        return (
            scale * (log_total - picked),
            (jnp.exp(first - log_total) - (1.0 - label)) * unit,
            (jnp.exp(second - log_total) - label) * unit,
        )

    for part in range(4):
        for image in range(nb):
            cost, first, second = head_of(part, image)
            loss = loss + cost
            bias_grad = [bias_grad[0] + first, bias_grad[1] + second]
            tile = jnp.where(level == 0, first, jnp.where(level == 1, second, 0.0))
            logit[0, part * nb + image] = tile
            head_grad = head_grad + jnp.dot(
                tile,
                a_three[part, 0, rows_of(image), :].astype(f32),
                preferred_element_type=f32,
                precision=highest,
            )

    def grad_three(part, image):
        return lax.dot_general(
            logit[0, part * nb + image],
            head,
            (((0,), (0,)), ((), ())),
            preferred_element_type=f32,
            precision=highest,
        )

    reduce_four[r, 2 * nb : 2 * nb + 8, :] = head_grad
    for row, value in enumerate([loss] + bias_grad):
        reduce_four[r, 2 * nb + 2 + row : 2 * nb + 3 + row, :] = jnp.broadcast_to(
            jnp.sum(value, 1, keepdims=True), (1, slim)
        )
    back_sums(reduce_four, z_three, dy_high, gain_three, shift_three, grad_three)
    total = all_reduce(3, reduce_four)

    def put_high(part, image, value):
        dz_high[1 + part // 2, part % 2, rows_of(image), :] = value

    gain_grad, shift_grad = back_apply(
        total, z_three, dy_high, inv_three, gain_three, size_high, put_high
    )
    sums_ref[b] = jnp.zeros_like(sums_ref[b])
    sums_ref[b, 4:5, :slim] = gain_grad
    sums_ref[b, 4:5, slim : 2 * slim] = shift_grad
    sums_ref[b, 5:6, :slim] = total[2 * nb : 2 * nb + 1]
    sums_ref[b, 5:6, slim : 2 * slim] = total[2 * nb + 1 : 2 * nb + 2]
    for row in range(3):
        sums_ref[b, 6 + row : 7 + row, :slim] = total[2 * nb + 2 + row : 2 * nb + 3 + row]
    sums_ref[b, 9:10, :] = jnp.broadcast_to(count, (1, wide))

    def edges(number, source_up, target_up, source_down, target_down):
        def higher():
            return remote(
                source_up,
                target_up,
                edge_send.at[number, 0],
                edge_recv.at[number, 0],
                ring(r + 1, nr),
                b,
            )

        def lower():
            return remote(
                source_down,
                target_down,
                edge_send.at[number, 1],
                edge_recv.at[number, 1],
                ring(r - 1, nr),
                b,
            )

        def begin():
            @pl.when(r + 1 < nr)
            def _():
                higher().start()

            @pl.when(r > 0)
            def _():
                lower().start()

        def finish():
            @pl.when(r + 1 < nr)
            def _():
                higher().wait_send()
                lower().wait_recv()

            @pl.when(r > 0)
            def _():
                lower().wait_send()
                higher().wait_recv()

        return begin, finish

    def widen_high(row):
        even, odd = dz_high[row, 0], dz_high[row, 1]
        shifted_high[row, 0, :, :slim] = odd
        shifted_high[row, 0, :, slim : 2 * slim] = even
        shifted_high[row, 0, :, 2 * slim :] = shift_down(odd.astype(f32)).astype(bf16)
        shifted_high[row, 1, :, :slim] = shift_up(even.astype(f32)).astype(bf16)
        shifted_high[row, 1, :, slim : 2 * slim] = odd
        shifted_high[row, 1, :, 2 * slim :] = even

    begin, finish = edges(0, dz_high.at[2], dz_high.at[0], dz_high.at[1], dz_high.at[3])
    begin()
    widen_high(1)
    widen_high(2)
    finish()
    widen_high(0)
    widen_high(3)
    spreads = []
    own_high = []
    for part in range(4):
        e, f = part // 2, part % 2
        total = 0.0
        for dy in range(3):
            total = total + dot_nn(
                shifted_high[e + 2 - dy, f], w_three[dy * taps_high : (dy + 1) * taps_high, :C0]
            )
        for j in range(nb):
            send_high[part, j] = total[:, j * slim : (j + 1) * slim].astype(bf16)

            @pl.when(b == j)
            def _():
                dy_high[part] = total[:, j * slim : (j + 1) * slim]

        spread = Spread(
            high_send.at[part],
            high_recv.at[part],
            lambda other, part=part: send_high.at[part, other],
            lambda j, part=part: recv_high.at[part, j],
        )
        spread.begin()
        spreads.append(spread)

    def put_grad(first, across, value, rows, start):
        for row, number in rows:
            for k in range(value.shape[1] // TILE):
                grad_ref[first + number * across + start + k] = value[
                    row : row + TILE, k * TILE : (k + 1) * TILE
                ].astype(bf16)

    out, width, taps, first = layers[3]
    for e in range(2):
        for f in range(2):
            turned_high[e, :, f * px : (f + 1) * px] = shifted_high[1 + e, f].T
    for dy in range(3):
        rows = [(dx * slim, 3 * dy + dx) for dx in range(3)]
        for half, source in enumerate((u_full, x_skip)):
            total = 0.0
            for e in range(2):
                for f in range(2):
                    value = source[e + dy, f].reshape(px, C0)
                    total = total + dot_nn(turned_high[e, :, f * px : (f + 1) * px], value)
            put_grad(first, width // TILE, total, rows, half * (C0 // TILE))
    for part in range(4):
        spreads[part].finish()
        total = dy_high[part]
        for step in range(1, nb):
            total = total + recv_high[part, ring(b + step, nb)].astype(f32)
        dub[:, part * slim : (part + 1) * slim] = total.astype(bf16)

    def input_low(number, product):
        for j in range(nb):
            total = product(j)
            send_low[j] = total.astype(bf16)

            @pl.when(b == j)
            def _():
                dy_low[0] = total

        spread = Spread(
            all_send.at[number],
            all_recv.at[number],
            lambda other: send_low.at[other],
            lambda j: recv_low.at[number - 1, j],
        )
        spread.begin()

        def finish():
            spread.finish()
            total = dy_low[0]
            for step in range(1, nb):
                total = total + recv_low[number - 1, ring(b + step, nb)].astype(f32)
            dy_low[0] = total

        return finish

    finish_sum = input_low(
        1, lambda j: dot_nn(dub[...], w_up[:, j * wide : (j + 1) * wide])
    )
    out, width, taps, first = layers[2]
    turned_low[: 4 * slim, :] = dub[...].T
    for j in range(nb):
        total = dot_nn(turned_low[: 4 * slim, :], a_two[:, j * wide : (j + 1) * wide])
        rows = [(part * slim, part) for part in range(4)]
        put_grad(first, width // TILE, total, rows, j * (wide // TILE))
    finish_sum()

    def back_low(number, z_ref, inv_ref, gain, shift):
        def grad_of(part, image):
            return dy_low[0, rows_of(image), :]

        buffer = reduce_wide.at[number - 2]
        back_sums(buffer, z_ref, dy_low, gain, shift, grad_of)
        total = all_reduce(number, buffer)

        def put(part, image, value):
            dz_low[1, rows_of(image), :] = value

        return back_apply(total, z_ref, dy_low, inv_ref, gain, size_low, put)

    def widen_low(row):
        value = dz_low[row]
        wider = value.astype(f32)
        shifted_low[row, :, :wide] = shift_up(wider).astype(bf16)
        shifted_low[row, :, wide : 2 * wide] = value
        shifted_low[row, :, 2 * wide :] = shift_down(wider).astype(bf16)

    def weight_low(number, source):
        out, width, taps, first = layers[number]
        turned_low[...] = shifted_low[1].T
        chunk = 2 * TILE
        for dy in range(3):
            rows = []
            for dx in range(3):
                for ob in range(wide // TILE):
                    rows.append((dx * wide + ob * TILE, ob * taps + 3 * dy + dx))
            for j in range(width // chunk):
                total = dot_nn(turned_low[...], source(dy, j * chunk, chunk))
                put_grad(first, width // TILE, total, rows, j * (chunk // TILE))

    gain_grad, shift_grad = back_low(4, z_two, inv_two, gain_two, shift_two)
    sums_ref[b, 2:3, :] = gain_grad
    sums_ref[b, 3:4, :] = shift_grad
    begin, finish = edges(1, dz_low.at[1], dz_low.at[0], dz_low.at[1], dz_low.at[2])
    begin()
    widen_low(1)
    finish()
    widen_low(0)
    widen_low(2)

    def product_two(j):
        total = 0.0
        for dy in range(3):
            total = total + dot_nn(
                shifted_low[2 - dy],
                w_two[3 * dy * wide : 3 * (dy + 1) * wide, j * wide : (j + 1) * wide],
            )
        return total

    finish_sum = input_low(2, product_two)
    weight_low(1, lambda dy, start, size: a_one[dy, :, start : start + size])
    finish_sum()
    gain_grad, shift_grad = back_low(5, z_one, inv_one, gain_one, shift_one)
    sums_ref[b, 0:1, :] = gain_grad
    sums_ref[b, 1:2, :] = shift_grad
    spread = Spread(
        all_send.at[3], all_recv.at[3], lambda other: sums_ref.at[b], lambda j: sums_ref.at[j]
    )
    spread.begin()
    widen_low(1)
    weight_low(0, lambda dy, start, size: x_one[dy].reshape(px, C0)[:, start : start + size])
    spread.finish()


def run_step(copies, place, bias, image, skip, lab, wide_rows, narrow_rows):
    nr, nb = lax.axis_size("rows"), lax.axis_size("blk")
    cols = image.shape[0]
    px = nb * cols
    wide, slim = C1 // nb, C0 // nb
    vmem = pl.BlockSpec(memory_space=pltpu.VMEM)
    smem = pl.BlockSpec(memory_space=pltpu.SMEM)
    dma = pltpu.SemaphoreType.DMA
    scratch = [
        pltpu.VMEM((3, nb, cols, C0), bf16),
        pltpu.VMEM((4, 2, nb, cols, C0), bf16),
        pltpu.VMEM((nb, 4, 8, cols), f32),
        pltpu.VMEM((9 * wide, C0), bf16),
        pltpu.VMEM((9 * wide, C1), bf16),
        pltpu.VMEM((4 * slim, C1), bf16),
        pltpu.VMEM((9 * slim, 2 * C0), bf16),
        pltpu.VMEM((3, px, C1), bf16),
        pltpu.VMEM((px, C1), bf16),
        pltpu.VMEM((4, 2, px, C0), bf16),
        pltpu.VMEM((1, px, wide), f32),
        pltpu.VMEM((1, px, wide), f32),
        pltpu.VMEM((4, px, slim), f32),
        pltpu.VMEM((1, px, wide), f32),
        pltpu.VMEM((4, px, slim), f32),
        pltpu.VMEM((8, wide), f32),
        pltpu.VMEM((8, wide), f32),
        pltpu.VMEM((8, slim), f32),
        pltpu.VMEM((3, px, wide), bf16),
        pltpu.VMEM((4, 2, px, slim), bf16),
        pltpu.VMEM((3, px, 3 * wide), bf16),
        pltpu.VMEM((4, 2, px, 3 * slim), bf16),
        pltpu.VMEM((3 * wide, px), bf16),
        pltpu.VMEM((2, 3 * slim, 2 * px), bf16),
        pltpu.VMEM((px, 4 * slim), bf16),
        pltpu.VMEM((4, nb, px, slim), bf16),
        pltpu.VMEM((4, nb, px, slim), bf16),
        pltpu.VMEM((nb, px, wide), bf16),
        pltpu.VMEM((2, nb, px, wide), bf16),
        pltpu.VMEM((nb, 4 * nb, 8, cols), f32),
        pltpu.VMEM((4, nr, 2 * nb + 8, wide), f32),
        pltpu.VMEM((2, nr, 2 * nb + 8, slim), f32),
        dma(()),
        dma((6, nb, 2)),
        dma((6, nb)),
        dma((6, nb, 2)),
        dma((6, nb, 2)),
        dma((6, nr)),
        dma((6, nr)),
        dma((4, nb)),
        dma((4, nb)),
        dma((4, nb)),
        dma((4, nb)),
        dma((2, 2)),
        dma((2, 2)),
    ]
    return pl.pallas_call(
        functools.partial(step_kernel, nr, nb, cols),
        out_shape=(
            jax.ShapeDtypeStruct(copies.shape, bf16),
            jax.ShapeDtypeStruct((nb, 16, wide), f32),
        ),
        in_specs=[pl.BlockSpec(memory_space=pl.ANY), smem, smem, vmem, vmem, vmem, vmem, vmem],
        out_specs=(vmem, vmem),
        scratch_shapes=scratch,
        compiler_params=pltpu.CompilerParams(
            collective_id=0, has_side_effects=True, vmem_limit_bytes=60 * 2**20
        ),
    )(copies, place, bias, image, skip, lab, wide_rows, narrow_rows)


LANES = 128


def inverse_factor_kernel(stat_ref, inverse_ref, factor_ref):
    order = stat_ref.shape[0]
    tile = (8, LANES)
    sub = lax.broadcasted_iota(jnp.int32, tile, 0)

    def eliminate(source_ref, base, start, first, count, accs):
        def body(group, accs):
            top = pl.multiple_of(group * 8, 8)
            for unit in range(8):
                value = source_ref[top + unit, pl.ds(start, 8), :]
                accs = tuple(
                    accs[c]
                    - value
                    * jnp.broadcast_to(factor_ref[top + unit, pl.ds(base + c, 1), :], tile)
                    for c in range(8)
                )
            return accs

        return list(lax.fori_loop(first, count, body, tuple(accs)))

    def block(kb, _):
        base = pl.multiple_of(kb * 8, 8)
        accs = [stat_ref[base + c, pl.ds(base, 8), :] for c in range(8)]
        accs = eliminate(factor_ref, base, base, 0, kb, accs)
        scale = []
        coef = {}
        for c in range(8):
            scale.append(jnp.broadcast_to(lax.rsqrt(accs[c][c : c + 1, :]), tile))
            accs[c] = accs[c] * scale[c]
            for d in range(c + 1, 8):
                coef[(c, d)] = jnp.broadcast_to(accs[c][d : d + 1, :], tile)
                accs[d] = accs[d] - accs[c] * coef[(c, d)]
        for c in range(8):
            factor_ref[base + c, pl.ds(base, 8), :] = jnp.where(sub >= c, accs[c], 0.0)

        def finish(accs, target_ref, start):
            accs = list(accs)
            for c in range(8):
                for e in range(c):
                    accs[c] = accs[c] - accs[e] * coef[(e, c)]
                accs[c] = accs[c] * scale[c]
                target_ref[base + c, pl.ds(start, 8), :] = accs[c]

        def below(group, _):
            start = pl.multiple_of(group * 8, 8)
            accs = [stat_ref[base + c, pl.ds(start, 8), :] for c in range(8)]
            finish(eliminate(factor_ref, base, start, 0, kb, accs), factor_ref, start)
            return 0

        def left(group, _):
            start = pl.multiple_of(group * 8, 8)
            accs = [jnp.zeros(tile, jnp.float32) for c in range(8)]
            finish(eliminate(inverse_ref, base, start, group, kb, accs), inverse_ref, start)
            return 0

        def clear(group, _):
            start = pl.multiple_of(group * 8, 8)
            for c in range(8):
                inverse_ref[base + c, pl.ds(start, 8), :] = jnp.zeros(tile, jnp.float32)
            return 0

        lax.fori_loop(kb + 1, order // 8, below, 0)
        lax.fori_loop(0, kb, left, 0)
        finish([jnp.where(sub == c, 1.0, 0.0) for c in range(8)], inverse_ref, base)
        lax.fori_loop(kb + 1, order // 8, clear, 0)
        return 0

    lax.fori_loop(0, order // 8, block, 0)


def product(left, right, left_dim, right_dim):
    return lax.dot_general(
        left,
        right,
        (((left_dim,), (right_dim,)), ((), ())),
        preferred_element_type=f32,
        precision=highest,
    )


def soap_block(index, grad, ins, outs):
    master_ref, first_ref, second_ref, left_ref, right_ref, left_stat_ref, right_stat_ref = ins
    left, right = left_ref[index], right_ref[index]
    rotated = product(product(left, grad, 0, 0), right, 1, 0)
    first = beta_one * first_ref[index] + (1.0 - beta_one) * rotated
    second = beta_two * second_ref[index] + (1.0 - beta_two) * rotated * rotated
    direction = (
        first
        / (1.0 - beta_one**STEP)
        / (jnp.sqrt(second / (1.0 - beta_two**STEP)) + adam_eps)
    )
    update = product(product(left, direction, 1, 0), right, 1, 1)
    master = master_ref[index]
    master = master - soap_rate * (update + soap_decay * master)
    values = [master, master.astype(bf16), first, second]
    moved = []
    for stat_ref, basis, dim in ((left_stat_ref, left, 1), (right_stat_ref, right, 0)):
        stat = beta_stat * stat_ref[index] + (1.0 - beta_stat) * product(grad, grad, dim, dim)
        values.append(stat)
        moved.append(product(stat, basis, 1, 0))
    values = values + moved + [product(value, value, 0, 0) for value in moved]
    for ref, value in zip(outs, values):
        ref[index] = value


def collect_kernel(nr, size, *refs):
    (owner_ref, grad_ref), refs = refs[:2], refs[2:]
    ins, refs = refs[:7], refs[7:]
    outs, refs = refs[:10], refs[10:]
    (
        out_a,
        in_a,
        out_b,
        in_b,
        total,
        in_buffer,
        out_buffer,
        copy_buffer,
        a_send,
        a_recv,
        b_send,
        b_recv,
        in_sem,
        out_sem,
    ) = refs
    r = lax.axis_index("rows")
    b = lax.axis_index("blk")
    core = lax.rem(r, 2)
    chip = lax.div(r, 2)
    chips = nr // 2
    mate = r + 1 - 2 * core
    count = ins[0].shape[0]
    chunks = count // size

    def device(chip, core):
        return {"rows": 2 * chip + core, "blk": b}

    barrier = pltpu.get_barrier_semaphore()
    pl.semaphore_signal(
        barrier, inc=1, device_id={"rows": mate, "blk": b}, device_id_type=MESH
    )

    def greet(step, _):
        pl.semaphore_signal(
            barrier,
            inc=1,
            device_id=device(lax.rem(chip + step, chips), core),
            device_id_type=MESH,
        )
        return 0

    lax.fori_loop(1, chips, greet, 0)
    pl.semaphore_wait(barrier, chips)

    def loads(chunk):
        return [
            pltpu.make_async_copy(
                ref.at[pl.ds(chunk * size, size)],
                in_buffer.at[chunk % 2, number],
                in_sem.at[chunk % 2, number],
            )
            for number, ref in enumerate(ins)
        ]

    def stores(chunk):
        copies = []
        for number, ref in enumerate(outs):
            source = (
                copy_buffer.at[chunk % 2]
                if number == 1
                else out_buffer.at[chunk % 2, number - (number > 1)]
            )
            copies.append(
                pltpu.make_async_copy(
                    source, ref.at[pl.ds(chunk * size, size)], out_sem.at[chunk % 2, number]
                )
            )
        return copies

    def mine(to_chip, to_core, chunk, index):
        return grad_ref[owner_ref[(2 * to_chip + to_core) * count + chunk * size + index]]

    def send_a(chunk):
        return pltpu.make_async_remote_copy(
            src_ref=out_a.at[chunk],
            dst_ref=in_a.at[chunk],
            send_sem=a_send.at[chunk],
            recv_sem=a_recv.at[chunk],
            device_id={"rows": mate, "blk": b},
            device_id_type=MESH,
        )

    def send_b(chunk, step):
        other = lax.rem(chip + step, chips)
        return pltpu.make_async_remote_copy(
            src_ref=out_b.at[chunk, other],
            dst_ref=in_b.at[chunk, chip],
            send_sem=b_send.at[chunk, step],
            recv_sem=b_recv.at[chunk, chip],
            device_id=device(other, core),
            device_id_type=MESH,
        )

    for copy in loads(0):
        copy.start()
    for chunk in range(chunks):

        def fill(n, _, chunk=chunk):
            to_chip, index = lax.div(n, size), lax.rem(n, size)
            out_a[chunk, to_chip, index] = mine(to_chip, 1 - core, chunk, index)
            return 0

        lax.fori_loop(0, chips * size, fill, 0)
        send_a(chunk).start()
    for chunk in range(chunks):
        send_a(chunk).wait_recv()

        def join(step, _, chunk=chunk):
            other = lax.rem(chip + step, chips)

            def each(index, _):
                value = mine(other, core, chunk, index).astype(f32)
                value = value + in_a[chunk, other, index].astype(f32)
                out_b[chunk, other, index] = value.astype(bf16)
                return 0

            lax.fori_loop(0, size, each, 0)
            send_b(chunk, step).start()
            return 0

        lax.fori_loop(1, chips, join, 0)

        def keep(index, _, chunk=chunk):
            value = mine(chip, core, chunk, index).astype(f32)
            total[chunk, index] = value + in_a[chunk, chip, index].astype(f32)
            return 0

        lax.fori_loop(0, size, keep, 0)
    for chunk in range(chunks):
        if chunk + 1 < chunks:
            for copy in loads(chunk + 1):
                copy.start()
        for copy in loads(chunk):
            copy.wait()
        if chunk >= 2:
            for copy in stores(chunk - 2):
                copy.wait()

        def arrive(step, _, chunk=chunk):
            other = lax.rem(chip + step, chips)
            pltpu.make_async_remote_copy(
                src_ref=out_b.at[chunk, other],
                dst_ref=in_b.at[chunk, other],
                send_sem=b_send.at[chunk, step],
                recv_sem=b_recv.at[chunk, other],
                device_id=device(other, core),
                device_id_type=MESH,
            ).wait_recv()
            return 0

        lax.fori_loop(1, chips, arrive, 0)
        slot = chunk % 2
        chunk_ins = [in_buffer.at[slot, number] for number in range(7)]
        chunk_outs = [out_buffer.at[slot, number] for number in range(9)]
        chunk_outs.insert(1, copy_buffer.at[slot])

        def work(index, _, chunk=chunk, chunk_ins=chunk_ins, chunk_outs=chunk_outs):
            grad = lax.fori_loop(
                1,
                chips,
                lambda step, value: value
                + in_b[chunk, lax.rem(chip + step, chips), index].astype(f32),
                total[chunk, index],
            )
            soap_block(index, grad, chunk_ins, chunk_outs)
            return 0

        lax.fori_loop(0, size, work, 0, unroll=2 if size % 2 == 0 else 1)
        for copy in stores(chunk):
            copy.start()
    for chunk in range(chunks):
        send_a(chunk).wait_send()
        lax.fori_loop(
            1, chips, lambda step, _, chunk=chunk: (send_b(chunk, step).wait_send(), 0)[1], 0
        )
        if chunk >= chunks - 2:
            for copy in stores(chunk):
                copy.wait()


def basis_kernel(
    left_gram_ref, right_gram_ref, left_ref, right_ref, new_left_ref, new_right_ref, stat_ref,
    inverse_ref, factor_ref
):
    order = left_gram_ref.shape[1]
    count = left_gram_ref.shape[0] // order
    spare = LANES - 2 * count

    def enter(row, _):
        rows = pl.ds(row, count, stride=order)
        values = [left_gram_ref[rows, :], right_gram_ref[rows, :]]
        if spare:
            column = lax.broadcasted_iota(jnp.int32, (spare, order), 1)
            values.append(jnp.where(column == row, 1.0, 0.0))
        stat_ref[row] = jnp.concatenate(values, 0).T
        return 0

    lax.fori_loop(0, order, enter, 0)
    inverse_factor_kernel(stat_ref, inverse_ref, factor_ref)

    def leave(row, _):
        rows = pl.ds(row, count, stride=order)
        value = inverse_ref[row].T
        new_left_ref[rows, :] = value[:count]
        new_right_ref[rows, :] = value[count : 2 * count]
        return 0

    lax.fori_loop(0, order, leave, 0)

    def solve(index, _):
        rows = pl.ds(pl.multiple_of(index * order, order), order)
        new_left_ref[rows, :] = product(left_ref[rows, :], new_left_ref[rows, :], 1, 1)
        new_right_ref[rows, :] = product(right_ref[rows, :], new_right_ref[rows, :], 1, 1)
        return 0

    lax.fori_loop(0, count, solve, 0, unroll=2 if count % 2 == 0 else 1)


def soap_update(blocks, owner, states):
    nr = lax.axis_size("rows")
    count, order = states[0].shape[0], states[0].shape[-1]
    size = 8 if count % 8 == 0 else count
    chunks = count // size
    anywhere = pl.BlockSpec(memory_space=pl.ANY)
    vmem = pl.BlockSpec(memory_space=pltpu.VMEM)
    shape = jax.ShapeDtypeStruct(states[0].shape, f32)
    dma = pltpu.SemaphoreType.DMA
    square = (order, order)
    results = pl.pallas_call(
        functools.partial(collect_kernel, nr, size),
        out_shape=(shape, jax.ShapeDtypeStruct(shape.shape, bf16)) + (shape,) * 8,
        in_specs=[pl.BlockSpec(memory_space=pltpu.SMEM), vmem] + [anywhere] * 7,
        out_specs=[anywhere] * 10,
        scratch_shapes=[
            pltpu.VMEM((chunks, nr // 2, size) + square, bf16),
            pltpu.VMEM((chunks, nr // 2, size) + square, bf16),
            pltpu.VMEM((chunks, nr // 2, size) + square, bf16),
            pltpu.VMEM((chunks, nr // 2, size) + square, bf16),
            pltpu.VMEM((chunks, size) + square, f32),
            pltpu.VMEM((2, 7, size) + square, f32),
            pltpu.VMEM((2, 9, size) + square, f32),
            pltpu.VMEM((2, size) + square, bf16),
            dma((chunks,)),
            dma((chunks,)),
            dma((chunks, nr // 2)),
            dma((chunks, nr // 2)),
            dma((2, 7)),
            dma((2, 10)),
        ],
        compiler_params=pltpu.CompilerParams(
            collective_id=1, has_side_effects=True, vmem_limit_bytes=60 * 2**20
        ),
    )(owner, blocks, *states)
    new_master, new_copy, new_first, new_second, new_left_stat, new_right_stat = results[:6]
    lanes = pltpu.VMEM((order, order, LANES), f32)
    flat = [value.reshape(count * order, order) for value in results[8:] + results[6:8]]
    new_left, new_right = pl.pallas_call(
        basis_kernel,
        out_shape=(jax.ShapeDtypeStruct(flat[0].shape, f32),) * 2,
        in_specs=[vmem] * 4,
        out_specs=(vmem, vmem),
        scratch_shapes=[lanes, lanes, lanes],
        compiler_params=pltpu.CompilerParams(vmem_limit_bytes=60 * 2**20),
    )(*flat)
    return [
        new_master,
        new_copy,
        new_first,
        new_second,
        new_left.reshape(shape.shape),
        new_right.reshape(shape.shape),
        new_left_stat,
        new_right_stat,
    ]


def adam_small(grads, value, first, second):
    first_new = beta_one * first + (1.0 - beta_one) * grads
    second_new = beta_two * second + (1.0 - beta_two) * grads * grads
    direction = (
        first_new
        / (1.0 - beta_one**STEP)
        / (jnp.sqrt(second_new / (1.0 - beta_two**STEP)) + adam_eps)
    )
    return (first_new, second_new, value - small_rate * (direction + small_decay * value))


def local(
    image,
    skip,
    labels,
    weight_map,
    valid,
    owner,
    master,
    first_moment,
    second_moment,
    left_basis,
    right_basis,
    left_stat,
    right_stat,
    norm_params,
    norm_first,
    norm_second,
    head_bias,
    bias_first,
    bias_second,
):
    shards = lax.axis_size("blk")
    shard = lax.axis_index("blk")
    cols = image.shape[2]
    copies = lax.all_gather(master.astype(bf16), "rows", axis=1, tiled=True)[0]
    slots = jnp.arange(owner.shape[0])
    place = jnp.sum(jnp.where(owner[None, :] == slots[:, None], slots[None, :], 0), 1)
    widths = (C1, C1, C1, C1, C0, C0)
    rows = []
    offset = 0
    for width in widths:
        part = width // shards
        rows.append(lax.dynamic_slice_in_dim(norm_params, offset + shard * part, part))
        offset = offset + width
    heads = norm_params[offset:].reshape(C0, 2)
    part = C0 // shards
    heads = lax.dynamic_slice_in_dim(heads, shard * part, part).T
    wide_rows = jnp.pad(jnp.stack(rows[:4]), ((0, 4), (0, 0)))
    narrow_rows = jnp.concatenate(
        [jnp.pad(jnp.stack(rows[4:]), ((0, 6), (0, 0))), jnp.pad(heads, ((0, 6), (0, 0)))]
    )
    valid_float = valid.astype(f32)
    scales = valid_float * weight_map.astype(f32) * 0.125
    lab = jnp.stack([scales, labels.astype(f32), valid_float]).reshape(3, 2, cols, 2)
    lab = lab.transpose(1, 3, 0, 2).reshape(4, 3, cols)
    lab = jnp.pad(lab, ((0, 0), (0, 5), (0, 0)))
    skip = skip.reshape(2, cols, 2, C0).transpose(0, 2, 1, 3)
    blocks, sums = run_step(
        copies, place.astype(jnp.int32), head_bias, image[0, 0], skip, lab, wide_rows, narrow_rows
    )
    loss_sum, valid_count = sums[0, 6, 0], sums[0, 9, 0]
    grad_bias = sums[0, 7:9, 0]
    grad_head = jnp.stack([sums[:, 5, :part].reshape(-1), sums[:, 5, part : 2 * part].reshape(-1)], 1)
    small = jnp.concatenate(
        [sums[:, row].reshape(-1) for row in range(4)]
        + [
            sums[:, 4, :part].reshape(-1),
            sums[:, 4, part : 2 * part].reshape(-1),
            grad_head.reshape(-1),
        ]
    )
    states = (
        master,
        first_moment,
        second_moment,
        left_basis,
        right_basis,
        left_stat,
        right_stat,
    )
    soap = soap_update(blocks, owner, [state[0] for state in states])
    soap = [value[None] for value in soap]
    norm_new = adam_small(small, norm_params, norm_first, norm_second)
    bias_new = adam_small(grad_bias, head_bias, bias_first, bias_second)
    return (
        loss_sum,
        valid_count,
        soap[0],
        soap[1],
        soap[2],
        soap[3],
        soap[4],
        soap[5],
        soap[6],
        soap[7],
        norm_new[0],
        norm_new[1],
        norm_new[2],
        bias_new[0],
        bias_new[1],
        bias_new[2],
    )


def solution(mesh):
    placed = (
        P("blk", "rows", None, None),
        P("blk", "rows", None, None),
        P("blk", "rows", None),
        P("blk", "rows", None),
        P("blk", "rows", None),
        P(),
        P("blk", "rows", None, None),
        P("blk", "rows", None, None),
        P("blk", "rows", None, None),
        P("blk", "rows", None, None),
        P("blk", "rows", None, None),
        P("blk", "rows", None, None),
        P("blk", "rows", None, None),
        P(),
        P(),
        P(),
        P(),
        P(),
        P(),
    )
    return jax.shard_map(
        local,
        mesh=mesh,
        in_specs=placed,
        out_specs=(
            P(),
            P(),
            P("blk", "rows", None, None),
            P("blk", "rows", None, None),
            P("blk", "rows", None, None),
            P("blk", "rows", None, None),
            P("blk", "rows", None, None),
            P("blk", "rows", None, None),
            P("blk", "rows", None, None),
            P("blk", "rows", None, None),
            P(),
            P(),
            P(),
            P(),
            P(),
            P(),
        ),
        check_vma=False,
    )
```

```python
import functools

import jax
import jax.numpy as jnp
from jax import lax
from jax.experimental import pallas as pl
from jax.experimental.pallas import tpu as pltpu
from jax.sharding import PartitionSpec as P

C0 = 512
C1 = 1024
GROUPS = 32
STEP = 10


beta_one = 0.9
beta_two = 0.999
beta_stat = 0.95
adam_eps = 1e-08
norm_eps = 1e-05
soap_rate = 0.008
soap_decay = 0.01
small_rate = 0.4
small_decay = 0.01
highest = lax.Precision.HIGHEST


MESH = pl.DeviceIdType.MESH
bf16 = jnp.bfloat16
f32 = jnp.float32
TILE = 128


def dot_nt(left, right):
    return lax.dot_general(left, right, (((1,), (1,)), ((), ())), preferred_element_type=f32)


def dot_nn(left, right):
    return jnp.dot(left, right, preferred_element_type=f32)


def sigmoid(value):
    return 1.0 / (1.0 + jnp.exp(-value))


def block_layers(nb):
    result = []
    first = 0
    for in_width, out_width, taps in ((C0, C1, 9), (C1, C1, 9), (C1, C0, 4), (2 * C0, C0, 9)):
        out = out_width // nb
        result.append((out, in_width, taps, first))
        first = first + out // TILE * taps * (in_width // TILE)
    return result


def step_kernel(
    nr,
    nb,
    cols,
    master_ref,
    place_ref,
    bias_ref,
    image_ref,
    skip_ref,
    lab_ref,
    wide_ref,
    narrow_ref,
    grad_ref,
    sums_ref,
    x_one,
    x_skip,
    x_lab,
    w_one,
    w_two,
    w_up,
    w_three,
    a_one,
    a_two,
    u_full,
    z_one,
    z_two,
    z_three,
    dy_low,
    dy_high,
    inv_one,
    inv_two,
    inv_three,
    dz_low,
    dz_high,
    shifted_low,
    shifted_high,
    turned_low,
    turned_high,
    dub,
    send_high,
    recv_high,
    send_low,
    recv_low,
    logit,
    reduce_wide,
    reduce_narrow,
    gather_send,
    gather_recv,
    line_send,
    line_recv,
    halo_send,
    halo_recv,
    red_send,
    red_recv,
    all_send,
    all_recv,
    high_send,
    high_recv,
    edge_send,
    edge_recv,
):
    r = lax.axis_index("rows")
    b = lax.axis_index("blk")
    px = nb * cols
    wide = C1 // nb
    slim = C0 // nb
    taps_high = 3 * slim
    layers = block_layers(nb)

    def remote(src, dst, send, recv, rows, blk):
        return pltpu.make_async_remote_copy(
            src_ref=src,
            dst_ref=dst,
            send_sem=send,
            recv_sem=recv,
            device_id={"rows": rows, "blk": blk},
            device_id_type=MESH,
        )

    def lanes(index, size):
        return pl.ds(pl.multiple_of(index * size, TILE), size)

    def ring(index, count):
        return lax.rem(index + count, count)

    barrier = pltpu.get_barrier_semaphore()

    def greet_rows(step, _):
        pl.semaphore_signal(
            barrier, inc=1, device_id={"rows": ring(r + step, nr), "blk": b}, device_id_type=MESH
        )
        return 0

    lax.fori_loop(1, nr, greet_rows, 0)
    for step in range(1, nb):
        pl.semaphore_signal(
            barrier, inc=1, device_id={"rows": r, "blk": ring(b + step, nb)}, device_id_type=MESH
        )
    pl.semaphore_wait(barrier, nr - 1 + nb - 1)

    class Exchange:
        def __init__(self, number, piece, up=None, down=None):
            self.number, self.piece, self.up, self.down = number, piece, up, down

        def right(self, j):
            return remote(
                self.piece(j),
                self.piece(j),
                line_send.at[self.number, j, 0],
                line_recv.at[self.number, j],
                r,
                ring(b + 1, nb),
            )

        def left(self, j):
            return remote(
                self.piece(j),
                self.piece(j),
                line_send.at[self.number, j, 1],
                line_recv.at[self.number, j],
                r,
                ring(b - 1, nb),
            )

        def higher(self, j):
            src, dst = self.up(j)
            return remote(
                src,
                dst,
                halo_send.at[self.number, j, 0],
                halo_recv.at[self.number, j, 0],
                ring(r + 1, nr),
                b,
            )

        def lower(self, j):
            src, dst = self.down(j)
            return remote(
                src,
                dst,
                halo_send.at[self.number, j, 1],
                halo_recv.at[self.number, j, 1],
                ring(r - 1, nr),
                b,
            )

        def halos(self, j):
            if self.up is None:
                return

            @pl.when(r + 1 < nr)
            def _():
                self.higher(j).start()

            @pl.when(r > 0)
            def _():
                self.lower(j).start()

        def begin(self):
            @pl.when(b + 1 < nb)
            def _():
                self.right(b).start()

            @pl.when(b > 0)
            def _():
                self.left(b).start()

            self.halos(b)

        def hop(self, k):
            @pl.when(b >= k)
            def _():
                self.right(b - k).wait_recv()

                @pl.when(b + 1 < nb)
                def _():
                    self.right(b - k).start()

                self.halos(b - k)

            @pl.when(b + k < nb)
            def _():
                self.left(b + k).wait_recv()

                @pl.when(b > 0)
                def _():
                    self.left(b + k).start()

                self.halos(b + k)

        def hops(self):
            for k in range(1, nb):
                self.hop(k)

        def finish(self):
            for k in range(nb):

                @pl.when((b >= k) & (b + 1 < nb))
                def _():
                    self.right(b - k).wait_send()

                @pl.when((b + k < nb) & (b > 0))
                def _():
                    self.left(b + k).wait_send()

            if self.up is None:
                return
            for j in range(nb):

                @pl.when(r + 1 < nr)
                def _():
                    self.higher(j).wait_send()
                    self.lower(j).wait_recv()

                @pl.when(r > 0)
                def _():
                    self.lower(j).wait_send()
                    self.higher(j).wait_recv()

    def reduce_start(number, buffer):
        def start(step, _):
            remote(
                buffer.at[r],
                buffer.at[r],
                red_send.at[number, step],
                red_recv.at[number, r],
                ring(r + step, nr),
                b,
            ).start()
            return 0

        lax.fori_loop(1, nr, start, 0)

    def reduce_finish(number, buffer):
        def wait(step, _):
            source = ring(r + step, nr)
            copy = remote(
                buffer.at[source],
                buffer.at[source],
                red_send.at[number, step],
                red_recv.at[number, source],
                source,
                b,
            )
            copy.wait_recv()
            copy.wait_send()
            return 0

        lax.fori_loop(1, nr, wait, 0)
        return lax.fori_loop(1, nr, lambda k, total: total + buffer[k], buffer[0])

    def all_reduce(number, buffer):
        reduce_start(number, buffer)
        return reduce_finish(number, buffer)

    class Spread:
        def __init__(self, send, recv, source, target):
            self.send, self.recv, self.source, self.target = send, recv, source, target

        def copy(self, step):
            other = ring(b + step, nb)
            return remote(
                self.source(other),
                self.target(b),
                self.send.at[step],
                self.recv.at[b],
                r,
                other,
            )

        def begin(self):
            for step in range(1, nb):
                self.copy(step).start()

        def finish(self):
            for step in range(1, nb):
                other = ring(b + step, nb)
                remote(
                    self.source(other),
                    self.target(other),
                    self.send.at[step],
                    self.recv.at[other],
                    r,
                    other,
                ).wait_recv()
                self.copy(step).wait_send()

    class Gather:
        def __init__(self):
            self.size = master_ref.shape[0]
            self.chips = nr // 2
            self.core = lax.rem(r, 2)
            self.chip = lax.div(r, 2)
            self.mate = r + 1 - 2 * self.core
            self.square = self.chips == 4 and self.size % 2 == 0
            self.halves = 2 if self.square else 1

        def piece(self, row, half):
            part = self.size // self.halves
            return grad_ref.at[pl.ds(row * self.size + half * part, part)]

        def move(self, kind, target, row, half):
            return remote(
                self.piece(row, half),
                self.piece(row, half),
                gather_send.at[kind, row, half],
                gather_recv.at[row, half],
                target,
                b,
            )

        def direct(self, target):
            return remote(
                self.piece(r, 0),
                self.piece(r, 0),
                gather_send.at[0, target, 0],
                gather_recv.at[r, 0],
                target,
                b,
            )

        def beside(self, step):
            return 2 * lax.rem(self.chip + step, self.chips) + self.core

        def other(self, bit):
            away = self.chip + bit - 2 * bit * lax.rem(lax.div(self.chip, bit), 2)
            return 2 * away + self.core

        def begin(self):
            def cast(index, _):
                grad_ref[r * self.size + index] = master_ref[index].astype(bf16)
                return 0

            lax.fori_loop(0, self.size, cast, 0)
            if self.square:
                for half in range(2):
                    self.move(2, self.mate, r, half).start()
                    self.move(0, self.other(1), r, 1 - half).start()
                    self.move(1, self.other(2), r, half).start()
            else:
                self.move(2, self.mate, r, 0).start()

                def send(step, _):
                    self.direct(self.beside(step)).start()
                    return 0

                lax.fori_loop(1, self.chips, send, 0)

        def arrived(self, row, half):
            self.move(2, self.mate, row, half).wait_recv()

        def hand(self, row, half):
            self.arrived(row, half)
            self.move(2, self.mate, row, half).start()

        def forward(self, moves):
            image, lab, skip = moves
            for k in range(1, nb):
                image.hop(k)
                lab.hop(k)
            if self.square:
                x, y = self.other(1), self.other(2)
                corner = 2 * (3 - self.chip) + self.core
                self.hand(y, 0)
                self.move(0, x, y, 0).start()
                self.hand(x, 1)
                self.move(1, y, x, 1).start()
                skip.hop(1)
                self.hand(x, 0)
                self.hand(y, 1)
                for k in range(2, nb):
                    skip.hop(k)
                self.hand(corner, 0)
                self.hand(corner, 1)
                rows = (r, x, y, corner)
                for half in range(2):
                    for row in rows:
                        self.arrived(row + 1 - 2 * self.core, half)
                for half in range(2):
                    for row in rows:
                        self.move(2, self.mate, row, half).wait_send()
                    self.move(0, x, r, half).wait_send()
                    self.move(1, y, r, half).wait_send()
                self.move(0, x, y, 0).wait_send()
                self.move(1, y, x, 1).wait_send()
            else:

                def pass_on(step, _):
                    self.hand(self.beside(step), 0)
                    return 0

                def close(step, _):
                    row = self.beside(step)
                    self.arrived(row + 1 - 2 * self.core, 0)
                    self.move(2, self.mate, row, 0).wait_send()
                    self.direct(row).wait_send()
                    return 0

                lax.fori_loop(1, self.chips, pass_on, 0)
                for k in range(1, nb):
                    skip.hop(k)
                self.arrived(self.mate, 0)
                self.move(2, self.mate, r, 0).wait_send()
                lax.fori_loop(1, self.chips, close, 0)

    position = lax.rem(lax.broadcasted_iota(jnp.int32, (px, TILE), 0), cols)

    def mask_of(value, column):
        hit = position[:, :1] == column
        return jnp.where(hit, 0.0, value)

    def shift_down(value):
        return mask_of(pltpu.roll(value, 1, 0), 0)

    def shift_up(value):
        return mask_of(pltpu.roll(value, px - 1, 0), cols - 1)

    def group_sum(value, size):
        width = value.shape[-1]
        bits = size.bit_length() - 1
        first = lax.shift_right_logical(lax.broadcasted_iota(jnp.int32, (width, width), 0), bits)
        second = lax.shift_right_logical(lax.broadcasted_iota(jnp.int32, (width, width), 1), bits)
        same = jnp.where(first == second, 1.0, 0.0).astype(f32)
        return jnp.dot(value, same, preferred_element_type=f32, precision=highest)

    def rows_of(image):
        return pl.ds(image * cols, cols)

    def norm_sums(buffer, z_ref):
        for image in range(nb):
            first = 0.0
            second = 0.0
            for part in range(z_ref.shape[0]):
                value = z_ref[part, rows_of(image), :]
                first = first + jnp.sum(value, 0, keepdims=True)
                second = second + jnp.sum(value * value, 0, keepdims=True)
            buffer[r, image : image + 1, :] = first
            buffer[r, nb + image : nb + image + 1, :] = second

    def norm_apply(total, z_ref, inv_ref, gain, shift, size, put):
        width = z_ref.shape[-1]
        number = nr * cols * z_ref.shape[0] * size
        sums = group_sum(total[: 2 * nb], size) / number
        mean = sums[:nb]
        inv = lax.rsqrt(sums[nb:] - mean * mean + norm_eps)
        inv_ref[:nb, :] = inv
        for part in range(z_ref.shape[0]):
            for image in range(nb):
                value = z_ref[part, rows_of(image), :]
                value = (value - mean[image : image + 1]) * inv[image : image + 1]
                z_ref[part, rows_of(image), :] = value
                normed = value * gain + shift
                put(part, image, (normed * sigmoid(normed)).astype(bf16))

    def back_sums(buffer, z_ref, dy_ref, gain, shift, grad_of):
        for image in range(nb):
            first = 0.0
            second = 0.0
            for part in range(z_ref.shape[0]):
                value = z_ref[part, rows_of(image), :]
                normed = value * gain + shift
                gate = sigmoid(normed)
                grad = grad_of(part, image) * gate * (1.0 + normed * (1.0 - gate))
                dy_ref[part, rows_of(image), :] = grad
                first = first + jnp.sum(grad, 0, keepdims=True)
                second = second + jnp.sum(grad * value, 0, keepdims=True)
            buffer[r, image : image + 1, :] = first
            buffer[r, nb + image : nb + image + 1, :] = second

    def back_apply(total, z_ref, dy_ref, inv_ref, gain, size, put):
        number = nr * cols * z_ref.shape[0] * size
        sums = group_sum(total[: 2 * nb] * gain, size) / number
        inv = inv_ref[:nb, :]
        for part in range(z_ref.shape[0]):
            for image in range(nb):
                one = slice(image, image + 1)
                two = slice(nb + image, nb + image + 1)
                value = dy_ref[part, rows_of(image), :] * gain - sums[one]
                value = value - z_ref[part, rows_of(image), :] * sums[two]
                put(part, image, (value * inv[one]).astype(bf16))
        shift_grad = jnp.sum(total[:nb], 0, keepdims=True)
        gain_grad = jnp.sum(total[nb : 2 * nb], 0, keepdims=True)
        return gain_grad, shift_grad

    gather = Gather()
    gather.begin()
    x_one[1, b] = image_ref[...]
    x_skip[1:3, :, b] = skip_ref[...]
    x_lab[b] = lab_ref[...]
    move_image = Exchange(
        0,
        lambda j: x_one.at[1, j],
        lambda j: (x_one.at[1, j], x_one.at[0, j]),
        lambda j: (x_one.at[1, j], x_one.at[2, j]),
    )
    move_skip = Exchange(
        1,
        lambda j: x_skip.at[pl.ds(1, 2), :, j],
        lambda j: (x_skip.at[2, :, j], x_skip.at[0, :, j]),
        lambda j: (x_skip.at[1, :, j], x_skip.at[3, :, j]),
    )
    move_lab = Exchange(2, lambda j: x_lab.at[j])
    moves = (move_image, move_lab, move_skip)
    for move in moves:
        move.begin()
    @pl.when(r == 0)
    def _():
        x_one[0] = jnp.zeros_like(x_one[0])
        x_skip[0] = jnp.zeros_like(x_skip[0])
        a_one[0] = jnp.zeros_like(a_one[0])
        u_full[0] = jnp.zeros_like(u_full[0])
        dz_low[0] = jnp.zeros_like(dz_low[0])
        dz_high[0] = jnp.zeros_like(dz_high[0])

    @pl.when(r == nr - 1)
    def _():
        x_one[2] = jnp.zeros_like(x_one[2])
        x_skip[3] = jnp.zeros_like(x_skip[3])
        a_one[2] = jnp.zeros_like(a_one[2])
        u_full[3] = jnp.zeros_like(u_full[3])
        dz_low[2] = jnp.zeros_like(dz_low[2])
        dz_high[3] = jnp.zeros_like(dz_high[3])

    gather.forward(moves)
    for move in moves:
        move.finish()

    def arrange(number, target):
        out, width, taps, first = layers[number]
        across = width // TILE

        def body(n, _):
            ib = lax.rem(n, across)
            t = lax.rem(lax.div(n, across), taps)
            ob = lax.div(n, across * taps)
            target[
                pl.ds(pl.multiple_of(t * out + ob * TILE, TILE), TILE), lanes(ib, TILE)
            ] = grad_ref[place_ref[first + n]]
            return 0

        lax.fori_loop(0, out // TILE * taps * across, body, 0)

    arrange(0, w_one)
    gain_one, shift_one = wide_ref[0:1, :], wide_ref[1:2, :]
    gain_two, shift_two = wide_ref[2:3, :], wide_ref[3:4, :]
    gain_three, shift_three = narrow_ref[0:1, :], narrow_ref[1:2, :]
    size_low, size_high = C1 // GROUPS, C0 // GROUPS

    def conv_low(z_ref, weight, source, lines=(0, 1, 2), more=False):
        def tap(dx):
            total = 0.0
            for dy in lines:
                first = (3 * dy + dx) * wide
                total = total + dot_nt(source(dy), weight[first : first + wide, :])
            return total

        if more:
            z_ref[0] += tap(1)
        else:
            z_ref[0] = tap(1)
        z_ref[0] += shift_down(tap(0))
        z_ref[0] += shift_up(tap(2))

    conv_low(z_one, w_one, lambda dy: x_one[dy].reshape(px, C0))
    reduce_one, reduce_two = reduce_wide.at[0], reduce_wide.at[1]
    norm_sums(reduce_one, z_one)
    count = 0.0
    for image in range(nb):
        for part in range(4):
            count = count + jnp.sum(x_lab[image, part, 2:3, :], 1, keepdims=True)
    reduce_one[r, 2 * nb : 2 * nb + 1, :] = jnp.broadcast_to(count, (1, wide))
    reduce_start(0, reduce_one)
    arrange(1, w_two)
    total = reduce_finish(0, reduce_one)
    count = total[2 * nb : 2 * nb + 1, :1]

    def put_one(part, image, value):
        a_one[1, rows_of(image), lanes(b, wide)] = value

    norm_apply(total, z_one, inv_one, gain_one, shift_one, size_low, put_one)
    move = Exchange(
        3,
        lambda j: a_one.at[1, :, lanes(j, wide)],
        lambda j: (a_one.at[1, :, lanes(j, wide)], a_one.at[0, :, lanes(j, wide)]),
        lambda j: (a_one.at[1, :, lanes(j, wide)], a_one.at[2, :, lanes(j, wide)]),
    )
    move.begin()
    move.hop(1)
    arrange(2, w_up)
    for k in range(2, nb):
        move.hop(k)
    arrange(3, w_three)
    conv_low(z_two, w_two, lambda dy: a_one[dy], (1,))
    move.finish()
    conv_low(z_two, w_two, lambda dy: a_one[dy], (0, 2), True)
    norm_sums(reduce_two, z_two)
    total = all_reduce(1, reduce_two)

    def put_two(part, image, value):
        a_two[rows_of(image), lanes(b, wide)] = value

    norm_apply(total, z_two, inv_two, gain_two, shift_two, size_low, put_two)
    move = Exchange(4, lambda j: a_two.at[:, lanes(j, wide)])
    move.begin()
    move.hops()
    move.finish()
    for part in range(4):
        u_full[1 + part // 2, part % 2, :, lanes(b, slim)] = dot_nt(
            a_two[...], w_up[part * slim : (part + 1) * slim, :]
        ).astype(bf16)
    move = Exchange(
        5,
        lambda j: u_full.at[pl.ds(1, 2), :, :, lanes(j, slim)],
        lambda j: (u_full.at[2, :, :, lanes(j, slim)], u_full.at[0, :, :, lanes(j, slim)]),
        lambda j: (u_full.at[1, :, :, lanes(j, slim)], u_full.at[3, :, :, lanes(j, slim)]),
    )
    def conv_high(product, more):
        for e in range(2):
            even, odd = product(e, 0), product(e, 1)
            first = even[:, slim : 2 * slim] + shift_down(odd[:, :slim]) + odd[:, 2 * slim :]
            second = odd[:, slim : 2 * slim] + even[:, :slim] + shift_up(even[:, 2 * slim :])
            if more:
                z_three[2 * e] += first
                z_three[2 * e + 1] += second
            else:
                z_three[2 * e] = first
                z_three[2 * e + 1] = second

    def high_product(source, start, lines):
        def product(e, f):
            total = 0.0
            for dy in lines[e]:
                weight = w_three[dy * taps_high : (dy + 1) * taps_high, start : start + C0]
                total = total + dot_nt(source[e + dy, f].reshape(px, C0), weight)
            return total

        return product

    every = ((0, 1, 2), (0, 1, 2))
    inner, outer = ((1, 2), (0, 1)), ((0,), (2,))
    move.begin()
    conv_high(high_product(x_skip, C0, every), False)
    move.hops()
    conv_high(high_product(u_full, 0, inner), True)
    move.finish()
    conv_high(high_product(u_full, 0, outer), True)
    reduce_three, reduce_four = reduce_narrow.at[0], reduce_narrow.at[1]
    norm_sums(reduce_three, z_three)
    total = all_reduce(2, reduce_three)
    a_three = send_high

    def put_three(part, image, value):
        a_three[part, 0, rows_of(image), :] = value

    norm_apply(total, z_three, inv_three, gain_three, shift_three, size_high, put_three)
    head_low = narrow_ref[8:16, :].astype(bf16)
    head = head_low.astype(f32)
    for part in range(4):
        for image in range(nb):
            logit[b, part * nb + image] = dot_nt(
                head_low, a_three[part, 0, rows_of(image), :]
            )
    spread = Spread(all_send.at[0], all_recv.at[0], lambda other: logit.at[b], lambda j: logit.at[j])
    spread.begin()
    spread.finish()
    loss = jnp.zeros((1, cols), f32)
    bias_grad = [jnp.zeros((1, cols), f32), jnp.zeros((1, cols), f32)]
    head_grad = jnp.zeros((8, slim), f32)
    level = lax.broadcasted_iota(jnp.int32, (8, cols), 0)

    def head_of(part, image):
        tile = logit[0, part * nb + image]
        for j in range(1, nb):
            tile = tile + logit[j, part * nb + image]
        first = tile[0:1, :] + bias_ref[0]
        second = tile[1:2, :] + bias_ref[1]
        scale = x_lab[image, part, 0:1, :]
        label = x_lab[image, part, 1:2, :]
        largest = jnp.maximum(first, second)
        log_total = jnp.log(jnp.exp(first - largest) + jnp.exp(second - largest)) + largest
        picked = first * (1.0 - label) + second * label
        unit = scale / count
        return (
            scale * (log_total - picked),
            (jnp.exp(first - log_total) - (1.0 - label)) * unit,
            (jnp.exp(second - log_total) - label) * unit,
        )

    for part in range(4):
        for image in range(nb):
            cost, first, second = head_of(part, image)
            loss = loss + cost
            bias_grad = [bias_grad[0] + first, bias_grad[1] + second]
            tile = jnp.where(level == 0, first, jnp.where(level == 1, second, 0.0))
            logit[0, part * nb + image] = tile
            head_grad = head_grad + jnp.dot(
                tile,
                a_three[part, 0, rows_of(image), :].astype(f32),
                preferred_element_type=f32,
                precision=highest,
            )

    def grad_three(part, image):
        return lax.dot_general(
            logit[0, part * nb + image],
            head,
            (((0,), (0,)), ((), ())),
            preferred_element_type=f32,
            precision=highest,
        )

    reduce_four[r, 2 * nb : 2 * nb + 8, :] = head_grad
    for row, value in enumerate([loss] + bias_grad):
        reduce_four[r, 2 * nb + 2 + row : 2 * nb + 3 + row, :] = jnp.broadcast_to(
            jnp.sum(value, 1, keepdims=True), (1, slim)
        )
    back_sums(reduce_four, z_three, dy_high, gain_three, shift_three, grad_three)
    total = all_reduce(3, reduce_four)

    def put_high(part, image, value):
        dz_high[1 + part // 2, part % 2, rows_of(image), :] = value

    gain_grad, shift_grad = back_apply(
        total, z_three, dy_high, inv_three, gain_three, size_high, put_high
    )
    sums_ref[b] = jnp.zeros_like(sums_ref[b])
    sums_ref[b, 4:5, :slim] = gain_grad
    sums_ref[b, 4:5, slim : 2 * slim] = shift_grad
    sums_ref[b, 5:6, :slim] = total[2 * nb : 2 * nb + 1]
    sums_ref[b, 5:6, slim : 2 * slim] = total[2 * nb + 1 : 2 * nb + 2]
    for row in range(3):
        sums_ref[b, 6 + row : 7 + row, :slim] = total[2 * nb + 2 + row : 2 * nb + 3 + row]
    sums_ref[b, 9:10, :] = jnp.broadcast_to(count, (1, wide))

    def edges(number, source_up, target_up, source_down, target_down):
        def higher():
            return remote(
                source_up,
                target_up,
                edge_send.at[number, 0],
                edge_recv.at[number, 0],
                ring(r + 1, nr),
                b,
            )

        def lower():
            return remote(
                source_down,
                target_down,
                edge_send.at[number, 1],
                edge_recv.at[number, 1],
                ring(r - 1, nr),
                b,
            )

        def begin():
            @pl.when(r + 1 < nr)
            def _():
                higher().start()

            @pl.when(r > 0)
            def _():
                lower().start()

        def finish():
            @pl.when(r + 1 < nr)
            def _():
                higher().wait_send()
                lower().wait_recv()

            @pl.when(r > 0)
            def _():
                lower().wait_send()
                higher().wait_recv()

        return begin, finish

    def widen_high(row):
        even, odd = dz_high[row, 0], dz_high[row, 1]
        shifted_high[row, 0, :, :slim] = odd
        shifted_high[row, 0, :, slim : 2 * slim] = even
        shifted_high[row, 0, :, 2 * slim :] = shift_down(odd.astype(f32)).astype(bf16)
        shifted_high[row, 1, :, :slim] = shift_up(even.astype(f32)).astype(bf16)
        shifted_high[row, 1, :, slim : 2 * slim] = odd
        shifted_high[row, 1, :, 2 * slim :] = even

    begin, finish = edges(0, dz_high.at[2], dz_high.at[0], dz_high.at[1], dz_high.at[3])
    begin()
    widen_high(1)
    widen_high(2)
    finish()
    widen_high(0)
    widen_high(3)
    spreads = []
    own_high = []
    for part in range(4):
        e, f = part // 2, part % 2
        total = 0.0
        for dy in range(3):
            total = total + dot_nn(
                shifted_high[e + 2 - dy, f], w_three[dy * taps_high : (dy + 1) * taps_high, :C0]
            )
        for j in range(nb):
            send_high[part, j] = total[:, j * slim : (j + 1) * slim].astype(bf16)

            @pl.when(b == j)
            def _():
                dy_high[part] = total[:, j * slim : (j + 1) * slim]

        spread = Spread(
            high_send.at[part],
            high_recv.at[part],
            lambda other, part=part: send_high.at[part, other],
            lambda j, part=part: recv_high.at[part, j],
        )
        spread.begin()
        spreads.append(spread)

    def put_grad(first, across, value, rows, start):
        for row, number in rows:
            for k in range(value.shape[1] // TILE):
                grad_ref[first + number * across + start + k] = value[
                    row : row + TILE, k * TILE : (k + 1) * TILE
                ].astype(bf16)

    out, width, taps, first = layers[3]
    for e in range(2):
        for f in range(2):
            turned_high[e, :, f * px : (f + 1) * px] = shifted_high[1 + e, f].T
    for dy in range(3):
        rows = [(dx * slim, 3 * dy + dx) for dx in range(3)]
        for half, source in enumerate((u_full, x_skip)):
            total = 0.0
            for e in range(2):
                for f in range(2):
                    value = source[e + dy, f].reshape(px, C0)
                    total = total + dot_nn(turned_high[e, :, f * px : (f + 1) * px], value)
            put_grad(first, width // TILE, total, rows, half * (C0 // TILE))
    for part in range(4):
        spreads[part].finish()
        total = dy_high[part]
        for step in range(1, nb):
            total = total + recv_high[part, ring(b + step, nb)].astype(f32)
        dub[:, part * slim : (part + 1) * slim] = total.astype(bf16)

    def input_low(number, product):
        for j in range(nb):
            total = product(j)
            send_low[j] = total.astype(bf16)

            @pl.when(b == j)
            def _():
                dy_low[0] = total

        spread = Spread(
            all_send.at[number],
            all_recv.at[number],
            lambda other: send_low.at[other],
            lambda j: recv_low.at[number - 1, j],
        )
        spread.begin()

        def finish():
            spread.finish()
            total = dy_low[0]
            for step in range(1, nb):
                total = total + recv_low[number - 1, ring(b + step, nb)].astype(f32)
            dy_low[0] = total

        return finish

    finish_sum = input_low(
        1, lambda j: dot_nn(dub[...], w_up[:, j * wide : (j + 1) * wide])
    )
    out, width, taps, first = layers[2]
    turned_low[: 4 * slim, :] = dub[...].T
    for j in range(nb):
        total = dot_nn(turned_low[: 4 * slim, :], a_two[:, j * wide : (j + 1) * wide])
        rows = [(part * slim, part) for part in range(4)]
        put_grad(first, width // TILE, total, rows, j * (wide // TILE))
    finish_sum()

    def back_low(number, z_ref, inv_ref, gain, shift):
        def grad_of(part, image):
            return dy_low[0, rows_of(image), :]

        buffer = reduce_wide.at[number - 2]
        back_sums(buffer, z_ref, dy_low, gain, shift, grad_of)
        total = all_reduce(number, buffer)

        def put(part, image, value):
            dz_low[1, rows_of(image), :] = value

        return back_apply(total, z_ref, dy_low, inv_ref, gain, size_low, put)

    def widen_low(row):
        value = dz_low[row]
        wider = value.astype(f32)
        shifted_low[row, :, :wide] = shift_up(wider).astype(bf16)
        shifted_low[row, :, wide : 2 * wide] = value
        shifted_low[row, :, 2 * wide :] = shift_down(wider).astype(bf16)

    def weight_low(number, source):
        out, width, taps, first = layers[number]
        turned_low[...] = shifted_low[1].T
        chunk = 2 * TILE
        for dy in range(3):
            rows = []
            for dx in range(3):
                for ob in range(wide // TILE):
                    rows.append((dx * wide + ob * TILE, ob * taps + 3 * dy + dx))
            for j in range(width // chunk):
                total = dot_nn(turned_low[...], source(dy, j * chunk, chunk))
                put_grad(first, width // TILE, total, rows, j * (chunk // TILE))

    gain_grad, shift_grad = back_low(4, z_two, inv_two, gain_two, shift_two)
    sums_ref[b, 2:3, :] = gain_grad
    sums_ref[b, 3:4, :] = shift_grad
    begin, finish = edges(1, dz_low.at[1], dz_low.at[0], dz_low.at[1], dz_low.at[2])
    begin()
    widen_low(1)
    finish()
    widen_low(0)
    widen_low(2)

    def product_two(j):
        total = 0.0
        for dy in range(3):
            total = total + dot_nn(
                shifted_low[2 - dy],
                w_two[3 * dy * wide : 3 * (dy + 1) * wide, j * wide : (j + 1) * wide],
            )
        return total

    finish_sum = input_low(2, product_two)
    weight_low(1, lambda dy, start, size: a_one[dy, :, start : start + size])
    finish_sum()
    gain_grad, shift_grad = back_low(5, z_one, inv_one, gain_one, shift_one)
    sums_ref[b, 0:1, :] = gain_grad
    sums_ref[b, 1:2, :] = shift_grad
    spread = Spread(
        all_send.at[3], all_recv.at[3], lambda other: sums_ref.at[b], lambda j: sums_ref.at[j]
    )
    spread.begin()
    widen_low(1)
    weight_low(0, lambda dy, start, size: x_one[dy].reshape(px, C0)[:, start : start + size])
    spread.finish()


def run_step(master, place, bias, image, skip, lab, wide_rows, narrow_rows):
    nr, nb = lax.axis_size("rows"), lax.axis_size("blk")
    cols = image.shape[0]
    px = nb * cols
    wide, slim = C1 // nb, C0 // nb
    vmem = pl.BlockSpec(memory_space=pltpu.VMEM)
    smem = pl.BlockSpec(memory_space=pltpu.SMEM)
    dma = pltpu.SemaphoreType.DMA
    scratch = [
        pltpu.VMEM((3, nb, cols, C0), bf16),
        pltpu.VMEM((4, 2, nb, cols, C0), bf16),
        pltpu.VMEM((nb, 4, 8, cols), f32),
        pltpu.VMEM((9 * wide, C0), bf16),
        pltpu.VMEM((9 * wide, C1), bf16),
        pltpu.VMEM((4 * slim, C1), bf16),
        pltpu.VMEM((9 * slim, 2 * C0), bf16),
        pltpu.VMEM((3, px, C1), bf16),
        pltpu.VMEM((px, C1), bf16),
        pltpu.VMEM((4, 2, px, C0), bf16),
        pltpu.VMEM((1, px, wide), f32),
        pltpu.VMEM((1, px, wide), f32),
        pltpu.VMEM((4, px, slim), f32),
        pltpu.VMEM((1, px, wide), f32),
        pltpu.VMEM((4, px, slim), f32),
        pltpu.VMEM((8, wide), f32),
        pltpu.VMEM((8, wide), f32),
        pltpu.VMEM((8, slim), f32),
        pltpu.VMEM((3, px, wide), bf16),
        pltpu.VMEM((4, 2, px, slim), bf16),
        pltpu.VMEM((3, px, 3 * wide), bf16),
        pltpu.VMEM((4, 2, px, 3 * slim), bf16),
        pltpu.VMEM((3 * wide, px), bf16),
        pltpu.VMEM((2, 3 * slim, 2 * px), bf16),
        pltpu.VMEM((px, 4 * slim), bf16),
        pltpu.VMEM((4, nb, px, slim), bf16),
        pltpu.VMEM((4, nb, px, slim), bf16),
        pltpu.VMEM((nb, px, wide), bf16),
        pltpu.VMEM((2, nb, px, wide), bf16),
        pltpu.VMEM((nb, 4 * nb, 8, cols), f32),
        pltpu.VMEM((4, nr, 2 * nb + 8, wide), f32),
        pltpu.VMEM((2, nr, 2 * nb + 8, slim), f32),
        dma((3, nr, 2)),
        dma((nr, 2)),
        dma((6, nb, 2)),
        dma((6, nb)),
        dma((6, nb, 2)),
        dma((6, nb, 2)),
        dma((6, nr)),
        dma((6, nr)),
        dma((4, nb)),
        dma((4, nb)),
        dma((4, nb)),
        dma((4, nb)),
        dma((2, 2)),
        dma((2, 2)),
    ]
    return pl.pallas_call(
        functools.partial(step_kernel, nr, nb, cols),
        out_shape=(
            jax.ShapeDtypeStruct((place.shape[0],) + master.shape[1:], bf16),
            jax.ShapeDtypeStruct((nb, 16, wide), f32),
        ),
        in_specs=[vmem, smem, smem, vmem, vmem, vmem, vmem, vmem],
        out_specs=(vmem, vmem),
        scratch_shapes=scratch,
        compiler_params=pltpu.CompilerParams(
            collective_id=0, has_side_effects=True, vmem_limit_bytes=60 * 2**20
        ),
    )(master, place, bias, image, skip, lab, wide_rows, narrow_rows)


def split(value):
    high = value.astype(bf16)
    return high, (value - high.astype(f32)).astype(bf16)


def product_three(left, right, right_dim):
    (a, b), (c, d) = left, right
    return lax.dot_general(
        jnp.concatenate([a, a, b], 1),
        jnp.concatenate([c, d, c], right_dim),
        (((1,), (right_dim,)), ((), ())),
        preferred_element_type=f32,
    )


def square_six(value):
    high = value.astype(bf16)
    rest = value - high.astype(f32)
    middle = rest.astype(bf16)
    low = (rest - middle.astype(f32)).astype(bf16)
    return lax.dot_general(
        jnp.concatenate([high, high, middle, high, middle, low], 1),
        jnp.concatenate([high, middle, high, low, middle, high], 1),
        (((1,), (1,)), ((), ())),
        preferred_element_type=f32,
    )


def soap_blocks(indices, grads, ins, outs):
    def every(function, *lists):
        return [function(*items) for items in zip(*lists)]

    def load(ref):
        return [ref[index] for index in indices]

    def store(ref, values):
        for index, value in zip(indices, values):
            ref[index] = value

    master_ref, first_ref, second_ref, left_ref, right_ref, left_stat_ref, right_stat_ref = ins
    left = load(left_ref)
    sides, bases = every(split, grads), every(split, load(right_ref))
    lefts, turned = every(split, left), every(lambda grad: split(grad.T), grads)

    def three(dim):
        return lambda one, two: product_three(one, two, dim)

    half = every(three(0), every(lambda value: split(value.T), left), sides)
    left_outer = every(three(1), sides, sides)
    rotated = every(three(0), every(split, half), bases)
    right_outer = every(three(1), turned, turned)
    first = every(
        lambda old, new: beta_one * old + (1.0 - beta_one) * new, load(first_ref), rotated
    )
    second = every(
        lambda old, new: beta_two * old + (1.0 - beta_two) * new * new, load(second_ref), rotated
    )
    store(outs[2], first)
    store(outs[3], second)
    direction = every(
        lambda one, two: one
        * (1.0 / (1.0 - beta_one**STEP))
        / (jnp.sqrt(two * (1.0 / (1.0 - beta_two**STEP))) + adam_eps),
        first,
        second,
    )
    half = every(three(0), lefts, every(split, direction))
    stats = []
    for ref, target, outer in (
        (left_stat_ref, outs[4], left_outer),
        (right_stat_ref, outs[5], right_outer),
    ):
        stat = every(
            lambda old, new: beta_stat * old + (1.0 - beta_stat) * new, load(ref), outer
        )
        store(target, stat)
        stats.append(every(split, stat))
    moved = every(three(0), stats[0], lefts)
    update = every(three(1), every(split, half), bases)
    moved_right = every(three(0), stats[1], bases)
    master = every(
        lambda old, new: old - soap_rate * (new + soap_decay * old), load(master_ref), update
    )
    store(outs[0], master)
    store(outs[1], every(lambda value: value.astype(bf16), master))
    store(outs[6], moved)
    store(outs[7], moved_right)
    store(outs[8], every(lambda value: square_six(value.T), moved))
    store(outs[9], every(lambda value: square_six(value.T), moved_right))


def collect_kernel(nr, size, *refs):
    (owner_ref, grad_ref), refs = refs[:2], refs[2:]
    ins, refs = refs[:7], refs[7:]
    outs, refs = refs[:10], refs[10:]
    (
        out_a,
        in_a,
        out_b,
        in_b,
        total,
        in_buffer,
        out_buffer,
        copy_buffer,
        a_send,
        a_recv,
        b_send,
        b_recv,
        in_sem,
        out_sem,
    ) = refs
    r = lax.axis_index("rows")
    b = lax.axis_index("blk")
    core = lax.rem(r, 2)
    chip = lax.div(r, 2)
    chips = nr // 2
    mate = r + 1 - 2 * core
    count = ins[0].shape[0]
    chunks = count // size

    def device(chip, core):
        return {"rows": 2 * chip + core, "blk": b}

    barrier = pltpu.get_barrier_semaphore()
    pl.semaphore_signal(
        barrier, inc=1, device_id={"rows": mate, "blk": b}, device_id_type=MESH
    )

    def greet(step, _):
        pl.semaphore_signal(
            barrier,
            inc=1,
            device_id=device(lax.rem(chip + step, chips), core),
            device_id_type=MESH,
        )
        return 0

    lax.fori_loop(1, chips, greet, 0)
    pl.semaphore_wait(barrier, chips)

    def loads(chunk):
        return [
            pltpu.make_async_copy(
                ref.at[pl.ds(chunk * size, size)],
                in_buffer.at[chunk % 2, number],
                in_sem.at[chunk % 2, number],
            )
            for number, ref in enumerate(ins)
        ]

    def stores(chunk):
        copies = []
        for number, ref in enumerate(outs):
            source = (
                copy_buffer.at[chunk % 2]
                if number == 1
                else out_buffer.at[chunk % 2, number - (number > 1)]
            )
            copies.append(
                pltpu.make_async_copy(
                    source, ref.at[pl.ds(chunk * size, size)], out_sem.at[chunk % 2, number]
                )
            )
        return copies

    def mine(to_chip, to_core, chunk, index):
        return grad_ref[owner_ref[(2 * to_chip + to_core) * count + chunk * size + index]]

    def send_a(chunk):
        return pltpu.make_async_remote_copy(
            src_ref=out_a.at[chunk],
            dst_ref=in_a.at[chunk],
            send_sem=a_send.at[chunk],
            recv_sem=a_recv.at[chunk],
            device_id={"rows": mate, "blk": b},
            device_id_type=MESH,
        )

    def send_b(chunk, step):
        other = lax.rem(chip + step, chips)
        return pltpu.make_async_remote_copy(
            src_ref=out_b.at[chunk, other],
            dst_ref=in_b.at[chunk, chip],
            send_sem=b_send.at[chunk, step],
            recv_sem=b_recv.at[chunk, chip],
            device_id=device(other, core),
            device_id_type=MESH,
        )

    for copy in loads(0):
        copy.start()
    for chunk in range(chunks):

        def fill(n, _, chunk=chunk):
            to_chip, index = lax.div(n, size), lax.rem(n, size)
            out_a[chunk, to_chip, index] = mine(to_chip, 1 - core, chunk, index)
            return 0

        lax.fori_loop(0, chips * size, fill, 0)
        send_a(chunk).start()
    for chunk in range(chunks):
        send_a(chunk).wait_recv()

        def join(step, _, chunk=chunk):
            other = lax.rem(chip + step, chips)

            def each(index, _):
                value = mine(other, core, chunk, index).astype(f32)
                value = value + in_a[chunk, other, index].astype(f32)
                out_b[chunk, other, index] = value.astype(bf16)
                return 0

            lax.fori_loop(0, size, each, 0)
            send_b(chunk, step).start()
            return 0

        lax.fori_loop(1, chips, join, 0)

        def keep(index, _, chunk=chunk):
            value = mine(chip, core, chunk, index).astype(f32)
            total[chunk, index] = value + in_a[chunk, chip, index].astype(f32)
            return 0

        lax.fori_loop(0, size, keep, 0)
    for chunk in range(chunks):
        if chunk + 1 < chunks:
            for copy in loads(chunk + 1):
                copy.start()
        for copy in loads(chunk):
            copy.wait()
        if chunk >= 2:
            for copy in stores(chunk - 2):
                copy.wait()

        def arrive(step, _, chunk=chunk):
            other = lax.rem(chip + step, chips)
            pltpu.make_async_remote_copy(
                src_ref=out_b.at[chunk, other],
                dst_ref=in_b.at[chunk, other],
                send_sem=b_send.at[chunk, step],
                recv_sem=b_recv.at[chunk, other],
                device_id=device(other, core),
                device_id_type=MESH,
            ).wait_recv()
            return 0

        lax.fori_loop(1, chips, arrive, 0)
        slot = chunk % 2
        chunk_ins = [in_buffer.at[slot, number] for number in range(7)]
        chunk_outs = [out_buffer.at[slot, number] for number in range(9)]
        chunk_outs.insert(1, copy_buffer.at[slot])

        grads = []
        for index in range(size):
            grads.append(
                lax.fori_loop(
                    1,
                    chips,
                    lambda step, value, chunk=chunk, index=index: value
                    + in_b[chunk, lax.rem(chip + step, chips), index].astype(f32),
                    total[chunk, index],
                )
            )
        soap_blocks(range(size), grads, chunk_ins, chunk_outs)
        for copy in stores(chunk):
            copy.start()
    for chunk in range(chunks):
        send_a(chunk).wait_send()
        lax.fori_loop(
            1, chips, lambda step, _, chunk=chunk: (send_b(chunk, step).wait_send(), 0)[1], 0
        )
        if chunk >= chunks - 2:
            for copy in stores(chunk):
                copy.wait()


def soap_update(blocks, owner, states):
    nr = lax.axis_size("rows")
    count, order = states[0].shape[0], states[0].shape[-1]
    size = 8 if count % 8 == 0 else count
    chunks = count // size
    anywhere = pl.BlockSpec(memory_space=pl.ANY)
    vmem = pl.BlockSpec(memory_space=pltpu.VMEM)
    shape = jax.ShapeDtypeStruct(states[0].shape, f32)
    dma = pltpu.SemaphoreType.DMA
    square = (order, order)
    results = pl.pallas_call(
        functools.partial(collect_kernel, nr, size),
        out_shape=(shape, jax.ShapeDtypeStruct(shape.shape, bf16)) + (shape,) * 8,
        in_specs=[pl.BlockSpec(memory_space=pltpu.SMEM), vmem] + [anywhere] * 7,
        out_specs=[anywhere] * 10,
        scratch_shapes=[
            pltpu.VMEM((chunks, nr // 2, size) + square, bf16),
            pltpu.VMEM((chunks, nr // 2, size) + square, bf16),
            pltpu.VMEM((chunks, nr // 2, size) + square, bf16),
            pltpu.VMEM((chunks, nr // 2, size) + square, bf16),
            pltpu.VMEM((chunks, size) + square, f32),
            pltpu.VMEM((2, 7, size) + square, f32),
            pltpu.VMEM((2, 9, size) + square, f32),
            pltpu.VMEM((2, size) + square, bf16),
            dma((chunks,)),
            dma((chunks,)),
            dma((chunks, nr // 2)),
            dma((chunks, nr // 2)),
            dma((2, 7)),
            dma((2, 10)),
        ],
        compiler_params=pltpu.CompilerParams(
            collective_id=1, has_side_effects=True, vmem_limit_bytes=60 * 2**20
        ),
    )(owner, blocks, *states)
    kept = list(results[:6])
    new_left, new_right, *kept = new_bases(results[6:8], results[8:], kept)
    new_master, new_copy, new_first, new_second, new_left_stat, new_right_stat = kept
    return [
        new_master,
        new_copy,
        new_first,
        new_second,
        new_left,
        new_right,
        new_left_stat,
        new_right_stat,
    ]


LANES = 128


def inverse_factor_kernel(stat_ref, inverse_ref, factor_ref):
    order = stat_ref.shape[0]
    tile = (8, LANES)
    sub = lax.broadcasted_iota(jnp.int32, tile, 0)
    groups = order // 8

    def eliminate(source_ref, base, starts, first, count, accs):
        width = len(starts)

        def body(group, accs):
            top = pl.multiple_of(group * 8, 8)
            accs = [list(acc) for acc in accs]
            for unit in range(8):
                values = [source_ref[top + unit, pl.ds(start, 8), :] for start in starts]
                for c in range(8):
                    scale = jnp.broadcast_to(
                        factor_ref[top + unit, pl.ds(base + c, 1), :], tile
                    )
                    for s in range(width):
                        accs[s][c] = accs[s][c] - values[s] * scale
            return tuple(tuple(acc) for acc in accs)

        return lax.fori_loop(first, count, body, tuple(tuple(acc) for acc in accs))

    def batches(first, last, run):
        total = last - first

        def at(group):
            return pl.multiple_of(group * 8, 8)

        def two(n, _):
            run(first + 2 * n, [at(first + 2 * n), at(first + 2 * n + 1)])
            return 0

        lax.fori_loop(0, lax.div(total, 2), two, 0)

        @pl.when(lax.rem(total, 2) == 1)
        def _():
            run(last - 1, [at(last - 1)])

    def block(kb, _):
        base = pl.multiple_of(kb * 8, 8)
        accs = [stat_ref[base + c, pl.ds(base, 8), :] for c in range(8)]
        accs = list(eliminate(factor_ref, base, [base], 0, kb, [accs])[0])
        scale = []
        coef = {}
        for c in range(8):
            scale.append(jnp.broadcast_to(lax.rsqrt(accs[c][c : c + 1, :]), tile))
            accs[c] = accs[c] * scale[c]
            for d in range(c + 1, 8):
                coef[(c, d)] = jnp.broadcast_to(accs[c][d : d + 1, :], tile)
                accs[d] = accs[d] - accs[c] * coef[(c, d)]
        for c in range(8):
            factor_ref[base + c, pl.ds(base, 8), :] = jnp.where(sub >= c, accs[c], 0.0)

        def finish(accs, target_ref, start):
            accs = list(accs)
            for c in range(8):
                for e in range(c):
                    accs[c] = accs[c] - accs[e] * coef[(e, c)]
                accs[c] = accs[c] * scale[c]
                target_ref[base + c, pl.ds(start, 8), :] = accs[c]

        def below(group, starts):
            accs = [[stat_ref[base + c, pl.ds(s, 8), :] for c in range(8)] for s in starts]
            accs = eliminate(factor_ref, base, starts, 0, kb, accs)
            for acc, start in zip(accs, starts):
                finish(acc, factor_ref, start)

        def left(group, starts):
            accs = [[jnp.zeros(tile, jnp.float32) for c in range(8)] for s in starts]
            accs = eliminate(inverse_ref, base, starts, group, kb, accs)
            for acc, start in zip(accs, starts):
                finish(acc, inverse_ref, start)

        def clear(group, _):
            start = pl.multiple_of(group * 8, 8)
            for c in range(8):
                inverse_ref[base + c, pl.ds(start, 8), :] = jnp.zeros(tile, jnp.float32)
            return 0

        batches(kb + 1, groups, below)
        batches(0, kb, left)
        finish([jnp.where(sub == c, 1.0, 0.0) for c in range(8)], inverse_ref, base)
        lax.fori_loop(kb + 1, groups, clear, 0)
        return 0

    lax.fori_loop(0, groups, block, 0)


def basis_kernel(left_gram_ref, right_gram_ref, left_ref, right_ref, *refs):
    number = (len(refs) - 7) // 3
    kept, new_left_ref, new_right_ref = refs[:number], refs[number], refs[number + 1]
    moved, refs = refs[number + 2 : 2 * number + 2], refs[2 * number + 2 :]
    stat_ref, inverse_ref, factor_ref, in_sem, out_sem, *halts = refs
    arriving = [
        pltpu.make_async_copy(source, halt, in_sem.at[n])
        for n, (source, halt) in enumerate(zip(kept, halts))
    ]
    leaving = [
        pltpu.make_async_copy(halt, target, out_sem.at[n])
        for n, (halt, target) in enumerate(zip(halts, moved))
    ]
    for copy in arriving:
        copy.start()
    order = left_gram_ref.shape[1]
    count = left_gram_ref.shape[0] // order
    spare = LANES - 2 * count

    def enter(row, _):
        rows = pl.ds(row, count, stride=order)
        values = [left_gram_ref[rows, :], right_gram_ref[rows, :]]
        if spare:
            column = lax.broadcasted_iota(jnp.int32, (spare, order), 1)
            values.append(jnp.where(column == row, 1.0, 0.0))
        stat_ref[row] = jnp.concatenate(values, 0).T
        return 0

    lax.fori_loop(0, order, enter, 0, unroll=8)
    for come, go in zip(arriving, leaving):
        come.wait()
        go.start()
    inverse_factor_kernel(stat_ref, inverse_ref, factor_ref)

    def leave(row, _):
        rows = pl.ds(row, count, stride=order)
        value = inverse_ref[row].T
        new_left_ref[rows, :] = value[:count]
        new_right_ref[rows, :] = value[count : 2 * count]
        return 0

    lax.fori_loop(0, order, leave, 0, unroll=8)

    def solve(index, _):
        rows = pl.ds(pl.multiple_of(index * order, order), order)
        for basis_ref, target_ref in ((left_ref, new_left_ref), (right_ref, new_right_ref)):
            target_ref[rows, :] = product_three(
                split(basis_ref[rows, :]), split(target_ref[rows, :]), 1
            )
        return 0

    lax.fori_loop(0, count, solve, 0, unroll=8 if count % 8 == 0 else 1)
    for copy in leaving:
        copy.wait()


def new_bases(products, grams, kept):
    count, order = products[0].shape[0], products[0].shape[-1]
    vmem = pl.BlockSpec(memory_space=pltpu.VMEM)
    anywhere = pl.BlockSpec(memory_space=pl.ANY)
    lanes = pltpu.VMEM((order, order, LANES), f32)
    flat = [value.reshape(count * order, order) for value in list(grams) + list(products)]
    results = pl.pallas_call(
        basis_kernel,
        out_shape=[jax.ShapeDtypeStruct(value.shape, value.dtype) for value in flat[:2] + kept],
        in_specs=[vmem] * 4 + [anywhere] * len(kept),
        out_specs=[vmem] * 2 + [anywhere] * len(kept),
        scratch_shapes=[lanes, lanes, lanes]
        + [pltpu.SemaphoreType.DMA((len(kept),))] * 2
        + [pltpu.VMEM(value.shape, value.dtype) for value in kept],
        compiler_params=pltpu.CompilerParams(vmem_limit_bytes=60 * 2**20),
    )(*flat, *kept)
    return [value.reshape(products[0].shape) for value in results[:2]] + list(results[2:])


def adam_small(grads, value, first, second):
    first_new = beta_one * first + (1.0 - beta_one) * grads
    second_new = beta_two * second + (1.0 - beta_two) * grads * grads
    direction = (
        first_new
        / (1.0 - beta_one**STEP)
        / (jnp.sqrt(second_new / (1.0 - beta_two**STEP)) + adam_eps)
    )
    return (first_new, second_new, value - small_rate * (direction + small_decay * value))


def local(
    image,
    skip,
    labels,
    weight_map,
    valid,
    owner,
    master,
    first_moment,
    second_moment,
    left_basis,
    right_basis,
    left_stat,
    right_stat,
    norm_params,
    norm_first,
    norm_second,
    head_bias,
    bias_first,
    bias_second,
):
    shards = lax.axis_size("blk")
    shard = lax.axis_index("blk")
    cols = image.shape[2]
    slots = jnp.arange(owner.shape[0])
    place = jnp.sum(jnp.where(owner[None, :] == slots[:, None], slots[None, :], 0), 1)
    widths = (C1, C1, C1, C1, C0, C0)
    rows = []
    offset = 0
    for width in widths:
        part = width // shards
        rows.append(lax.dynamic_slice_in_dim(norm_params, offset + shard * part, part))
        offset = offset + width
    heads = norm_params[offset:].reshape(C0, 2)
    part = C0 // shards
    heads = lax.dynamic_slice_in_dim(heads, shard * part, part).T
    wide_rows = jnp.pad(jnp.stack(rows[:4]), ((0, 4), (0, 0)))
    narrow_rows = jnp.concatenate(
        [jnp.pad(jnp.stack(rows[4:]), ((0, 6), (0, 0))), jnp.pad(heads, ((0, 6), (0, 0)))]
    )
    valid_float = valid.astype(f32)
    scales = valid_float * weight_map.astype(f32) * 0.125
    lab = jnp.stack([scales, labels.astype(f32), valid_float]).reshape(3, 2, cols, 2)
    lab = lab.transpose(1, 3, 0, 2).reshape(4, 3, cols)
    lab = jnp.pad(lab, ((0, 0), (0, 5), (0, 0)))
    skip = skip.reshape(2, cols, 2, C0).transpose(0, 2, 1, 3)
    blocks, sums = run_step(
        master[0], place.astype(jnp.int32), head_bias, image[0, 0], skip, lab, wide_rows, narrow_rows
    )
    loss_sum, valid_count = sums[0, 6, 0], sums[0, 9, 0]
    grad_bias = sums[0, 7:9, 0]
    grad_head = jnp.stack([sums[:, 5, :part].reshape(-1), sums[:, 5, part : 2 * part].reshape(-1)], 1)
    small = jnp.concatenate(
        [sums[:, row].reshape(-1) for row in range(4)]
        + [
            sums[:, 4, :part].reshape(-1),
            sums[:, 4, part : 2 * part].reshape(-1),
            grad_head.reshape(-1),
        ]
    )
    states = (
        master,
        first_moment,
        second_moment,
        left_basis,
        right_basis,
        left_stat,
        right_stat,
    )
    soap = soap_update(blocks, owner, [state[0] for state in states])
    soap = [value[None] for value in soap]
    norm_new = adam_small(small, norm_params, norm_first, norm_second)
    bias_new = adam_small(grad_bias, head_bias, bias_first, bias_second)
    return (
        loss_sum,
        valid_count,
        soap[0],
        soap[1],
        soap[2],
        soap[3],
        soap[4],
        soap[5],
        soap[6],
        soap[7],
        norm_new[0],
        norm_new[1],
        norm_new[2],
        bias_new[0],
        bias_new[1],
        bias_new[2],
    )


def solution(mesh):
    placed = (
        P("blk", "rows", None, None),
        P("blk", "rows", None, None),
        P("blk", "rows", None),
        P("blk", "rows", None),
        P("blk", "rows", None),
        P(),
        P("blk", "rows", None, None),
        P("blk", "rows", None, None),
        P("blk", "rows", None, None),
        P("blk", "rows", None, None),
        P("blk", "rows", None, None),
        P("blk", "rows", None, None),
        P("blk", "rows", None, None),
        P(),
        P(),
        P(),
        P(),
        P(),
        P(),
    )
    return jax.shard_map(
        local,
        mesh=mesh,
        in_specs=placed,
        out_specs=(
            P(),
            P(),
            P("blk", "rows", None, None),
            P("blk", "rows", None, None),
            P("blk", "rows", None, None),
            P("blk", "rows", None, None),
            P("blk", "rows", None, None),
            P("blk", "rows", None, None),
            P("blk", "rows", None, None),
            P("blk", "rows", None, None),
            P(),
            P(),
            P(),
            P(),
            P(),
            P(),
        ),
        check_vma=False,
    )
```

```python
import functools

import jax
import jax.numpy as jnp
from jax import lax
from jax.experimental import pallas as pl
from jax.experimental.pallas import tpu as pltpu
from jax.sharding import PartitionSpec as P

C0 = 512
C1 = 1024
GROUPS = 32
STEP = 10


beta_one = 0.9
beta_two = 0.999
beta_stat = 0.95
adam_eps = 1e-08
norm_eps = 1e-05
soap_rate = 0.008
soap_decay = 0.01
small_rate = 0.4
small_decay = 0.01
highest = lax.Precision.HIGHEST


MESH = pl.DeviceIdType.MESH
bf16 = jnp.bfloat16
f32 = jnp.float32
TILE = 128


def dot_nt(left, right):
    return lax.dot_general(left, right, (((1,), (1,)), ((), ())), preferred_element_type=f32)


def dot_nn(left, right):
    return jnp.dot(left, right, preferred_element_type=f32)


def sigmoid(value):
    return 1.0 / (1.0 + jnp.exp(-value))


def block_layers(nb):
    result = []
    first = 0
    for in_width, out_width, taps in ((C0, C1, 9), (C1, C1, 9), (C1, C0, 4), (2 * C0, C0, 9)):
        out = out_width // nb
        result.append((out, in_width, taps, first))
        first = first + out // TILE * taps * (in_width // TILE)
    return result


def step_kernel(
    nr,
    nb,
    cols,
    master_ref,
    place_ref,
    bias_ref,
    image_ref,
    skip_ref,
    lab_ref,
    wide_ref,
    narrow_ref,
    grad_ref,
    sums_ref,
    x_one,
    x_skip,
    x_lab,
    w_one,
    w_two,
    w_up,
    w_three,
    a_one,
    a_two,
    u_full,
    z_one,
    z_two,
    z_three,
    dy_low,
    dy_high,
    inv_one,
    inv_two,
    inv_three,
    dz_low,
    dz_high,
    shifted_low,
    shifted_high,
    turned_low,
    turned_high,
    dub,
    send_high,
    recv_high,
    send_low,
    recv_low,
    logit,
    reduce_wide,
    reduce_narrow,
    gather_send,
    gather_recv,
    line_send,
    line_recv,
    halo_send,
    halo_recv,
    red_send,
    red_recv,
    all_send,
    all_recv,
    high_send,
    high_recv,
    edge_send,
    edge_recv,
):
    r = lax.axis_index("rows")
    b = lax.axis_index("blk")
    px = nb * cols
    wide = C1 // nb
    slim = C0 // nb
    taps_high = 3 * slim
    layers = block_layers(nb)

    def remote(src, dst, send, recv, rows, blk):
        return pltpu.make_async_remote_copy(
            src_ref=src,
            dst_ref=dst,
            send_sem=send,
            recv_sem=recv,
            device_id={"rows": rows, "blk": blk},
            device_id_type=MESH,
        )

    def lanes(index, size):
        return pl.ds(pl.multiple_of(index * size, TILE), size)

    def ring(index, count):
        return lax.rem(index + count, count)

    barrier = pltpu.get_barrier_semaphore()

    def greet_rows(step, _):
        pl.semaphore_signal(
            barrier, inc=1, device_id={"rows": ring(r + step, nr), "blk": b}, device_id_type=MESH
        )
        return 0

    lax.fori_loop(1, nr, greet_rows, 0)
    for step in range(1, nb):
        pl.semaphore_signal(
            barrier, inc=1, device_id={"rows": r, "blk": ring(b + step, nb)}, device_id_type=MESH
        )
    pl.semaphore_wait(barrier, nr - 1 + nb - 1)

    class Exchange:
        def __init__(self, number, piece, up=None, down=None):
            self.number, self.piece, self.up, self.down = number, piece, up, down

        def right(self, j):
            return remote(
                self.piece(j),
                self.piece(j),
                line_send.at[self.number, j, 0],
                line_recv.at[self.number, j],
                r,
                ring(b + 1, nb),
            )

        def left(self, j):
            return remote(
                self.piece(j),
                self.piece(j),
                line_send.at[self.number, j, 1],
                line_recv.at[self.number, j],
                r,
                ring(b - 1, nb),
            )

        def higher(self, j):
            src, dst = self.up(j)
            return remote(
                src,
                dst,
                halo_send.at[self.number, j, 0],
                halo_recv.at[self.number, j, 0],
                ring(r + 1, nr),
                b,
            )

        def lower(self, j):
            src, dst = self.down(j)
            return remote(
                src,
                dst,
                halo_send.at[self.number, j, 1],
                halo_recv.at[self.number, j, 1],
                ring(r - 1, nr),
                b,
            )

        def halos(self, j):
            if self.up is None:
                return

            @pl.when(r + 1 < nr)
            def _():
                self.higher(j).start()

            @pl.when(r > 0)
            def _():
                self.lower(j).start()

        def begin(self):
            @pl.when(b + 1 < nb)
            def _():
                self.right(b).start()

            @pl.when(b > 0)
            def _():
                self.left(b).start()

            self.halos(b)

        def hop(self, k):
            @pl.when(b >= k)
            def _():
                self.right(b - k).wait_recv()

                @pl.when(b + 1 < nb)
                def _():
                    self.right(b - k).start()

                self.halos(b - k)

            @pl.when(b + k < nb)
            def _():
                self.left(b + k).wait_recv()

                @pl.when(b > 0)
                def _():
                    self.left(b + k).start()

                self.halos(b + k)

        def hops(self):
            for k in range(1, nb):
                self.hop(k)

        def finish(self):
            for k in range(nb):

                @pl.when((b >= k) & (b + 1 < nb))
                def _():
                    self.right(b - k).wait_send()

                @pl.when((b + k < nb) & (b > 0))
                def _():
                    self.left(b + k).wait_send()

            if self.up is None:
                return
            for j in range(nb):

                @pl.when(r + 1 < nr)
                def _():
                    self.higher(j).wait_send()
                    self.lower(j).wait_recv()

                @pl.when(r > 0)
                def _():
                    self.lower(j).wait_send()
                    self.higher(j).wait_recv()

    def reduce_start(number, buffer):
        def start(step, _):
            remote(
                buffer.at[r],
                buffer.at[r],
                red_send.at[number, step],
                red_recv.at[number, r],
                ring(r + step, nr),
                b,
            ).start()
            return 0

        lax.fori_loop(1, nr, start, 0, unroll=nr <= 8)

    def reduce_finish(number, buffer):
        def wait(step, _):
            source = ring(r + step, nr)
            copy = remote(
                buffer.at[source],
                buffer.at[source],
                red_send.at[number, step],
                red_recv.at[number, source],
                source,
                b,
            )
            copy.wait_recv()
            copy.wait_send()
            return 0

        lax.fori_loop(1, nr, wait, 0, unroll=nr <= 8)
        return lax.fori_loop(
            1, nr, lambda k, total: total + buffer[k], buffer[0], unroll=nr <= 8
        )

    def all_reduce(number, buffer):
        reduce_start(number, buffer)
        return reduce_finish(number, buffer)

    class Spread:
        def __init__(self, send, recv, source, target):
            self.send, self.recv, self.source, self.target = send, recv, source, target

        def copy(self, step):
            other = ring(b + step, nb)
            return remote(
                self.source(other),
                self.target(b),
                self.send.at[step],
                self.recv.at[b],
                r,
                other,
            )

        def begin(self):
            for step in range(1, nb):
                self.copy(step).start()

        def finish(self):
            for step in range(1, nb):
                other = ring(b + step, nb)
                remote(
                    self.source(other),
                    self.target(other),
                    self.send.at[step],
                    self.recv.at[other],
                    r,
                    other,
                ).wait_recv()
                self.copy(step).wait_send()

    class Gather:
        def __init__(self):
            self.size = master_ref.shape[0]
            self.chips = nr // 2
            self.core = lax.rem(r, 2)
            self.chip = lax.div(r, 2)
            self.mate = r + 1 - 2 * self.core
            self.square = self.chips == 4 and self.size % 2 == 0
            self.halves = 2 if self.square else 1

        def piece(self, row, half):
            part = self.size // self.halves
            return grad_ref.at[pl.ds(row * self.size + half * part, part)]

        def move(self, kind, target, row, half):
            return remote(
                self.piece(row, half),
                self.piece(row, half),
                gather_send.at[kind, row, half],
                gather_recv.at[row, half],
                target,
                b,
            )

        def direct(self, target):
            return remote(
                self.piece(r, 0),
                self.piece(r, 0),
                gather_send.at[0, target, 0],
                gather_recv.at[r, 0],
                target,
                b,
            )

        def beside(self, step):
            return 2 * lax.rem(self.chip + step, self.chips) + self.core

        def other(self, bit):
            away = self.chip + bit - 2 * bit * lax.rem(lax.div(self.chip, bit), 2)
            return 2 * away + self.core

        def begin(self):
            def cast(index, _):
                grad_ref[r * self.size + index] = master_ref[index].astype(bf16)
                return 0

            lax.fori_loop(0, self.size, cast, 0)
            if self.square:
                for half in range(2):
                    self.move(2, self.mate, r, half).start()
                    self.move(0, self.other(1), r, 1 - half).start()
                    self.move(1, self.other(2), r, half).start()
            else:
                self.move(2, self.mate, r, 0).start()

                def send(step, _):
                    self.direct(self.beside(step)).start()
                    return 0

                lax.fori_loop(1, self.chips, send, 0)

        def arrived(self, row, half):
            self.move(2, self.mate, row, half).wait_recv()

        def hand(self, row, half):
            self.arrived(row, half)
            self.move(2, self.mate, row, half).start()

        def forward(self, moves):
            image, lab, skip = moves
            for k in range(1, nb):
                image.hop(k)
                lab.hop(k)
            if self.square:
                x, y = self.other(1), self.other(2)
                corner = 2 * (3 - self.chip) + self.core
                self.hand(y, 0)
                self.move(0, x, y, 0).start()
                self.hand(x, 1)
                self.move(1, y, x, 1).start()
                skip.hop(1)
                self.hand(x, 0)
                self.hand(y, 1)
                self.hand(corner, 0)
                self.hand(corner, 1)
                rows = (r, x, y, corner)
                for half in range(2):
                    for row in rows:
                        self.arrived(row + 1 - 2 * self.core, half)
                for half in range(2):
                    for row in rows:
                        self.move(2, self.mate, row, half).wait_send()
                    self.move(0, x, r, half).wait_send()
                    self.move(1, y, r, half).wait_send()
                self.move(0, x, y, 0).wait_send()
                self.move(1, y, x, 1).wait_send()
            else:

                def pass_on(step, _):
                    self.hand(self.beside(step), 0)
                    return 0

                def close(step, _):
                    row = self.beside(step)
                    self.arrived(row + 1 - 2 * self.core, 0)
                    self.move(2, self.mate, row, 0).wait_send()
                    self.direct(row).wait_send()
                    return 0

                lax.fori_loop(1, self.chips, pass_on, 0)
                skip.hop(1)
                self.arrived(self.mate, 0)
                self.move(2, self.mate, r, 0).wait_send()
                lax.fori_loop(1, self.chips, close, 0)

    position = lax.rem(lax.broadcasted_iota(jnp.int32, (px, TILE), 0), cols)

    def mask_of(value, column):
        hit = position[:, :1] == column
        return jnp.where(hit, 0.0, value)

    def shift_down(value):
        return mask_of(pltpu.roll(value, 1, 0), 0)

    def shift_up(value):
        return mask_of(pltpu.roll(value, px - 1, 0), cols - 1)

    def group_sum(value, size):
        width = value.shape[-1]
        bits = size.bit_length() - 1
        first = lax.shift_right_logical(lax.broadcasted_iota(jnp.int32, (width, width), 0), bits)
        second = lax.shift_right_logical(lax.broadcasted_iota(jnp.int32, (width, width), 1), bits)
        same = jnp.where(first == second, 1.0, 0.0).astype(f32)
        return jnp.dot(value, same, preferred_element_type=f32, precision=highest)

    def rows_of(image):
        return pl.ds(image * cols, cols)

    def norm_sums(buffer, z_ref):
        for image in range(nb):
            first = 0.0
            second = 0.0
            for part in range(z_ref.shape[0]):
                value = z_ref[part, rows_of(image), :]
                first = first + jnp.sum(value, 0, keepdims=True)
                second = second + jnp.sum(value * value, 0, keepdims=True)
            buffer[r, image : image + 1, :] = first
            buffer[r, nb + image : nb + image + 1, :] = second

    def norm_apply(total, z_ref, inv_ref, gain, shift, size, put):
        width = z_ref.shape[-1]
        number = nr * cols * z_ref.shape[0] * size
        sums = group_sum(total[: 2 * nb], size) / number
        mean = sums[:nb]
        inv = lax.rsqrt(sums[nb:] - mean * mean + norm_eps)
        inv_ref[:nb, :] = inv
        for part in range(z_ref.shape[0]):
            for image in range(nb):
                value = z_ref[part, rows_of(image), :]
                value = (value - mean[image : image + 1]) * inv[image : image + 1]
                z_ref[part, rows_of(image), :] = value
                normed = value * gain + shift
                put(part, image, (normed * sigmoid(normed)).astype(bf16))

    def back_sums(buffer, z_ref, dy_ref, gain, shift, grad_of):
        for image in range(nb):
            first = 0.0
            second = 0.0
            for part in range(z_ref.shape[0]):
                value = z_ref[part, rows_of(image), :]
                normed = value * gain + shift
                gate = sigmoid(normed)
                grad = grad_of(part, image) * gate * (1.0 + normed * (1.0 - gate))
                dy_ref[part, rows_of(image), :] = grad
                first = first + jnp.sum(grad, 0, keepdims=True)
                second = second + jnp.sum(grad * value, 0, keepdims=True)
            buffer[r, image : image + 1, :] = first
            buffer[r, nb + image : nb + image + 1, :] = second

    def back_apply(total, z_ref, dy_ref, inv_ref, gain, size, put):
        number = nr * cols * z_ref.shape[0] * size
        sums = group_sum(total[: 2 * nb] * gain, size) / number
        inv = inv_ref[:nb, :]
        for part in range(z_ref.shape[0]):
            for image in range(nb):
                one = slice(image, image + 1)
                two = slice(nb + image, nb + image + 1)
                value = dy_ref[part, rows_of(image), :] * gain - sums[one]
                value = value - z_ref[part, rows_of(image), :] * sums[two]
                put(part, image, (value * inv[one]).astype(bf16))
        shift_grad = jnp.sum(total[:nb], 0, keepdims=True)
        gain_grad = jnp.sum(total[nb : 2 * nb], 0, keepdims=True)
        return gain_grad, shift_grad

    gather = Gather()
    gather.begin()
    x_one[1, b] = image_ref[...]
    x_skip[1:3, :, b] = skip_ref[...]
    x_lab[b] = lab_ref[...]
    move_image = Exchange(
        0,
        lambda j: x_one.at[1, j],
        lambda j: (x_one.at[1, j], x_one.at[0, j]),
        lambda j: (x_one.at[1, j], x_one.at[2, j]),
    )
    move_skip = Exchange(
        1,
        lambda j: x_skip.at[pl.ds(1, 2), :, j],
        lambda j: (x_skip.at[2, :, j], x_skip.at[0, :, j]),
        lambda j: (x_skip.at[1, :, j], x_skip.at[3, :, j]),
    )
    move_lab = Exchange(2, lambda j: x_lab.at[j])
    moves = (move_image, move_lab, move_skip)
    for move in moves:
        move.begin()
    @pl.when(r == 0)
    def _():
        x_one[0] = jnp.zeros_like(x_one[0])
        x_skip[0] = jnp.zeros_like(x_skip[0])
        a_one[0] = jnp.zeros_like(a_one[0])
        u_full[0] = jnp.zeros_like(u_full[0])
        dz_low[0] = jnp.zeros_like(dz_low[0])
        dz_high[0] = jnp.zeros_like(dz_high[0])

    @pl.when(r == nr - 1)
    def _():
        x_one[2] = jnp.zeros_like(x_one[2])
        x_skip[3] = jnp.zeros_like(x_skip[3])
        a_one[2] = jnp.zeros_like(a_one[2])
        u_full[3] = jnp.zeros_like(u_full[3])
        dz_low[2] = jnp.zeros_like(dz_low[2])
        dz_high[3] = jnp.zeros_like(dz_high[3])

    gather.forward(moves)
    move_image.finish()
    move_lab.finish()
    middle = max(1, nb // 2)
    for k in range(2, middle + 1):
        move_skip.hop(k)

    def arrange(number, target):
        out, width, taps, first = layers[number]
        across = width // TILE

        def body(n, _):
            ib = lax.rem(n, across)
            t = lax.rem(lax.div(n, across), taps)
            ob = lax.div(n, across * taps)
            target[
                pl.ds(pl.multiple_of(t * out + ob * TILE, TILE), TILE), lanes(ib, TILE)
            ] = grad_ref[place_ref[first + n]]
            return 0

        lax.fori_loop(0, out // TILE * taps * across, body, 0)

    arrange(0, w_one)
    gain_one, shift_one = wide_ref[0:1, :], wide_ref[1:2, :]
    gain_two, shift_two = wide_ref[2:3, :], wide_ref[3:4, :]
    gain_three, shift_three = narrow_ref[0:1, :], narrow_ref[1:2, :]
    size_low, size_high = C1 // GROUPS, C0 // GROUPS

    def conv_low(z_ref, weight, source, lines=(0, 1, 2), more=False):
        def tap(dx):
            total = 0.0
            for dy in lines:
                first = (3 * dy + dx) * wide
                total = total + dot_nt(source(dy), weight[first : first + wide, :])
            return total

        if more:
            z_ref[0] += tap(1)
        else:
            z_ref[0] = tap(1)
        z_ref[0] += shift_down(tap(0))
        z_ref[0] += shift_up(tap(2))

    conv_low(z_one, w_one, lambda dy: x_one[dy].reshape(px, C0))
    reduce_one, reduce_two = reduce_wide.at[0], reduce_wide.at[1]
    norm_sums(reduce_one, z_one)
    count = 0.0
    for image in range(nb):
        for part in range(4):
            count = count + jnp.sum(x_lab[image, part, 2:3, :], 1, keepdims=True)
    reduce_one[r, 2 * nb : 2 * nb + 1, :] = jnp.broadcast_to(count, (1, wide))
    reduce_start(0, reduce_one)
    arrange(1, w_two)
    total = reduce_finish(0, reduce_one)
    count = total[2 * nb : 2 * nb + 1, :1]

    def put_one(part, image, value):
        a_one[1, rows_of(image), lanes(b, wide)] = value

    norm_apply(total, z_one, inv_one, gain_one, shift_one, size_low, put_one)
    move = Exchange(
        3,
        lambda j: a_one.at[1, :, lanes(j, wide)],
        lambda j: (a_one.at[1, :, lanes(j, wide)], a_one.at[0, :, lanes(j, wide)]),
        lambda j: (a_one.at[1, :, lanes(j, wide)], a_one.at[2, :, lanes(j, wide)]),
    )
    move.begin()
    move.hop(1)
    arrange(2, w_up)
    for k in range(2, nb):
        move.hop(k)
    arrange(3, w_three)
    conv_low(z_two, w_two, lambda dy: a_one[dy], (1,))
    move.finish()
    for k in range(middle + 1, nb):
        move_skip.hop(k)
    conv_low(z_two, w_two, lambda dy: a_one[dy], (0, 2), True)
    norm_sums(reduce_two, z_two)
    total = all_reduce(1, reduce_two)

    def put_two(part, image, value):
        a_two[rows_of(image), lanes(b, wide)] = value

    norm_apply(total, z_two, inv_two, gain_two, shift_two, size_low, put_two)
    move = Exchange(4, lambda j: a_two.at[:, lanes(j, wide)])
    move.begin()
    move.hops()
    move.finish()
    for part in range(4):
        u_full[1 + part // 2, part % 2, :, lanes(b, slim)] = dot_nt(
            a_two[...], w_up[part * slim : (part + 1) * slim, :]
        ).astype(bf16)
    move = Exchange(
        5,
        lambda j: u_full.at[pl.ds(1, 2), :, :, lanes(j, slim)],
        lambda j: (u_full.at[2, :, :, lanes(j, slim)], u_full.at[0, :, :, lanes(j, slim)]),
        lambda j: (u_full.at[1, :, :, lanes(j, slim)], u_full.at[3, :, :, lanes(j, slim)]),
    )
    def conv_high(product, more):
        for e in range(2):
            even, odd = product(e, 0), product(e, 1)
            first = even[:, slim : 2 * slim] + shift_down(odd[:, :slim]) + odd[:, 2 * slim :]
            second = odd[:, slim : 2 * slim] + even[:, :slim] + shift_up(even[:, 2 * slim :])
            if more:
                z_three[2 * e] += first
                z_three[2 * e + 1] += second
            else:
                z_three[2 * e] = first
                z_three[2 * e + 1] = second

    def high_product(source, start, lines):
        def product(e, f):
            total = 0.0
            for dy in lines[e]:
                weight = w_three[dy * taps_high : (dy + 1) * taps_high, start : start + C0]
                total = total + dot_nt(source[e + dy, f].reshape(px, C0), weight)
            return total

        return product

    every = ((0, 1, 2), (0, 1, 2))
    inner, outer = ((1, 2), (0, 1)), ((0,), (2,))
    move.begin()
    move_skip.finish()
    conv_high(high_product(x_skip, C0, every), False)
    move.hops()
    conv_high(high_product(u_full, 0, inner), True)
    move.finish()
    conv_high(high_product(u_full, 0, outer), True)
    reduce_three, reduce_four = reduce_narrow.at[0], reduce_narrow.at[1]
    norm_sums(reduce_three, z_three)
    total = all_reduce(2, reduce_three)
    a_three = send_high

    def put_three(part, image, value):
        a_three[part, 0, rows_of(image), :] = value

    norm_apply(total, z_three, inv_three, gain_three, shift_three, size_high, put_three)
    head_low = narrow_ref[8:16, :].astype(bf16)
    head = head_low.astype(f32)
    for part in range(4):
        for image in range(nb):
            logit[b, part * nb + image] = dot_nt(
                head_low, a_three[part, 0, rows_of(image), :]
            )
    spread = Spread(all_send.at[0], all_recv.at[0], lambda other: logit.at[b], lambda j: logit.at[j])
    spread.begin()
    spread.finish()
    loss = jnp.zeros((1, cols), f32)
    bias_grad = [jnp.zeros((1, cols), f32), jnp.zeros((1, cols), f32)]
    head_grad = jnp.zeros((8, slim), f32)
    level = lax.broadcasted_iota(jnp.int32, (8, cols), 0)

    def head_of(part, image):
        tile = logit[0, part * nb + image]
        for j in range(1, nb):
            tile = tile + logit[j, part * nb + image]
        first = tile[0:1, :] + bias_ref[0]
        second = tile[1:2, :] + bias_ref[1]
        scale = x_lab[image, part, 0:1, :]
        label = x_lab[image, part, 1:2, :]
        largest = jnp.maximum(first, second)
        log_total = jnp.log(jnp.exp(first - largest) + jnp.exp(second - largest)) + largest
        picked = first * (1.0 - label) + second * label
        unit = scale / count
        return (
            scale * (log_total - picked),
            (jnp.exp(first - log_total) - (1.0 - label)) * unit,
            (jnp.exp(second - log_total) - label) * unit,
        )

    for part in range(4):
        for image in range(nb):
            cost, first, second = head_of(part, image)
            loss = loss + cost
            bias_grad = [bias_grad[0] + first, bias_grad[1] + second]
            tile = jnp.where(level == 0, first, jnp.where(level == 1, second, 0.0))
            logit[0, part * nb + image] = tile
            head_grad = head_grad + jnp.dot(
                tile,
                a_three[part, 0, rows_of(image), :].astype(f32),
                preferred_element_type=f32,
                precision=highest,
            )

    def grad_three(part, image):
        return lax.dot_general(
            logit[0, part * nb + image],
            head,
            (((0,), (0,)), ((), ())),
            preferred_element_type=f32,
            precision=highest,
        )

    reduce_four[r, 2 * nb : 2 * nb + 8, :] = head_grad
    for row, value in enumerate([loss] + bias_grad):
        reduce_four[r, 2 * nb + 2 + row : 2 * nb + 3 + row, :] = jnp.broadcast_to(
            jnp.sum(value, 1, keepdims=True), (1, slim)
        )
    back_sums(reduce_four, z_three, dy_high, gain_three, shift_three, grad_three)
    total = all_reduce(3, reduce_four)

    def put_high(part, image, value):
        dz_high[1 + part // 2, part % 2, rows_of(image), :] = value

    gain_grad, shift_grad = back_apply(
        total, z_three, dy_high, inv_three, gain_three, size_high, put_high
    )
    sums_ref[b] = jnp.zeros_like(sums_ref[b])
    sums_ref[b, 4:5, :slim] = gain_grad
    sums_ref[b, 4:5, slim : 2 * slim] = shift_grad
    sums_ref[b, 5:6, :slim] = total[2 * nb : 2 * nb + 1]
    sums_ref[b, 5:6, slim : 2 * slim] = total[2 * nb + 1 : 2 * nb + 2]
    for row in range(3):
        sums_ref[b, 6 + row : 7 + row, :slim] = total[2 * nb + 2 + row : 2 * nb + 3 + row]
    sums_ref[b, 9:10, :] = jnp.broadcast_to(count, (1, wide))

    def edges(number, source_up, target_up, source_down, target_down):
        def higher():
            return remote(
                source_up,
                target_up,
                edge_send.at[number, 0],
                edge_recv.at[number, 0],
                ring(r + 1, nr),
                b,
            )

        def lower():
            return remote(
                source_down,
                target_down,
                edge_send.at[number, 1],
                edge_recv.at[number, 1],
                ring(r - 1, nr),
                b,
            )

        def begin():
            @pl.when(r + 1 < nr)
            def _():
                higher().start()

            @pl.when(r > 0)
            def _():
                lower().start()

        def finish():
            @pl.when(r + 1 < nr)
            def _():
                higher().wait_send()
                lower().wait_recv()

            @pl.when(r > 0)
            def _():
                lower().wait_send()
                higher().wait_recv()

        return begin, finish

    def widen_high(row):
        even, odd = dz_high[row, 0], dz_high[row, 1]
        shifted_high[row, 0, :, :slim] = odd
        shifted_high[row, 0, :, slim : 2 * slim] = even
        shifted_high[row, 0, :, 2 * slim :] = shift_down(odd.astype(f32)).astype(bf16)
        shifted_high[row, 1, :, :slim] = shift_up(even.astype(f32)).astype(bf16)
        shifted_high[row, 1, :, slim : 2 * slim] = odd
        shifted_high[row, 1, :, 2 * slim :] = even

    begin, finish = edges(0, dz_high.at[2], dz_high.at[0], dz_high.at[1], dz_high.at[3])
    begin()
    widen_high(1)
    widen_high(2)
    finish()
    widen_high(0)
    widen_high(3)
    spreads = []
    own_high = []
    for part in range(4):
        e, f = part // 2, part % 2
        total = 0.0
        for dy in range(3):
            total = total + dot_nn(
                shifted_high[e + 2 - dy, f], w_three[dy * taps_high : (dy + 1) * taps_high, :C0]
            )
        for j in range(nb):
            send_high[part, j] = total[:, j * slim : (j + 1) * slim].astype(bf16)

            @pl.when(b == j)
            def _():
                dy_high[part] = total[:, j * slim : (j + 1) * slim]

        spread = Spread(
            high_send.at[part],
            high_recv.at[part],
            lambda other, part=part: send_high.at[part, other],
            lambda j, part=part: recv_high.at[part, j],
        )
        spread.begin()
        spreads.append(spread)

    def put_grad(first, across, value, rows, start):
        for row, number in rows:
            for k in range(value.shape[1] // TILE):
                grad_ref[first + number * across + start + k] = value[
                    row : row + TILE, k * TILE : (k + 1) * TILE
                ].astype(bf16)

    out, width, taps, first = layers[3]
    for e in range(2):
        for f in range(2):
            turned_high[e, :, f * px : (f + 1) * px] = shifted_high[1 + e, f].T
    for dy in range(3):
        rows = [(dx * slim, 3 * dy + dx) for dx in range(3)]
        for half, source in enumerate((u_full, x_skip)):
            total = 0.0
            for e in range(2):
                for f in range(2):
                    value = source[e + dy, f].reshape(px, C0)
                    total = total + dot_nn(turned_high[e, :, f * px : (f + 1) * px], value)
            put_grad(first, width // TILE, total, rows, half * (C0 // TILE))
    for part in range(4):
        spreads[part].finish()
        total = dy_high[part]
        for step in range(1, nb):
            total = total + recv_high[part, ring(b + step, nb)].astype(f32)
        dub[:, part * slim : (part + 1) * slim] = total.astype(bf16)

    def input_low(number, product):
        for j in range(nb):
            total = product(j)
            send_low[j] = total.astype(bf16)

            @pl.when(b == j)
            def _():
                dy_low[0] = total

        spread = Spread(
            all_send.at[number],
            all_recv.at[number],
            lambda other: send_low.at[other],
            lambda j: recv_low.at[number - 1, j],
        )
        spread.begin()

        def finish():
            spread.finish()
            total = dy_low[0]
            for step in range(1, nb):
                total = total + recv_low[number - 1, ring(b + step, nb)].astype(f32)
            dy_low[0] = total

        return finish

    finish_sum = input_low(
        1, lambda j: dot_nn(dub[...], w_up[:, j * wide : (j + 1) * wide])
    )
    out, width, taps, first = layers[2]
    turned_low[: 4 * slim, :] = dub[...].T
    for j in range(nb):
        total = dot_nn(turned_low[: 4 * slim, :], a_two[:, j * wide : (j + 1) * wide])
        rows = [(part * slim, part) for part in range(4)]
        put_grad(first, width // TILE, total, rows, j * (wide // TILE))
    finish_sum()

    def back_low(number, z_ref, inv_ref, gain, shift):
        def grad_of(part, image):
            return dy_low[0, rows_of(image), :]

        buffer = reduce_wide.at[number - 2]
        back_sums(buffer, z_ref, dy_low, gain, shift, grad_of)
        total = all_reduce(number, buffer)

        def put(part, image, value):
            dz_low[1, rows_of(image), :] = value

        return back_apply(total, z_ref, dy_low, inv_ref, gain, size_low, put)

    def widen_low(row):
        value = dz_low[row]
        wider = value.astype(f32)
        shifted_low[row, :, :wide] = shift_up(wider).astype(bf16)
        shifted_low[row, :, wide : 2 * wide] = value
        shifted_low[row, :, 2 * wide :] = shift_down(wider).astype(bf16)

    def weight_low(number, source):
        out, width, taps, first = layers[number]
        turned_low[...] = shifted_low[1].T
        chunk = 2 * TILE
        for dy in range(3):
            rows = []
            for dx in range(3):
                for ob in range(wide // TILE):
                    rows.append((dx * wide + ob * TILE, ob * taps + 3 * dy + dx))
            for j in range(width // chunk):
                total = dot_nn(turned_low[...], source(dy, j * chunk, chunk))
                put_grad(first, width // TILE, total, rows, j * (chunk // TILE))

    gain_grad, shift_grad = back_low(4, z_two, inv_two, gain_two, shift_two)
    sums_ref[b, 2:3, :] = gain_grad
    sums_ref[b, 3:4, :] = shift_grad
    begin, finish = edges(1, dz_low.at[1], dz_low.at[0], dz_low.at[1], dz_low.at[2])
    begin()
    widen_low(1)
    finish()
    widen_low(0)
    widen_low(2)

    def product_two(j):
        total = 0.0
        for dy in range(3):
            total = total + dot_nn(
                shifted_low[2 - dy],
                w_two[3 * dy * wide : 3 * (dy + 1) * wide, j * wide : (j + 1) * wide],
            )
        return total

    finish_sum = input_low(2, product_two)
    weight_low(1, lambda dy, start, size: a_one[dy, :, start : start + size])
    finish_sum()
    gain_grad, shift_grad = back_low(5, z_one, inv_one, gain_one, shift_one)
    sums_ref[b, 0:1, :] = gain_grad
    sums_ref[b, 1:2, :] = shift_grad
    spread = Spread(
        all_send.at[3], all_recv.at[3], lambda other: sums_ref.at[b], lambda j: sums_ref.at[j]
    )
    spread.begin()
    widen_low(1)
    weight_low(0, lambda dy, start, size: x_one[dy].reshape(px, C0)[:, start : start + size])
    spread.finish()


def run_step(master, place, bias, image, skip, lab, wide_rows, narrow_rows):
    nr, nb = lax.axis_size("rows"), lax.axis_size("blk")
    cols = image.shape[0]
    px = nb * cols
    wide, slim = C1 // nb, C0 // nb
    vmem = pl.BlockSpec(memory_space=pltpu.VMEM)
    smem = pl.BlockSpec(memory_space=pltpu.SMEM)
    dma = pltpu.SemaphoreType.DMA
    scratch = [
        pltpu.VMEM((3, nb, cols, C0), bf16),
        pltpu.VMEM((4, 2, nb, cols, C0), bf16),
        pltpu.VMEM((nb, 4, 8, cols), f32),
        pltpu.VMEM((9 * wide, C0), bf16),
        pltpu.VMEM((9 * wide, C1), bf16),
        pltpu.VMEM((4 * slim, C1), bf16),
        pltpu.VMEM((9 * slim, 2 * C0), bf16),
        pltpu.VMEM((3, px, C1), bf16),
        pltpu.VMEM((px, C1), bf16),
        pltpu.VMEM((4, 2, px, C0), bf16),
        pltpu.VMEM((1, px, wide), f32),
        pltpu.VMEM((1, px, wide), f32),
        pltpu.VMEM((4, px, slim), f32),
        pltpu.VMEM((1, px, wide), f32),
        pltpu.VMEM((4, px, slim), f32),
        pltpu.VMEM((8, wide), f32),
        pltpu.VMEM((8, wide), f32),
        pltpu.VMEM((8, slim), f32),
        pltpu.VMEM((3, px, wide), bf16),
        pltpu.VMEM((4, 2, px, slim), bf16),
        pltpu.VMEM((3, px, 3 * wide), bf16),
        pltpu.VMEM((4, 2, px, 3 * slim), bf16),
        pltpu.VMEM((3 * wide, px), bf16),
        pltpu.VMEM((2, 3 * slim, 2 * px), bf16),
        pltpu.VMEM((px, 4 * slim), bf16),
        pltpu.VMEM((4, nb, px, slim), bf16),
        pltpu.VMEM((4, nb, px, slim), bf16),
        pltpu.VMEM((nb, px, wide), bf16),
        pltpu.VMEM((2, nb, px, wide), bf16),
        pltpu.VMEM((nb, 4 * nb, 8, cols), f32),
        pltpu.VMEM((4, nr, 2 * nb + 8, wide), f32),
        pltpu.VMEM((2, nr, 2 * nb + 8, slim), f32),
        dma((3, nr, 2)),
        dma((nr, 2)),
        dma((6, nb, 2)),
        dma((6, nb)),
        dma((6, nb, 2)),
        dma((6, nb, 2)),
        dma((6, nr)),
        dma((6, nr)),
        dma((4, nb)),
        dma((4, nb)),
        dma((4, nb)),
        dma((4, nb)),
        dma((2, 2)),
        dma((2, 2)),
    ]
    return pl.pallas_call(
        functools.partial(step_kernel, nr, nb, cols),
        out_shape=(
            jax.ShapeDtypeStruct((place.shape[0],) + master.shape[1:], bf16),
            jax.ShapeDtypeStruct((nb, 16, wide), f32),
        ),
        in_specs=[vmem, smem, smem, vmem, vmem, vmem, vmem, vmem],
        out_specs=(vmem, vmem),
        scratch_shapes=scratch,
        compiler_params=pltpu.CompilerParams(
            collective_id=0, has_side_effects=True, vmem_limit_bytes=60 * 2**20
        ),
    )(master, place, bias, image, skip, lab, wide_rows, narrow_rows)


def split(value):
    high = value.astype(bf16)
    return high, (value - high.astype(f32)).astype(bf16)


def product_three(left, right, right_dim):
    (a, b), (c, d) = left, right
    return lax.dot_general(
        jnp.concatenate([a, a, b], 1),
        jnp.concatenate([c, d, c], right_dim),
        (((1,), (right_dim,)), ((), ())),
        preferred_element_type=f32,
    )


def square_six(value):
    high = value.astype(bf16)
    rest = value - high.astype(f32)
    middle = rest.astype(bf16)
    low = (rest - middle.astype(f32)).astype(bf16)
    return lax.dot_general(
        jnp.concatenate([high, high, middle, high, middle, low], 1),
        jnp.concatenate([high, middle, high, low, middle, high], 1),
        (((1,), (1,)), ((), ())),
        preferred_element_type=f32,
    )


def soap_blocks(indices, grads, ins, outs):
    def every(function, *lists):
        return [function(*items) for items in zip(*lists)]

    def load(ref):
        return [ref[index] for index in indices]

    def store(ref, values):
        for index, value in zip(indices, values):
            ref[index] = value

    master_ref, first_ref, second_ref, left_ref, right_ref, left_stat_ref, right_stat_ref = ins
    left = load(left_ref)
    sides, bases = every(split, grads), every(split, load(right_ref))
    lefts, turned = every(split, left), every(lambda grad: split(grad.T), grads)

    def three(dim):
        return lambda one, two: product_three(one, two, dim)

    half = every(three(0), every(lambda value: split(value.T), left), sides)
    left_outer = every(three(1), sides, sides)
    rotated = every(three(0), every(split, half), bases)
    right_outer = every(three(1), turned, turned)
    first = every(
        lambda old, new: beta_one * old + (1.0 - beta_one) * new, load(first_ref), rotated
    )
    second = every(
        lambda old, new: beta_two * old + (1.0 - beta_two) * new * new, load(second_ref), rotated
    )
    store(outs[2], first)
    store(outs[3], second)
    direction = every(
        lambda one, two: one
        * (1.0 / (1.0 - beta_one**STEP))
        / (jnp.sqrt(two * (1.0 / (1.0 - beta_two**STEP))) + adam_eps),
        first,
        second,
    )
    half = every(three(0), lefts, every(split, direction))
    stats = []
    for ref, target, outer in (
        (left_stat_ref, outs[4], left_outer),
        (right_stat_ref, outs[5], right_outer),
    ):
        stat = every(
            lambda old, new: beta_stat * old + (1.0 - beta_stat) * new, load(ref), outer
        )
        store(target, stat)
        stats.append(every(split, stat))
    moved = every(three(0), stats[0], lefts)
    update = every(three(1), every(split, half), bases)
    moved_right = every(three(0), stats[1], bases)
    master = every(
        lambda old, new: old - soap_rate * (new + soap_decay * old), load(master_ref), update
    )
    store(outs[0], master)
    store(outs[1], every(lambda value: value.astype(bf16), master))
    store(outs[6], moved)
    store(outs[7], moved_right)
    store(outs[8], every(lambda value: square_six(value.T), moved))
    store(outs[9], every(lambda value: square_six(value.T), moved_right))


def collect_kernel(nr, size, *refs):
    (owner_ref, grad_ref), refs = refs[:2], refs[2:]
    ins, refs = refs[:7], refs[7:]
    outs, refs = refs[:10], refs[10:]
    (
        out_a,
        in_a,
        out_b,
        in_b,
        total,
        in_buffer,
        out_buffer,
        copy_buffer,
        a_send,
        a_recv,
        b_send,
        b_recv,
        in_sem,
        out_sem,
    ) = refs
    r = lax.axis_index("rows")
    b = lax.axis_index("blk")
    core = lax.rem(r, 2)
    chip = lax.div(r, 2)
    chips = nr // 2
    mate = r + 1 - 2 * core
    count = ins[0].shape[0]
    chunks = count // size
    square = in_square(chips, size)
    half = size // 2

    def device(chip, core):
        return {"rows": 2 * chip + core, "blk": b}

    barrier = pltpu.get_barrier_semaphore()
    pl.semaphore_signal(
        barrier, inc=1, device_id={"rows": mate, "blk": b}, device_id_type=MESH
    )

    def greet(step, _):
        pl.semaphore_signal(
            barrier,
            inc=1,
            device_id=device(lax.rem(chip + step, chips), core),
            device_id_type=MESH,
        )
        return 0

    lax.fori_loop(1, chips, greet, 0)

    def loads(chunk):
        return [
            pltpu.make_async_copy(
                ref.at[pl.ds(chunk * size, size)],
                in_buffer.at[chunk % 2, number],
                in_sem.at[chunk % 2, number],
            )
            for number, ref in enumerate(ins)
        ]

    def stores(chunk):
        copies = []
        for number, ref in enumerate(outs):
            source = (
                copy_buffer.at[chunk % 2]
                if number == 1
                else out_buffer.at[chunk % 2, number - (number > 1)]
            )
            copies.append(
                pltpu.make_async_copy(
                    source, ref.at[pl.ds(chunk * size, size)], out_sem.at[chunk % 2, number]
                )
            )
        return copies

    def mine(to_chip, to_core, chunk, index):
        return grad_ref[owner_ref[(2 * to_chip + to_core) * count + chunk * size + index]]

    def joined(to_chip, chunk, index):
        value = mine(to_chip, core, chunk, index).astype(f32)
        return value + in_a[chunk, to_chip, index].astype(f32)

    def send_a(chunk):
        return pltpu.make_async_remote_copy(
            src_ref=out_a.at[chunk],
            dst_ref=in_a.at[chunk],
            send_sem=a_send.at[chunk],
            recv_sem=a_recv.at[chunk],
            device_id={"rows": mate, "blk": b},
            device_id_type=MESH,
        )

    def fill_a(chunk):
        def fill(n, _):
            to_chip, index = lax.div(n, size), lax.rem(n, size)
            out_a[chunk, to_chip, index] = mine(to_chip, 1 - core, chunk, index)
            return 0

        lax.fori_loop(0, chips * size, fill, 0)
        send_a(chunk).start()

    class Straight:
        def copy(self, chunk, step, source):
            other = lax.rem(chip + step, chips)
            return pltpu.make_async_remote_copy(
                src_ref=out_b.at[chunk, other],
                dst_ref=in_b.at[chunk, source],
                send_sem=b_send.at[chunk, step],
                recv_sem=b_recv.at[chunk, source],
                device_id=device(other, core),
                device_id_type=MESH,
            )

        def first(self, chunk):
            def join(step, _):
                other = lax.rem(chip + step, chips)

                def each(index, _):
                    out_b[chunk, other, index] = joined(other, chunk, index).astype(bf16)
                    return 0

                lax.fori_loop(0, size, each, 0)
                self.copy(chunk, step, chip).start()
                return 0

            lax.fori_loop(1, chips, join, 0)

        def second(self, chunk):
            pass

        def arrive(self, chunk):
            def wait(step, _):
                self.copy(chunk, step, lax.rem(chip + step, chips)).wait_recv()
                return 0

            lax.fori_loop(1, chips, wait, 0)

        def grad(self, chunk, index):
            return lax.fori_loop(
                1,
                chips,
                lambda step, value: value
                + in_b[chunk, lax.rem(chip + step, chips), index].astype(f32),
                total[chunk, index],
            )

        def close(self, chunk):
            def wait(step, _):
                self.copy(chunk, step, chip).wait_send()
                return 0

            lax.fori_loop(1, chips, wait, 0)

    class Square:
        def __init__(self):
            self.x = chip + 1 - 2 * lax.rem(chip, 2)
            self.y = chip + 2 - 4 * lax.div(chip, 2)
            self.corner = 3 - chip

        def one(self, chunk, way):
            return pltpu.make_async_remote_copy(
                src_ref=out_b.at[chunk, pl.ds(2 * way, 2)],
                dst_ref=in_b.at[chunk, pl.ds(2 * way, 2)],
                send_sem=b_send.at[chunk, way],
                recv_sem=b_recv.at[chunk, way],
                device_id=device((self.x, self.y)[way], core),
                device_id_type=MESH,
            )

        def two(self, chunk, way):
            return pltpu.make_async_remote_copy(
                src_ref=out_b.at[chunk, 4 + way],
                dst_ref=in_b.at[chunk, 4 + way],
                send_sem=b_send.at[chunk, 2 + way],
                recv_sem=b_recv.at[chunk, 2 + way],
                device_id=device((self.y, self.x)[way], core),
                device_id_type=MESH,
            )

        def first(self, chunk):
            for way, near in enumerate((self.x, self.y)):

                def each(index, _, way=way, near=near):
                    slot = way * half + index
                    out_b[chunk, 2 * way, index] = joined(near, chunk, slot).astype(bf16)
                    value = joined(self.corner, chunk, slot)
                    out_b[chunk, 2 * way + 1, index] = value.astype(bf16)
                    return 0

                lax.fori_loop(0, half, each, 0)
                self.one(chunk, way).start()

        def second(self, chunk):
            for way, far in enumerate((self.y, self.x)):
                self.one(chunk, way).wait_recv()

                def each(index, _, way=way, far=far):
                    value = joined(far, chunk, way * half + index)
                    value = value + in_b[chunk, 2 * way + 1, index].astype(f32)
                    out_b[chunk, 4 + way, index] = value.astype(bf16)
                    return 0

                lax.fori_loop(0, half, each, 0)
                self.two(chunk, way).start()

        def arrive(self, chunk):
            for way in range(2):
                self.two(chunk, way).wait_recv()

        def grad(self, chunk, index):
            way, place = index // half, index % half
            value = total[chunk, index] + in_b[chunk, 2 * way, place].astype(f32)
            return value + in_b[chunk, 4 + way, place].astype(f32)

        def close(self, chunk):
            for way in range(2):
                self.one(chunk, way).wait_send()
                self.two(chunk, way).wait_send()

    plan = Square() if square else Straight()

    def keep(chunk):
        def each(index, _):
            total[chunk, index] = joined(chip, chunk, index)
            return 0

        lax.fori_loop(0, size, each, 0)

    def work(chunk):
        plan.arrive(chunk)
        for copy in loads(chunk):
            copy.wait()
        if chunk >= 2:
            for copy in stores(chunk - 2):
                copy.wait()
        slot = chunk % 2
        chunk_ins = [in_buffer.at[slot, number] for number in range(7)]
        chunk_outs = [out_buffer.at[slot, number] for number in range(9)]
        chunk_outs.insert(1, copy_buffer.at[slot])
        grads = [plan.grad(chunk, index) for index in range(size)]
        soap_blocks(range(size), grads, chunk_ins, chunk_outs)
        for copy in stores(chunk):
            copy.start()
        if chunk + 2 < chunks:
            for copy in loads(chunk + 2):
                copy.start()

    for chunk in range(min(2, chunks)):
        for copy in loads(chunk):
            copy.start()
    pl.semaphore_wait(barrier, chips)
    for chunk in range(chunks):
        fill_a(chunk)
    for chunk in range(chunks + 2):
        if chunk < chunks:
            send_a(chunk).wait_recv()
            plan.first(chunk)
            keep(chunk)
        if 1 <= chunk <= chunks:
            plan.second(chunk - 1)
        if chunk >= 2:
            work(chunk - 2)
    for chunk in range(chunks):
        send_a(chunk).wait_send()
        plan.close(chunk)
        if chunk >= chunks - 2:
            for copy in stores(chunk):
                copy.wait()


def in_square(chips, size):
    return chips == 4 and size % 2 == 0


def soap_update(blocks, owner, states):
    nr = lax.axis_size("rows")
    count, order = states[0].shape[0], states[0].shape[-1]
    size = 8 if count % 8 == 0 else count
    chunks = count // size
    anywhere = pl.BlockSpec(memory_space=pl.ANY)
    vmem = pl.BlockSpec(memory_space=pltpu.VMEM)
    shape = jax.ShapeDtypeStruct(states[0].shape, f32)
    dma = pltpu.SemaphoreType.DMA
    square = (order, order)
    chips = nr // 2
    parts = (6, size // 2) if in_square(chips, size) else (chips, size)
    results = pl.pallas_call(
        functools.partial(collect_kernel, nr, size),
        out_shape=(shape, jax.ShapeDtypeStruct(shape.shape, bf16)) + (shape,) * 8,
        in_specs=[pl.BlockSpec(memory_space=pltpu.SMEM), vmem] + [anywhere] * 7,
        out_specs=[anywhere] * 10,
        scratch_shapes=[
            pltpu.VMEM((chunks, chips, size) + square, bf16),
            pltpu.VMEM((chunks, chips, size) + square, bf16),
            pltpu.VMEM((chunks,) + parts + square, bf16),
            pltpu.VMEM((chunks,) + parts + square, bf16),
            pltpu.VMEM((chunks, size) + square, f32),
            pltpu.VMEM((2, 7, size) + square, f32),
            pltpu.VMEM((2, 9, size) + square, f32),
            pltpu.VMEM((2, size) + square, bf16),
            dma((chunks,)),
            dma((chunks,)),
            dma((chunks, chips)),
            dma((chunks, chips)),
            dma((2, 7)),
            dma((2, 10)),
        ],
        compiler_params=pltpu.CompilerParams(
            collective_id=1, has_side_effects=True, vmem_limit_bytes=60 * 2**20
        ),
    )(owner, blocks, *states)
    kept = list(results[:6])
    new_left, new_right, *kept = new_bases(results[6:8], results[8:], kept)
    new_master, new_copy, new_first, new_second, new_left_stat, new_right_stat = kept
    return [
        new_master,
        new_copy,
        new_first,
        new_second,
        new_left,
        new_right,
        new_left_stat,
        new_right_stat,
    ]


LANES = 128


def inverse_factor_kernel(stat_ref, inverse_ref, factor_ref):
    order = stat_ref.shape[0]
    tile = (8, LANES)
    sub = lax.broadcasted_iota(jnp.int32, tile, 0)
    groups = order // 8

    def eliminate(source_ref, base, starts, first, count, accs):
        width = len(starts)

        def body(group, accs):
            top = pl.multiple_of(group * 8, 8)
            accs = [list(acc) for acc in accs]
            for unit in range(8):
                values = [source_ref[top + unit, pl.ds(start, 8), :] for start in starts]
                for c in range(8):
                    scale = jnp.broadcast_to(
                        factor_ref[top + unit, pl.ds(base + c, 1), :], tile
                    )
                    for s in range(width):
                        accs[s][c] = accs[s][c] - values[s] * scale
            return tuple(tuple(acc) for acc in accs)

        return lax.fori_loop(first, count, body, tuple(tuple(acc) for acc in accs))

    def batches(first, last, run):
        total = last - first

        def at(group):
            return pl.multiple_of(group * 8, 8)

        def two(n, _):
            run(first + 2 * n, [at(first + 2 * n), at(first + 2 * n + 1)])
            return 0

        lax.fori_loop(0, lax.div(total, 2), two, 0)

        @pl.when(lax.rem(total, 2) == 1)
        def _():
            run(last - 1, [at(last - 1)])

    def block(kb, _):
        base = pl.multiple_of(kb * 8, 8)
        accs = [stat_ref[base + c, pl.ds(base, 8), :] for c in range(8)]
        accs = list(eliminate(factor_ref, base, [base], 0, kb, [accs])[0])
        scale = []
        coef = {}
        for c in range(8):
            scale.append(jnp.broadcast_to(lax.rsqrt(accs[c][c : c + 1, :]), tile))
            accs[c] = accs[c] * scale[c]
            for d in range(c + 1, 8):
                coef[(c, d)] = jnp.broadcast_to(accs[c][d : d + 1, :], tile)
                accs[d] = accs[d] - accs[c] * coef[(c, d)]
        for c in range(8):
            factor_ref[base + c, pl.ds(base, 8), :] = jnp.where(sub >= c, accs[c], 0.0)

        def finish(accs, target_ref, start):
            accs = list(accs)
            for c in range(8):
                for e in range(c):
                    accs[c] = accs[c] - accs[e] * coef[(e, c)]
                accs[c] = accs[c] * scale[c]
                target_ref[base + c, pl.ds(start, 8), :] = accs[c]

        def below(group, starts):
            accs = [[stat_ref[base + c, pl.ds(s, 8), :] for c in range(8)] for s in starts]
            accs = eliminate(factor_ref, base, starts, 0, kb, accs)
            for acc, start in zip(accs, starts):
                finish(acc, factor_ref, start)

        def left(group, starts):
            accs = [[jnp.zeros(tile, jnp.float32) for c in range(8)] for s in starts]
            accs = eliminate(inverse_ref, base, starts, group, kb, accs)
            for acc, start in zip(accs, starts):
                finish(acc, inverse_ref, start)

        def clear(group, _):
            start = pl.multiple_of(group * 8, 8)
            for c in range(8):
                inverse_ref[base + c, pl.ds(start, 8), :] = jnp.zeros(tile, jnp.float32)
            return 0

        batches(kb + 1, groups, below)
        batches(0, kb, left)
        finish([jnp.where(sub == c, 1.0, 0.0) for c in range(8)], inverse_ref, base)
        lax.fori_loop(kb + 1, groups, clear, 0)
        return 0

    lax.fori_loop(0, groups, block, 0)


def basis_kernel(left_gram_ref, right_gram_ref, left_ref, right_ref, *refs):
    number = (len(refs) - 7) // 3
    kept, new_left_ref, new_right_ref = refs[:number], refs[number], refs[number + 1]
    moved, refs = refs[number + 2 : 2 * number + 2], refs[2 * number + 2 :]
    stat_ref, inverse_ref, factor_ref, in_sem, out_sem, *halts = refs
    arriving = [
        pltpu.make_async_copy(source, halt, in_sem.at[n])
        for n, (source, halt) in enumerate(zip(kept, halts))
    ]
    leaving = [
        pltpu.make_async_copy(halt, target, out_sem.at[n])
        for n, (halt, target) in enumerate(zip(halts, moved))
    ]
    for copy in arriving:
        copy.start()
    order = left_gram_ref.shape[1]
    count = left_gram_ref.shape[0] // order
    spare = LANES - 2 * count

    def enter(row, _):
        rows = pl.ds(row, count, stride=order)
        values = [left_gram_ref[rows, :], right_gram_ref[rows, :]]
        if spare:
            column = lax.broadcasted_iota(jnp.int32, (spare, order), 1)
            values.append(jnp.where(column == row, 1.0, 0.0))
        stat_ref[row] = jnp.concatenate(values, 0).T
        return 0

    lax.fori_loop(0, order, enter, 0, unroll=8)
    for come, go in zip(arriving, leaving):
        come.wait()
        go.start()
    inverse_factor_kernel(stat_ref, inverse_ref, factor_ref)

    def leave(row, _):
        rows = pl.ds(row, count, stride=order)
        value = inverse_ref[row].T
        new_left_ref[rows, :] = value[:count]
        new_right_ref[rows, :] = value[count : 2 * count]
        return 0

    lax.fori_loop(0, order, leave, 0, unroll=8)

    def solve(index, _):
        rows = pl.ds(pl.multiple_of(index * order, order), order)
        for basis_ref, target_ref in ((left_ref, new_left_ref), (right_ref, new_right_ref)):
            target_ref[rows, :] = product_three(
                split(basis_ref[rows, :]), split(target_ref[rows, :]), 1
            )
        return 0

    lax.fori_loop(0, count, solve, 0, unroll=8 if count % 8 == 0 else 1)
    for copy in leaving:
        copy.wait()


def new_bases(products, grams, kept):
    count, order = products[0].shape[0], products[0].shape[-1]
    vmem = pl.BlockSpec(memory_space=pltpu.VMEM)
    anywhere = pl.BlockSpec(memory_space=pl.ANY)
    lanes = pltpu.VMEM((order, order, LANES), f32)
    flat = [value.reshape(count * order, order) for value in list(grams) + list(products)]
    results = pl.pallas_call(
        basis_kernel,
        out_shape=[jax.ShapeDtypeStruct(value.shape, value.dtype) for value in flat[:2] + kept],
        in_specs=[vmem] * 4 + [anywhere] * len(kept),
        out_specs=[vmem] * 2 + [anywhere] * len(kept),
        scratch_shapes=[lanes, lanes, lanes]
        + [pltpu.SemaphoreType.DMA((len(kept),))] * 2
        + [pltpu.VMEM(value.shape, value.dtype) for value in kept],
        compiler_params=pltpu.CompilerParams(vmem_limit_bytes=60 * 2**20),
    )(*flat, *kept)
    return [value.reshape(products[0].shape) for value in results[:2]] + list(results[2:])


def adam_small(grads, value, first, second):
    first_new = beta_one * first + (1.0 - beta_one) * grads
    second_new = beta_two * second + (1.0 - beta_two) * grads * grads
    direction = (
        first_new
        / (1.0 - beta_one**STEP)
        / (jnp.sqrt(second_new / (1.0 - beta_two**STEP)) + adam_eps)
    )
    return (first_new, second_new, value - small_rate * (direction + small_decay * value))


def local(
    image,
    skip,
    labels,
    weight_map,
    valid,
    owner,
    master,
    first_moment,
    second_moment,
    left_basis,
    right_basis,
    left_stat,
    right_stat,
    norm_params,
    norm_first,
    norm_second,
    head_bias,
    bias_first,
    bias_second,
):
    shards = lax.axis_size("blk")
    shard = lax.axis_index("blk")
    cols = image.shape[2]
    slots = jnp.arange(owner.shape[0])
    place = jnp.sum(jnp.where(owner[None, :] == slots[:, None], slots[None, :], 0), 1)
    widths = (C1, C1, C1, C1, C0, C0)
    rows = []
    offset = 0
    for width in widths:
        part = width // shards
        rows.append(lax.dynamic_slice_in_dim(norm_params, offset + shard * part, part))
        offset = offset + width
    heads = norm_params[offset:].reshape(C0, 2)
    part = C0 // shards
    heads = lax.dynamic_slice_in_dim(heads, shard * part, part).T
    wide_rows = jnp.pad(jnp.stack(rows[:4]), ((0, 4), (0, 0)))
    narrow_rows = jnp.concatenate(
        [jnp.pad(jnp.stack(rows[4:]), ((0, 6), (0, 0))), jnp.pad(heads, ((0, 6), (0, 0)))]
    )
    valid_float = valid.astype(f32)
    scales = valid_float * weight_map.astype(f32) * 0.125
    lab = jnp.stack([scales, labels.astype(f32), valid_float]).reshape(3, 2, cols, 2)
    lab = lab.transpose(1, 3, 0, 2).reshape(4, 3, cols)
    lab = jnp.pad(lab, ((0, 0), (0, 5), (0, 0)))
    skip = skip.reshape(2, cols, 2, C0).transpose(0, 2, 1, 3)
    blocks, sums = run_step(
        master[0], place.astype(jnp.int32), head_bias, image[0, 0], skip, lab, wide_rows, narrow_rows
    )
    loss_sum, valid_count = sums[0, 6, 0], sums[0, 9, 0]
    grad_bias = sums[0, 7:9, 0]
    grad_head = jnp.stack([sums[:, 5, :part].reshape(-1), sums[:, 5, part : 2 * part].reshape(-1)], 1)
    small = jnp.concatenate(
        [sums[:, row].reshape(-1) for row in range(4)]
        + [
            sums[:, 4, :part].reshape(-1),
            sums[:, 4, part : 2 * part].reshape(-1),
            grad_head.reshape(-1),
        ]
    )
    states = (
        master,
        first_moment,
        second_moment,
        left_basis,
        right_basis,
        left_stat,
        right_stat,
    )
    soap = soap_update(blocks, owner, [state[0] for state in states])
    soap = [value[None] for value in soap]
    norm_new = adam_small(small, norm_params, norm_first, norm_second)
    bias_new = adam_small(grad_bias, head_bias, bias_first, bias_second)
    return (
        loss_sum,
        valid_count,
        soap[0],
        soap[1],
        soap[2],
        soap[3],
        soap[4],
        soap[5],
        soap[6],
        soap[7],
        norm_new[0],
        norm_new[1],
        norm_new[2],
        bias_new[0],
        bias_new[1],
        bias_new[2],
    )


def solution(mesh):
    placed = (
        P("blk", "rows", None, None),
        P("blk", "rows", None, None),
        P("blk", "rows", None),
        P("blk", "rows", None),
        P("blk", "rows", None),
        P(),
        P("blk", "rows", None, None),
        P("blk", "rows", None, None),
        P("blk", "rows", None, None),
        P("blk", "rows", None, None),
        P("blk", "rows", None, None),
        P("blk", "rows", None, None),
        P("blk", "rows", None, None),
        P(),
        P(),
        P(),
        P(),
        P(),
        P(),
    )
    return jax.shard_map(
        local,
        mesh=mesh,
        in_specs=placed,
        out_specs=(
            P(),
            P(),
            P("blk", "rows", None, None),
            P("blk", "rows", None, None),
            P("blk", "rows", None, None),
            P("blk", "rows", None, None),
            P("blk", "rows", None, None),
            P("blk", "rows", None, None),
            P("blk", "rows", None, None),
            P("blk", "rows", None, None),
            P(),
            P(),
            P(),
            P(),
            P(),
            P(),
        ),
        check_vma=False,
    )
```

```python
import functools

import jax
import jax.numpy as jnp
from jax import lax
from jax.experimental import pallas as pl
from jax.experimental.pallas import tpu as pltpu
from jax.sharding import PartitionSpec as P

C0 = 512
C1 = 1024
GROUPS = 32
STEP = 10


beta_one = 0.9
beta_two = 0.999
beta_stat = 0.95
adam_eps = 1e-08
norm_eps = 1e-05
soap_rate = 0.008
soap_decay = 0.01
small_rate = 0.4
small_decay = 0.01
highest = lax.Precision.HIGHEST


MESH = pl.DeviceIdType.MESH
bf16 = jnp.bfloat16
f32 = jnp.float32
TILE = 128


def dot_nt(left, right):
    return lax.dot_general(left, right, (((1,), (1,)), ((), ())), preferred_element_type=f32)


def dot_nn(left, right):
    return jnp.dot(left, right, preferred_element_type=f32)


def sigmoid(value):
    return 1.0 / (1.0 + jnp.exp(-value))


def block_layers(nb):
    result = []
    first = 0
    for in_width, out_width, taps in ((C0, C1, 9), (C1, C1, 9), (C1, C0, 4), (2 * C0, C0, 9)):
        out = out_width // nb
        result.append((out, in_width, taps, first))
        first = first + out // TILE * taps * (in_width // TILE)
    return result


def step_kernel(
    nr,
    nb,
    cols,
    master_ref,
    place_ref,
    bias_ref,
    image_ref,
    skip_ref,
    lab_ref,
    params_ref,
    head_ref,
    grad_ref,
    sums_ref,
    x_one,
    x_skip,
    x_lab,
    w_one,
    w_two,
    w_up,
    w_three,
    a_one,
    a_two,
    u_full,
    z_one,
    z_two,
    z_three,
    dy_low,
    dy_high,
    inv_one,
    inv_two,
    inv_three,
    dz_low,
    dz_high,
    shifted_low,
    shifted_high,
    turned_low,
    turned_high,
    dub,
    send_high,
    recv_high,
    send_low,
    recv_low,
    logit,
    reduce_wide,
    reduce_narrow,
    gather_send,
    gather_recv,
    line_send,
    line_recv,
    halo_send,
    halo_recv,
    red_send,
    red_recv,
    all_send,
    all_recv,
    high_send,
    high_recv,
    edge_send,
    edge_recv,
):
    r = lax.axis_index("rows")
    b = lax.axis_index("blk")
    px = nb * cols
    wide = C1 // nb
    slim = C0 // nb
    taps_high = 3 * slim
    layers = block_layers(nb)

    def remote(src, dst, send, recv, rows, blk):
        return pltpu.make_async_remote_copy(
            src_ref=src,
            dst_ref=dst,
            send_sem=send,
            recv_sem=recv,
            device_id={"rows": rows, "blk": blk},
            device_id_type=MESH,
        )

    def lanes(index, size):
        return pl.ds(pl.multiple_of(index * size, TILE), size)

    def ring(index, count):
        return lax.rem(index + count, count)

    barrier = pltpu.get_barrier_semaphore()

    def greet_rows(step, _):
        pl.semaphore_signal(
            barrier, inc=1, device_id={"rows": ring(r + step, nr), "blk": b}, device_id_type=MESH
        )
        return 0

    lax.fori_loop(1, nr, greet_rows, 0)
    for step in range(1, nb):
        pl.semaphore_signal(
            barrier, inc=1, device_id={"rows": r, "blk": ring(b + step, nb)}, device_id_type=MESH
        )
    pl.semaphore_wait(barrier, nr - 1 + nb - 1)

    class Exchange:
        def __init__(self, number, piece, up=None, down=None):
            self.number, self.piece, self.up, self.down = number, piece, up, down

        def right(self, j):
            return remote(
                self.piece(j),
                self.piece(j),
                line_send.at[self.number, j, 0],
                line_recv.at[self.number, j],
                r,
                ring(b + 1, nb),
            )

        def left(self, j):
            return remote(
                self.piece(j),
                self.piece(j),
                line_send.at[self.number, j, 1],
                line_recv.at[self.number, j],
                r,
                ring(b - 1, nb),
            )

        def higher(self, j):
            src, dst = self.up(j)
            return remote(
                src,
                dst,
                halo_send.at[self.number, j, 0],
                halo_recv.at[self.number, j, 0],
                ring(r + 1, nr),
                b,
            )

        def lower(self, j):
            src, dst = self.down(j)
            return remote(
                src,
                dst,
                halo_send.at[self.number, j, 1],
                halo_recv.at[self.number, j, 1],
                ring(r - 1, nr),
                b,
            )

        def halos(self, j):
            if self.up is None:
                return

            @pl.when(r + 1 < nr)
            def _():
                self.higher(j).start()

            @pl.when(r > 0)
            def _():
                self.lower(j).start()

        def begin(self):
            @pl.when(b + 1 < nb)
            def _():
                self.right(b).start()

            @pl.when(b > 0)
            def _():
                self.left(b).start()

            self.halos(b)

        def hop(self, k):
            @pl.when(b >= k)
            def _():
                self.right(b - k).wait_recv()

                @pl.when(b + 1 < nb)
                def _():
                    self.right(b - k).start()

                self.halos(b - k)

            @pl.when(b + k < nb)
            def _():
                self.left(b + k).wait_recv()

                @pl.when(b > 0)
                def _():
                    self.left(b + k).start()

                self.halos(b + k)

        def hops(self):
            for k in range(1, nb):
                self.hop(k)

        def finish(self):
            for k in range(nb):

                @pl.when((b >= k) & (b + 1 < nb))
                def _():
                    self.right(b - k).wait_send()

                @pl.when((b + k < nb) & (b > 0))
                def _():
                    self.left(b + k).wait_send()

            if self.up is None:
                return
            for j in range(nb):

                @pl.when(r + 1 < nr)
                def _():
                    self.higher(j).wait_send()
                    self.lower(j).wait_recv()

                @pl.when(r > 0)
                def _():
                    self.lower(j).wait_send()
                    self.higher(j).wait_recv()

    def reduce_start(number, buffer):
        def start(step, _):
            remote(
                buffer.at[r],
                buffer.at[r],
                red_send.at[number, step],
                red_recv.at[number, r],
                ring(r + step, nr),
                b,
            ).start()
            return 0

        lax.fori_loop(1, nr, start, 0, unroll=nr <= 8)

    def reduce_finish(number, buffer):
        def wait(step, _):
            source = ring(r + step, nr)
            copy = remote(
                buffer.at[source],
                buffer.at[source],
                red_send.at[number, step],
                red_recv.at[number, source],
                source,
                b,
            )
            copy.wait_recv()
            copy.wait_send()
            return 0

        lax.fori_loop(1, nr, wait, 0, unroll=nr <= 8)
        return lax.fori_loop(
            1, nr, lambda k, total: total + buffer[k], buffer[0], unroll=nr <= 8
        )

    def all_reduce(number, buffer):
        reduce_start(number, buffer)
        return reduce_finish(number, buffer)

    class Spread:
        def __init__(self, send, recv, source, target):
            self.send, self.recv, self.source, self.target = send, recv, source, target

        def copy(self, step):
            other = ring(b + step, nb)
            return remote(
                self.source(other),
                self.target(b),
                self.send.at[step],
                self.recv.at[b],
                r,
                other,
            )

        def begin(self):
            for step in range(1, nb):
                self.copy(step).start()

        def finish(self):
            for step in range(1, nb):
                other = ring(b + step, nb)
                remote(
                    self.source(other),
                    self.target(other),
                    self.send.at[step],
                    self.recv.at[other],
                    r,
                    other,
                ).wait_recv()
                self.copy(step).wait_send()

    class Gather:
        def __init__(self):
            self.size = master_ref.shape[0]
            self.chips = nr // 2
            self.core = lax.rem(r, 2)
            self.chip = lax.div(r, 2)
            self.mate = r + 1 - 2 * self.core
            self.square = self.chips == 4 and self.size % 2 == 0
            self.halves = 2 if self.square else 1

        def piece(self, row, half):
            part = self.size // self.halves
            return grad_ref.at[pl.ds(row * self.size + half * part, part)]

        def move(self, kind, target, row, half):
            return remote(
                self.piece(row, half),
                self.piece(row, half),
                gather_send.at[kind, row, half],
                gather_recv.at[row, half],
                target,
                b,
            )

        def direct(self, target):
            return remote(
                self.piece(r, 0),
                self.piece(r, 0),
                gather_send.at[0, target, 0],
                gather_recv.at[r, 0],
                target,
                b,
            )

        def beside(self, step):
            return 2 * lax.rem(self.chip + step, self.chips) + self.core

        def other(self, bit):
            away = self.chip + bit - 2 * bit * lax.rem(lax.div(self.chip, bit), 2)
            return 2 * away + self.core

        def begin(self):
            def cast(index, _):
                grad_ref[r * self.size + index] = master_ref[index].astype(bf16)
                return 0

            lax.fori_loop(0, self.size, cast, 0)
            if self.square:
                for half in range(2):
                    self.move(2, self.mate, r, half).start()
                    self.move(0, self.other(1), r, 1 - half).start()
                    self.move(1, self.other(2), r, half).start()
            else:
                self.move(2, self.mate, r, 0).start()

                def send(step, _):
                    self.direct(self.beside(step)).start()
                    return 0

                lax.fori_loop(1, self.chips, send, 0)

        def arrived(self, row, half):
            self.move(2, self.mate, row, half).wait_recv()

        def hand(self, row, half):
            self.arrived(row, half)
            self.move(2, self.mate, row, half).start()

        def forward(self, moves):
            image, lab, skip = moves
            for k in range(1, nb):
                image.hop(k)
                lab.hop(k)
            if self.square:
                x, y = self.other(1), self.other(2)
                corner = 2 * (3 - self.chip) + self.core
                self.hand(y, 0)
                self.move(0, x, y, 0).start()
                self.hand(x, 1)
                self.move(1, y, x, 1).start()
                skip.hop(1)
                self.hand(x, 0)
                self.hand(y, 1)
                self.hand(corner, 0)
                self.hand(corner, 1)
                rows = (r, x, y, corner)
                for half in range(2):
                    for row in rows:
                        self.arrived(row + 1 - 2 * self.core, half)
                for half in range(2):
                    for row in rows:
                        self.move(2, self.mate, row, half).wait_send()
                    self.move(0, x, r, half).wait_send()
                    self.move(1, y, r, half).wait_send()
                self.move(0, x, y, 0).wait_send()
                self.move(1, y, x, 1).wait_send()
            else:

                def pass_on(step, _):
                    self.hand(self.beside(step), 0)
                    return 0

                def close(step, _):
                    row = self.beside(step)
                    self.arrived(row + 1 - 2 * self.core, 0)
                    self.move(2, self.mate, row, 0).wait_send()
                    self.direct(row).wait_send()
                    return 0

                lax.fori_loop(1, self.chips, pass_on, 0)
                skip.hop(1)
                self.arrived(self.mate, 0)
                self.move(2, self.mate, r, 0).wait_send()
                lax.fori_loop(1, self.chips, close, 0)

    position = lax.rem(lax.broadcasted_iota(jnp.int32, (px, TILE), 0), cols)

    def mask_of(value, column):
        hit = position[:, :1] == column
        return jnp.where(hit, 0.0, value)

    def shift_down(value):
        return mask_of(pltpu.roll(value, 1, 0), 0)

    def shift_up(value):
        return mask_of(pltpu.roll(value, px - 1, 0), cols - 1)

    def group_sum(value, size):
        width = value.shape[-1]
        bits = size.bit_length() - 1
        first = lax.shift_right_logical(lax.broadcasted_iota(jnp.int32, (width, width), 0), bits)
        second = lax.shift_right_logical(lax.broadcasted_iota(jnp.int32, (width, width), 1), bits)
        same = jnp.where(first == second, 1.0, 0.0).astype(f32)
        return jnp.dot(value, same, preferred_element_type=f32, precision=highest)

    def rows_of(image):
        return pl.ds(image * cols, cols)

    def norm_sums(buffer, z_ref):
        for image in range(nb):
            first = 0.0
            second = 0.0
            for part in range(z_ref.shape[0]):
                value = z_ref[part, rows_of(image), :]
                first = first + jnp.sum(value, 0, keepdims=True)
                second = second + jnp.sum(value * value, 0, keepdims=True)
            buffer[r, image : image + 1, :] = first
            buffer[r, nb + image : nb + image + 1, :] = second

    def norm_apply(total, z_ref, inv_ref, gain, shift, size, put):
        width = z_ref.shape[-1]
        number = nr * cols * z_ref.shape[0] * size
        sums = group_sum(total[: 2 * nb], size) / number
        mean = sums[:nb]
        inv = lax.rsqrt(sums[nb:] - mean * mean + norm_eps)
        inv_ref[:nb, :] = inv
        for part in range(z_ref.shape[0]):
            for image in range(nb):
                value = z_ref[part, rows_of(image), :]
                value = (value - mean[image : image + 1]) * inv[image : image + 1]
                z_ref[part, rows_of(image), :] = value
                normed = value * gain + shift
                put(part, image, (normed * sigmoid(normed)).astype(bf16))

    def back_sums(buffer, z_ref, dy_ref, gain, shift, grad_of):
        for image in range(nb):
            first = 0.0
            second = 0.0
            for part in range(z_ref.shape[0]):
                value = z_ref[part, rows_of(image), :]
                normed = value * gain + shift
                gate = sigmoid(normed)
                grad = grad_of(part, image) * gate * (1.0 + normed * (1.0 - gate))
                dy_ref[part, rows_of(image), :] = grad
                first = first + jnp.sum(grad, 0, keepdims=True)
                second = second + jnp.sum(grad * value, 0, keepdims=True)
            buffer[r, image : image + 1, :] = first
            buffer[r, nb + image : nb + image + 1, :] = second

    def back_apply(total, z_ref, dy_ref, inv_ref, gain, size, put):
        number = nr * cols * z_ref.shape[0] * size
        sums = group_sum(total[: 2 * nb] * gain, size) / number
        inv = inv_ref[:nb, :]
        for part in range(z_ref.shape[0]):
            for image in range(nb):
                one = slice(image, image + 1)
                two = slice(nb + image, nb + image + 1)
                value = dy_ref[part, rows_of(image), :] * gain - sums[one]
                value = value - z_ref[part, rows_of(image), :] * sums[two]
                put(part, image, (value * inv[one]).astype(bf16))
        shift_grad = jnp.sum(total[:nb], 0, keepdims=True)
        gain_grad = jnp.sum(total[nb : 2 * nb], 0, keepdims=True)
        return gain_grad, shift_grad

    gather = Gather()
    gather.begin()
    x_one[1, b] = image_ref[...]
    x_skip[1:3, :, b] = skip_ref[...]
    x_lab[b] = lab_ref[...]
    move_image = Exchange(
        0,
        lambda j: x_one.at[1, j],
        lambda j: (x_one.at[1, j], x_one.at[0, j]),
        lambda j: (x_one.at[1, j], x_one.at[2, j]),
    )
    move_skip = Exchange(
        1,
        lambda j: x_skip.at[pl.ds(1, 2), :, j],
        lambda j: (x_skip.at[2, :, j], x_skip.at[0, :, j]),
        lambda j: (x_skip.at[1, :, j], x_skip.at[3, :, j]),
    )
    move_lab = Exchange(2, lambda j: x_lab.at[j])
    moves = (move_image, move_lab, move_skip)
    for move in moves:
        move.begin()
    @pl.when(r == 0)
    def _():
        x_one[0] = jnp.zeros_like(x_one[0])
        x_skip[0] = jnp.zeros_like(x_skip[0])
        a_one[0] = jnp.zeros_like(a_one[0])
        u_full[0] = jnp.zeros_like(u_full[0])
        dz_low[0] = jnp.zeros_like(dz_low[0])
        dz_high[0] = jnp.zeros_like(dz_high[0])

    @pl.when(r == nr - 1)
    def _():
        x_one[2] = jnp.zeros_like(x_one[2])
        x_skip[3] = jnp.zeros_like(x_skip[3])
        a_one[2] = jnp.zeros_like(a_one[2])
        u_full[3] = jnp.zeros_like(u_full[3])
        dz_low[2] = jnp.zeros_like(dz_low[2])
        dz_high[3] = jnp.zeros_like(dz_high[3])

    gather.forward(moves)
    move_image.finish()
    move_lab.finish()
    middle = max(1, nb // 2)
    for k in range(2, middle + 1):
        move_skip.hop(k)

    def arrange(number, target):
        out, width, taps, first = layers[number]
        across = width // TILE

        def body(n, _):
            ib = lax.rem(n, across)
            t = lax.rem(lax.div(n, across), taps)
            ob = lax.div(n, across * taps)
            target[
                pl.ds(pl.multiple_of(t * out + ob * TILE, TILE), TILE), lanes(ib, TILE)
            ] = grad_ref[place_ref[first + n]]
            return 0

        lax.fori_loop(0, out // TILE * taps * across, body, 0)

    arrange(0, w_one)
    def own_params(first, width):
        start = first // TILE + b * (width // TILE)
        return jnp.concatenate(
            [params_ref[pl.ds(start + n, 1), :] for n in range(width // TILE)], 1
        )

    gain_one, shift_one, gain_two, shift_two = [own_params(n * C1, wide) for n in range(4)]
    gain_three, shift_three = [own_params(4 * C1 + n * C0, slim) for n in range(2)]
    size_low, size_high = C1 // GROUPS, C0 // GROUPS

    def conv_low(z_ref, weight, source, lines=(0, 1, 2), more=False):
        def tap(dx):
            total = 0.0
            for dy in lines:
                first = (3 * dy + dx) * wide
                total = total + dot_nt(source(dy), weight[first : first + wide, :])
            return total

        if more:
            z_ref[0] += tap(1)
        else:
            z_ref[0] = tap(1)
        z_ref[0] += shift_down(tap(0))
        z_ref[0] += shift_up(tap(2))

    conv_low(z_one, w_one, lambda dy: x_one[dy].reshape(px, C0))
    reduce_one, reduce_two = reduce_wide.at[0], reduce_wide.at[1]
    norm_sums(reduce_one, z_one)
    count = 0.0
    for image in range(nb):
        for part in range(4):
            count = count + jnp.sum(x_lab[image, part, 2:3, :], 1, keepdims=True)
    reduce_one[r, 2 * nb : 2 * nb + 1, :] = jnp.broadcast_to(count, (1, wide))
    reduce_start(0, reduce_one)
    arrange(1, w_two)
    total = reduce_finish(0, reduce_one)
    count = total[2 * nb : 2 * nb + 1, :1]

    def put_one(part, image, value):
        a_one[1, rows_of(image), lanes(b, wide)] = value

    norm_apply(total, z_one, inv_one, gain_one, shift_one, size_low, put_one)
    move = Exchange(
        3,
        lambda j: a_one.at[1, :, lanes(j, wide)],
        lambda j: (a_one.at[1, :, lanes(j, wide)], a_one.at[0, :, lanes(j, wide)]),
        lambda j: (a_one.at[1, :, lanes(j, wide)], a_one.at[2, :, lanes(j, wide)]),
    )
    move.begin()
    move.hop(1)
    arrange(2, w_up)
    for k in range(2, nb):
        move.hop(k)
    arrange(3, w_three)
    conv_low(z_two, w_two, lambda dy: a_one[dy], (1,))
    move.finish()
    for k in range(middle + 1, nb):
        move_skip.hop(k)
    conv_low(z_two, w_two, lambda dy: a_one[dy], (0, 2), True)
    norm_sums(reduce_two, z_two)
    total = all_reduce(1, reduce_two)

    def put_two(part, image, value):
        a_two[rows_of(image), lanes(b, wide)] = value

    norm_apply(total, z_two, inv_two, gain_two, shift_two, size_low, put_two)
    move = Exchange(4, lambda j: a_two.at[:, lanes(j, wide)])
    move.begin()
    move.hops()
    move.finish()
    for part in range(4):
        u_full[1 + part // 2, part % 2, :, lanes(b, slim)] = dot_nt(
            a_two[...], w_up[part * slim : (part + 1) * slim, :]
        ).astype(bf16)
    move = Exchange(
        5,
        lambda j: u_full.at[pl.ds(1, 2), :, :, lanes(j, slim)],
        lambda j: (u_full.at[2, :, :, lanes(j, slim)], u_full.at[0, :, :, lanes(j, slim)]),
        lambda j: (u_full.at[1, :, :, lanes(j, slim)], u_full.at[3, :, :, lanes(j, slim)]),
    )
    def conv_high(product, more):
        for e in range(2):
            even, odd = product(e, 0), product(e, 1)
            first = even[:, slim : 2 * slim] + shift_down(odd[:, :slim]) + odd[:, 2 * slim :]
            second = odd[:, slim : 2 * slim] + even[:, :slim] + shift_up(even[:, 2 * slim :])
            if more:
                z_three[2 * e] += first
                z_three[2 * e + 1] += second
            else:
                z_three[2 * e] = first
                z_three[2 * e + 1] = second

    def high_product(source, start, lines):
        def product(e, f):
            total = 0.0
            for dy in lines[e]:
                weight = w_three[dy * taps_high : (dy + 1) * taps_high, start : start + C0]
                total = total + dot_nt(source[e + dy, f].reshape(px, C0), weight)
            return total

        return product

    every = ((0, 1, 2), (0, 1, 2))
    inner, outer = ((1, 2), (0, 1)), ((0,), (2,))
    move.begin()
    move_skip.finish()
    conv_high(high_product(x_skip, C0, every), False)
    move.hops()
    conv_high(high_product(u_full, 0, inner), True)
    move.finish()
    conv_high(high_product(u_full, 0, outer), True)
    reduce_three, reduce_four = reduce_narrow.at[0], reduce_narrow.at[1]
    norm_sums(reduce_three, z_three)
    total = all_reduce(2, reduce_three)
    a_three = send_high

    def put_three(part, image, value):
        a_three[part, 0, rows_of(image), :] = value

    norm_apply(total, z_three, inv_three, gain_three, shift_three, size_high, put_three)
    head_low = head_ref[...].astype(bf16)
    head = head_low.astype(f32)
    for part in range(4):
        for image in range(nb):
            logit[b, part * nb + image] = dot_nt(
                head_low, a_three[part, 0, rows_of(image), :]
            )
    spread = Spread(all_send.at[0], all_recv.at[0], lambda other: logit.at[b], lambda j: logit.at[j])
    spread.begin()
    spread.finish()
    loss = jnp.zeros((1, cols), f32)
    bias_grad = [jnp.zeros((1, cols), f32), jnp.zeros((1, cols), f32)]
    head_grad = jnp.zeros((8, slim), f32)
    level = lax.broadcasted_iota(jnp.int32, (8, cols), 0)

    def head_of(part, image):
        tile = logit[0, part * nb + image]
        for j in range(1, nb):
            tile = tile + logit[j, part * nb + image]
        first = tile[0:1, :] + bias_ref[0]
        second = tile[1:2, :] + bias_ref[1]
        label = x_lab[image, part, 0:1, :]
        scale = x_lab[image, part, 1:2, :] * x_lab[image, part, 2:3, :] * 0.125
        largest = jnp.maximum(first, second)
        log_total = jnp.log(jnp.exp(first - largest) + jnp.exp(second - largest)) + largest
        picked = first * (1.0 - label) + second * label
        unit = scale / count
        return (
            scale * (log_total - picked),
            (jnp.exp(first - log_total) - (1.0 - label)) * unit,
            (jnp.exp(second - log_total) - label) * unit,
        )

    for part in range(4):
        for image in range(nb):
            cost, first, second = head_of(part, image)
            loss = loss + cost
            bias_grad = [bias_grad[0] + first, bias_grad[1] + second]
            tile = jnp.where(level == 0, first, jnp.where(level == 1, second, 0.0))
            logit[0, part * nb + image] = tile
            head_grad = head_grad + jnp.dot(
                tile,
                a_three[part, 0, rows_of(image), :].astype(f32),
                preferred_element_type=f32,
                precision=highest,
            )

    def grad_three(part, image):
        return lax.dot_general(
            logit[0, part * nb + image],
            head,
            (((0,), (0,)), ((), ())),
            preferred_element_type=f32,
            precision=highest,
        )

    reduce_four[r, 2 * nb : 2 * nb + 8, :] = head_grad
    for row, value in enumerate([loss] + bias_grad):
        reduce_four[r, 2 * nb + 2 + row : 2 * nb + 3 + row, :] = jnp.broadcast_to(
            jnp.sum(value, 1, keepdims=True), (1, slim)
        )
    back_sums(reduce_four, z_three, dy_high, gain_three, shift_three, grad_three)
    total = all_reduce(3, reduce_four)

    def put_high(part, image, value):
        dz_high[1 + part // 2, part % 2, rows_of(image), :] = value

    gain_grad, shift_grad = back_apply(
        total, z_three, dy_high, inv_three, gain_three, size_high, put_high
    )
    sums_ref[b] = jnp.zeros_like(sums_ref[b])
    sums_ref[b, 4:5, :slim] = gain_grad
    sums_ref[b, 4:5, slim : 2 * slim] = shift_grad
    sums_ref[b, 5:6, :slim] = total[2 * nb : 2 * nb + 1]
    sums_ref[b, 5:6, slim : 2 * slim] = total[2 * nb + 1 : 2 * nb + 2]
    for row in range(3):
        sums_ref[b, 6 + row : 7 + row, :slim] = total[2 * nb + 2 + row : 2 * nb + 3 + row]
    sums_ref[b, 9:10, :] = jnp.broadcast_to(count, (1, wide))

    def edges(number, source_up, target_up, source_down, target_down):
        def higher():
            return remote(
                source_up,
                target_up,
                edge_send.at[number, 0],
                edge_recv.at[number, 0],
                ring(r + 1, nr),
                b,
            )

        def lower():
            return remote(
                source_down,
                target_down,
                edge_send.at[number, 1],
                edge_recv.at[number, 1],
                ring(r - 1, nr),
                b,
            )

        def begin():
            @pl.when(r + 1 < nr)
            def _():
                higher().start()

            @pl.when(r > 0)
            def _():
                lower().start()

        def finish():
            @pl.when(r + 1 < nr)
            def _():
                higher().wait_send()
                lower().wait_recv()

            @pl.when(r > 0)
            def _():
                lower().wait_send()
                higher().wait_recv()

        return begin, finish

    def widen_high(row):
        even, odd = dz_high[row, 0], dz_high[row, 1]
        shifted_high[row, 0, :, :slim] = odd
        shifted_high[row, 0, :, slim : 2 * slim] = even
        shifted_high[row, 0, :, 2 * slim :] = shift_down(odd.astype(f32)).astype(bf16)
        shifted_high[row, 1, :, :slim] = shift_up(even.astype(f32)).astype(bf16)
        shifted_high[row, 1, :, slim : 2 * slim] = odd
        shifted_high[row, 1, :, 2 * slim :] = even

    begin, finish = edges(0, dz_high.at[2], dz_high.at[0], dz_high.at[1], dz_high.at[3])
    begin()
    widen_high(1)
    widen_high(2)
    finish()
    widen_high(0)
    widen_high(3)
    spreads = []
    own_high = []
    for part in range(4):
        e, f = part // 2, part % 2
        total = 0.0
        for dy in range(3):
            total = total + dot_nn(
                shifted_high[e + 2 - dy, f], w_three[dy * taps_high : (dy + 1) * taps_high, :C0]
            )
        for j in range(nb):
            send_high[part, j] = total[:, j * slim : (j + 1) * slim].astype(bf16)

            @pl.when(b == j)
            def _():
                dy_high[part] = total[:, j * slim : (j + 1) * slim]

        spread = Spread(
            high_send.at[part],
            high_recv.at[part],
            lambda other, part=part: send_high.at[part, other],
            lambda j, part=part: recv_high.at[part, j],
        )
        spread.begin()
        spreads.append(spread)

    def put_grad(first, across, value, rows, start):
        for row, number in rows:
            for k in range(value.shape[1] // TILE):
                grad_ref[first + number * across + start + k] = value[
                    row : row + TILE, k * TILE : (k + 1) * TILE
                ].astype(bf16)

    out, width, taps, first = layers[3]
    for e in range(2):
        for f in range(2):
            turned_high[e, :, f * px : (f + 1) * px] = shifted_high[1 + e, f].T
    for dy in range(3):
        rows = [(dx * slim, 3 * dy + dx) for dx in range(3)]
        for half, source in enumerate((u_full, x_skip)):
            total = 0.0
            for e in range(2):
                for f in range(2):
                    value = source[e + dy, f].reshape(px, C0)
                    total = total + dot_nn(turned_high[e, :, f * px : (f + 1) * px], value)
            put_grad(first, width // TILE, total, rows, half * (C0 // TILE))
    for part in range(4):
        spreads[part].finish()
        total = dy_high[part]
        for step in range(1, nb):
            total = total + recv_high[part, ring(b + step, nb)].astype(f32)
        dub[:, part * slim : (part + 1) * slim] = total.astype(bf16)

    def input_low(number, product):
        for j in range(nb):
            total = product(j)
            send_low[j] = total.astype(bf16)

            @pl.when(b == j)
            def _():
                dy_low[0] = total

        spread = Spread(
            all_send.at[number],
            all_recv.at[number],
            lambda other: send_low.at[other],
            lambda j: recv_low.at[number - 1, j],
        )
        spread.begin()

        def finish():
            spread.finish()
            total = dy_low[0]
            for step in range(1, nb):
                total = total + recv_low[number - 1, ring(b + step, nb)].astype(f32)
            dy_low[0] = total

        return finish

    finish_sum = input_low(
        1, lambda j: dot_nn(dub[...], w_up[:, j * wide : (j + 1) * wide])
    )
    out, width, taps, first = layers[2]
    turned_low[: 4 * slim, :] = dub[...].T
    for j in range(nb):
        total = dot_nn(turned_low[: 4 * slim, :], a_two[:, j * wide : (j + 1) * wide])
        rows = [(part * slim, part) for part in range(4)]
        put_grad(first, width // TILE, total, rows, j * (wide // TILE))
    finish_sum()

    def back_low(number, z_ref, inv_ref, gain, shift):
        def grad_of(part, image):
            return dy_low[0, rows_of(image), :]

        buffer = reduce_wide.at[number - 2]
        back_sums(buffer, z_ref, dy_low, gain, shift, grad_of)
        total = all_reduce(number, buffer)

        def put(part, image, value):
            dz_low[1, rows_of(image), :] = value

        return back_apply(total, z_ref, dy_low, inv_ref, gain, size_low, put)

    def widen_low(row):
        value = dz_low[row]
        wider = value.astype(f32)
        shifted_low[row, :, :wide] = shift_up(wider).astype(bf16)
        shifted_low[row, :, wide : 2 * wide] = value
        shifted_low[row, :, 2 * wide :] = shift_down(wider).astype(bf16)

    def weight_low(number, source):
        out, width, taps, first = layers[number]
        turned_low[...] = shifted_low[1].T
        chunk = 2 * TILE
        for dy in range(3):
            rows = []
            for dx in range(3):
                for ob in range(wide // TILE):
                    rows.append((dx * wide + ob * TILE, ob * taps + 3 * dy + dx))
            for j in range(width // chunk):
                total = dot_nn(turned_low[...], source(dy, j * chunk, chunk))
                put_grad(first, width // TILE, total, rows, j * (chunk // TILE))

    gain_grad, shift_grad = back_low(4, z_two, inv_two, gain_two, shift_two)
    sums_ref[b, 2:3, :] = gain_grad
    sums_ref[b, 3:4, :] = shift_grad
    begin, finish = edges(1, dz_low.at[1], dz_low.at[0], dz_low.at[1], dz_low.at[2])
    begin()
    widen_low(1)
    finish()
    widen_low(0)
    widen_low(2)

    def product_two(j):
        total = 0.0
        for dy in range(3):
            total = total + dot_nn(
                shifted_low[2 - dy],
                w_two[3 * dy * wide : 3 * (dy + 1) * wide, j * wide : (j + 1) * wide],
            )
        return total

    finish_sum = input_low(2, product_two)
    weight_low(1, lambda dy, start, size: a_one[dy, :, start : start + size])
    finish_sum()
    gain_grad, shift_grad = back_low(5, z_one, inv_one, gain_one, shift_one)
    sums_ref[b, 0:1, :] = gain_grad
    sums_ref[b, 1:2, :] = shift_grad
    spread = Spread(
        all_send.at[3], all_recv.at[3], lambda other: sums_ref.at[b], lambda j: sums_ref.at[j]
    )
    spread.begin()
    widen_low(1)
    weight_low(0, lambda dy, start, size: x_one[dy].reshape(px, C0)[:, start : start + size])
    spread.finish()


def run_step(master, place, bias, image, skip, lab, params, head):
    nr, nb = lax.axis_size("rows"), lax.axis_size("blk")
    cols = image.shape[0]
    px = nb * cols
    wide, slim = C1 // nb, C0 // nb
    vmem = pl.BlockSpec(memory_space=pltpu.VMEM)
    smem = pl.BlockSpec(memory_space=pltpu.SMEM)
    dma = pltpu.SemaphoreType.DMA
    scratch = [
        pltpu.VMEM((3, nb, cols, C0), bf16),
        pltpu.VMEM((4, 2, nb, cols, C0), bf16),
        pltpu.VMEM((nb, 4, 8, cols), f32),
        pltpu.VMEM((9 * wide, C0), bf16),
        pltpu.VMEM((9 * wide, C1), bf16),
        pltpu.VMEM((4 * slim, C1), bf16),
        pltpu.VMEM((9 * slim, 2 * C0), bf16),
        pltpu.VMEM((3, px, C1), bf16),
        pltpu.VMEM((px, C1), bf16),
        pltpu.VMEM((4, 2, px, C0), bf16),
        pltpu.VMEM((1, px, wide), f32),
        pltpu.VMEM((1, px, wide), f32),
        pltpu.VMEM((4, px, slim), f32),
        pltpu.VMEM((1, px, wide), f32),
        pltpu.VMEM((4, px, slim), f32),
        pltpu.VMEM((8, wide), f32),
        pltpu.VMEM((8, wide), f32),
        pltpu.VMEM((8, slim), f32),
        pltpu.VMEM((3, px, wide), bf16),
        pltpu.VMEM((4, 2, px, slim), bf16),
        pltpu.VMEM((3, px, 3 * wide), bf16),
        pltpu.VMEM((4, 2, px, 3 * slim), bf16),
        pltpu.VMEM((3 * wide, px), bf16),
        pltpu.VMEM((2, 3 * slim, 2 * px), bf16),
        pltpu.VMEM((px, 4 * slim), bf16),
        pltpu.VMEM((4, nb, px, slim), bf16),
        pltpu.VMEM((4, nb, px, slim), bf16),
        pltpu.VMEM((nb, px, wide), bf16),
        pltpu.VMEM((2, nb, px, wide), bf16),
        pltpu.VMEM((nb, 4 * nb, 8, cols), f32),
        pltpu.VMEM((4, nr, 2 * nb + 8, wide), f32),
        pltpu.VMEM((2, nr, 2 * nb + 8, slim), f32),
        dma((3, nr, 2)),
        dma((nr, 2)),
        dma((6, nb, 2)),
        dma((6, nb)),
        dma((6, nb, 2)),
        dma((6, nb, 2)),
        dma((6, nr)),
        dma((6, nr)),
        dma((4, nb)),
        dma((4, nb)),
        dma((4, nb)),
        dma((4, nb)),
        dma((2, 2)),
        dma((2, 2)),
    ]
    return pl.pallas_call(
        functools.partial(step_kernel, nr, nb, cols),
        out_shape=(
            jax.ShapeDtypeStruct((place.shape[0],) + master.shape[1:], bf16),
            jax.ShapeDtypeStruct((nb, 16, wide), f32),
        ),
        in_specs=[vmem, smem, smem, vmem, vmem, vmem, vmem, vmem],
        out_specs=(vmem, vmem),
        scratch_shapes=scratch,
        compiler_params=pltpu.CompilerParams(
            collective_id=0, has_side_effects=True, vmem_limit_bytes=60 * 2**20
        ),
    )(master, place, bias, image, skip, lab, params, head)


LANES = 128


def inverse_factor_kernel(stat_ref, inverse_ref, factor_ref):
    order = stat_ref.shape[0]
    tile = (8, LANES)
    sub = lax.broadcasted_iota(jnp.int32, tile, 0)
    groups = order // 8

    def eliminate(source_ref, base, starts, first, count, accs):
        width = len(starts)

        def body(group, accs):
            top = pl.multiple_of(group * 8, 8)
            accs = [list(acc) for acc in accs]
            for unit in range(8):
                values = [source_ref[top + unit, pl.ds(start, 8), :] for start in starts]
                for c in range(8):
                    scale = jnp.broadcast_to(
                        factor_ref[top + unit, pl.ds(base + c, 1), :], tile
                    )
                    for s in range(width):
                        accs[s][c] = accs[s][c] - values[s] * scale
            return tuple(tuple(acc) for acc in accs)

        return lax.fori_loop(first, count, body, tuple(tuple(acc) for acc in accs))

    def batches(first, last, run):
        total = last - first

        def at(group):
            return pl.multiple_of(group * 8, 8)

        def two(n, _):
            run(first + 2 * n, [at(first + 2 * n), at(first + 2 * n + 1)])
            return 0

        lax.fori_loop(0, lax.div(total, 2), two, 0)

        @pl.when(lax.rem(total, 2) == 1)
        def _():
            run(last - 1, [at(last - 1)])

    def block(kb, _):
        base = pl.multiple_of(kb * 8, 8)
        accs = [stat_ref[base + c, pl.ds(base, 8), :] for c in range(8)]
        accs = list(eliminate(factor_ref, base, [base], 0, kb, [accs])[0])
        scale = []
        coef = {}
        for c in range(8):
            scale.append(jnp.broadcast_to(lax.rsqrt(accs[c][c : c + 1, :]), tile))
            accs[c] = accs[c] * scale[c]
            for d in range(c + 1, 8):
                coef[(c, d)] = jnp.broadcast_to(accs[c][d : d + 1, :], tile)
                accs[d] = accs[d] - accs[c] * coef[(c, d)]
        for c in range(8):
            factor_ref[base + c, pl.ds(base, 8), :] = jnp.where(sub >= c, accs[c], 0.0)

        def finish(accs, target_ref, start):
            accs = list(accs)
            for c in range(8):
                for e in range(c):
                    accs[c] = accs[c] - accs[e] * coef[(e, c)]
                accs[c] = accs[c] * scale[c]
                target_ref[base + c, pl.ds(start, 8), :] = accs[c]

        def below(group, starts):
            accs = [[stat_ref[base + c, pl.ds(s, 8), :] for c in range(8)] for s in starts]
            accs = eliminate(factor_ref, base, starts, 0, kb, accs)
            for acc, start in zip(accs, starts):
                finish(acc, factor_ref, start)

        def left(group, starts):
            accs = [[jnp.zeros(tile, jnp.float32) for c in range(8)] for s in starts]
            accs = eliminate(inverse_ref, base, starts, group, kb, accs)
            for acc, start in zip(accs, starts):
                finish(acc, inverse_ref, start)

        def clear(group, _):
            start = pl.multiple_of(group * 8, 8)
            for c in range(8):
                inverse_ref[base + c, pl.ds(start, 8), :] = jnp.zeros(tile, jnp.float32)
            return 0

        batches(kb + 1, groups, below)
        batches(0, kb, left)
        finish([jnp.where(sub == c, 1.0, 0.0) for c in range(8)], inverse_ref, base)
        lax.fori_loop(kb + 1, groups, clear, 0)
        return 0

    lax.fori_loop(0, groups, block, 0)


def split(value):
    high = value.astype(bf16)
    return high, (value - high.astype(f32)).astype(bf16)


def split_three(value):
    high = value.astype(bf16)
    rest = value - high.astype(f32)
    middle = rest.astype(bf16)
    return high, middle, (rest - middle.astype(f32)).astype(bf16)


def diagonal(pair):
    u, v = pair
    empty = jnp.zeros_like(u)
    return jnp.concatenate(
        [jnp.concatenate([u, empty], 1), jnp.concatenate([empty, v], 1)], 0
    )


def pair_product(packed, pair):
    a, b = split(packed)
    u, v = [split(value) for value in pair]
    c, d = diagonal((u[0], v[0])), diagonal((u[1], v[1]))
    result = dot_nn(jnp.concatenate([a, a, b], 1), jnp.concatenate([c, d, c], 0))
    order = packed.shape[1]
    return result[:, :order], result[:, order:]


def pair_cross(one, two):
    a, b = [jnp.concatenate(half, 1) for half in zip(*[split(value) for value in one])]
    c, d = [diagonal(half) for half in zip(*[split(value) for value in two])]
    return dot_nt(jnp.concatenate([a, a, b], 1), jnp.concatenate([c, d, c], 1))


def pair_square(pair):
    thirds = list(zip(*[split_three(value) for value in pair]))
    a, b, c = [jnp.concatenate(third, 1) for third in thirds]
    d, e, f = [diagonal(third) for third in thirds]
    return dot_nt(
        jnp.concatenate([a, a, b, a, b, c], 1), jnp.concatenate([d, e, d, f, e, d], 1)
    )


def product_three(left, right, right_dim):
    (a, b), (c, d) = left, right
    return lax.dot_general(
        jnp.concatenate([a, a, b], 1),
        jnp.concatenate([c, d, c], right_dim),
        (((1,), (right_dim,)), ((), ())),
        preferred_element_type=f32,
    )


def soap_blocks(indices, grads, ins, outs):
    def every(function, *lists):
        return [function(*items) for items in zip(*lists)]

    def load(ref):
        return [ref[index] for index in indices]

    def store(ref, values):
        for index, value in zip(indices, values):
            ref[index] = value

    master_ref, first_ref, second_ref, left_ref, right_ref, left_stat_ref, right_stat_ref = ins
    left = load(left_ref)
    sides, bases = every(split, grads), every(split, load(right_ref))
    lefts, turned = every(split, left), every(lambda grad: split(grad.T), grads)

    def three(dim):
        return lambda one, two: product_three(one, two, dim)

    lefts_turned = every(lambda value: split(value.T), left)
    half = every(three(0), lefts_turned, sides)
    left_outer = every(three(1), sides, sides)
    rotated = every(three(0), every(split, half), bases)
    right_outer = every(three(1), turned, turned)
    first = every(
        lambda old, new: beta_one * old + (1.0 - beta_one) * new, load(first_ref), rotated
    )
    second = every(
        lambda old, new: beta_two * old + (1.0 - beta_two) * new * new, load(second_ref), rotated
    )
    store(outs[2], first)
    store(outs[3], second)
    direction = every(
        lambda one, two: one
        * (1.0 / (1.0 - beta_one**STEP))
        / (jnp.sqrt(two * (1.0 / (1.0 - beta_two**STEP))) + adam_eps),
        first,
        second,
    )
    half = every(three(0), lefts, every(split, direction))
    stats = []
    for ref, target, outer in (
        (left_stat_ref, outs[4], left_outer),
        (right_stat_ref, outs[5], right_outer),
    ):
        stat = every(
            lambda old, new: beta_stat * old + (1.0 - beta_stat) * new, load(ref), outer
        )
        store(target, stat)
        stats.append(every(split, stat))
    moved = every(three(0), lefts_turned, stats[0])
    update = every(three(1), every(split, half), bases)
    moved_right = every(
        lambda stat, basis: product_three(stat, basis, 0).T, stats[1], bases
    )
    master = every(
        lambda old, new: old - soap_rate * (new + soap_decay * old), load(master_ref), update
    )
    store(outs[0], master)
    store(outs[1], every(lambda value: value.astype(bf16), master))
    store(outs[6], moved)
    store(outs[7], moved_right)
    middle = moved[0].shape[0] // 2
    store(
        outs[8],
        every(lambda one, two: pair_square((one[:middle], two[:middle])), moved, moved_right),
    )


def collect_kernel(nr, size, *refs):
    (owner_ref, grad_ref), refs = refs[:2], refs[2:]
    ins, refs = refs[:7], refs[7:]
    outs, refs = refs[:9], refs[9:]
    (
        out_a,
        in_a,
        out_b,
        in_b,
        total,
        in_buffer,
        out_buffer,
        copy_buffer,
        gram_buffer,
        a_send,
        a_recv,
        b_send,
        b_recv,
        in_sem,
        out_sem,
    ) = refs
    r = lax.axis_index("rows")
    b = lax.axis_index("blk")
    core = lax.rem(r, 2)
    chip = lax.div(r, 2)
    chips = nr // 2
    mate = r + 1 - 2 * core
    count = ins[0].shape[0]
    chunks = count // size
    square = in_square(chips, size)
    half = size // 2

    def device(chip, core):
        return {"rows": 2 * chip + core, "blk": b}

    barrier = pltpu.get_barrier_semaphore()
    pl.semaphore_signal(
        barrier, inc=1, device_id={"rows": mate, "blk": b}, device_id_type=MESH
    )

    def greet(step, _):
        pl.semaphore_signal(
            barrier,
            inc=1,
            device_id=device(lax.rem(chip + step, chips), core),
            device_id_type=MESH,
        )
        return 0

    lax.fori_loop(1, chips, greet, 0)

    def loads(chunk):
        return [
            pltpu.make_async_copy(
                ref.at[pl.ds(chunk * size, size)],
                in_buffer.at[chunk % 2, number],
                in_sem.at[chunk % 2, number],
            )
            for number, ref in enumerate(ins)
        ]

    def stores(chunk):
        copies = []
        for number, ref in enumerate(outs):
            if number in (1, 8):
                source = {1: copy_buffer, 8: gram_buffer}[number].at[chunk % 2]
            else:
                source = out_buffer.at[chunk % 2, number - (number > 1)]
            copies.append(
                pltpu.make_async_copy(
                    source, ref.at[pl.ds(chunk * size, size)], out_sem.at[chunk % 2, number]
                )
            )
        return copies

    def mine(to_chip, to_core, chunk, index):
        return grad_ref[owner_ref[(2 * to_chip + to_core) * count + chunk * size + index]]

    def joined(to_chip, chunk, index):
        value = mine(to_chip, core, chunk, index).astype(f32)
        return value + in_a[chunk, to_chip, index].astype(f32)

    def send_a(chunk):
        return pltpu.make_async_remote_copy(
            src_ref=out_a.at[chunk],
            dst_ref=in_a.at[chunk],
            send_sem=a_send.at[chunk],
            recv_sem=a_recv.at[chunk],
            device_id={"rows": mate, "blk": b},
            device_id_type=MESH,
        )

    def fill_a(chunk):
        def fill(n, _):
            to_chip, index = lax.div(n, size), lax.rem(n, size)
            out_a[chunk, to_chip, index] = mine(to_chip, 1 - core, chunk, index)
            return 0

        lax.fori_loop(0, chips * size, fill, 0)
        send_a(chunk).start()

    class Straight:
        def copy(self, chunk, step, source):
            other = lax.rem(chip + step, chips)
            return pltpu.make_async_remote_copy(
                src_ref=out_b.at[chunk, other],
                dst_ref=in_b.at[chunk, source],
                send_sem=b_send.at[chunk, step],
                recv_sem=b_recv.at[chunk, source],
                device_id=device(other, core),
                device_id_type=MESH,
            )

        def first(self, chunk):
            def join(step, _):
                other = lax.rem(chip + step, chips)

                def each(index, _):
                    out_b[chunk, other, index] = joined(other, chunk, index).astype(bf16)
                    return 0

                lax.fori_loop(0, size, each, 0)
                self.copy(chunk, step, chip).start()
                return 0

            lax.fori_loop(1, chips, join, 0)

        def second(self, chunk):
            pass

        def arrive(self, chunk):
            def wait(step, _):
                self.copy(chunk, step, lax.rem(chip + step, chips)).wait_recv()
                return 0

            lax.fori_loop(1, chips, wait, 0)

        def grad(self, chunk, index):
            return lax.fori_loop(
                1,
                chips,
                lambda step, value: value
                + in_b[chunk, lax.rem(chip + step, chips), index].astype(f32),
                total[chunk, index],
            )

        def close(self, chunk):
            def wait(step, _):
                self.copy(chunk, step, chip).wait_send()
                return 0

            lax.fori_loop(1, chips, wait, 0)

    class Square:
        def __init__(self):
            self.x = chip + 1 - 2 * lax.rem(chip, 2)
            self.y = chip + 2 - 4 * lax.div(chip, 2)
            self.corner = 3 - chip

        def one(self, chunk, way):
            return pltpu.make_async_remote_copy(
                src_ref=out_b.at[chunk, pl.ds(2 * way, 2)],
                dst_ref=in_b.at[chunk, pl.ds(2 * way, 2)],
                send_sem=b_send.at[chunk, way],
                recv_sem=b_recv.at[chunk, way],
                device_id=device((self.x, self.y)[way], core),
                device_id_type=MESH,
            )

        def two(self, chunk, way):
            return pltpu.make_async_remote_copy(
                src_ref=out_b.at[chunk, 4 + way],
                dst_ref=in_b.at[chunk, 4 + way],
                send_sem=b_send.at[chunk, 2 + way],
                recv_sem=b_recv.at[chunk, 2 + way],
                device_id=device((self.y, self.x)[way], core),
                device_id_type=MESH,
            )

        def first(self, chunk):
            for way, near in enumerate((self.x, self.y)):

                def each(index, _, way=way, near=near):
                    slot = way * half + index
                    out_b[chunk, 2 * way, index] = joined(near, chunk, slot).astype(bf16)
                    value = joined(self.corner, chunk, slot)
                    out_b[chunk, 2 * way + 1, index] = value.astype(bf16)
                    return 0

                lax.fori_loop(0, half, each, 0)
                self.one(chunk, way).start()

        def second(self, chunk):
            for way, far in enumerate((self.y, self.x)):
                self.one(chunk, way).wait_recv()

                def each(index, _, way=way, far=far):
                    value = joined(far, chunk, way * half + index)
                    value = value + in_b[chunk, 2 * way + 1, index].astype(f32)
                    out_b[chunk, 4 + way, index] = value.astype(bf16)
                    return 0

                lax.fori_loop(0, half, each, 0)
                self.two(chunk, way).start()

        def arrive(self, chunk):
            for way in range(2):
                self.two(chunk, way).wait_recv()

        def grad(self, chunk, index):
            way, place = index // half, index % half
            value = total[chunk, index] + in_b[chunk, 2 * way, place].astype(f32)
            return value + in_b[chunk, 4 + way, place].astype(f32)

        def close(self, chunk):
            for way in range(2):
                self.one(chunk, way).wait_send()
                self.two(chunk, way).wait_send()

    plan = Square() if square else Straight()

    def keep(chunk):
        def each(index, _):
            total[chunk, index] = joined(chip, chunk, index)
            return 0

        lax.fori_loop(0, size, each, 0)

    def work(chunk):
        plan.arrive(chunk)
        for copy in loads(chunk):
            copy.wait()
        if chunk >= 2:
            for copy in stores(chunk - 2):
                copy.wait()
        slot = chunk % 2
        chunk_ins = [in_buffer.at[slot, number] for number in range(7)]
        chunk_outs = [out_buffer.at[slot, number] for number in range(7)]
        chunk_outs.insert(1, copy_buffer.at[slot])
        chunk_outs.append(gram_buffer.at[slot])
        grads = [plan.grad(chunk, index) for index in range(size)]
        soap_blocks(range(size), grads, chunk_ins, chunk_outs)
        for copy in stores(chunk):
            copy.start()
        if chunk + 2 < chunks:
            for copy in loads(chunk + 2):
                copy.start()

    for chunk in range(min(2, chunks)):
        for copy in loads(chunk):
            copy.start()
    pl.semaphore_wait(barrier, chips)
    for chunk in range(chunks):
        fill_a(chunk)
    for chunk in range(chunks + 2):
        if chunk < chunks:
            send_a(chunk).wait_recv()
            plan.first(chunk)
            keep(chunk)
        if 1 <= chunk <= chunks:
            plan.second(chunk - 1)
        if chunk >= 2:
            work(chunk - 2)
    for chunk in range(chunks):
        send_a(chunk).wait_send()
        plan.close(chunk)
        if chunk >= chunks - 2:
            for copy in stores(chunk):
                copy.wait()


def in_square(chips, size):
    return chips == 4 and size % 2 == 0


def soap_update(blocks, owner, states):
    nr = lax.axis_size("rows")
    count, order = states[0].shape[0], states[0].shape[-1]
    size = 8 if count % 8 == 0 else count
    chunks = count // size
    anywhere = pl.BlockSpec(memory_space=pl.ANY)
    vmem = pl.BlockSpec(memory_space=pltpu.VMEM)
    shape = jax.ShapeDtypeStruct(states[0].shape, f32)
    dma = pltpu.SemaphoreType.DMA
    square = (order, order)
    chips = nr // 2
    parts = (6, size // 2) if in_square(chips, size) else (chips, size)
    results = pl.pallas_call(
        functools.partial(collect_kernel, nr, size),
        out_shape=(shape, jax.ShapeDtypeStruct(shape.shape, bf16)) + (shape,) * 6
        + (jax.ShapeDtypeStruct((count, order // 2, order), f32),),
        in_specs=[pl.BlockSpec(memory_space=pltpu.SMEM), vmem] + [anywhere] * 7,
        out_specs=[anywhere] * 9,
        scratch_shapes=[
            pltpu.VMEM((chunks, chips, size) + square, bf16),
            pltpu.VMEM((chunks, chips, size) + square, bf16),
            pltpu.VMEM((chunks,) + parts + square, bf16),
            pltpu.VMEM((chunks,) + parts + square, bf16),
            pltpu.VMEM((chunks, size) + square, f32),
            pltpu.VMEM((2, 7, size) + square, f32),
            pltpu.VMEM((2, 7, size) + square, f32),
            pltpu.VMEM((2, size) + square, bf16),
            pltpu.VMEM((2, size, order // 2, order), f32),
            dma((chunks,)),
            dma((chunks,)),
            dma((chunks, chips)),
            dma((chunks, chips)),
            dma((2, 7)),
            dma((2, 9)),
        ],
        compiler_params=pltpu.CompilerParams(
            collective_id=1, has_side_effects=True, vmem_limit_bytes=60 * 2**20
        ),
    )(owner, blocks, *states)
    kept = list(results[:6])
    new_left, new_right, *kept = new_bases(results[6:8], results[8], kept)
    new_master, new_copy, new_first, new_second, new_left_stat, new_right_stat = kept
    return [
        new_master,
        new_copy,
        new_first,
        new_second,
        new_left,
        new_right,
        new_left_stat,
        new_right_stat,
    ]


def basis_kernel(gram_ref, left_ref, right_ref, *refs):
    number = (len(refs) - 9) // 3
    kept, new_left_ref, new_right_ref = refs[:number], refs[number], refs[number + 1]
    moved, refs = refs[number + 2 : 2 * number + 2], refs[2 * number + 2 :]
    stat_ref, inverse_ref, factor_ref, solve_ref, rest_ref, in_sem, out_sem, *halts = refs
    arriving = [
        pltpu.make_async_copy(source, halt, in_sem.at[n])
        for n, (source, halt) in enumerate(zip(kept, halts))
    ]
    leaving = [
        pltpu.make_async_copy(halt, target, out_sem.at[n])
        for n, (halt, target) in enumerate(zip(halts, moved))
    ]
    for copy in arriving:
        copy.start()
    count, order = left_ref.shape[0], left_ref.shape[1]
    half = order // 2
    width = next(size for size in (8, 5, 4, 2, 1) if count % size == 0)
    column = lax.broadcasted_iota(jnp.int32, (half, order), 1)

    def invert(source_ref):
        def enter(row, _):
            value = source_ref[pl.ds(row, count, stride=half), :]
            if count < half:
                spare = column[: half - count]
                spare = (spare == row) | (spare == row + half)
                value = jnp.concatenate([value, jnp.where(spare, 1.0, 0.0)], 0)
            value = jnp.concatenate([value, pltpu.roll(value, half, 1)], 0)
            stat_ref[row] = value.T[:half]
            return 0

        lax.fori_loop(0, half, enter, 0, unroll=8)
        inverse_factor_kernel(stat_ref, inverse_ref, factor_ref)

        def leave(row, _):
            value = inverse_ref[row]
            value = jnp.concatenate([value, value], 0).T
            solve_ref[pl.ds(row, count, stride=half), :] = jnp.where(
                column[:count] < half, value[:count], value[half : half + count]
            )
            return 0

        lax.fori_loop(0, half, leave, 0, unroll=8)

    def rows(index):
        return pl.ds(pl.multiple_of(index * half, half), half)

    def project(step, _):
        blocks = [step * width + n for n in range(width)]
        first = [(left_ref[n, :half], right_ref[n, :half]) for n in blocks]
        second = [(left_ref[n, half:], right_ref[n, half:]) for n in blocks]
        first = [pair_product(solve_ref[rows(n), :], pair) for n, pair in zip(blocks, first)]
        cross = [pair_cross(one, two) for one, two in zip(second, first)]
        shares = [pair_product(value, pair) for value, pair in zip(cross, first)]
        second = [
            (pair[0] - share[0], pair[1] - share[1]) for pair, share in zip(second, shares)
        ]
        squares = [pair_square(pair) for pair in second]
        for n, one, two, value in zip(blocks, first, second, squares):
            for side, ref in enumerate((new_left_ref, new_right_ref)):
                ref[n, :half] = one[side]
                ref[n, half:] = two[side]
            rest_ref[rows(n), :] = value
        return 0

    def complete(step, _):
        blocks = [step * width + n for n in range(width)]
        refs = (new_left_ref, new_right_ref)
        second = [
            pair_product(solve_ref[rows(n), :], [ref[n, half:] for ref in refs]) for n in blocks
        ]
        for n, pair in zip(blocks, second):
            for ref, value in zip(refs, pair):
                ref[n] = jnp.concatenate([ref[n, :half], value], 0).T
        return 0

    invert(gram_ref)
    for come, go in zip(arriving, leaving):
        come.wait()
        go.start()
    lax.fori_loop(0, count // width, project, 0)
    invert(rest_ref)
    lax.fori_loop(0, count // width, complete, 0)
    for copy in leaving:
        copy.wait()


def new_bases(products, grams, kept):
    count, order = products[0].shape[0], products[0].shape[-1]
    half = order // 2
    vmem = pl.BlockSpec(memory_space=pltpu.VMEM)
    anywhere = pl.BlockSpec(memory_space=pl.ANY)
    lanes = pltpu.VMEM((half, half, LANES), f32)
    flat = pltpu.VMEM((count * half, order), f32)
    return pl.pallas_call(
        basis_kernel,
        out_shape=[
            jax.ShapeDtypeStruct(value.shape, value.dtype) for value in list(products) + kept
        ],
        in_specs=[vmem] * 3 + [anywhere] * len(kept),
        out_specs=[vmem] * 2 + [anywhere] * len(kept),
        scratch_shapes=[lanes, lanes, lanes, flat, flat]
        + [pltpu.SemaphoreType.DMA((len(kept),))] * 2
        + [pltpu.VMEM(value.shape, value.dtype) for value in kept],
        compiler_params=pltpu.CompilerParams(vmem_limit_bytes=60 * 2**20),
    )(grams.reshape(count * half, order), *products, *kept)


def adam_small(grads, value, first, second):
    first_new = beta_one * first + (1.0 - beta_one) * grads
    second_new = beta_two * second + (1.0 - beta_two) * grads * grads
    direction = (
        first_new
        / (1.0 - beta_one**STEP)
        / (jnp.sqrt(second_new / (1.0 - beta_two**STEP)) + adam_eps)
    )
    return (first_new, second_new, value - small_rate * (direction + small_decay * value))


def local(
    image,
    skip,
    labels,
    weight_map,
    valid,
    owner,
    master,
    first_moment,
    second_moment,
    left_basis,
    right_basis,
    left_stat,
    right_stat,
    norm_params,
    norm_first,
    norm_second,
    head_bias,
    bias_first,
    bias_second,
):
    shards = lax.axis_size("blk")
    shard = lax.axis_index("blk")
    cols = image.shape[2]
    slots = jnp.arange(owner.shape[0])
    place = jnp.sum(jnp.where(owner[None, :] == slots[:, None], slots[None, :], 0), 1)
    widths = (C1, C1, C1, C1, C0, C0)
    heads = norm_params[sum(widths) :].reshape(C0, 2)
    part = C0 // shards
    heads = lax.dynamic_slice_in_dim(heads, shard * part, part).T
    heads = jnp.pad(heads, ((0, 6), (0, 0)))
    lab = jnp.stack([labels, weight_map, valid]).astype(f32).reshape(3, 2, cols, 2)
    lab = jnp.pad(lab.transpose(1, 3, 0, 2).reshape(4, 3, cols), ((0, 0), (0, 5), (0, 0)))
    skip = skip.reshape(2, cols, 2, C0).transpose(0, 2, 1, 3)
    blocks, sums = run_step(
        master[0],
        place.astype(jnp.int32),
        head_bias,
        image[0, 0],
        skip,
        lab,
        norm_params.reshape(-1, TILE),
        heads,
    )
    loss_sum, valid_count = sums[0, 6, 0], sums[0, 9, 0]
    grad_bias = sums[0, 7:9, 0]
    grad_head = jnp.stack([sums[:, 5, :part].reshape(-1), sums[:, 5, part : 2 * part].reshape(-1)], 1)
    small = jnp.concatenate(
        [sums[:, row].reshape(-1) for row in range(4)]
        + [
            sums[:, 4, :part].reshape(-1),
            sums[:, 4, part : 2 * part].reshape(-1),
            grad_head.reshape(-1),
        ]
    )
    states = (
        master,
        first_moment,
        second_moment,
        left_basis,
        right_basis,
        left_stat,
        right_stat,
    )
    soap = soap_update(blocks, owner, [state[0] for state in states])
    soap = [value[None] for value in soap]
    norm_new = adam_small(small, norm_params, norm_first, norm_second)
    bias_new = adam_small(grad_bias, head_bias, bias_first, bias_second)
    return (
        loss_sum,
        valid_count,
        soap[0],
        soap[1],
        soap[2],
        soap[3],
        soap[4],
        soap[5],
        soap[6],
        soap[7],
        norm_new[0],
        norm_new[1],
        norm_new[2],
        bias_new[0],
        bias_new[1],
        bias_new[2],
    )


def solution(mesh):
    placed = (
        P("blk", "rows", None, None),
        P("blk", "rows", None, None),
        P("blk", "rows", None),
        P("blk", "rows", None),
        P("blk", "rows", None),
        P(),
        P("blk", "rows", None, None),
        P("blk", "rows", None, None),
        P("blk", "rows", None, None),
        P("blk", "rows", None, None),
        P("blk", "rows", None, None),
        P("blk", "rows", None, None),
        P("blk", "rows", None, None),
        P(),
        P(),
        P(),
        P(),
        P(),
        P(),
    )
    return jax.shard_map(
        local,
        mesh=mesh,
        in_specs=placed,
        out_specs=(
            P(),
            P(),
            P("blk", "rows", None, None),
            P("blk", "rows", None, None),
            P("blk", "rows", None, None),
            P("blk", "rows", None, None),
            P("blk", "rows", None, None),
            P("blk", "rows", None, None),
            P("blk", "rows", None, None),
            P("blk", "rows", None, None),
            P(),
            P(),
            P(),
            P(),
            P(),
            P(),
        ),
        check_vma=False,
    )
```

```python
import functools

import jax
import jax.numpy as jnp
from jax import lax
from jax.experimental import pallas as pl
from jax.experimental.pallas import tpu as pltpu
from jax.sharding import PartitionSpec as P

C0 = 512
C1 = 1024
GROUPS = 32
STEP = 10


beta_one = 0.9
beta_two = 0.999
beta_stat = 0.95
adam_eps = 1e-08
norm_eps = 1e-05
soap_rate = 0.008
soap_decay = 0.01
small_rate = 0.4
small_decay = 0.01
highest = lax.Precision.HIGHEST


MESH = pl.DeviceIdType.MESH
bf16 = jnp.bfloat16
f32 = jnp.float32
TILE = 128


def dot_nt(left, right):
    return lax.dot_general(left, right, (((1,), (1,)), ((), ())), preferred_element_type=f32)


def dot_nn(left, right):
    return jnp.dot(left, right, preferred_element_type=f32)


def sigmoid(value):
    return 1.0 / (1.0 + jnp.exp(-value))


def block_layers(nb):
    result = []
    first = 0
    for in_width, out_width, taps in ((C0, C1, 9), (C1, C1, 9), (C1, C0, 4), (2 * C0, C0, 9)):
        out = out_width // nb
        result.append((out, in_width, taps, first))
        first = first + out // TILE * taps * (in_width // TILE)
    return result


def step_kernel(
    nr,
    nb,
    cols,
    master_ref,
    place_ref,
    bias_ref,
    image_ref,
    skip_ref,
    lab_ref,
    params_ref,
    head_ref,
    blocks_ref,
    sums_ref,
    grad_ref,
    local_sem,
    x_one,
    x_skip,
    x_lab,
    w_one,
    w_two,
    w_up,
    w_three,
    a_one,
    a_two,
    u_full,
    z_one,
    z_two,
    z_three,
    dy_low,
    dy_high,
    inv_one,
    inv_two,
    inv_three,
    dz_low,
    dz_high,
    shifted_low,
    shifted_high,
    turned_low,
    turned_high,
    dub,
    send_high,
    recv_high,
    send_low,
    recv_low,
    logit,
    grad_logit,
    reduce_wide,
    reduce_narrow,
    gather_send,
    gather_recv,
    line_send,
    line_recv,
    halo_send,
    halo_recv,
    red_send,
    red_recv,
    all_send,
    all_recv,
    high_send,
    high_recv,
    edge_send,
    edge_recv,
):
    r = lax.axis_index("rows")
    b = lax.axis_index("blk")
    px = nb * cols
    wide = C1 // nb
    slim = C0 // nb
    taps_high = 3 * slim
    layers = block_layers(nb)

    def remote(src, dst, send, recv, rows, blk):
        return pltpu.make_async_remote_copy(
            src_ref=src,
            dst_ref=dst,
            send_sem=send,
            recv_sem=recv,
            device_id={"rows": rows, "blk": blk},
            device_id_type=MESH,
        )

    def lanes(index, size):
        return pl.ds(pl.multiple_of(index * size, TILE), size)

    def ring(index, count):
        return lax.rem(index + count, count)

    barrier = pltpu.get_barrier_semaphore()

    def greet_rows(step, _):
        pl.semaphore_signal(
            barrier, inc=1, device_id={"rows": ring(r + step, nr), "blk": b}, device_id_type=MESH
        )
        return 0

    lax.fori_loop(1, nr, greet_rows, 0)
    for step in range(1, nb):
        pl.semaphore_signal(
            barrier, inc=1, device_id={"rows": r, "blk": ring(b + step, nb)}, device_id_type=MESH
        )
    pl.semaphore_wait(barrier, nr - 1 + nb - 1)

    class Exchange:
        def __init__(self, number, piece, up=None, down=None):
            self.number, self.piece, self.up, self.down = number, piece, up, down

        def right(self, j):
            return remote(
                self.piece(j),
                self.piece(j),
                line_send.at[self.number, j, 0],
                line_recv.at[self.number, j],
                r,
                ring(b + 1, nb),
            )

        def left(self, j):
            return remote(
                self.piece(j),
                self.piece(j),
                line_send.at[self.number, j, 1],
                line_recv.at[self.number, j],
                r,
                ring(b - 1, nb),
            )

        def higher(self, j):
            src, dst = self.up(j)
            return remote(
                src,
                dst,
                halo_send.at[self.number, j, 0],
                halo_recv.at[self.number, j, 0],
                ring(r + 1, nr),
                b,
            )

        def lower(self, j):
            src, dst = self.down(j)
            return remote(
                src,
                dst,
                halo_send.at[self.number, j, 1],
                halo_recv.at[self.number, j, 1],
                ring(r - 1, nr),
                b,
            )

        def halos(self, j):
            if self.up is None:
                return

            @pl.when(r + 1 < nr)
            def _():
                self.higher(j).start()

            @pl.when(r > 0)
            def _():
                self.lower(j).start()

        def begin(self):
            @pl.when(b + 1 < nb)
            def _():
                self.right(b).start()

            @pl.when(b > 0)
            def _():
                self.left(b).start()

            self.halos(b)

        def hop(self, k):
            @pl.when(b >= k)
            def _():
                self.right(b - k).wait_recv()

                @pl.when(b + 1 < nb)
                def _():
                    self.right(b - k).start()

                self.halos(b - k)

            @pl.when(b + k < nb)
            def _():
                self.left(b + k).wait_recv()

                @pl.when(b > 0)
                def _():
                    self.left(b + k).start()

                self.halos(b + k)

        def hops(self):
            for k in range(1, nb):
                self.hop(k)

        def finish(self):
            for k in range(nb):

                @pl.when((b >= k) & (b + 1 < nb))
                def _():
                    self.right(b - k).wait_send()

                @pl.when((b + k < nb) & (b > 0))
                def _():
                    self.left(b + k).wait_send()

            if self.up is None:
                return
            for j in range(nb):

                @pl.when(r + 1 < nr)
                def _():
                    self.higher(j).wait_send()
                    self.lower(j).wait_recv()

                @pl.when(r > 0)
                def _():
                    self.lower(j).wait_send()
                    self.higher(j).wait_recv()

    def reduce_start(number, buffer):
        def start(step, _):
            remote(
                buffer.at[r],
                buffer.at[r],
                red_send.at[number, step],
                red_recv.at[number, r],
                ring(r + step, nr),
                b,
            ).start()
            return 0

        lax.fori_loop(1, nr, start, 0, unroll=nr <= 8)

    def reduce_finish(number, buffer):
        def wait(step, _):
            source = ring(r + step, nr)
            copy = remote(
                buffer.at[source],
                buffer.at[source],
                red_send.at[number, step],
                red_recv.at[number, source],
                source,
                b,
            )
            copy.wait_recv()
            copy.wait_send()
            return 0

        lax.fori_loop(1, nr, wait, 0, unroll=nr <= 8)
        return lax.fori_loop(
            1, nr, lambda k, total: total + buffer[k], buffer[0], unroll=nr <= 8
        )

    def all_reduce(number, buffer):
        reduce_start(number, buffer)
        return reduce_finish(number, buffer)

    class Spread:
        def __init__(self, send, recv, source, target):
            self.send, self.recv, self.source, self.target = send, recv, source, target

        def copy(self, step):
            other = ring(b + step, nb)
            return remote(
                self.source(other),
                self.target(b),
                self.send.at[step],
                self.recv.at[b],
                r,
                other,
            )

        def begin(self):
            for step in range(1, nb):
                self.copy(step).start()

        def finish(self):
            for step in range(1, nb):
                other = ring(b + step, nb)
                remote(
                    self.source(other),
                    self.target(other),
                    self.send.at[step],
                    self.recv.at[other],
                    r,
                    other,
                ).wait_recv()
                self.copy(step).wait_send()

    class Gather:
        def __init__(self):
            self.size = master_ref.shape[0]
            self.chips = nr // 2
            self.core = lax.rem(r, 2)
            self.chip = lax.div(r, 2)
            self.mate = r + 1 - 2 * self.core
            self.square = self.chips == 4 and self.size % 2 == 0
            self.halves = 2 if self.square else 1

        def piece(self, row, half):
            part = self.size // self.halves
            return grad_ref.at[pl.ds(row * self.size + half * part, part)]

        def move(self, kind, target, row, half):
            return remote(
                self.piece(row, half),
                self.piece(row, half),
                gather_send.at[kind, row, half],
                gather_recv.at[row, half],
                target,
                b,
            )

        def direct(self, target):
            return remote(
                self.piece(r, 0),
                self.piece(r, 0),
                gather_send.at[0, target, 0],
                gather_recv.at[r, 0],
                target,
                b,
            )

        def beside(self, step):
            return 2 * lax.rem(self.chip + step, self.chips) + self.core

        def other(self, bit):
            away = self.chip + bit - 2 * bit * lax.rem(lax.div(self.chip, bit), 2)
            return 2 * away + self.core

        def begin(self):
            def cast(index, _):
                grad_ref[r * self.size + index] = master_ref[index].astype(bf16)
                return 0

            lax.fori_loop(0, self.size, cast, 0)
            if self.square:
                for half in range(2):
                    self.move(2, self.mate, r, half).start()
                    self.move(0, self.other(1), r, 1 - half).start()
                    self.move(1, self.other(2), r, half).start()
            else:
                self.move(2, self.mate, r, 0).start()

                def send(step, _):
                    self.direct(self.beside(step)).start()
                    return 0

                lax.fori_loop(1, self.chips, send, 0)

        def arrived(self, row, half):
            self.move(2, self.mate, row, half).wait_recv()

        def hand(self, row, half):
            self.arrived(row, half)
            self.move(2, self.mate, row, half).start()

        def forward(self, moves):
            image, lab, skip = moves
            for k in range(1, nb):
                image.hop(k)
                lab.hop(k)
            if self.square:
                x, y = self.other(1), self.other(2)
                corner = 2 * (3 - self.chip) + self.core
                self.hand(y, 0)
                self.move(0, x, y, 0).start()
                self.hand(x, 1)
                self.move(1, y, x, 1).start()
                skip.hop(1)
                self.hand(x, 0)
                self.hand(y, 1)
                self.hand(corner, 0)
                self.hand(corner, 1)
                rows = (r, x, y, corner)
                for half in range(2):
                    for row in rows:
                        self.arrived(row + 1 - 2 * self.core, half)
                for half in range(2):
                    for row in rows:
                        self.move(2, self.mate, row, half).wait_send()
                    self.move(0, x, r, half).wait_send()
                    self.move(1, y, r, half).wait_send()
                self.move(0, x, y, 0).wait_send()
                self.move(1, y, x, 1).wait_send()
            else:

                def pass_on(step, _):
                    self.hand(self.beside(step), 0)
                    return 0

                def close(step, _):
                    row = self.beside(step)
                    self.arrived(row + 1 - 2 * self.core, 0)
                    self.move(2, self.mate, row, 0).wait_send()
                    self.direct(row).wait_send()
                    return 0

                lax.fori_loop(1, self.chips, pass_on, 0)
                skip.hop(1)
                self.arrived(self.mate, 0)
                self.move(2, self.mate, r, 0).wait_send()
                lax.fori_loop(1, self.chips, close, 0)

    position = lax.rem(lax.broadcasted_iota(jnp.int32, (px, TILE), 0), cols)

    def mask_of(value, column):
        hit = position[:, :1] == column
        return jnp.where(hit, 0.0, value)

    def shift_down(value):
        return mask_of(pltpu.roll(value, 1, 0), 0)

    def shift_up(value):
        return mask_of(pltpu.roll(value, px - 1, 0), cols - 1)

    def group_sum(value, size):
        width = value.shape[-1]
        bits = size.bit_length() - 1
        first = lax.shift_right_logical(lax.broadcasted_iota(jnp.int32, (width, width), 0), bits)
        second = lax.shift_right_logical(lax.broadcasted_iota(jnp.int32, (width, width), 1), bits)
        same = jnp.where(first == second, 1.0, 0.0).astype(f32)
        return jnp.dot(value, same, preferred_element_type=f32, precision=highest)

    def rows_of(image):
        return pl.ds(image * cols, cols)

    def norm_sums(buffer, z_ref):
        for image in range(nb):
            first = 0.0
            second = 0.0
            for part in range(z_ref.shape[0]):
                value = z_ref[part, rows_of(image), :]
                first = first + jnp.sum(value, 0, keepdims=True)
                second = second + jnp.sum(value * value, 0, keepdims=True)
            buffer[r, image : image + 1, :] = first
            buffer[r, nb + image : nb + image + 1, :] = second

    def norm_apply(total, z_ref, inv_ref, gain, shift, size, put):
        width = z_ref.shape[-1]
        number = nr * cols * z_ref.shape[0] * size
        sums = group_sum(total[: 2 * nb], size) / number
        mean = sums[:nb]
        inv = lax.rsqrt(sums[nb:] - mean * mean + norm_eps)
        inv_ref[:nb, :] = inv
        for part in range(z_ref.shape[0]):
            for image in range(nb):
                value = z_ref[part, rows_of(image), :]
                value = (value - mean[image : image + 1]) * inv[image : image + 1]
                z_ref[part, rows_of(image), :] = value
                normed = value * gain + shift
                put(part, image, (normed * sigmoid(normed)).astype(bf16))

    def back_sums(buffer, z_ref, dy_ref, gain, shift, grad_of):
        for image in range(nb):
            first = 0.0
            second = 0.0
            for part in range(z_ref.shape[0]):
                value = z_ref[part, rows_of(image), :]
                normed = value * gain + shift
                gate = sigmoid(normed)
                grad = grad_of(part, image) * gate * (1.0 + normed * (1.0 - gate))
                dy_ref[part, rows_of(image), :] = grad
                first = first + jnp.sum(grad, 0, keepdims=True)
                second = second + jnp.sum(grad * value, 0, keepdims=True)
            buffer[r, image : image + 1, :] = first
            buffer[r, nb + image : nb + image + 1, :] = second

    def back_apply(total, z_ref, dy_ref, inv_ref, gain, size, put):
        number = nr * cols * z_ref.shape[0] * size
        sums = group_sum(total[: 2 * nb] * gain, size) / number
        inv = inv_ref[:nb, :]
        for part in range(z_ref.shape[0]):
            for image in range(nb):
                one = slice(image, image + 1)
                two = slice(nb + image, nb + image + 1)
                value = dy_ref[part, rows_of(image), :] * gain - sums[one]
                value = value - z_ref[part, rows_of(image), :] * sums[two]
                put(part, image, (value * inv[one]).astype(bf16))
        shift_grad = jnp.sum(total[:nb], 0, keepdims=True)
        gain_grad = jnp.sum(total[nb : 2 * nb], 0, keepdims=True)
        return gain_grad, shift_grad

    gather = Gather()
    gather.begin()
    x_one[1, b] = image_ref[...]
    x_skip[1:3, :, b] = skip_ref[...]
    x_lab[b] = lab_ref[...]
    move_image = Exchange(
        0,
        lambda j: x_one.at[1, j],
        lambda j: (x_one.at[1, j], x_one.at[0, j]),
        lambda j: (x_one.at[1, j], x_one.at[2, j]),
    )
    move_skip = Exchange(
        1,
        lambda j: x_skip.at[pl.ds(1, 2), :, j],
        lambda j: (x_skip.at[2, :, j], x_skip.at[0, :, j]),
        lambda j: (x_skip.at[1, :, j], x_skip.at[3, :, j]),
    )
    move_lab = Exchange(2, lambda j: x_lab.at[j])
    moves = (move_image, move_lab, move_skip)
    for move in moves:
        move.begin()
    @pl.when(r == 0)
    def _():
        x_one[0] = jnp.zeros_like(x_one[0])
        x_skip[0] = jnp.zeros_like(x_skip[0])
        a_one[0] = jnp.zeros_like(a_one[0])
        u_full[0] = jnp.zeros_like(u_full[0])
        dz_low[0] = jnp.zeros_like(dz_low[0])
        dz_high[0] = jnp.zeros_like(dz_high[0])

    @pl.when(r == nr - 1)
    def _():
        x_one[2] = jnp.zeros_like(x_one[2])
        x_skip[3] = jnp.zeros_like(x_skip[3])
        a_one[2] = jnp.zeros_like(a_one[2])
        u_full[3] = jnp.zeros_like(u_full[3])
        dz_low[2] = jnp.zeros_like(dz_low[2])
        dz_high[3] = jnp.zeros_like(dz_high[3])

    gather.forward(moves)
    move_image.finish()
    move_lab.finish()
    middle = max(1, nb // 2)
    for k in range(2, middle + 1):
        move_skip.hop(k)

    def arrange(number, target):
        out, width, taps, first = layers[number]
        across = width // TILE

        def body(n, _):
            ib = lax.rem(n, across)
            t = lax.rem(lax.div(n, across), taps)
            ob = lax.div(n, across * taps)
            target[
                pl.ds(pl.multiple_of(t * out + ob * TILE, TILE), TILE), lanes(ib, TILE)
            ] = grad_ref[place_ref[first + n]]
            return 0

        lax.fori_loop(0, out // TILE * taps * across, body, 0)

    arrange(0, w_one)
    def own_params(first, width):
        start = first // TILE + b * (width // TILE)
        return jnp.concatenate(
            [params_ref[pl.ds(start + n, 1), :] for n in range(width // TILE)], 1
        )

    gain_one, shift_one, gain_two, shift_two = [own_params(n * C1, wide) for n in range(4)]
    gain_three, shift_three = [own_params(4 * C1 + n * C0, slim) for n in range(2)]
    size_low, size_high = C1 // GROUPS, C0 // GROUPS

    def conv_low(z_ref, weight, source, lines=(0, 1, 2), more=False):
        def tap(dx):
            total = 0.0
            for dy in lines:
                first = (3 * dy + dx) * wide
                total = total + dot_nt(source(dy), weight[first : first + wide, :])
            return total

        if more:
            z_ref[0] += tap(1)
        else:
            z_ref[0] = tap(1)
        z_ref[0] += shift_down(tap(0))
        z_ref[0] += shift_up(tap(2))

    conv_low(z_one, w_one, lambda dy: x_one[dy].reshape(px, C0))
    reduce_one, reduce_two = reduce_wide.at[0], reduce_wide.at[1]
    norm_sums(reduce_one, z_one)
    count = 0.0
    for image in range(nb):
        for part in range(4):
            count = count + jnp.sum(x_lab[image, part, 2:3, :], 1, keepdims=True)
    reduce_one[r, 2 * nb : 2 * nb + 1, :] = jnp.broadcast_to(count, (1, wide))
    reduce_start(0, reduce_one)
    arrange(1, w_two)
    total = reduce_finish(0, reduce_one)
    count = total[2 * nb : 2 * nb + 1, :1]

    def put_one(part, image, value):
        a_one[1, rows_of(image), lanes(b, wide)] = value

    norm_apply(total, z_one, inv_one, gain_one, shift_one, size_low, put_one)
    move = Exchange(
        3,
        lambda j: a_one.at[1, :, lanes(j, wide)],
        lambda j: (a_one.at[1, :, lanes(j, wide)], a_one.at[0, :, lanes(j, wide)]),
        lambda j: (a_one.at[1, :, lanes(j, wide)], a_one.at[2, :, lanes(j, wide)]),
    )
    move.begin()
    move.hop(1)
    arrange(2, w_up)
    for k in range(2, nb):
        move.hop(k)
    arrange(3, w_three)
    conv_low(z_two, w_two, lambda dy: a_one[dy], (1,))
    move.finish()
    for k in range(middle + 1, nb):
        move_skip.hop(k)
    conv_low(z_two, w_two, lambda dy: a_one[dy], (0, 2), True)
    norm_sums(reduce_two, z_two)
    total = all_reduce(1, reduce_two)

    def put_two(part, image, value):
        a_two[rows_of(image), lanes(b, wide)] = value

    norm_apply(total, z_two, inv_two, gain_two, shift_two, size_low, put_two)
    move = Exchange(4, lambda j: a_two.at[:, lanes(j, wide)])
    move.begin()
    move.hops()
    move.finish()
    for part in range(4):
        u_full[1 + part // 2, part % 2, :, lanes(b, slim)] = dot_nt(
            a_two[...], w_up[part * slim : (part + 1) * slim, :]
        ).astype(bf16)
    move = Exchange(
        5,
        lambda j: u_full.at[pl.ds(1, 2), :, :, lanes(j, slim)],
        lambda j: (u_full.at[2, :, :, lanes(j, slim)], u_full.at[0, :, :, lanes(j, slim)]),
        lambda j: (u_full.at[1, :, :, lanes(j, slim)], u_full.at[3, :, :, lanes(j, slim)]),
    )
    def conv_high(product, more):
        for e in range(2):
            even, odd = product(e, 0), product(e, 1)
            first = even[:, slim : 2 * slim] + shift_down(odd[:, :slim]) + odd[:, 2 * slim :]
            second = odd[:, slim : 2 * slim] + even[:, :slim] + shift_up(even[:, 2 * slim :])
            if more:
                z_three[2 * e] += first
                z_three[2 * e + 1] += second
            else:
                z_three[2 * e] = first
                z_three[2 * e + 1] = second

    def high_product(source, start, lines):
        def product(e, f):
            total = 0.0
            for dy in lines[e]:
                weight = w_three[dy * taps_high : (dy + 1) * taps_high, start : start + C0]
                total = total + dot_nt(source[e + dy, f].reshape(px, C0), weight)
            return total

        return product

    every = ((0, 1, 2), (0, 1, 2))
    inner, outer = ((1, 2), (0, 1)), ((0,), (2,))
    move.begin()
    move_skip.finish()
    conv_high(high_product(x_skip, C0, every), False)
    move.hops()
    conv_high(high_product(u_full, 0, inner), True)
    move.finish()
    conv_high(high_product(u_full, 0, outer), True)
    reduce_three, reduce_four = reduce_narrow.at[0], reduce_narrow.at[1]
    norm_sums(reduce_three, z_three)
    total = all_reduce(2, reduce_three)
    a_three = send_high

    def put_three(part, image, value):
        a_three[part, 0, rows_of(image), :] = value

    norm_apply(total, z_three, inv_three, gain_three, shift_three, size_high, put_three)
    head_low = head_ref[...].astype(bf16)
    head = head_low.astype(f32)
    for part in range(4):
        for image in range(nb):
            tile = dot_nt(head_low, a_three[part, 0, rows_of(image), :])
            logit[b, part, 2 * image : 2 * image + 2, :] = tile[:2]
    spread = Spread(all_send.at[0], all_recv.at[0], lambda other: logit.at[b], lambda j: logit.at[j])
    spread.begin()
    spread.finish()
    loss = jnp.zeros((1, cols), f32)
    bias_grad = [jnp.zeros((1, cols), f32), jnp.zeros((1, cols), f32)]
    head_grad = jnp.zeros((8, slim), f32)
    level = lax.broadcasted_iota(jnp.int32, (8, cols), 0)

    def head_of(part, image):
        two = slice(2 * image, 2 * image + 2)
        tile = logit[0, part, two, :]
        for j in range(1, nb):
            tile = tile + logit[j, part, two, :]
        first = tile[0:1, :] + bias_ref[0]
        second = tile[1:2, :] + bias_ref[1]
        label = x_lab[image, part, 0:1, :]
        scale = x_lab[image, part, 1:2, :] * x_lab[image, part, 2:3, :] * 0.125
        largest = jnp.maximum(first, second)
        log_total = jnp.log(jnp.exp(first - largest) + jnp.exp(second - largest)) + largest
        picked = first * (1.0 - label) + second * label
        unit = scale / count
        return (
            scale * (log_total - picked),
            (jnp.exp(first - log_total) - (1.0 - label)) * unit,
            (jnp.exp(second - log_total) - label) * unit,
        )

    for part in range(4):
        for image in range(nb):
            cost, first, second = head_of(part, image)
            loss = loss + cost
            bias_grad = [bias_grad[0] + first, bias_grad[1] + second]
            tile = jnp.where(level == 0, first, jnp.where(level == 1, second, 0.0))
            grad_logit[part * nb + image] = tile
            head_grad = head_grad + jnp.dot(
                tile,
                a_three[part, 0, rows_of(image), :].astype(f32),
                preferred_element_type=f32,
                precision=highest,
            )

    def grad_three(part, image):
        return lax.dot_general(
            grad_logit[part * nb + image],
            head,
            (((0,), (0,)), ((), ())),
            preferred_element_type=f32,
            precision=highest,
        )

    reduce_four[r, 2 * nb : 2 * nb + 8, :] = head_grad
    for row, value in enumerate([loss] + bias_grad):
        reduce_four[r, 2 * nb + 2 + row : 2 * nb + 3 + row, :] = jnp.broadcast_to(
            jnp.sum(value, 1, keepdims=True), (1, slim)
        )
    back_sums(reduce_four, z_three, dy_high, gain_three, shift_three, grad_three)
    total = all_reduce(3, reduce_four)

    def put_high(part, image, value):
        dz_high[1 + part // 2, part % 2, rows_of(image), :] = value

    gain_grad, shift_grad = back_apply(
        total, z_three, dy_high, inv_three, gain_three, size_high, put_high
    )
    sums_ref[b] = jnp.zeros_like(sums_ref[b])
    sums_ref[b, 4:5, :slim] = gain_grad
    sums_ref[b, 4:5, slim : 2 * slim] = shift_grad
    sums_ref[b, 5:6, :slim] = total[2 * nb : 2 * nb + 1]
    sums_ref[b, 5:6, slim : 2 * slim] = total[2 * nb + 1 : 2 * nb + 2]
    for row in range(3):
        sums_ref[b, 6 + row : 7 + row, :slim] = total[2 * nb + 2 + row : 2 * nb + 3 + row]
    sums_ref[b, 9:10, :] = jnp.broadcast_to(count, (1, wide))

    def edges(number, source_up, target_up, source_down, target_down):
        def higher():
            return remote(
                source_up,
                target_up,
                edge_send.at[number, 0],
                edge_recv.at[number, 0],
                ring(r + 1, nr),
                b,
            )

        def lower():
            return remote(
                source_down,
                target_down,
                edge_send.at[number, 1],
                edge_recv.at[number, 1],
                ring(r - 1, nr),
                b,
            )

        def begin():
            @pl.when(r + 1 < nr)
            def _():
                higher().start()

            @pl.when(r > 0)
            def _():
                lower().start()

        def finish():
            @pl.when(r + 1 < nr)
            def _():
                higher().wait_send()
                lower().wait_recv()

            @pl.when(r > 0)
            def _():
                lower().wait_send()
                higher().wait_recv()

        return begin, finish

    def widen_high(row):
        even, odd = dz_high[row, 0], dz_high[row, 1]
        shifted_high[row, 0, :, :slim] = odd
        shifted_high[row, 0, :, slim : 2 * slim] = even
        shifted_high[row, 0, :, 2 * slim :] = shift_down(odd.astype(f32)).astype(bf16)
        shifted_high[row, 1, :, :slim] = shift_up(even.astype(f32)).astype(bf16)
        shifted_high[row, 1, :, slim : 2 * slim] = odd
        shifted_high[row, 1, :, 2 * slim :] = even

    def put_grad(first, across, value, rows, start):
        for row, number in rows:
            for k in range(value.shape[1] // TILE):
                grad_ref[first + number * across + start + k] = value[
                    row : row + TILE, k * TILE : (k + 1) * TILE
                ].astype(bf16)

    def weight_high(dy):
        out, width, taps, first = layers[3]
        rows = [(dx * slim, 3 * dy + dx) for dx in range(3)]
        for half, source in enumerate((u_full, x_skip)):
            total = 0.0
            for e in range(2):
                for f in range(2):
                    value = source[e + dy, f].reshape(px, C0)
                    total = total + dot_nn(turned_high[e, :, f * px : (f + 1) * px], value)
            put_grad(first, width // TILE, total, rows, half * (C0 // TILE))

    begin, finish = edges(0, dz_high.at[2], dz_high.at[0], dz_high.at[1], dz_high.at[3])
    begin()
    widen_high(1)
    widen_high(2)
    for e in range(2):
        for f in range(2):
            turned_high[e, :, f * px : (f + 1) * px] = shifted_high[1 + e, f].T
    weight_high(0)
    finish()
    widen_high(0)
    widen_high(3)
    spreads = []
    own_high = []
    for part in range(4):
        e, f = part // 2, part % 2
        total = 0.0
        for dy in range(3):
            total = total + dot_nn(
                shifted_high[e + 2 - dy, f], w_three[dy * taps_high : (dy + 1) * taps_high, :C0]
            )
        for j in range(nb):
            send_high[part, j] = total[:, j * slim : (j + 1) * slim].astype(bf16)

            @pl.when(b == j)
            def _():
                dy_high[part] = total[:, j * slim : (j + 1) * slim]

        spread = Spread(
            high_send.at[part],
            high_recv.at[part],
            lambda other, part=part: send_high.at[part, other],
            lambda j, part=part: recv_high.at[part, j],
        )
        spread.begin()
        spreads.append(spread)

    weight_high(1)
    weight_high(2)
    for part in range(4):
        spreads[part].finish()
        total = dy_high[part]
        for step in range(1, nb):
            total = total + recv_high[part, ring(b + step, nb)].astype(f32)
        dub[:, part * slim : (part + 1) * slim] = total.astype(bf16)

    def input_low(number, product):
        for j in range(nb):
            total = product(j)
            send_low[j] = total.astype(bf16)

            @pl.when(b == j)
            def _():
                dy_low[0] = total

        spread = Spread(
            all_send.at[number],
            all_recv.at[number],
            lambda other: send_low.at[other],
            lambda j: recv_low.at[number - 1, j],
        )
        spread.begin()

        def finish():
            spread.finish()
            total = dy_low[0]
            for step in range(1, nb):
                total = total + recv_low[number - 1, ring(b + step, nb)].astype(f32)
            dy_low[0] = total

        return finish

    finish_sum = input_low(
        1, lambda j: dot_nn(dub[...], w_up[:, j * wide : (j + 1) * wide])
    )
    out, width, taps, first = layers[2]
    turned_low[: 4 * slim, :] = dub[...].T
    for j in range(nb):
        total = dot_nn(turned_low[: 4 * slim, :], a_two[:, j * wide : (j + 1) * wide])
        rows = [(part * slim, part) for part in range(4)]
        put_grad(first, width // TILE, total, rows, j * (wide // TILE))
    finish_sum()

    def back_low(number, z_ref, inv_ref, gain, shift):
        def grad_of(part, image):
            return dy_low[0, rows_of(image), :]

        buffer = reduce_wide.at[number - 2]
        back_sums(buffer, z_ref, dy_low, gain, shift, grad_of)
        total = all_reduce(number, buffer)

        def put(part, image, value):
            dz_low[1, rows_of(image), :] = value

        return back_apply(total, z_ref, dy_low, inv_ref, gain, size_low, put)

    def widen_low(row):
        value = dz_low[row]
        wider = value.astype(f32)
        shifted_low[row, :, :wide] = shift_up(wider).astype(bf16)
        shifted_low[row, :, wide : 2 * wide] = value
        shifted_low[row, :, 2 * wide :] = shift_down(wider).astype(bf16)

    def weight_low(number, source, lines):
        out, width, taps, first = layers[number]
        chunk = 2 * TILE
        for dy in lines:
            rows = []
            for dx in range(3):
                for ob in range(wide // TILE):
                    rows.append((dx * wide + ob * TILE, ob * taps + 3 * dy + dx))
            for j in range(width // chunk):
                total = dot_nn(turned_low[...], source(dy, j * chunk, chunk))
                put_grad(first, width // TILE, total, rows, j * (chunk // TILE))

    gain_grad, shift_grad = back_low(4, z_two, inv_two, gain_two, shift_two)
    sums_ref[b, 2:3, :] = gain_grad
    sums_ref[b, 3:4, :] = shift_grad
    begin, finish = edges(1, dz_low.at[1], dz_low.at[0], dz_low.at[1], dz_low.at[2])
    begin()
    widen_low(1)
    turned_low[...] = shifted_low[1].T
    weight_low(1, lambda dy, start, size: a_one[dy, :, start : start + size], (0,))
    finish()
    widen_low(0)
    widen_low(2)

    def product_two(j):
        total = 0.0
        for dy in range(3):
            total = total + dot_nn(
                shifted_low[2 - dy],
                w_two[3 * dy * wide : 3 * (dy + 1) * wide, j * wide : (j + 1) * wide],
            )
        return total

    finish_sum = input_low(2, product_two)
    weight_low(1, lambda dy, start, size: a_one[dy, :, start : start + size], (1, 2))
    ready = pltpu.make_async_copy(
        grad_ref.at[pl.ds(layers[1][3], grad_ref.shape[0] - layers[1][3])],
        blocks_ref.at[pl.ds(layers[1][3], grad_ref.shape[0] - layers[1][3])],
        local_sem.at[0],
    )
    ready.start()
    finish_sum()
    gain_grad, shift_grad = back_low(5, z_one, inv_one, gain_one, shift_one)
    sums_ref[b, 0:1, :] = gain_grad
    sums_ref[b, 1:2, :] = shift_grad
    spread = Spread(
        all_send.at[3], all_recv.at[3], lambda other: sums_ref.at[b], lambda j: sums_ref.at[j]
    )
    spread.begin()
    widen_low(1)
    turned_low[...] = shifted_low[1].T
    weight_low(
        0, lambda dy, start, size: x_one[dy].reshape(px, C0)[:, start : start + size], (0, 1, 2)
    )
    last = pltpu.make_async_copy(
        grad_ref.at[pl.ds(0, layers[1][3])], blocks_ref.at[pl.ds(0, layers[1][3])], local_sem.at[1]
    )
    last.start()
    spread.finish()
    ready.wait()
    last.wait()


def run_step(master, place, bias, image, skip, lab, params, head):
    nr, nb = lax.axis_size("rows"), lax.axis_size("blk")
    cols = image.shape[0]
    px = nb * cols
    wide, slim = C1 // nb, C0 // nb
    vmem = pl.BlockSpec(memory_space=pltpu.VMEM)
    smem = pl.BlockSpec(memory_space=pltpu.SMEM)
    dma = pltpu.SemaphoreType.DMA
    scratch = [
        pltpu.VMEM((place.shape[0],) + master.shape[1:], bf16),
        dma((2,)),
        pltpu.VMEM((3, nb, cols, C0), bf16),
        pltpu.VMEM((4, 2, nb, cols, C0), bf16),
        pltpu.VMEM((nb, 4, 8, cols), f32),
        pltpu.VMEM((9 * wide, C0), bf16),
        pltpu.VMEM((9 * wide, C1), bf16),
        pltpu.VMEM((4 * slim, C1), bf16),
        pltpu.VMEM((9 * slim, 2 * C0), bf16),
        pltpu.VMEM((3, px, C1), bf16),
        pltpu.VMEM((px, C1), bf16),
        pltpu.VMEM((4, 2, px, C0), bf16),
        pltpu.VMEM((1, px, wide), f32),
        pltpu.VMEM((1, px, wide), f32),
        pltpu.VMEM((4, px, slim), f32),
        pltpu.VMEM((1, px, wide), f32),
        pltpu.VMEM((4, px, slim), f32),
        pltpu.VMEM((8, wide), f32),
        pltpu.VMEM((8, wide), f32),
        pltpu.VMEM((8, slim), f32),
        pltpu.VMEM((3, px, wide), bf16),
        pltpu.VMEM((4, 2, px, slim), bf16),
        pltpu.VMEM((3, px, 3 * wide), bf16),
        pltpu.VMEM((4, 2, px, 3 * slim), bf16),
        pltpu.VMEM((3 * wide, px), bf16),
        pltpu.VMEM((2, 3 * slim, 2 * px), bf16),
        pltpu.VMEM((px, 4 * slim), bf16),
        pltpu.VMEM((4, nb, px, slim), bf16),
        pltpu.VMEM((4, nb, px, slim), bf16),
        pltpu.VMEM((nb, px, wide), bf16),
        pltpu.VMEM((2, nb, px, wide), bf16),
        pltpu.VMEM((nb, 4, 2 * nb, cols), f32),
        pltpu.VMEM((4 * nb, 8, cols), f32),
        pltpu.VMEM((4, nr, 2 * nb + 8, wide), f32),
        pltpu.VMEM((2, nr, 2 * nb + 8, slim), f32),
        dma((3, nr, 2)),
        dma((nr, 2)),
        dma((6, nb, 2)),
        dma((6, nb)),
        dma((6, nb, 2)),
        dma((6, nb, 2)),
        dma((6, nr)),
        dma((6, nr)),
        dma((4, nb)),
        dma((4, nb)),
        dma((4, nb)),
        dma((4, nb)),
        dma((2, 2)),
        dma((2, 2)),
    ]
    return pl.pallas_call(
        functools.partial(step_kernel, nr, nb, cols),
        out_shape=(
            jax.ShapeDtypeStruct((place.shape[0],) + master.shape[1:], bf16),
            jax.ShapeDtypeStruct((nb, 16, wide), f32),
        ),
        in_specs=[vmem, smem, smem, vmem, vmem, vmem, vmem, vmem],
        out_specs=(pl.BlockSpec(memory_space=pl.ANY), vmem),
        scratch_shapes=scratch,
        compiler_params=pltpu.CompilerParams(
            collective_id=0, has_side_effects=True, vmem_limit_bytes=60 * 2**20
        ),
    )(master, place, bias, image, skip, lab, params, head)


LANES = 128


def inverse_factor_kernel(stat_ref, inverse_ref, factor_ref):
    order = stat_ref.shape[0]
    tile = (8, LANES)
    sub = lax.broadcasted_iota(jnp.int32, tile, 0)
    groups = order // 8

    def eliminate(source_ref, base, starts, first, count, accs):
        width = len(starts)

        def body(group, accs):
            top = pl.multiple_of(group * 8, 8)
            accs = [list(acc) for acc in accs]
            for unit in range(8):
                values = [source_ref[top + unit, pl.ds(start, 8), :] for start in starts]
                for c in range(8):
                    scale = jnp.broadcast_to(
                        factor_ref[top + unit, pl.ds(base + c, 1), :], tile
                    )
                    for s in range(width):
                        accs[s][c] = accs[s][c] - values[s] * scale
            return tuple(tuple(acc) for acc in accs)

        return lax.fori_loop(first, count, body, tuple(tuple(acc) for acc in accs))

    def batches(first, last, run):
        total = last - first

        def at(group):
            return pl.multiple_of(group * 8, 8)

        def two(n, _):
            run(first + 2 * n, [at(first + 2 * n), at(first + 2 * n + 1)])
            return 0

        lax.fori_loop(0, lax.div(total, 2), two, 0)

        @pl.when(lax.rem(total, 2) == 1)
        def _():
            run(last - 1, [at(last - 1)])

    def block(kb, _):
        base = pl.multiple_of(kb * 8, 8)
        accs = [stat_ref[base + c, pl.ds(base, 8), :] for c in range(8)]
        accs = list(eliminate(factor_ref, base, [base], 0, kb, [accs])[0])
        scale = []
        coef = {}
        for c in range(8):
            scale.append(jnp.broadcast_to(lax.rsqrt(accs[c][c : c + 1, :]), tile))
            accs[c] = accs[c] * scale[c]
            for d in range(c + 1, 8):
                coef[(c, d)] = jnp.broadcast_to(accs[c][d : d + 1, :], tile)
                accs[d] = accs[d] - accs[c] * coef[(c, d)]
        for c in range(8):
            factor_ref[base + c, pl.ds(base, 8), :] = jnp.where(sub >= c, accs[c], 0.0)

        def finish(accs, target_ref, start):
            accs = list(accs)
            for c in range(8):
                for e in range(c):
                    accs[c] = accs[c] - accs[e] * coef[(e, c)]
                accs[c] = accs[c] * scale[c]
                target_ref[base + c, pl.ds(start, 8), :] = accs[c]

        def below(group, starts):
            accs = [[stat_ref[base + c, pl.ds(s, 8), :] for c in range(8)] for s in starts]
            accs = eliminate(factor_ref, base, starts, 0, kb, accs)
            for acc, start in zip(accs, starts):
                finish(acc, factor_ref, start)

        def left(group, starts):
            accs = [[jnp.zeros(tile, jnp.float32) for c in range(8)] for s in starts]
            accs = eliminate(inverse_ref, base, starts, group, kb, accs)
            for acc, start in zip(accs, starts):
                finish(acc, inverse_ref, start)

        def clear(group, _):
            start = pl.multiple_of(group * 8, 8)
            for c in range(8):
                inverse_ref[base + c, pl.ds(start, 8), :] = jnp.zeros(tile, jnp.float32)
            return 0

        batches(kb + 1, groups, below)
        batches(0, kb, left)
        finish([jnp.where(sub == c, 1.0, 0.0) for c in range(8)], inverse_ref, base)
        lax.fori_loop(kb + 1, groups, clear, 0)
        return 0

    lax.fori_loop(0, groups, block, 0)


def split(value):
    high = value.astype(bf16)
    return high, (value - high.astype(f32)).astype(bf16)


def split_three(value):
    high = value.astype(bf16)
    rest = value - high.astype(f32)
    middle = rest.astype(bf16)
    return high, middle, (rest - middle.astype(f32)).astype(bf16)


def diagonal(pair):
    u, v = pair
    empty = jnp.zeros_like(u)
    return jnp.concatenate(
        [jnp.concatenate([u, empty], 1), jnp.concatenate([empty, v], 1)], 0
    )


def pair_product(packed, pair):
    a, b = split(packed)
    u, v = [split(value) for value in pair]
    c, d = diagonal((u[0], v[0])), diagonal((u[1], v[1]))
    result = dot_nn(jnp.concatenate([a, a, b], 1), jnp.concatenate([c, d, c], 0))
    order = packed.shape[1]
    return result[:, :order], result[:, order:]


def pair_cross(one, two):
    a, b = [jnp.concatenate(half, 1) for half in zip(*[split(value) for value in one])]
    c, d = [diagonal(half) for half in zip(*[split(value) for value in two])]
    return dot_nt(jnp.concatenate([a, a, b], 1), jnp.concatenate([c, d, c], 1))


def pair_square(pair):
    thirds = list(zip(*[split_three(value) for value in pair]))
    a, b, c = [jnp.concatenate(third, 1) for third in thirds]
    d, e, f = [diagonal(third) for third in thirds]
    return dot_nt(
        jnp.concatenate([a, a, b, a, b, c], 1), jnp.concatenate([d, e, d, f, e, d], 1)
    )


def product_three(left, right, right_dim):
    (a, b), (c, d) = left, right
    return lax.dot_general(
        jnp.concatenate([a, a, b], 1),
        jnp.concatenate([c, d, c], right_dim),
        (((1,), (right_dim,)), ((), ())),
        preferred_element_type=f32,
    )


def soap_blocks(indices, grads, ins, outs):
    def every(function, *lists):
        return [function(*items) for items in zip(*lists)]

    def load(ref):
        return [ref[index] for index in indices]

    def store(ref, values):
        for index, value in zip(indices, values):
            ref[index] = value

    master_ref, first_ref, second_ref, left_ref, right_ref, left_stat_ref, right_stat_ref = ins
    left = load(left_ref)
    sides, bases = every(split, grads), every(split, load(right_ref))
    lefts, turned = every(split, left), every(lambda grad: split(grad.T), grads)

    def three(dim):
        return lambda one, two: product_three(one, two, dim)

    lefts_turned = every(lambda value: split(value.T), left)
    half = every(three(0), lefts_turned, sides)
    left_outer = every(three(1), sides, sides)
    rotated = every(three(0), every(split, half), bases)
    right_outer = every(three(1), turned, turned)
    first = every(
        lambda old, new: beta_one * old + (1.0 - beta_one) * new, load(first_ref), rotated
    )
    second = every(
        lambda old, new: beta_two * old + (1.0 - beta_two) * new * new, load(second_ref), rotated
    )
    store(outs[2], first)
    store(outs[3], second)
    direction = every(
        lambda one, two: one
        * (1.0 / (1.0 - beta_one**STEP))
        / (jnp.sqrt(two * (1.0 / (1.0 - beta_two**STEP))) + adam_eps),
        first,
        second,
    )
    half = every(three(0), lefts, every(split, direction))
    stats = []
    for ref, target, outer in (
        (left_stat_ref, outs[4], left_outer),
        (right_stat_ref, outs[5], right_outer),
    ):
        stat = every(
            lambda old, new: beta_stat * old + (1.0 - beta_stat) * new, load(ref), outer
        )
        store(target, stat)
        stats.append(every(split, stat))
    moved = every(three(0), lefts_turned, stats[0])
    update = every(three(1), every(split, half), bases)
    moved_right = every(
        lambda stat, basis: product_three(stat, basis, 0).T, stats[1], bases
    )
    master = every(
        lambda old, new: old - soap_rate * (new + soap_decay * old), load(master_ref), update
    )
    store(outs[0], master)
    store(outs[1], every(lambda value: value.astype(bf16), master))
    store(outs[6], moved)
    store(outs[7], moved_right)
    middle = moved[0].shape[0] // 2
    store(
        outs[8],
        every(lambda one, two: pair_square((one[:middle], two[:middle])), moved, moved_right),
    )


def collect_kernel(nr, size, *refs):
    (owner_ref, blocks_ref), refs = refs[:2], refs[2:]
    ins, refs = refs[:7], refs[7:]
    outs, refs = refs[:9], refs[9:]
    (
        out_a,
        in_a,
        out_b,
        in_b,
        total,
        in_buffer,
        out_buffer,
        copy_buffer,
        gram_buffer,
        grad_ref,
        local_sem,
        a_send,
        a_recv,
        b_send,
        b_recv,
        in_sem,
        out_sem,
    ) = refs
    r = lax.axis_index("rows")
    b = lax.axis_index("blk")
    core = lax.rem(r, 2)
    chip = lax.div(r, 2)
    chips = nr // 2
    mate = r + 1 - 2 * core
    count = ins[0].shape[0]
    chunks = count // size
    square = in_square(chips, size)
    half = size // 2

    def device(chip, core):
        return {"rows": 2 * chip + core, "blk": b}

    stage = pltpu.make_async_copy(blocks_ref, grad_ref, local_sem)
    stage.start()
    barrier = pltpu.get_barrier_semaphore()
    pl.semaphore_signal(
        barrier, inc=1, device_id={"rows": mate, "blk": b}, device_id_type=MESH
    )

    def greet(step, _):
        pl.semaphore_signal(
            barrier,
            inc=1,
            device_id=device(lax.rem(chip + step, chips), core),
            device_id_type=MESH,
        )
        return 0

    lax.fori_loop(1, chips, greet, 0)

    def loads(chunk):
        return [
            pltpu.make_async_copy(
                ref.at[pl.ds(chunk * size, size)],
                in_buffer.at[chunk % 2, number],
                in_sem.at[chunk % 2, number],
            )
            for number, ref in enumerate(ins)
        ]

    def stores(chunk):
        copies = []
        for number, ref in enumerate(outs):
            if number in (1, 8):
                source = {1: copy_buffer, 8: gram_buffer}[number].at[chunk % 2]
            else:
                source = out_buffer.at[chunk % 2, number - (number > 1)]
            copies.append(
                pltpu.make_async_copy(
                    source, ref.at[pl.ds(chunk * size, size)], out_sem.at[chunk % 2, number]
                )
            )
        return copies

    def mine(to_chip, to_core, chunk, index):
        return grad_ref[owner_ref[(2 * to_chip + to_core) * count + chunk * size + index]]

    def joined(to_chip, chunk, index):
        value = mine(to_chip, core, chunk, index).astype(f32)
        return value + in_a[chunk, to_chip, index].astype(f32)

    def send_a(chunk):
        return pltpu.make_async_remote_copy(
            src_ref=out_a.at[chunk],
            dst_ref=in_a.at[chunk],
            send_sem=a_send.at[chunk],
            recv_sem=a_recv.at[chunk],
            device_id={"rows": mate, "blk": b},
            device_id_type=MESH,
        )

    def fill_a(chunk):
        def fill(n, _):
            to_chip, index = lax.div(n, size), lax.rem(n, size)
            out_a[chunk, to_chip, index] = mine(to_chip, 1 - core, chunk, index)
            return 0

        lax.fori_loop(0, chips * size, fill, 0)
        send_a(chunk).start()

    class Straight:
        def copy(self, chunk, step, source):
            other = lax.rem(chip + step, chips)
            return pltpu.make_async_remote_copy(
                src_ref=out_b.at[chunk, other],
                dst_ref=in_b.at[chunk, source],
                send_sem=b_send.at[chunk, step],
                recv_sem=b_recv.at[chunk, source],
                device_id=device(other, core),
                device_id_type=MESH,
            )

        def first(self, chunk):
            def join(step, _):
                other = lax.rem(chip + step, chips)

                def each(index, _):
                    out_b[chunk, other, index] = joined(other, chunk, index).astype(bf16)
                    return 0

                lax.fori_loop(0, size, each, 0)
                self.copy(chunk, step, chip).start()
                return 0

            lax.fori_loop(1, chips, join, 0)

        def second(self, chunk):
            pass

        def arrive(self, chunk):
            def wait(step, _):
                self.copy(chunk, step, lax.rem(chip + step, chips)).wait_recv()
                return 0

            lax.fori_loop(1, chips, wait, 0)

        def grad(self, chunk, index):
            return lax.fori_loop(
                1,
                chips,
                lambda step, value: value
                + in_b[chunk, lax.rem(chip + step, chips), index].astype(f32),
                total[chunk, index],
            )

        def close(self, chunk):
            def wait(step, _):
                self.copy(chunk, step, chip).wait_send()
                return 0

            lax.fori_loop(1, chips, wait, 0)

    class Square:
        def __init__(self):
            self.x = chip + 1 - 2 * lax.rem(chip, 2)
            self.y = chip + 2 - 4 * lax.div(chip, 2)
            self.corner = 3 - chip

        def one(self, chunk, way):
            return pltpu.make_async_remote_copy(
                src_ref=out_b.at[chunk, pl.ds(2 * way, 2)],
                dst_ref=in_b.at[chunk, pl.ds(2 * way, 2)],
                send_sem=b_send.at[chunk, way],
                recv_sem=b_recv.at[chunk, way],
                device_id=device((self.x, self.y)[way], core),
                device_id_type=MESH,
            )

        def two(self, chunk, way):
            return pltpu.make_async_remote_copy(
                src_ref=out_b.at[chunk, 4 + way],
                dst_ref=in_b.at[chunk, 4 + way],
                send_sem=b_send.at[chunk, 2 + way],
                recv_sem=b_recv.at[chunk, 2 + way],
                device_id=device((self.y, self.x)[way], core),
                device_id_type=MESH,
            )

        def first(self, chunk):
            for way, near in enumerate((self.x, self.y)):

                def each(index, _, way=way, near=near):
                    slot = way * half + index
                    out_b[chunk, 2 * way, index] = joined(near, chunk, slot).astype(bf16)
                    value = joined(self.corner, chunk, slot)
                    out_b[chunk, 2 * way + 1, index] = value.astype(bf16)
                    return 0

                lax.fori_loop(0, half, each, 0)
                self.one(chunk, way).start()

        def second(self, chunk):
            for way, far in enumerate((self.y, self.x)):
                self.one(chunk, way).wait_recv()

                def each(index, _, way=way, far=far):
                    value = joined(far, chunk, way * half + index)
                    value = value + in_b[chunk, 2 * way + 1, index].astype(f32)
                    out_b[chunk, 4 + way, index] = value.astype(bf16)
                    return 0

                lax.fori_loop(0, half, each, 0)
                self.two(chunk, way).start()

        def arrive(self, chunk):
            for way in range(2):
                self.two(chunk, way).wait_recv()

        def grad(self, chunk, index):
            way, place = index // half, index % half
            value = total[chunk, index] + in_b[chunk, 2 * way, place].astype(f32)
            return value + in_b[chunk, 4 + way, place].astype(f32)

        def close(self, chunk):
            for way in range(2):
                self.one(chunk, way).wait_send()
                self.two(chunk, way).wait_send()

    plan = Square() if square else Straight()

    def keep(chunk):
        def each(index, _):
            total[chunk, index] = joined(chip, chunk, index)
            return 0

        lax.fori_loop(0, size, each, 0)

    def work(chunk):
        plan.arrive(chunk)
        for copy in loads(chunk):
            copy.wait()
        if chunk >= 2:
            for copy in stores(chunk - 2):
                copy.wait()
        slot = chunk % 2
        chunk_ins = [in_buffer.at[slot, number] for number in range(7)]
        chunk_outs = [out_buffer.at[slot, number] for number in range(7)]
        chunk_outs.insert(1, copy_buffer.at[slot])
        chunk_outs.append(gram_buffer.at[slot])
        grads = [plan.grad(chunk, index) for index in range(size)]
        soap_blocks(range(size), grads, chunk_ins, chunk_outs)
        for copy in stores(chunk):
            copy.start()
        if chunk + 2 < chunks:
            for copy in loads(chunk + 2):
                copy.start()

    for chunk in range(min(2, chunks)):
        for copy in loads(chunk):
            copy.start()
    pl.semaphore_wait(barrier, chips)
    stage.wait()
    for chunk in range(chunks):
        fill_a(chunk)
    for chunk in range(chunks + 2):
        if chunk < chunks:
            send_a(chunk).wait_recv()
            plan.first(chunk)
            keep(chunk)
        if 1 <= chunk <= chunks:
            plan.second(chunk - 1)
        if chunk >= 2:
            work(chunk - 2)
    for chunk in range(chunks):
        send_a(chunk).wait_send()
        plan.close(chunk)
        if chunk >= chunks - 2:
            for copy in stores(chunk):
                copy.wait()


def in_square(chips, size):
    return chips == 4 and size % 2 == 0


def soap_update(blocks, owner, states):
    nr = lax.axis_size("rows")
    count, order = states[0].shape[0], states[0].shape[-1]
    size = 8 if count % 8 == 0 else count
    chunks = count // size
    anywhere = pl.BlockSpec(memory_space=pl.ANY)
    vmem = pl.BlockSpec(memory_space=pltpu.VMEM)
    shape = jax.ShapeDtypeStruct(states[0].shape, f32)
    dma = pltpu.SemaphoreType.DMA
    square = (order, order)
    chips = nr // 2
    parts = (6, size // 2) if in_square(chips, size) else (chips, size)
    results = pl.pallas_call(
        functools.partial(collect_kernel, nr, size),
        out_shape=(shape, jax.ShapeDtypeStruct(shape.shape, bf16)) + (shape,) * 6
        + (jax.ShapeDtypeStruct((count, order // 2, order), f32),),
        in_specs=[pl.BlockSpec(memory_space=pltpu.SMEM)] + [anywhere] * 8,
        out_specs=[anywhere] * 9,
        scratch_shapes=[
            pltpu.VMEM((chunks, chips, size) + square, bf16),
            pltpu.VMEM((chunks, chips, size) + square, bf16),
            pltpu.VMEM((chunks,) + parts + square, bf16),
            pltpu.VMEM((chunks,) + parts + square, bf16),
            pltpu.VMEM((chunks, size) + square, f32),
            pltpu.VMEM((2, 7, size) + square, f32),
            pltpu.VMEM((2, 7, size) + square, f32),
            pltpu.VMEM((2, size) + square, bf16),
            pltpu.VMEM((2, size, order // 2, order), f32),
            pltpu.VMEM(blocks.shape, bf16),
            dma(()),
            dma((chunks,)),
            dma((chunks,)),
            dma((chunks, chips)),
            dma((chunks, chips)),
            dma((2, 7)),
            dma((2, 9)),
        ],
        compiler_params=pltpu.CompilerParams(
            collective_id=1, has_side_effects=True, vmem_limit_bytes=60 * 2**20
        ),
    )(owner, blocks, *states)
    kept = list(results[:6])
    new_left, new_right, *kept = new_bases(results[6:8], results[8], kept)
    new_master, new_copy, new_first, new_second, new_left_stat, new_right_stat = kept
    return [
        new_master,
        new_copy,
        new_first,
        new_second,
        new_left,
        new_right,
        new_left_stat,
        new_right_stat,
    ]


def basis_kernel(gram_ref, left_ref, right_ref, *refs):
    number = (len(refs) - 9) // 3
    kept, new_left_ref, new_right_ref = refs[:number], refs[number], refs[number + 1]
    moved, refs = refs[number + 2 : 2 * number + 2], refs[2 * number + 2 :]
    stat_ref, inverse_ref, factor_ref, solve_ref, rest_ref, in_sem, out_sem, *halts = refs
    arriving = [
        pltpu.make_async_copy(source, halt, in_sem.at[n])
        for n, (source, halt) in enumerate(zip(kept, halts))
    ]
    leaving = [
        pltpu.make_async_copy(halt, target, out_sem.at[n])
        for n, (halt, target) in enumerate(zip(halts, moved))
    ]
    for copy in arriving:
        copy.start()
    count, order = left_ref.shape[0], left_ref.shape[1]
    half = order // 2
    width = next(size for size in (8, 5, 4, 2, 1) if count % size == 0)
    column = lax.broadcasted_iota(jnp.int32, (half, order), 1)

    def invert(source_ref):
        def enter(row, _):
            value = source_ref[pl.ds(row, count, stride=half), :]
            if count < half:
                spare = column[: half - count]
                spare = (spare == row) | (spare == row + half)
                value = jnp.concatenate([value, jnp.where(spare, 1.0, 0.0)], 0)
            value = jnp.concatenate([value, pltpu.roll(value, half, 1)], 0)
            stat_ref[row] = value.T[:half]
            return 0

        lax.fori_loop(0, half, enter, 0, unroll=8)
        inverse_factor_kernel(stat_ref, inverse_ref, factor_ref)

        def leave(row, _):
            value = inverse_ref[row]
            value = jnp.concatenate([value, value], 0).T
            solve_ref[pl.ds(row, count, stride=half), :] = jnp.where(
                column[:count] < half, value[:count], value[half : half + count]
            )
            return 0

        lax.fori_loop(0, half, leave, 0, unroll=8)

    def rows(index):
        return pl.ds(pl.multiple_of(index * half, half), half)

    def project(step, _):
        blocks = [step * width + n for n in range(width)]
        first = [(left_ref[n, :half], right_ref[n, :half]) for n in blocks]
        second = [(left_ref[n, half:], right_ref[n, half:]) for n in blocks]
        first = [pair_product(solve_ref[rows(n), :], pair) for n, pair in zip(blocks, first)]
        cross = [pair_cross(one, two) for one, two in zip(second, first)]
        shares = [pair_product(value, pair) for value, pair in zip(cross, first)]
        second = [
            (pair[0] - share[0], pair[1] - share[1]) for pair, share in zip(second, shares)
        ]
        squares = [pair_square(pair) for pair in second]
        for n, one, two, value in zip(blocks, first, second, squares):
            for side, ref in enumerate((new_left_ref, new_right_ref)):
                ref[n, :half] = one[side]
                ref[n, half:] = two[side]
            rest_ref[rows(n), :] = value
        return 0

    def complete(step, _):
        blocks = [step * width + n for n in range(width)]
        refs = (new_left_ref, new_right_ref)
        second = [
            pair_product(solve_ref[rows(n), :], [ref[n, half:] for ref in refs]) for n in blocks
        ]
        for n, pair in zip(blocks, second):
            for ref, value in zip(refs, pair):
                ref[n] = jnp.concatenate([ref[n, :half], value], 0).T
        return 0

    invert(gram_ref)
    for come, go in zip(arriving, leaving):
        come.wait()
        go.start()
    lax.fori_loop(0, count // width, project, 0)
    invert(rest_ref)
    lax.fori_loop(0, count // width, complete, 0)
    for copy in leaving:
        copy.wait()


def new_bases(products, grams, kept):
    count, order = products[0].shape[0], products[0].shape[-1]
    half = order // 2
    vmem = pl.BlockSpec(memory_space=pltpu.VMEM)
    anywhere = pl.BlockSpec(memory_space=pl.ANY)
    lanes = pltpu.VMEM((half, half, LANES), f32)
    flat = pltpu.VMEM((count * half, order), f32)
    return pl.pallas_call(
        basis_kernel,
        out_shape=[
            jax.ShapeDtypeStruct(value.shape, value.dtype) for value in list(products) + kept
        ],
        in_specs=[vmem] * 3 + [anywhere] * len(kept),
        out_specs=[vmem] * 2 + [anywhere] * len(kept),
        scratch_shapes=[lanes, lanes, lanes, flat, flat]
        + [pltpu.SemaphoreType.DMA((len(kept),))] * 2
        + [pltpu.VMEM(value.shape, value.dtype) for value in kept],
        compiler_params=pltpu.CompilerParams(vmem_limit_bytes=60 * 2**20),
    )(grams.reshape(count * half, order), *products, *kept)


def adam_small(grads, value, first, second):
    first_new = beta_one * first + (1.0 - beta_one) * grads
    second_new = beta_two * second + (1.0 - beta_two) * grads * grads
    direction = (
        first_new
        / (1.0 - beta_one**STEP)
        / (jnp.sqrt(second_new / (1.0 - beta_two**STEP)) + adam_eps)
    )
    return (first_new, second_new, value - small_rate * (direction + small_decay * value))


def local(
    image,
    skip,
    labels,
    weight_map,
    valid,
    owner,
    master,
    first_moment,
    second_moment,
    left_basis,
    right_basis,
    left_stat,
    right_stat,
    norm_params,
    norm_first,
    norm_second,
    head_bias,
    bias_first,
    bias_second,
):
    shards = lax.axis_size("blk")
    shard = lax.axis_index("blk")
    cols = image.shape[2]
    slots = jnp.arange(owner.shape[0])
    place = jnp.sum(jnp.where(owner[None, :] == slots[:, None], slots[None, :], 0), 1)
    widths = (C1, C1, C1, C1, C0, C0)
    heads = norm_params[sum(widths) :].reshape(C0, 2)
    part = C0 // shards
    heads = lax.dynamic_slice_in_dim(heads, shard * part, part).T
    heads = jnp.pad(heads, ((0, 6), (0, 0)))
    lab = jnp.stack([labels, weight_map, valid]).astype(f32).reshape(3, 2, cols, 2)
    lab = jnp.pad(lab.transpose(1, 3, 0, 2).reshape(4, 3, cols), ((0, 0), (0, 5), (0, 0)))
    skip = skip.reshape(2, cols, 2, C0).transpose(0, 2, 1, 3)
    blocks, sums = run_step(
        master[0],
        place.astype(jnp.int32),
        head_bias,
        image[0, 0],
        skip,
        lab,
        norm_params.reshape(-1, TILE),
        heads,
    )
    loss_sum, valid_count = sums[0, 6, 0], sums[0, 9, 0]
    grad_bias = sums[0, 7:9, 0]
    grad_head = jnp.stack([sums[:, 5, :part].reshape(-1), sums[:, 5, part : 2 * part].reshape(-1)], 1)
    small = jnp.concatenate(
        [sums[:, row].reshape(-1) for row in range(4)]
        + [
            sums[:, 4, :part].reshape(-1),
            sums[:, 4, part : 2 * part].reshape(-1),
            grad_head.reshape(-1),
        ]
    )
    states = (
        master,
        first_moment,
        second_moment,
        left_basis,
        right_basis,
        left_stat,
        right_stat,
    )
    soap = soap_update(blocks, owner, [state[0] for state in states])
    soap = [value[None] for value in soap]
    norm_new = adam_small(small, norm_params, norm_first, norm_second)
    bias_new = adam_small(grad_bias, head_bias, bias_first, bias_second)
    return (
        loss_sum,
        valid_count,
        soap[0],
        soap[1],
        soap[2],
        soap[3],
        soap[4],
        soap[5],
        soap[6],
        soap[7],
        norm_new[0],
        norm_new[1],
        norm_new[2],
        bias_new[0],
        bias_new[1],
        bias_new[2],
    )


def solution(mesh):
    placed = (
        P("blk", "rows", None, None),
        P("blk", "rows", None, None),
        P("blk", "rows", None),
        P("blk", "rows", None),
        P("blk", "rows", None),
        P(),
        P("blk", "rows", None, None),
        P("blk", "rows", None, None),
        P("blk", "rows", None, None),
        P("blk", "rows", None, None),
        P("blk", "rows", None, None),
        P("blk", "rows", None, None),
        P("blk", "rows", None, None),
        P(),
        P(),
        P(),
        P(),
        P(),
        P(),
    )
    return jax.shard_map(
        local,
        mesh=mesh,
        in_specs=placed,
        out_specs=(
            P(),
            P(),
            P("blk", "rows", None, None),
            P("blk", "rows", None, None),
            P("blk", "rows", None, None),
            P("blk", "rows", None, None),
            P("blk", "rows", None, None),
            P("blk", "rows", None, None),
            P("blk", "rows", None, None),
            P("blk", "rows", None, None),
            P(),
            P(),
            P(),
            P(),
            P(),
            P(),
        ),
        check_vma=False,
    )
```

```python
import functools

import jax
import jax.numpy as jnp
from jax import lax
from jax.experimental import pallas as pl
from jax.experimental.pallas import tpu as pltpu
from jax.sharding import PartitionSpec as P

C0 = 512
C1 = 1024
GROUPS = 32
STEP = 10


beta_one = 0.9
beta_two = 0.999
beta_stat = 0.95
adam_eps = 1e-08
norm_eps = 1e-05
soap_rate = 0.008
soap_decay = 0.01
small_rate = 0.4
small_decay = 0.01
highest = lax.Precision.HIGHEST


MESH = pl.DeviceIdType.MESH
bf16 = jnp.bfloat16
f32 = jnp.float32
TILE = 128


def dot_nt(left, right):
    return lax.dot_general(left, right, (((1,), (1,)), ((), ())), preferred_element_type=f32)


def dot_nn(left, right):
    return jnp.dot(left, right, preferred_element_type=f32)


def sigmoid(value):
    return 1.0 / (1.0 + jnp.exp(-value))


def block_layers(nb):
    result = []
    first = 0
    for in_width, out_width, taps in ((C0, C1, 9), (C1, C1, 9), (C1, C0, 4), (2 * C0, C0, 9)):
        out = out_width // nb
        result.append((out, in_width, taps, first))
        first = first + out // TILE * taps * (in_width // TILE)
    return result


def step_kernel(
    nr,
    nb,
    cols,
    master_ref,
    place_ref,
    bias_ref,
    image_ref,
    skip_ref,
    labels_ref,
    map_ref,
    valid_ref,
    params_ref,
    blocks_ref,
    sums_ref,
    grad_ref,
    local_sem,
    x_one,
    x_skip,
    x_lab,
    w_one,
    w_two,
    w_up,
    w_three,
    a_one,
    a_two,
    u_full,
    z_one,
    z_two,
    z_three,
    dy_low,
    dy_high,
    inv_one,
    inv_two,
    inv_three,
    dz_low,
    dz_high,
    shifted_low,
    shifted_high,
    turned_low,
    turned_high,
    dub,
    send_high,
    recv_high,
    send_low,
    recv_low,
    logit,
    grad_logit,
    reduce_wide,
    reduce_narrow,
    gather_send,
    gather_recv,
    line_send,
    line_recv,
    halo_send,
    halo_recv,
    red_send,
    red_recv,
    all_send,
    all_recv,
    high_send,
    high_recv,
    edge_send,
    edge_recv,
):
    r = lax.axis_index("rows")
    b = lax.axis_index("blk")
    px = nb * cols
    wide = C1 // nb
    slim = C0 // nb
    taps_high = 3 * slim
    layers = block_layers(nb)

    def remote(src, dst, send, recv, rows, blk):
        return pltpu.make_async_remote_copy(
            src_ref=src,
            dst_ref=dst,
            send_sem=send,
            recv_sem=recv,
            device_id={"rows": rows, "blk": blk},
            device_id_type=MESH,
        )

    def lanes(index, size):
        return pl.ds(pl.multiple_of(index * size, TILE), size)

    def ring(index, count):
        return lax.rem(index + count, count)

    barrier = pltpu.get_barrier_semaphore()

    def greet_rows(step, _):
        pl.semaphore_signal(
            barrier, inc=1, device_id={"rows": ring(r + step, nr), "blk": b}, device_id_type=MESH
        )
        return 0

    lax.fori_loop(1, nr, greet_rows, 0)
    for step in range(1, nb):
        pl.semaphore_signal(
            barrier, inc=1, device_id={"rows": r, "blk": ring(b + step, nb)}, device_id_type=MESH
        )
    pl.semaphore_wait(barrier, nr - 1 + nb - 1)

    class Exchange:
        def __init__(self, number, piece, up=None, down=None):
            self.number, self.piece, self.up, self.down = number, piece, up, down

        def right(self, j):
            return remote(
                self.piece(j),
                self.piece(j),
                line_send.at[self.number, j, 0],
                line_recv.at[self.number, j],
                r,
                ring(b + 1, nb),
            )

        def left(self, j):
            return remote(
                self.piece(j),
                self.piece(j),
                line_send.at[self.number, j, 1],
                line_recv.at[self.number, j],
                r,
                ring(b - 1, nb),
            )

        def higher(self, j):
            src, dst = self.up(j)
            return remote(
                src,
                dst,
                halo_send.at[self.number, j, 0],
                halo_recv.at[self.number, j, 0],
                ring(r + 1, nr),
                b,
            )

        def lower(self, j):
            src, dst = self.down(j)
            return remote(
                src,
                dst,
                halo_send.at[self.number, j, 1],
                halo_recv.at[self.number, j, 1],
                ring(r - 1, nr),
                b,
            )

        def halos(self, j):
            if self.up is None:
                return

            @pl.when(r + 1 < nr)
            def _():
                self.higher(j).start()

            @pl.when(r > 0)
            def _():
                self.lower(j).start()

        def begin(self):
            @pl.when(b + 1 < nb)
            def _():
                self.right(b).start()

            @pl.when(b > 0)
            def _():
                self.left(b).start()

            self.halos(b)

        def hop(self, k):
            @pl.when(b >= k)
            def _():
                self.right(b - k).wait_recv()

                @pl.when(b + 1 < nb)
                def _():
                    self.right(b - k).start()

                self.halos(b - k)

            @pl.when(b + k < nb)
            def _():
                self.left(b + k).wait_recv()

                @pl.when(b > 0)
                def _():
                    self.left(b + k).start()

                self.halos(b + k)

        def hops(self):
            for k in range(1, nb):
                self.hop(k)

        def finish(self):
            for k in range(nb):

                @pl.when((b >= k) & (b + 1 < nb))
                def _():
                    self.right(b - k).wait_send()

                @pl.when((b + k < nb) & (b > 0))
                def _():
                    self.left(b + k).wait_send()

            if self.up is None:
                return
            for j in range(nb):

                @pl.when(r + 1 < nr)
                def _():
                    self.higher(j).wait_send()
                    self.lower(j).wait_recv()

                @pl.when(r > 0)
                def _():
                    self.lower(j).wait_send()
                    self.higher(j).wait_recv()

    def reduce_start(number, buffer):
        def start(step, _):
            remote(
                buffer.at[r],
                buffer.at[r],
                red_send.at[number, step],
                red_recv.at[number, r],
                ring(r + step, nr),
                b,
            ).start()
            return 0

        lax.fori_loop(1, nr, start, 0, unroll=nr <= 8)

    def reduce_finish(number, buffer):
        def wait(step, _):
            source = ring(r + step, nr)
            copy = remote(
                buffer.at[source],
                buffer.at[source],
                red_send.at[number, step],
                red_recv.at[number, source],
                source,
                b,
            )
            copy.wait_recv()
            copy.wait_send()
            return 0

        lax.fori_loop(1, nr, wait, 0, unroll=nr <= 8)
        return lax.fori_loop(
            1, nr, lambda k, total: total + buffer[k], buffer[0], unroll=nr <= 8
        )

    def all_reduce(number, buffer):
        reduce_start(number, buffer)
        return reduce_finish(number, buffer)

    class Spread:
        def __init__(self, send, recv, source, target):
            self.send, self.recv, self.source, self.target = send, recv, source, target

        def copy(self, step):
            other = ring(b + step, nb)
            return remote(
                self.source(other),
                self.target(b),
                self.send.at[step],
                self.recv.at[b],
                r,
                other,
            )

        def begin(self):
            for step in range(1, nb):
                self.copy(step).start()

        def finish(self):
            for step in range(1, nb):
                other = ring(b + step, nb)
                remote(
                    self.source(other),
                    self.target(other),
                    self.send.at[step],
                    self.recv.at[other],
                    r,
                    other,
                ).wait_recv()
                self.copy(step).wait_send()

    class Gather:
        def __init__(self):
            self.size = master_ref.shape[0]
            self.chips = nr // 2
            self.core = lax.rem(r, 2)
            self.chip = lax.div(r, 2)
            self.mate = r + 1 - 2 * self.core
            self.square = self.chips == 4 and self.size % 2 == 0
            self.halves = 2 if self.square else 1

        def piece(self, row, half):
            part = self.size // self.halves
            return grad_ref.at[pl.ds(row * self.size + half * part, part)]

        def move(self, kind, target, row, half):
            return remote(
                self.piece(row, half),
                self.piece(row, half),
                gather_send.at[kind, row, half],
                gather_recv.at[row, half],
                target,
                b,
            )

        def direct(self, target):
            return remote(
                self.piece(r, 0),
                self.piece(r, 0),
                gather_send.at[0, target, 0],
                gather_recv.at[r, 0],
                target,
                b,
            )

        def beside(self, step):
            return 2 * lax.rem(self.chip + step, self.chips) + self.core

        def other(self, bit):
            away = self.chip + bit - 2 * bit * lax.rem(lax.div(self.chip, bit), 2)
            return 2 * away + self.core

        def begin(self):
            def cast(index, _):
                grad_ref[r * self.size + index] = master_ref[index].astype(bf16)
                return 0

            lax.fori_loop(0, self.size, cast, 0)
            if self.square:
                for half in range(2):
                    self.move(2, self.mate, r, half).start()
                    self.move(0, self.other(1), r, 1 - half).start()
                    self.move(1, self.other(2), r, half).start()
            else:
                self.move(2, self.mate, r, 0).start()

                def send(step, _):
                    self.direct(self.beside(step)).start()
                    return 0

                lax.fori_loop(1, self.chips, send, 0)

        def arrived(self, row, half):
            self.move(2, self.mate, row, half).wait_recv()

        def hand(self, row, half):
            self.arrived(row, half)
            self.move(2, self.mate, row, half).start()

        def forward(self, moves):
            image, lab, skip = moves
            for k in range(1, nb):
                image.hop(k)
                lab.hop(k)
            if self.square:
                x, y = self.other(1), self.other(2)
                corner = 2 * (3 - self.chip) + self.core
                self.hand(y, 0)
                self.move(0, x, y, 0).start()
                self.hand(x, 1)
                self.move(1, y, x, 1).start()
                skip.hop(1)
                self.hand(x, 0)
                self.hand(y, 1)
                self.hand(corner, 0)
                self.hand(corner, 1)
                rows = (r, x, y, corner)
                for half in range(2):
                    for row in rows:
                        self.arrived(row + 1 - 2 * self.core, half)
                for half in range(2):
                    for row in rows:
                        self.move(2, self.mate, row, half).wait_send()
                    self.move(0, x, r, half).wait_send()
                    self.move(1, y, r, half).wait_send()
                self.move(0, x, y, 0).wait_send()
                self.move(1, y, x, 1).wait_send()
            else:

                def pass_on(step, _):
                    self.hand(self.beside(step), 0)
                    return 0

                def close(step, _):
                    row = self.beside(step)
                    self.arrived(row + 1 - 2 * self.core, 0)
                    self.move(2, self.mate, row, 0).wait_send()
                    self.direct(row).wait_send()
                    return 0

                lax.fori_loop(1, self.chips, pass_on, 0)
                skip.hop(1)
                self.arrived(self.mate, 0)
                self.move(2, self.mate, r, 0).wait_send()
                lax.fori_loop(1, self.chips, close, 0)

    position = lax.rem(lax.broadcasted_iota(jnp.int32, (px, TILE), 0), cols)

    def mask_of(value, column):
        hit = position[:, :1] == column
        return jnp.where(hit, 0.0, value)

    def shift_down(value):
        return mask_of(pltpu.roll(value, 1, 0), 0)

    def shift_up(value):
        return mask_of(pltpu.roll(value, px - 1, 0), cols - 1)

    def group_sum(value, size):
        width = value.shape[-1]
        bits = size.bit_length() - 1
        first = lax.shift_right_logical(lax.broadcasted_iota(jnp.int32, (width, width), 0), bits)
        second = lax.shift_right_logical(lax.broadcasted_iota(jnp.int32, (width, width), 1), bits)
        same = jnp.where(first == second, 1.0, 0.0).astype(f32)
        return jnp.dot(value, same, preferred_element_type=f32, precision=highest)

    def rows_of(image):
        return pl.ds(image * cols, cols)

    def norm_sums(buffer, z_ref):
        for image in range(nb):
            first = 0.0
            second = 0.0
            for part in range(z_ref.shape[0]):
                value = z_ref[part, rows_of(image), :]
                first = first + jnp.sum(value, 0, keepdims=True)
                second = second + jnp.sum(value * value, 0, keepdims=True)
            buffer[r, image : image + 1, :] = first
            buffer[r, nb + image : nb + image + 1, :] = second

    def norm_apply(total, z_ref, inv_ref, gain, shift, size, put):
        width = z_ref.shape[-1]
        number = nr * cols * z_ref.shape[0] * size
        sums = group_sum(total[: 2 * nb], size) / number
        mean = sums[:nb]
        inv = lax.rsqrt(sums[nb:] - mean * mean + norm_eps)
        inv_ref[:nb, :] = inv
        for part in range(z_ref.shape[0]):
            for image in range(nb):
                value = z_ref[part, rows_of(image), :]
                value = (value - mean[image : image + 1]) * inv[image : image + 1]
                z_ref[part, rows_of(image), :] = value
                normed = value * gain + shift
                put(part, image, (normed * sigmoid(normed)).astype(bf16))

    def back_sums(buffer, z_ref, dy_ref, gain, shift, grad_of):
        for image in range(nb):
            first = 0.0
            second = 0.0
            for part in range(z_ref.shape[0]):
                value = z_ref[part, rows_of(image), :]
                normed = value * gain + shift
                gate = sigmoid(normed)
                grad = grad_of(part, image) * gate * (1.0 + normed * (1.0 - gate))
                dy_ref[part, rows_of(image), :] = grad
                first = first + jnp.sum(grad, 0, keepdims=True)
                second = second + jnp.sum(grad * value, 0, keepdims=True)
            buffer[r, image : image + 1, :] = first
            buffer[r, nb + image : nb + image + 1, :] = second

    def back_apply(total, z_ref, dy_ref, inv_ref, gain, size, put):
        number = nr * cols * z_ref.shape[0] * size
        sums = group_sum(total[: 2 * nb] * gain, size) / number
        inv = inv_ref[:nb, :]
        for part in range(z_ref.shape[0]):
            for image in range(nb):
                one = slice(image, image + 1)
                two = slice(nb + image, nb + image + 1)
                value = dy_ref[part, rows_of(image), :] * gain - sums[one]
                value = value - z_ref[part, rows_of(image), :] * sums[two]
                put(part, image, (value * inv[one]).astype(bf16))
        shift_grad = jnp.sum(total[:nb], 0, keepdims=True)
        gain_grad = jnp.sum(total[nb : 2 * nb], 0, keepdims=True)
        return gain_grad, shift_grad

    gather = Gather()
    gather.begin()
    x_one[1, b] = image_ref[...]

    def pick(shape, dim, stride, start):
        index = lax.broadcasted_iota(jnp.int32, shape, dim)
        target = stride * lax.broadcasted_iota(jnp.int32, shape, 1 - dim) + start
        return jnp.where(index == target, 1.0, 0.0).astype(bf16)

    values = [ref[...].astype(f32) for ref in (labels_ref, map_ref, valid_ref)]
    values = jnp.concatenate(values + [jnp.zeros_like(values[0])], 0).astype(bf16)
    for f in range(2):
        x_lab[b, f] = dot_nn(values, pick((2 * cols, cols), 0, 2, f))
        for e in range(2):
            value = dot_nn(pick((cols, 2 * cols), 1, 2, f), skip_ref[e])
            x_skip[1 + e, f, b] = value.astype(bf16)
    move_image = Exchange(
        0,
        lambda j: x_one.at[1, j],
        lambda j: (x_one.at[1, j], x_one.at[0, j]),
        lambda j: (x_one.at[1, j], x_one.at[2, j]),
    )
    move_skip = Exchange(
        1,
        lambda j: x_skip.at[pl.ds(1, 2), :, j],
        lambda j: (x_skip.at[2, :, j], x_skip.at[0, :, j]),
        lambda j: (x_skip.at[1, :, j], x_skip.at[3, :, j]),
    )
    move_lab = Exchange(2, lambda j: x_lab.at[j])
    moves = (move_image, move_lab, move_skip)
    for move in moves:
        move.begin()
    @pl.when(r == 0)
    def _():
        x_one[0] = jnp.zeros_like(x_one[0])
        x_skip[0] = jnp.zeros_like(x_skip[0])
        a_one[0] = jnp.zeros_like(a_one[0])
        u_full[0] = jnp.zeros_like(u_full[0])
        dz_low[0] = jnp.zeros_like(dz_low[0])
        dz_high[0] = jnp.zeros_like(dz_high[0])

    @pl.when(r == nr - 1)
    def _():
        x_one[2] = jnp.zeros_like(x_one[2])
        x_skip[3] = jnp.zeros_like(x_skip[3])
        a_one[2] = jnp.zeros_like(a_one[2])
        u_full[3] = jnp.zeros_like(u_full[3])
        dz_low[2] = jnp.zeros_like(dz_low[2])
        dz_high[3] = jnp.zeros_like(dz_high[3])

    gather.forward(moves)
    move_image.finish()
    move_lab.finish()
    middle = max(1, nb // 2)
    for k in range(2, middle + 1):
        move_skip.hop(k)

    def arrange(number, target):
        out, width, taps, first = layers[number]
        across = width // TILE

        def body(n, _):
            ib = lax.rem(n, across)
            t = lax.rem(lax.div(n, across), taps)
            ob = lax.div(n, across * taps)
            target[
                pl.ds(pl.multiple_of(t * out + ob * TILE, TILE), TILE), lanes(ib, TILE)
            ] = grad_ref[place_ref[first + n]]
            return 0

        lax.fori_loop(0, out // TILE * taps * across, body, 0)

    arrange(0, w_one)
    def own_params(first, width):
        start = first // TILE + b * (width // TILE)
        return jnp.concatenate(
            [params_ref[pl.ds(start + n, 1), :] for n in range(width // TILE)], 1
        )

    gain_one, shift_one, gain_two, shift_two = [own_params(n * C1, wide) for n in range(4)]
    gain_three, shift_three = [own_params(4 * C1 + n * C0, slim) for n in range(2)]
    size_low, size_high = C1 // GROUPS, C0 // GROUPS

    def conv_low(z_ref, weight, source, lines=(0, 1, 2), more=False):
        def tap(dx):
            total = 0.0
            for dy in lines:
                first = (3 * dy + dx) * wide
                total = total + dot_nt(source(dy), weight[first : first + wide, :])
            return total

        if more:
            z_ref[0] += tap(1)
        else:
            z_ref[0] = tap(1)
        z_ref[0] += shift_down(tap(0))
        z_ref[0] += shift_up(tap(2))

    conv_low(z_one, w_one, lambda dy: x_one[dy].reshape(px, C0))
    reduce_one, reduce_two = reduce_wide.at[0], reduce_wide.at[1]
    norm_sums(reduce_one, z_one)
    count = 0.0
    for image in range(nb):
        for part in range(4):
            line = 4 + part // 2
            value = x_lab[image, part % 2, line : line + 1, :]
            count = count + jnp.sum(value, 1, keepdims=True)
    reduce_one[r, 2 * nb : 2 * nb + 1, :] = jnp.broadcast_to(count, (1, wide))
    reduce_start(0, reduce_one)
    arrange(1, w_two)
    total = reduce_finish(0, reduce_one)
    count = total[2 * nb : 2 * nb + 1, :1]

    def put_one(part, image, value):
        a_one[1, rows_of(image), lanes(b, wide)] = value

    norm_apply(total, z_one, inv_one, gain_one, shift_one, size_low, put_one)
    move = Exchange(
        3,
        lambda j: a_one.at[1, :, lanes(j, wide)],
        lambda j: (a_one.at[1, :, lanes(j, wide)], a_one.at[0, :, lanes(j, wide)]),
        lambda j: (a_one.at[1, :, lanes(j, wide)], a_one.at[2, :, lanes(j, wide)]),
    )
    move.begin()
    move.hop(1)
    arrange(2, w_up)
    for k in range(2, nb):
        move.hop(k)
    arrange(3, w_three)
    conv_low(z_two, w_two, lambda dy: a_one[dy], (1,))
    move.finish()
    for k in range(middle + 1, nb):
        move_skip.hop(k)
    conv_low(z_two, w_two, lambda dy: a_one[dy], (0, 2), True)
    norm_sums(reduce_two, z_two)
    total = all_reduce(1, reduce_two)

    def put_two(part, image, value):
        a_two[rows_of(image), lanes(b, wide)] = value

    norm_apply(total, z_two, inv_two, gain_two, shift_two, size_low, put_two)
    move = Exchange(4, lambda j: a_two.at[:, lanes(j, wide)])
    move.begin()
    move.hops()
    move.finish()
    for part in range(4):
        u_full[1 + part // 2, part % 2, :, lanes(b, slim)] = dot_nt(
            a_two[...], w_up[part * slim : (part + 1) * slim, :]
        ).astype(bf16)
    move = Exchange(
        5,
        lambda j: u_full.at[pl.ds(1, 2), :, :, lanes(j, slim)],
        lambda j: (u_full.at[2, :, :, lanes(j, slim)], u_full.at[0, :, :, lanes(j, slim)]),
        lambda j: (u_full.at[1, :, :, lanes(j, slim)], u_full.at[3, :, :, lanes(j, slim)]),
    )
    def conv_high(product, more):
        for e in range(2):
            even, odd = product(e, 0), product(e, 1)
            first = even[:, slim : 2 * slim] + shift_down(odd[:, :slim]) + odd[:, 2 * slim :]
            second = odd[:, slim : 2 * slim] + even[:, :slim] + shift_up(even[:, 2 * slim :])
            if more:
                z_three[2 * e] += first
                z_three[2 * e + 1] += second
            else:
                z_three[2 * e] = first
                z_three[2 * e + 1] = second

    def high_product(source, start, lines):
        def product(e, f):
            total = 0.0
            for dy in lines[e]:
                weight = w_three[dy * taps_high : (dy + 1) * taps_high, start : start + C0]
                total = total + dot_nt(source[e + dy, f].reshape(px, C0), weight)
            return total

        return product

    every = ((0, 1, 2), (0, 1, 2))
    inner, outer = ((1, 2), (0, 1)), ((0,), (2,))
    move.begin()
    move_skip.finish()
    conv_high(high_product(x_skip, C0, every), False)
    move.hops()
    conv_high(high_product(u_full, 0, inner), True)
    move.finish()
    conv_high(high_product(u_full, 0, outer), True)
    reduce_three, reduce_four = reduce_narrow.at[0], reduce_narrow.at[1]
    norm_sums(reduce_three, z_three)
    total = all_reduce(2, reduce_three)
    a_three = send_high

    def put_three(part, image, value):
        a_three[part, 0, rows_of(image), :] = value

    norm_apply(total, z_three, inv_three, gain_three, shift_three, size_high, put_three)
    pairs = 2 * slim // TILE
    start = (4 * C1 + 2 * C0) // TILE + b * pairs
    head = []
    for number in range(2):
        total = 0.0
        for n in range(pairs):
            value = params_ref[pl.ds(start + n, 1), :].astype(bf16)
            total = total + dot_nn(value, pick((TILE, slim), 0, 2, number - TILE * n))
        head.append(total)
    head = jnp.concatenate(head + [jnp.zeros((6, slim), f32)], 0)
    head_low = head.astype(bf16)
    for part in range(4):
        for image in range(nb):
            tile = dot_nt(head_low, a_three[part, 0, rows_of(image), :])
            logit[b, part, 2 * image : 2 * image + 2, :] = tile[:2]
    spread = Spread(all_send.at[0], all_recv.at[0], lambda other: logit.at[b], lambda j: logit.at[j])
    spread.begin()
    spread.finish()
    loss = jnp.zeros((1, cols), f32)
    bias_grad = [jnp.zeros((1, cols), f32), jnp.zeros((1, cols), f32)]
    head_grad = jnp.zeros((8, slim), f32)
    level = lax.broadcasted_iota(jnp.int32, (8, cols), 0)

    def head_of(part, image):
        two = slice(2 * image, 2 * image + 2)
        tile = logit[0, part, two, :]
        for j in range(1, nb):
            tile = tile + logit[j, part, two, :]
        first = tile[0:1, :] + bias_ref[0]
        second = tile[1:2, :] + bias_ref[1]
        e, f = part // 2, part % 2
        label, level_map, counted = [
            x_lab[image, f, line : line + 1, :] for line in (e, 2 + e, 4 + e)
        ]
        scale = counted * level_map * 0.125
        largest = jnp.maximum(first, second)
        log_total = jnp.log(jnp.exp(first - largest) + jnp.exp(second - largest)) + largest
        picked = first * (1.0 - label) + second * label
        unit = scale / count
        return (
            scale * (log_total - picked),
            (jnp.exp(first - log_total) - (1.0 - label)) * unit,
            (jnp.exp(second - log_total) - label) * unit,
        )

    for part in range(4):
        for image in range(nb):
            cost, first, second = head_of(part, image)
            loss = loss + cost
            bias_grad = [bias_grad[0] + first, bias_grad[1] + second]
            tile = jnp.where(level == 0, first, jnp.where(level == 1, second, 0.0))
            grad_logit[part * nb + image] = tile
            head_grad = head_grad + jnp.dot(
                tile,
                a_three[part, 0, rows_of(image), :].astype(f32),
                preferred_element_type=f32,
                precision=highest,
            )

    def grad_three(part, image):
        return lax.dot_general(
            grad_logit[part * nb + image],
            head,
            (((0,), (0,)), ((), ())),
            preferred_element_type=f32,
            precision=highest,
        )

    reduce_four[r, 2 * nb : 2 * nb + 8, :] = head_grad
    for row, value in enumerate([loss] + bias_grad):
        reduce_four[r, 2 * nb + 2 + row : 2 * nb + 3 + row, :] = jnp.broadcast_to(
            jnp.sum(value, 1, keepdims=True), (1, slim)
        )
    back_sums(reduce_four, z_three, dy_high, gain_three, shift_three, grad_three)
    total = all_reduce(3, reduce_four)

    def put_high(part, image, value):
        dz_high[1 + part // 2, part % 2, rows_of(image), :] = value

    gain_grad, shift_grad = back_apply(
        total, z_three, dy_high, inv_three, gain_three, size_high, put_high
    )
    sums_ref[b] = jnp.zeros_like(sums_ref[b])
    sums_ref[b, 4:5, :slim] = gain_grad
    sums_ref[b, 4:5, slim : 2 * slim] = shift_grad
    sums_ref[b, 5:6, :slim] = total[2 * nb : 2 * nb + 1]
    sums_ref[b, 5:6, slim : 2 * slim] = total[2 * nb + 1 : 2 * nb + 2]
    for row in range(3):
        sums_ref[b, 6 + row : 7 + row, :slim] = total[2 * nb + 2 + row : 2 * nb + 3 + row]
    sums_ref[b, 9:10, :] = jnp.broadcast_to(count, (1, wide))

    def edges(number, source_up, target_up, source_down, target_down):
        def higher():
            return remote(
                source_up,
                target_up,
                edge_send.at[number, 0],
                edge_recv.at[number, 0],
                ring(r + 1, nr),
                b,
            )

        def lower():
            return remote(
                source_down,
                target_down,
                edge_send.at[number, 1],
                edge_recv.at[number, 1],
                ring(r - 1, nr),
                b,
            )

        def begin():
            @pl.when(r + 1 < nr)
            def _():
                higher().start()

            @pl.when(r > 0)
            def _():
                lower().start()

        def finish():
            @pl.when(r + 1 < nr)
            def _():
                higher().wait_send()
                lower().wait_recv()

            @pl.when(r > 0)
            def _():
                lower().wait_send()
                higher().wait_recv()

        return begin, finish

    def widen_high(row):
        even, odd = dz_high[row, 0], dz_high[row, 1]
        shifted_high[row, 0, :, :slim] = odd
        shifted_high[row, 0, :, slim : 2 * slim] = even
        shifted_high[row, 0, :, 2 * slim :] = shift_down(odd.astype(f32)).astype(bf16)
        shifted_high[row, 1, :, :slim] = shift_up(even.astype(f32)).astype(bf16)
        shifted_high[row, 1, :, slim : 2 * slim] = odd
        shifted_high[row, 1, :, 2 * slim :] = even

    def put_grad(first, across, value, rows, start):
        for row, number in rows:
            for k in range(value.shape[1] // TILE):
                grad_ref[first + number * across + start + k] = value[
                    row : row + TILE, k * TILE : (k + 1) * TILE
                ].astype(bf16)

    def weight_high(dy):
        out, width, taps, first = layers[3]
        rows = [(dx * slim, 3 * dy + dx) for dx in range(3)]
        for half, source in enumerate((u_full, x_skip)):
            total = 0.0
            for e in range(2):
                for f in range(2):
                    value = source[e + dy, f].reshape(px, C0)
                    total = total + dot_nn(turned_high[e, :, f * px : (f + 1) * px], value)
            put_grad(first, width // TILE, total, rows, half * (C0 // TILE))

    begin, finish = edges(0, dz_high.at[2], dz_high.at[0], dz_high.at[1], dz_high.at[3])
    begin()
    widen_high(1)
    widen_high(2)
    for e in range(2):
        for f in range(2):
            turned_high[e, :, f * px : (f + 1) * px] = shifted_high[1 + e, f].T
    weight_high(0)
    finish()
    widen_high(0)
    widen_high(3)
    spreads = []
    own_high = []
    for part in range(4):
        e, f = part // 2, part % 2
        total = 0.0
        for dy in range(3):
            total = total + dot_nn(
                shifted_high[e + 2 - dy, f], w_three[dy * taps_high : (dy + 1) * taps_high, :C0]
            )
        for j in range(nb):
            send_high[part, j] = total[:, j * slim : (j + 1) * slim].astype(bf16)

            @pl.when(b == j)
            def _():
                dy_high[part] = total[:, j * slim : (j + 1) * slim]

        spread = Spread(
            high_send.at[part],
            high_recv.at[part],
            lambda other, part=part: send_high.at[part, other],
            lambda j, part=part: recv_high.at[part, j],
        )
        spread.begin()
        spreads.append(spread)

    weight_high(1)
    weight_high(2)
    for part in range(4):
        spreads[part].finish()
        total = dy_high[part]
        for step in range(1, nb):
            total = total + recv_high[part, ring(b + step, nb)].astype(f32)
        dub[:, part * slim : (part + 1) * slim] = total.astype(bf16)

    def input_low(number, product):
        for j in range(nb):
            total = product(j)
            send_low[j] = total.astype(bf16)

            @pl.when(b == j)
            def _():
                dy_low[0] = total

        spread = Spread(
            all_send.at[number],
            all_recv.at[number],
            lambda other: send_low.at[other],
            lambda j: recv_low.at[number - 1, j],
        )
        spread.begin()

        def finish():
            spread.finish()
            total = dy_low[0]
            for step in range(1, nb):
                total = total + recv_low[number - 1, ring(b + step, nb)].astype(f32)
            dy_low[0] = total

        return finish

    finish_sum = input_low(
        1, lambda j: dot_nn(dub[...], w_up[:, j * wide : (j + 1) * wide])
    )
    out, width, taps, first = layers[2]
    turned_low[: 4 * slim, :] = dub[...].T
    for j in range(nb):
        total = dot_nn(turned_low[: 4 * slim, :], a_two[:, j * wide : (j + 1) * wide])
        rows = [(part * slim, part) for part in range(4)]
        put_grad(first, width // TILE, total, rows, j * (wide // TILE))
    finish_sum()

    def back_low(number, z_ref, inv_ref, gain, shift):
        def grad_of(part, image):
            return dy_low[0, rows_of(image), :]

        buffer = reduce_wide.at[number - 2]
        back_sums(buffer, z_ref, dy_low, gain, shift, grad_of)
        total = all_reduce(number, buffer)

        def put(part, image, value):
            dz_low[1, rows_of(image), :] = value

        return back_apply(total, z_ref, dy_low, inv_ref, gain, size_low, put)

    def widen_low(row):
        value = dz_low[row]
        wider = value.astype(f32)
        shifted_low[row, :, :wide] = shift_up(wider).astype(bf16)
        shifted_low[row, :, wide : 2 * wide] = value
        shifted_low[row, :, 2 * wide :] = shift_down(wider).astype(bf16)

    def weight_low(number, source, lines):
        out, width, taps, first = layers[number]
        chunk = 2 * TILE
        for dy in lines:
            rows = []
            for dx in range(3):
                for ob in range(wide // TILE):
                    rows.append((dx * wide + ob * TILE, ob * taps + 3 * dy + dx))
            for j in range(width // chunk):
                total = dot_nn(turned_low[...], source(dy, j * chunk, chunk))
                put_grad(first, width // TILE, total, rows, j * (chunk // TILE))

    gain_grad, shift_grad = back_low(4, z_two, inv_two, gain_two, shift_two)
    sums_ref[b, 2:3, :] = gain_grad
    sums_ref[b, 3:4, :] = shift_grad
    begin, finish = edges(1, dz_low.at[1], dz_low.at[0], dz_low.at[1], dz_low.at[2])
    begin()
    widen_low(1)
    turned_low[...] = shifted_low[1].T
    weight_low(1, lambda dy, start, size: a_one[dy, :, start : start + size], (0,))
    finish()
    widen_low(0)
    widen_low(2)

    def product_two(j):
        total = 0.0
        for dy in range(3):
            total = total + dot_nn(
                shifted_low[2 - dy],
                w_two[3 * dy * wide : 3 * (dy + 1) * wide, j * wide : (j + 1) * wide],
            )
        return total

    finish_sum = input_low(2, product_two)
    weight_low(1, lambda dy, start, size: a_one[dy, :, start : start + size], (1, 2))
    ready = pltpu.make_async_copy(
        grad_ref.at[pl.ds(layers[1][3], grad_ref.shape[0] - layers[1][3])],
        blocks_ref.at[pl.ds(layers[1][3], grad_ref.shape[0] - layers[1][3])],
        local_sem.at[0],
    )
    ready.start()
    finish_sum()
    gain_grad, shift_grad = back_low(5, z_one, inv_one, gain_one, shift_one)
    sums_ref[b, 0:1, :] = gain_grad
    sums_ref[b, 1:2, :] = shift_grad
    spread = Spread(
        all_send.at[3], all_recv.at[3], lambda other: sums_ref.at[b], lambda j: sums_ref.at[j]
    )
    spread.begin()
    widen_low(1)
    turned_low[...] = shifted_low[1].T
    weight_low(
        0, lambda dy, start, size: x_one[dy].reshape(px, C0)[:, start : start + size], (0, 1, 2)
    )
    last = pltpu.make_async_copy(
        grad_ref.at[pl.ds(0, layers[1][3])], blocks_ref.at[pl.ds(0, layers[1][3])], local_sem.at[1]
    )
    last.start()
    spread.finish()
    ready.wait()
    last.wait()


def run_step(master, place, bias, image, skip, labels, weight_map, valid, params):
    nr, nb = lax.axis_size("rows"), lax.axis_size("blk")
    cols = image.shape[0]
    px = nb * cols
    wide, slim = C1 // nb, C0 // nb
    vmem = pl.BlockSpec(memory_space=pltpu.VMEM)
    smem = pl.BlockSpec(memory_space=pltpu.SMEM)
    dma = pltpu.SemaphoreType.DMA
    scratch = [
        pltpu.VMEM((place.shape[0],) + master.shape[1:], bf16),
        dma((2,)),
        pltpu.VMEM((3, nb, cols, C0), bf16),
        pltpu.VMEM((4, 2, nb, cols, C0), bf16),
        pltpu.VMEM((nb, 2, 8, cols), f32),
        pltpu.VMEM((9 * wide, C0), bf16),
        pltpu.VMEM((9 * wide, C1), bf16),
        pltpu.VMEM((4 * slim, C1), bf16),
        pltpu.VMEM((9 * slim, 2 * C0), bf16),
        pltpu.VMEM((3, px, C1), bf16),
        pltpu.VMEM((px, C1), bf16),
        pltpu.VMEM((4, 2, px, C0), bf16),
        pltpu.VMEM((1, px, wide), f32),
        pltpu.VMEM((1, px, wide), f32),
        pltpu.VMEM((4, px, slim), f32),
        pltpu.VMEM((1, px, wide), f32),
        pltpu.VMEM((4, px, slim), f32),
        pltpu.VMEM((8, wide), f32),
        pltpu.VMEM((8, wide), f32),
        pltpu.VMEM((8, slim), f32),
        pltpu.VMEM((3, px, wide), bf16),
        pltpu.VMEM((4, 2, px, slim), bf16),
        pltpu.VMEM((3, px, 3 * wide), bf16),
        pltpu.VMEM((4, 2, px, 3 * slim), bf16),
        pltpu.VMEM((3 * wide, px), bf16),
        pltpu.VMEM((2, 3 * slim, 2 * px), bf16),
        pltpu.VMEM((px, 4 * slim), bf16),
        pltpu.VMEM((4, nb, px, slim), bf16),
        pltpu.VMEM((4, nb, px, slim), bf16),
        pltpu.VMEM((nb, px, wide), bf16),
        pltpu.VMEM((2, nb, px, wide), bf16),
        pltpu.VMEM((nb, 4, 2 * nb, cols), f32),
        pltpu.VMEM((4 * nb, 8, cols), f32),
        pltpu.VMEM((4, nr, 2 * nb + 8, wide), f32),
        pltpu.VMEM((2, nr, 2 * nb + 8, slim), f32),
        dma((3, nr, 2)),
        dma((nr, 2)),
        dma((6, nb, 2)),
        dma((6, nb)),
        dma((6, nb, 2)),
        dma((6, nb, 2)),
        dma((6, nr)),
        dma((6, nr)),
        dma((4, nb)),
        dma((4, nb)),
        dma((4, nb)),
        dma((4, nb)),
        dma((2, 2)),
        dma((2, 2)),
    ]
    return pl.pallas_call(
        functools.partial(step_kernel, nr, nb, cols),
        out_shape=(
            jax.ShapeDtypeStruct((place.shape[0],) + master.shape[1:], bf16),
            jax.ShapeDtypeStruct((nb, 16, wide), f32),
        ),
        in_specs=[vmem, smem, smem] + [vmem] * 6,
        out_specs=(pl.BlockSpec(memory_space=pl.ANY), vmem),
        scratch_shapes=scratch,
        compiler_params=pltpu.CompilerParams(
            collective_id=0, has_side_effects=True, vmem_limit_bytes=60 * 2**20
        ),
    )(master, place, bias, image, skip, labels, weight_map, valid, params)


LANES = 128


def inverse_factor_kernel(stat_ref, inverse_ref, factor_ref):
    order = stat_ref.shape[0]
    tile = (8, LANES)
    sub = lax.broadcasted_iota(jnp.int32, tile, 0)
    groups = order // 8

    def eliminate(source_ref, base, starts, first, count, accs):
        width = len(starts)

        def body(group, accs):
            top = pl.multiple_of(group * 8, 8)
            accs = [list(acc) for acc in accs]
            for unit in range(8):
                values = [source_ref[top + unit, pl.ds(start, 8), :] for start in starts]
                for c in range(8):
                    scale = jnp.broadcast_to(
                        factor_ref[top + unit, pl.ds(base + c, 1), :], tile
                    )
                    for s in range(width):
                        accs[s][c] = accs[s][c] - values[s] * scale
            return tuple(tuple(acc) for acc in accs)

        return lax.fori_loop(first, count, body, tuple(tuple(acc) for acc in accs))

    def batches(first, last, run):
        total = last - first

        def at(group):
            return pl.multiple_of(group * 8, 8)

        def two(n, _):
            run(first + 2 * n, [at(first + 2 * n), at(first + 2 * n + 1)])
            return 0

        lax.fori_loop(0, lax.div(total, 2), two, 0)

        @pl.when(lax.rem(total, 2) == 1)
        def _():
            run(last - 1, [at(last - 1)])

    def block(kb, _):
        base = pl.multiple_of(kb * 8, 8)
        accs = [stat_ref[base + c, pl.ds(base, 8), :] for c in range(8)]
        accs = list(eliminate(factor_ref, base, [base], 0, kb, [accs])[0])
        scale = []
        coef = {}
        for c in range(8):
            scale.append(jnp.broadcast_to(lax.rsqrt(accs[c][c : c + 1, :]), tile))
            accs[c] = accs[c] * scale[c]
            for d in range(c + 1, 8):
                coef[(c, d)] = jnp.broadcast_to(accs[c][d : d + 1, :], tile)
                accs[d] = accs[d] - accs[c] * coef[(c, d)]
        for c in range(8):
            factor_ref[base + c, pl.ds(base, 8), :] = jnp.where(sub >= c, accs[c], 0.0)

        def finish(accs, target_ref, start):
            accs = list(accs)
            for c in range(8):
                for e in range(c):
                    accs[c] = accs[c] - accs[e] * coef[(e, c)]
                accs[c] = accs[c] * scale[c]
                target_ref[base + c, pl.ds(start, 8), :] = accs[c]

        def below(group, starts):
            accs = [[stat_ref[base + c, pl.ds(s, 8), :] for c in range(8)] for s in starts]
            accs = eliminate(factor_ref, base, starts, 0, kb, accs)
            for acc, start in zip(accs, starts):
                finish(acc, factor_ref, start)

        def left(group, starts):
            accs = [[jnp.zeros(tile, jnp.float32) for c in range(8)] for s in starts]
            accs = eliminate(inverse_ref, base, starts, group, kb, accs)
            for acc, start in zip(accs, starts):
                finish(acc, inverse_ref, start)

        def clear(group, _):
            start = pl.multiple_of(group * 8, 8)
            for c in range(8):
                inverse_ref[base + c, pl.ds(start, 8), :] = jnp.zeros(tile, jnp.float32)
            return 0

        batches(kb + 1, groups, below)
        batches(0, kb, left)
        finish([jnp.where(sub == c, 1.0, 0.0) for c in range(8)], inverse_ref, base)
        lax.fori_loop(kb + 1, groups, clear, 0)
        return 0

    lax.fori_loop(0, groups, block, 0)


def split(value):
    high = value.astype(bf16)
    return high, (value - high.astype(f32)).astype(bf16)


def split_three(value):
    high = value.astype(bf16)
    rest = value - high.astype(f32)
    middle = rest.astype(bf16)
    return high, middle, (rest - middle.astype(f32)).astype(bf16)


def diagonal(pair):
    u, v = pair
    empty = jnp.zeros_like(u)
    return jnp.concatenate(
        [jnp.concatenate([u, empty], 1), jnp.concatenate([empty, v], 1)], 0
    )


def pair_product(packed, pair):
    a, b = split(packed)
    u, v = [split(value) for value in pair]
    c, d = diagonal((u[0], v[0])), diagonal((u[1], v[1]))
    result = dot_nn(jnp.concatenate([a, a, b], 1), jnp.concatenate([c, d, c], 0))
    order = packed.shape[1]
    return result[:, :order], result[:, order:]


def pair_cross(one, two):
    a, b = [jnp.concatenate(half, 1) for half in zip(*[split(value) for value in one])]
    c, d = [diagonal(half) for half in zip(*[split(value) for value in two])]
    return dot_nt(jnp.concatenate([a, a, b], 1), jnp.concatenate([c, d, c], 1))


def pair_square(pair):
    thirds = list(zip(*[split_three(value) for value in pair]))
    a, b, c = [jnp.concatenate(third, 1) for third in thirds]
    d, e, f = [diagonal(third) for third in thirds]
    return dot_nt(
        jnp.concatenate([a, a, b, a, b, c], 1), jnp.concatenate([d, e, d, f, e, d], 1)
    )


def product_three(left, right, right_dim):
    (a, b), (c, d) = left, right
    return lax.dot_general(
        jnp.concatenate([a, a, b], 1),
        jnp.concatenate([c, d, c], right_dim),
        (((1,), (right_dim,)), ((), ())),
        preferred_element_type=f32,
    )


def soap_blocks(indices, grads, ins, outs):
    def every(function, *lists):
        return [function(*items) for items in zip(*lists)]

    def load(ref):
        return [ref[index] for index in indices]

    def store(ref, values):
        for index, value in zip(indices, values):
            ref[index] = value

    master_ref, first_ref, second_ref, left_ref, right_ref, left_stat_ref, right_stat_ref = ins
    left = load(left_ref)
    sides, bases = every(split, grads), every(split, load(right_ref))
    lefts, turned = every(split, left), every(lambda grad: split(grad.T), grads)

    def three(dim):
        return lambda one, two: product_three(one, two, dim)

    lefts_turned = every(lambda value: split(value.T), left)
    half = every(three(0), lefts_turned, sides)
    left_outer = every(three(1), sides, sides)
    rotated = every(three(0), every(split, half), bases)
    right_outer = every(three(1), turned, turned)
    first = every(
        lambda old, new: beta_one * old + (1.0 - beta_one) * new, load(first_ref), rotated
    )
    second = every(
        lambda old, new: beta_two * old + (1.0 - beta_two) * new * new, load(second_ref), rotated
    )
    store(outs[2], first)
    store(outs[3], second)
    direction = every(
        lambda one, two: one
        * (1.0 / (1.0 - beta_one**STEP))
        / (jnp.sqrt(two * (1.0 / (1.0 - beta_two**STEP))) + adam_eps),
        first,
        second,
    )
    half = every(three(0), lefts, every(split, direction))
    stats = []
    for ref, target, outer in (
        (left_stat_ref, outs[4], left_outer),
        (right_stat_ref, outs[5], right_outer),
    ):
        stat = every(
            lambda old, new: beta_stat * old + (1.0 - beta_stat) * new, load(ref), outer
        )
        store(target, stat)
        stats.append(every(split, stat))
    moved = every(three(0), lefts_turned, stats[0])
    update = every(three(1), every(split, half), bases)
    moved_right = every(
        lambda stat, basis: product_three(stat, basis, 0).T, stats[1], bases
    )
    master = every(
        lambda old, new: old - soap_rate * (new + soap_decay * old), load(master_ref), update
    )
    store(outs[0], master)
    store(outs[1], every(lambda value: value.astype(bf16), master))
    store(outs[6], moved)
    store(outs[7], moved_right)
    middle = moved[0].shape[0] // 2
    store(
        outs[8],
        every(lambda one, two: pair_square((one[:middle], two[:middle])), moved, moved_right),
    )


def collect_kernel(nr, size, *refs):
    (owner_ref, blocks_ref), refs = refs[:2], refs[2:]
    ins, refs = refs[:7], refs[7:]
    outs, refs = refs[:9], refs[9:]
    (
        out_a,
        in_a,
        out_b,
        in_b,
        total,
        in_buffer,
        out_buffer,
        copy_buffer,
        gram_buffer,
        grad_ref,
        local_sem,
        a_send,
        a_recv,
        b_send,
        b_recv,
        in_sem,
        out_sem,
    ) = refs
    r = lax.axis_index("rows")
    b = lax.axis_index("blk")
    core = lax.rem(r, 2)
    chip = lax.div(r, 2)
    chips = nr // 2
    mate = r + 1 - 2 * core
    count = ins[0].shape[0]
    chunks = count // size
    square = in_square(chips, size)
    half = size // 2

    def device(chip, core):
        return {"rows": 2 * chip + core, "blk": b}

    stage = pltpu.make_async_copy(blocks_ref, grad_ref, local_sem)
    stage.start()
    barrier = pltpu.get_barrier_semaphore()
    pl.semaphore_signal(
        barrier, inc=1, device_id={"rows": mate, "blk": b}, device_id_type=MESH
    )

    def greet(step, _):
        pl.semaphore_signal(
            barrier,
            inc=1,
            device_id=device(lax.rem(chip + step, chips), core),
            device_id_type=MESH,
        )
        return 0

    lax.fori_loop(1, chips, greet, 0)

    def loads(chunk):
        return [
            pltpu.make_async_copy(
                ref.at[pl.ds(chunk * size, size)],
                in_buffer.at[chunk % 2, number],
                in_sem.at[chunk % 2, number],
            )
            for number, ref in enumerate(ins)
        ]

    def stores(chunk):
        copies = []
        for number, ref in enumerate(outs):
            if number in (1, 8):
                source = {1: copy_buffer, 8: gram_buffer}[number].at[chunk % 2]
            else:
                source = out_buffer.at[chunk % 2, number - (number > 1)]
            copies.append(
                pltpu.make_async_copy(
                    source, ref.at[pl.ds(chunk * size, size)], out_sem.at[chunk % 2, number]
                )
            )
        return copies

    def mine(to_chip, to_core, chunk, index):
        return grad_ref[owner_ref[(2 * to_chip + to_core) * count + chunk * size + index]]

    def joined(to_chip, chunk, index):
        value = mine(to_chip, core, chunk, index).astype(f32)
        return value + in_a[chunk, to_chip, index].astype(f32)

    def send_a(chunk):
        return pltpu.make_async_remote_copy(
            src_ref=out_a.at[chunk],
            dst_ref=in_a.at[chunk],
            send_sem=a_send.at[chunk],
            recv_sem=a_recv.at[chunk],
            device_id={"rows": mate, "blk": b},
            device_id_type=MESH,
        )

    def fill_a(chunk):
        def fill(n, _):
            to_chip, index = lax.div(n, size), lax.rem(n, size)
            out_a[chunk, to_chip, index] = mine(to_chip, 1 - core, chunk, index)
            return 0

        lax.fori_loop(0, chips * size, fill, 0)
        send_a(chunk).start()

    class Straight:
        def copy(self, chunk, step, source):
            other = lax.rem(chip + step, chips)
            return pltpu.make_async_remote_copy(
                src_ref=out_b.at[chunk, other],
                dst_ref=in_b.at[chunk, source],
                send_sem=b_send.at[chunk, step],
                recv_sem=b_recv.at[chunk, source],
                device_id=device(other, core),
                device_id_type=MESH,
            )

        def first(self, chunk):
            def join(step, _):
                other = lax.rem(chip + step, chips)

                def each(index, _):
                    out_b[chunk, other, index] = joined(other, chunk, index).astype(bf16)
                    return 0

                lax.fori_loop(0, size, each, 0)
                self.copy(chunk, step, chip).start()
                return 0

            lax.fori_loop(1, chips, join, 0)

        def second(self, chunk):
            pass

        def arrive(self, chunk):
            def wait(step, _):
                self.copy(chunk, step, lax.rem(chip + step, chips)).wait_recv()
                return 0

            lax.fori_loop(1, chips, wait, 0)

        def grad(self, chunk, index):
            return lax.fori_loop(
                1,
                chips,
                lambda step, value: value
                + in_b[chunk, lax.rem(chip + step, chips), index].astype(f32),
                total[chunk, index],
            )

        def close(self, chunk):
            def wait(step, _):
                self.copy(chunk, step, chip).wait_send()
                return 0

            lax.fori_loop(1, chips, wait, 0)

    class Square:
        def __init__(self):
            self.x = chip + 1 - 2 * lax.rem(chip, 2)
            self.y = chip + 2 - 4 * lax.div(chip, 2)
            self.corner = 3 - chip

        def one(self, chunk, way):
            return pltpu.make_async_remote_copy(
                src_ref=out_b.at[chunk, pl.ds(2 * way, 2)],
                dst_ref=in_b.at[chunk, pl.ds(2 * way, 2)],
                send_sem=b_send.at[chunk, way],
                recv_sem=b_recv.at[chunk, way],
                device_id=device((self.x, self.y)[way], core),
                device_id_type=MESH,
            )

        def two(self, chunk, way):
            return pltpu.make_async_remote_copy(
                src_ref=out_b.at[chunk, 4 + way],
                dst_ref=in_b.at[chunk, 4 + way],
                send_sem=b_send.at[chunk, 2 + way],
                recv_sem=b_recv.at[chunk, 2 + way],
                device_id=device((self.y, self.x)[way], core),
                device_id_type=MESH,
            )

        def first(self, chunk):
            for way, near in enumerate((self.x, self.y)):

                def each(index, _, way=way, near=near):
                    slot = way * half + index
                    out_b[chunk, 2 * way, index] = joined(near, chunk, slot).astype(bf16)
                    value = joined(self.corner, chunk, slot)
                    out_b[chunk, 2 * way + 1, index] = value.astype(bf16)
                    return 0

                lax.fori_loop(0, half, each, 0)
                self.one(chunk, way).start()

        def second(self, chunk):
            for way, far in enumerate((self.y, self.x)):
                self.one(chunk, way).wait_recv()

                def each(index, _, way=way, far=far):
                    value = joined(far, chunk, way * half + index)
                    value = value + in_b[chunk, 2 * way + 1, index].astype(f32)
                    out_b[chunk, 4 + way, index] = value.astype(bf16)
                    return 0

                lax.fori_loop(0, half, each, 0)
                self.two(chunk, way).start()

        def arrive(self, chunk):
            for way in range(2):
                self.two(chunk, way).wait_recv()

        def grad(self, chunk, index):
            way, place = index // half, index % half
            value = total[chunk, index] + in_b[chunk, 2 * way, place].astype(f32)
            return value + in_b[chunk, 4 + way, place].astype(f32)

        def close(self, chunk):
            for way in range(2):
                self.one(chunk, way).wait_send()
                self.two(chunk, way).wait_send()

    plan = Square() if square else Straight()

    def keep(chunk):
        def each(index, _):
            total[chunk, index] = joined(chip, chunk, index)
            return 0

        lax.fori_loop(0, size, each, 0)

    def work(chunk):
        plan.arrive(chunk)
        for copy in loads(chunk):
            copy.wait()
        if chunk >= 2:
            for copy in stores(chunk - 2):
                copy.wait()
        slot = chunk % 2
        chunk_ins = [in_buffer.at[slot, number] for number in range(7)]
        chunk_outs = [out_buffer.at[slot, number] for number in range(7)]
        chunk_outs.insert(1, copy_buffer.at[slot])
        chunk_outs.append(gram_buffer.at[slot])
        grads = [plan.grad(chunk, index) for index in range(size)]
        soap_blocks(range(size), grads, chunk_ins, chunk_outs)
        for copy in stores(chunk):
            copy.start()
        if chunk + 2 < chunks:
            for copy in loads(chunk + 2):
                copy.start()

    for chunk in range(min(2, chunks)):
        for copy in loads(chunk):
            copy.start()
    pl.semaphore_wait(barrier, chips)
    stage.wait()
    for chunk in range(chunks):
        fill_a(chunk)
    for chunk in range(chunks + 2):
        if chunk < chunks:
            send_a(chunk).wait_recv()
            plan.first(chunk)
            keep(chunk)
        if 1 <= chunk <= chunks:
            plan.second(chunk - 1)
        if chunk >= 2:
            work(chunk - 2)
    for chunk in range(chunks):
        send_a(chunk).wait_send()
        plan.close(chunk)
        if chunk >= chunks - 2:
            for copy in stores(chunk):
                copy.wait()


def in_square(chips, size):
    return chips == 4 and size % 2 == 0


def soap_update(blocks, owner, states):
    nr = lax.axis_size("rows")
    count, order = states[0].shape[0], states[0].shape[-1]
    size = 8 if count % 8 == 0 else count
    chunks = count // size
    anywhere = pl.BlockSpec(memory_space=pl.ANY)
    vmem = pl.BlockSpec(memory_space=pltpu.VMEM)
    shape = jax.ShapeDtypeStruct(states[0].shape, f32)
    dma = pltpu.SemaphoreType.DMA
    square = (order, order)
    chips = nr // 2
    parts = (6, size // 2) if in_square(chips, size) else (chips, size)
    results = pl.pallas_call(
        functools.partial(collect_kernel, nr, size),
        out_shape=(shape, jax.ShapeDtypeStruct(shape.shape, bf16)) + (shape,) * 6
        + (jax.ShapeDtypeStruct((count, order // 2, order), f32),),
        in_specs=[pl.BlockSpec(memory_space=pltpu.SMEM)] + [anywhere] * 8,
        out_specs=[anywhere] * 9,
        scratch_shapes=[
            pltpu.VMEM((chunks, chips, size) + square, bf16),
            pltpu.VMEM((chunks, chips, size) + square, bf16),
            pltpu.VMEM((chunks,) + parts + square, bf16),
            pltpu.VMEM((chunks,) + parts + square, bf16),
            pltpu.VMEM((chunks, size) + square, f32),
            pltpu.VMEM((2, 7, size) + square, f32),
            pltpu.VMEM((2, 7, size) + square, f32),
            pltpu.VMEM((2, size) + square, bf16),
            pltpu.VMEM((2, size, order // 2, order), f32),
            pltpu.VMEM(blocks.shape, bf16),
            dma(()),
            dma((chunks,)),
            dma((chunks,)),
            dma((chunks, chips)),
            dma((chunks, chips)),
            dma((2, 7)),
            dma((2, 9)),
        ],
        compiler_params=pltpu.CompilerParams(
            collective_id=1, has_side_effects=True, vmem_limit_bytes=60 * 2**20
        ),
    )(owner, blocks, *states)
    kept = list(results[:6])
    new_left, new_right, *kept = new_bases(results[6:8], results[8], kept)
    new_master, new_copy, new_first, new_second, new_left_stat, new_right_stat = kept
    return [
        new_master,
        new_copy,
        new_first,
        new_second,
        new_left,
        new_right,
        new_left_stat,
        new_right_stat,
    ]


def basis_kernel(gram_ref, left_ref, right_ref, *refs):
    number = (len(refs) - 9) // 3
    kept, new_left_ref, new_right_ref = refs[:number], refs[number], refs[number + 1]
    moved, refs = refs[number + 2 : 2 * number + 2], refs[2 * number + 2 :]
    stat_ref, inverse_ref, factor_ref, solve_ref, rest_ref, in_sem, out_sem, *halts = refs
    arriving = [
        pltpu.make_async_copy(source, halt, in_sem.at[n])
        for n, (source, halt) in enumerate(zip(kept, halts))
    ]
    leaving = [
        pltpu.make_async_copy(halt, target, out_sem.at[n])
        for n, (halt, target) in enumerate(zip(halts, moved))
    ]
    for copy in arriving:
        copy.start()
    count, order = left_ref.shape[0], left_ref.shape[1]
    half = order // 2
    width = next(size for size in (8, 5, 4, 2, 1) if count % size == 0)
    column = lax.broadcasted_iota(jnp.int32, (half, order), 1)

    def invert(source_ref):
        def enter(row, _):
            value = source_ref[pl.ds(row, count, stride=half), :]
            if count < half:
                spare = column[: half - count]
                spare = (spare == row) | (spare == row + half)
                value = jnp.concatenate([value, jnp.where(spare, 1.0, 0.0)], 0)
            value = jnp.concatenate([value, pltpu.roll(value, half, 1)], 0)
            stat_ref[row] = value.T[:half]
            return 0

        lax.fori_loop(0, half, enter, 0, unroll=8)
        inverse_factor_kernel(stat_ref, inverse_ref, factor_ref)

        def leave(row, _):
            value = inverse_ref[row]
            value = jnp.concatenate([value, value], 0).T
            solve_ref[pl.ds(row, count, stride=half), :] = jnp.where(
                column[:count] < half, value[:count], value[half : half + count]
            )
            return 0

        lax.fori_loop(0, half, leave, 0, unroll=8)

    def rows(index):
        return pl.ds(pl.multiple_of(index * half, half), half)

    def project(step, _):
        blocks = [step * width + n for n in range(width)]
        first = [(left_ref[n, :half], right_ref[n, :half]) for n in blocks]
        second = [(left_ref[n, half:], right_ref[n, half:]) for n in blocks]
        first = [pair_product(solve_ref[rows(n), :], pair) for n, pair in zip(blocks, first)]
        cross = [pair_cross(one, two) for one, two in zip(second, first)]
        shares = [pair_product(value, pair) for value, pair in zip(cross, first)]
        second = [
            (pair[0] - share[0], pair[1] - share[1]) for pair, share in zip(second, shares)
        ]
        squares = [pair_square(pair) for pair in second]
        for n, one, two, value in zip(blocks, first, second, squares):
            for side, ref in enumerate((new_left_ref, new_right_ref)):
                ref[n, :half] = one[side]
                ref[n, half:] = two[side]
            rest_ref[rows(n), :] = value
        return 0

    def complete(step, _):
        blocks = [step * width + n for n in range(width)]
        refs = (new_left_ref, new_right_ref)
        second = [
            pair_product(solve_ref[rows(n), :], [ref[n, half:] for ref in refs]) for n in blocks
        ]
        for n, pair in zip(blocks, second):
            for ref, value in zip(refs, pair):
                ref[n] = jnp.concatenate([ref[n, :half], value], 0).T
        return 0

    invert(gram_ref)
    for come, go in zip(arriving, leaving):
        come.wait()
        go.start()
    lax.fori_loop(0, count // width, project, 0)
    invert(rest_ref)
    lax.fori_loop(0, count // width, complete, 0)
    for copy in leaving:
        copy.wait()


def new_bases(products, grams, kept):
    count, order = products[0].shape[0], products[0].shape[-1]
    half = order // 2
    vmem = pl.BlockSpec(memory_space=pltpu.VMEM)
    anywhere = pl.BlockSpec(memory_space=pl.ANY)
    lanes = pltpu.VMEM((half, half, LANES), f32)
    flat = pltpu.VMEM((count * half, order), f32)
    return pl.pallas_call(
        basis_kernel,
        out_shape=[
            jax.ShapeDtypeStruct(value.shape, value.dtype) for value in list(products) + kept
        ],
        in_specs=[vmem] * 3 + [anywhere] * len(kept),
        out_specs=[vmem] * 2 + [anywhere] * len(kept),
        scratch_shapes=[lanes, lanes, lanes, flat, flat]
        + [pltpu.SemaphoreType.DMA((len(kept),))] * 2
        + [pltpu.VMEM(value.shape, value.dtype) for value in kept],
        compiler_params=pltpu.CompilerParams(vmem_limit_bytes=60 * 2**20),
    )(grams.reshape(count * half, order), *products, *kept)


def adam_small(grads, value, first, second):
    first_new = beta_one * first + (1.0 - beta_one) * grads
    second_new = beta_two * second + (1.0 - beta_two) * grads * grads
    direction = (
        first_new
        / (1.0 - beta_one**STEP)
        / (jnp.sqrt(second_new / (1.0 - beta_two**STEP)) + adam_eps)
    )
    return (first_new, second_new, value - small_rate * (direction + small_decay * value))


def local(
    image,
    skip,
    labels,
    weight_map,
    valid,
    owner,
    master,
    first_moment,
    second_moment,
    left_basis,
    right_basis,
    left_stat,
    right_stat,
    norm_params,
    norm_first,
    norm_second,
    head_bias,
    bias_first,
    bias_second,
):
    shards = lax.axis_size("blk")
    slots = jnp.arange(owner.shape[0])
    place = jnp.sum(jnp.where(owner[None, :] == slots[:, None], slots[None, :], 0), 1)
    part = C0 // shards
    blocks, sums = run_step(
        master[0],
        place.astype(jnp.int32),
        head_bias,
        image[0, 0],
        skip[0],
        labels[0],
        weight_map[0],
        valid[0],
        norm_params.reshape(-1, TILE),
    )
    loss_sum, valid_count = sums[0, 6, 0], sums[0, 9, 0]
    grad_bias = sums[0, 7:9, 0]
    grad_head = jnp.stack([sums[:, 5, :part].reshape(-1), sums[:, 5, part : 2 * part].reshape(-1)], 1)
    small = jnp.concatenate(
        [sums[:, row].reshape(-1) for row in range(4)]
        + [
            sums[:, 4, :part].reshape(-1),
            sums[:, 4, part : 2 * part].reshape(-1),
            grad_head.reshape(-1),
        ]
    )
    states = (
        master,
        first_moment,
        second_moment,
        left_basis,
        right_basis,
        left_stat,
        right_stat,
    )
    soap = soap_update(blocks, owner, [state[0] for state in states])
    soap = [value[None] for value in soap]
    norm_new = adam_small(small, norm_params, norm_first, norm_second)
    bias_new = adam_small(grad_bias, head_bias, bias_first, bias_second)
    return (
        loss_sum,
        valid_count,
        soap[0],
        soap[1],
        soap[2],
        soap[3],
        soap[4],
        soap[5],
        soap[6],
        soap[7],
        norm_new[0],
        norm_new[1],
        norm_new[2],
        bias_new[0],
        bias_new[1],
        bias_new[2],
    )


def solution(mesh):
    placed = (
        P("blk", "rows", None, None),
        P("blk", "rows", None, None),
        P("blk", "rows", None),
        P("blk", "rows", None),
        P("blk", "rows", None),
        P(),
        P("blk", "rows", None, None),
        P("blk", "rows", None, None),
        P("blk", "rows", None, None),
        P("blk", "rows", None, None),
        P("blk", "rows", None, None),
        P("blk", "rows", None, None),
        P("blk", "rows", None, None),
        P(),
        P(),
        P(),
        P(),
        P(),
        P(),
    )
    return jax.shard_map(
        local,
        mesh=mesh,
        in_specs=placed,
        out_specs=(
            P(),
            P(),
            P("blk", "rows", None, None),
            P("blk", "rows", None, None),
            P("blk", "rows", None, None),
            P("blk", "rows", None, None),
            P("blk", "rows", None, None),
            P("blk", "rows", None, None),
            P("blk", "rows", None, None),
            P("blk", "rows", None, None),
            P(),
            P(),
            P(),
            P(),
            P(),
            P(),
        ),
        check_vma=False,
    )
```

```python
import functools

import jax
import jax.numpy as jnp
from jax import lax
from jax.experimental import pallas as pl
from jax.experimental.pallas import tpu as pltpu
from jax.sharding import PartitionSpec as P

C0 = 512
C1 = 1024
GROUPS = 32
STEP = 10


beta_one = 0.9
beta_two = 0.999
beta_stat = 0.95
adam_eps = 1e-08
norm_eps = 1e-05
soap_rate = 0.008
soap_decay = 0.01
small_rate = 0.4
small_decay = 0.01
highest = lax.Precision.HIGHEST


MESH = pl.DeviceIdType.MESH
bf16 = jnp.bfloat16
f32 = jnp.float32
TILE = 128


def dot_nt(left, right):
    return lax.dot_general(left, right, (((1,), (1,)), ((), ())), preferred_element_type=f32)


def dot_nn(left, right):
    return jnp.dot(left, right, preferred_element_type=f32)


def sigmoid(value):
    return 1.0 / (1.0 + jnp.exp(-value))


def block_layers(nb):
    result = []
    first = 0
    for in_width, out_width, taps in ((C0, C1, 9), (C1, C1, 9), (C1, C0, 4), (2 * C0, C0, 9)):
        out = out_width // nb
        result.append((out, in_width, taps, first))
        first = first + out // TILE * taps * (in_width // TILE)
    return result


def step_kernel(
    nr,
    nb,
    cols,
    master_ref,
    place_ref,
    bias_ref,
    image_ref,
    skip_ref,
    labels_ref,
    map_ref,
    valid_ref,
    params_ref,
    blocks_ref,
    sums_ref,
    grad_ref,
    local_sem,
    x_one,
    x_skip,
    x_lab,
    w_one,
    w_two,
    w_up,
    w_three,
    a_one,
    a_two,
    u_full,
    z_one,
    z_two,
    z_three,
    dy_low,
    dy_high,
    inv_one,
    inv_two,
    inv_three,
    dz_low,
    dz_high,
    shifted_low,
    shifted_high,
    turned_low,
    turned_high,
    dub,
    send_high,
    recv_high,
    send_low,
    recv_low,
    logit,
    grad_logit,
    reduce_wide,
    reduce_narrow,
    gather_send,
    gather_recv,
    line_send,
    line_recv,
    halo_send,
    halo_recv,
    red_send,
    red_recv,
    all_send,
    all_recv,
    high_send,
    high_recv,
    edge_send,
    edge_recv,
):
    r = lax.axis_index("rows")
    b = lax.axis_index("blk")
    px = nb * cols
    wide = C1 // nb
    slim = C0 // nb
    taps_high = 3 * slim
    layers = block_layers(nb)

    def remote(src, dst, send, recv, rows, blk):
        return pltpu.make_async_remote_copy(
            src_ref=src,
            dst_ref=dst,
            send_sem=send,
            recv_sem=recv,
            device_id={"rows": rows, "blk": blk},
            device_id_type=MESH,
        )

    def lanes(index, size):
        return pl.ds(pl.multiple_of(index * size, TILE), size)

    def ring(index, count):
        return lax.rem(index + count, count)

    barrier = pltpu.get_barrier_semaphore()

    def greet_rows(step, _):
        pl.semaphore_signal(
            barrier, inc=1, device_id={"rows": ring(r + step, nr), "blk": b}, device_id_type=MESH
        )
        return 0

    lax.fori_loop(1, nr, greet_rows, 0)
    for step in range(1, nb):
        pl.semaphore_signal(
            barrier, inc=1, device_id={"rows": r, "blk": ring(b + step, nb)}, device_id_type=MESH
        )
    pl.semaphore_wait(barrier, nr - 1 + nb - 1)

    class Exchange:
        def __init__(self, number, piece, up=None, down=None):
            self.number, self.piece, self.up, self.down = number, piece, up, down

        def right(self, j):
            return remote(
                self.piece(j),
                self.piece(j),
                line_send.at[self.number, j, 0],
                line_recv.at[self.number, j],
                r,
                ring(b + 1, nb),
            )

        def left(self, j):
            return remote(
                self.piece(j),
                self.piece(j),
                line_send.at[self.number, j, 1],
                line_recv.at[self.number, j],
                r,
                ring(b - 1, nb),
            )

        def higher(self, j):
            src, dst = self.up(j)
            return remote(
                src,
                dst,
                halo_send.at[self.number, j, 0],
                halo_recv.at[self.number, j, 0],
                ring(r + 1, nr),
                b,
            )

        def lower(self, j):
            src, dst = self.down(j)
            return remote(
                src,
                dst,
                halo_send.at[self.number, j, 1],
                halo_recv.at[self.number, j, 1],
                ring(r - 1, nr),
                b,
            )

        def halos(self, j):
            if self.up is None:
                return

            @pl.when(r + 1 < nr)
            def _():
                self.higher(j).start()

            @pl.when(r > 0)
            def _():
                self.lower(j).start()

        def begin(self):
            @pl.when(b + 1 < nb)
            def _():
                self.right(b).start()

            @pl.when(b > 0)
            def _():
                self.left(b).start()

            self.halos(b)

        def hop(self, k):
            @pl.when(b >= k)
            def _():
                self.right(b - k).wait_recv()

                @pl.when(b + 1 < nb)
                def _():
                    self.right(b - k).start()

                self.halos(b - k)

            @pl.when(b + k < nb)
            def _():
                self.left(b + k).wait_recv()

                @pl.when(b > 0)
                def _():
                    self.left(b + k).start()

                self.halos(b + k)

        def hops(self):
            for k in range(1, nb):
                self.hop(k)

        def finish(self):
            for k in range(nb):

                @pl.when((b >= k) & (b + 1 < nb))
                def _():
                    self.right(b - k).wait_send()

                @pl.when((b + k < nb) & (b > 0))
                def _():
                    self.left(b + k).wait_send()

            if self.up is None:
                return
            for j in range(nb):

                @pl.when(r + 1 < nr)
                def _():
                    self.higher(j).wait_send()
                    self.lower(j).wait_recv()

                @pl.when(r > 0)
                def _():
                    self.lower(j).wait_send()
                    self.higher(j).wait_recv()

    def reduce_start(number, buffer):
        def start(step, _):
            remote(
                buffer.at[r],
                buffer.at[r],
                red_send.at[number, step],
                red_recv.at[number, r],
                ring(r + step, nr),
                b,
            ).start()
            return 0

        lax.fori_loop(1, nr, start, 0, unroll=nr <= 8)

    def reduce_finish(number, buffer):
        def wait(step, _):
            source = ring(r + step, nr)
            copy = remote(
                buffer.at[source],
                buffer.at[source],
                red_send.at[number, step],
                red_recv.at[number, source],
                source,
                b,
            )
            copy.wait_recv()
            copy.wait_send()
            return 0

        lax.fori_loop(1, nr, wait, 0, unroll=nr <= 8)
        return lax.fori_loop(
            1, nr, lambda k, total: total + buffer[k], buffer[0], unroll=nr <= 8
        )

    def all_reduce(number, buffer):
        reduce_start(number, buffer)
        return reduce_finish(number, buffer)

    class Spread:
        def __init__(self, send, recv, source, target):
            self.send, self.recv, self.source, self.target = send, recv, source, target

        def copy(self, step):
            other = ring(b + step, nb)
            return remote(
                self.source(other),
                self.target(b),
                self.send.at[step],
                self.recv.at[b],
                r,
                other,
            )

        def begin(self):
            for step in range(1, nb):
                self.copy(step).start()

        def finish(self):
            for step in range(1, nb):
                other = ring(b + step, nb)
                remote(
                    self.source(other),
                    self.target(other),
                    self.send.at[step],
                    self.recv.at[other],
                    r,
                    other,
                ).wait_recv()
                self.copy(step).wait_send()

    class Gather:
        def __init__(self):
            self.size = master_ref.shape[0]
            self.chips = nr // 2
            self.core = lax.rem(r, 2)
            self.chip = lax.div(r, 2)
            self.mate = r + 1 - 2 * self.core
            self.square = self.chips == 4 and self.size % 2 == 0
            self.halves = 2 if self.square else 1

        def piece(self, row, half):
            part = self.size // self.halves
            return grad_ref.at[pl.ds(row * self.size + half * part, part)]

        def move(self, kind, target, row, half):
            return remote(
                self.piece(row, half),
                self.piece(row, half),
                gather_send.at[kind, row, half],
                gather_recv.at[row, half],
                target,
                b,
            )

        def direct(self, target):
            return remote(
                self.piece(r, 0),
                self.piece(r, 0),
                gather_send.at[0, target, 0],
                gather_recv.at[r, 0],
                target,
                b,
            )

        def beside(self, step):
            return 2 * lax.rem(self.chip + step, self.chips) + self.core

        def other(self, bit):
            away = self.chip + bit - 2 * bit * lax.rem(lax.div(self.chip, bit), 2)
            return 2 * away + self.core

        def begin(self):
            def cast(index, _):
                grad_ref[r * self.size + index] = master_ref[index].astype(bf16)
                return 0

            lax.fori_loop(0, self.size, cast, 0)
            if self.square:
                for half in range(2):
                    self.move(2, self.mate, r, half).start()
                    self.move(0, self.other(1), r, 1 - half).start()
                    self.move(1, self.other(2), r, half).start()
            else:
                self.move(2, self.mate, r, 0).start()

                def send(step, _):
                    self.direct(self.beside(step)).start()
                    return 0

                lax.fori_loop(1, self.chips, send, 0)

        def arrived(self, row, half):
            self.move(2, self.mate, row, half).wait_recv()

        def hand(self, row, half):
            self.arrived(row, half)
            self.move(2, self.mate, row, half).start()

        def forward(self, moves):
            image, lab, skip = moves
            for k in range(1, nb):
                image.hop(k)
                lab.hop(k)
            if self.square:
                x, y = self.other(1), self.other(2)
                corner = 2 * (3 - self.chip) + self.core
                self.hand(y, 0)
                self.move(0, x, y, 0).start()
                self.hand(x, 1)
                self.move(1, y, x, 1).start()
                skip.hop(1)
                self.hand(x, 0)
                self.hand(y, 1)
                self.hand(corner, 0)
                self.hand(corner, 1)
                rows = (r, x, y, corner)
                for half in range(2):
                    for row in rows:
                        self.arrived(row + 1 - 2 * self.core, half)
                for half in range(2):
                    for row in rows:
                        self.move(2, self.mate, row, half).wait_send()
                    self.move(0, x, r, half).wait_send()
                    self.move(1, y, r, half).wait_send()
                self.move(0, x, y, 0).wait_send()
                self.move(1, y, x, 1).wait_send()
            else:

                def pass_on(step, _):
                    self.hand(self.beside(step), 0)
                    return 0

                def close(step, _):
                    row = self.beside(step)
                    self.arrived(row + 1 - 2 * self.core, 0)
                    self.move(2, self.mate, row, 0).wait_send()
                    self.direct(row).wait_send()
                    return 0

                lax.fori_loop(1, self.chips, pass_on, 0)
                skip.hop(1)
                self.arrived(self.mate, 0)
                self.move(2, self.mate, r, 0).wait_send()
                lax.fori_loop(1, self.chips, close, 0)

    position = lax.rem(lax.broadcasted_iota(jnp.int32, (px, TILE), 0), cols)

    def mask_of(value, column):
        hit = position[:, :1] == column
        return jnp.where(hit, 0.0, value)

    def shift_down(value):
        return mask_of(pltpu.roll(value, 1, 0), 0)

    def shift_up(value):
        return mask_of(pltpu.roll(value, px - 1, 0), cols - 1)

    def group_sum(value, size):
        width = value.shape[-1]
        bits = size.bit_length() - 1
        first = lax.shift_right_logical(lax.broadcasted_iota(jnp.int32, (width, width), 0), bits)
        second = lax.shift_right_logical(lax.broadcasted_iota(jnp.int32, (width, width), 1), bits)
        same = jnp.where(first == second, 1.0, 0.0).astype(f32)
        return jnp.dot(value, same, preferred_element_type=f32, precision=highest)

    def rows_of(image):
        return pl.ds(image * cols, cols)

    def norm_sums(buffer, z_ref):
        for image in range(nb):
            first = 0.0
            second = 0.0
            for part in range(z_ref.shape[0]):
                value = z_ref[part, rows_of(image), :]
                first = first + jnp.sum(value, 0, keepdims=True)
                second = second + jnp.sum(value * value, 0, keepdims=True)
            buffer[r, image : image + 1, :] = first
            buffer[r, nb + image : nb + image + 1, :] = second

    def norm_apply(total, z_ref, inv_ref, gain, shift, size, put):
        width = z_ref.shape[-1]
        number = nr * cols * z_ref.shape[0] * size
        sums = group_sum(total[: 2 * nb], size) / number
        mean = sums[:nb]
        inv = lax.rsqrt(sums[nb:] - mean * mean + norm_eps)
        inv_ref[:nb, :] = inv
        for part in range(z_ref.shape[0]):
            for image in range(nb):
                value = z_ref[part, rows_of(image), :]
                value = (value - mean[image : image + 1]) * inv[image : image + 1]
                z_ref[part, rows_of(image), :] = value
                normed = value * gain + shift
                put(part, image, (normed * sigmoid(normed)).astype(bf16))

    def back_sums(buffer, z_ref, dy_ref, gain, shift, grad_of):
        for image in range(nb):
            first = 0.0
            second = 0.0
            for part in range(z_ref.shape[0]):
                value = z_ref[part, rows_of(image), :]
                normed = value * gain + shift
                gate = sigmoid(normed)
                grad = grad_of(part, image) * gate * (1.0 + normed * (1.0 - gate))
                dy_ref[part, rows_of(image), :] = grad
                first = first + jnp.sum(grad, 0, keepdims=True)
                second = second + jnp.sum(grad * value, 0, keepdims=True)
            buffer[r, image : image + 1, :] = first
            buffer[r, nb + image : nb + image + 1, :] = second

    def back_apply(total, z_ref, dy_ref, inv_ref, gain, size, put):
        number = nr * cols * z_ref.shape[0] * size
        sums = group_sum(total[: 2 * nb] * gain, size) / number
        inv = inv_ref[:nb, :]
        for part in range(z_ref.shape[0]):
            for image in range(nb):
                one = slice(image, image + 1)
                two = slice(nb + image, nb + image + 1)
                value = dy_ref[part, rows_of(image), :] * gain - sums[one]
                value = value - z_ref[part, rows_of(image), :] * sums[two]
                put(part, image, (value * inv[one]).astype(bf16))
        shift_grad = jnp.sum(total[:nb], 0, keepdims=True)
        gain_grad = jnp.sum(total[nb : 2 * nb], 0, keepdims=True)
        return gain_grad, shift_grad

    gather = Gather()
    gather.begin()
    x_one[1, b] = image_ref[...]

    def pick(shape, dim, stride, start):
        index = lax.broadcasted_iota(jnp.int32, shape, dim)
        target = stride * lax.broadcasted_iota(jnp.int32, shape, 1 - dim) + start
        return jnp.where(index == target, 1.0, 0.0).astype(bf16)

    values = [ref[...].astype(f32) for ref in (labels_ref, map_ref, valid_ref)]
    values = jnp.concatenate(values + [jnp.zeros_like(values[0])], 0).astype(bf16)
    for f in range(2):
        x_lab[b, f] = dot_nn(values, pick((2 * cols, cols), 0, 2, f))
        for e in range(2):
            value = dot_nn(pick((cols, 2 * cols), 1, 2, f), skip_ref[e])
            x_skip[1 + e, f, b] = value.astype(bf16)
    move_image = Exchange(
        0,
        lambda j: x_one.at[1, j],
        lambda j: (x_one.at[1, j], x_one.at[0, j]),
        lambda j: (x_one.at[1, j], x_one.at[2, j]),
    )
    move_skip = Exchange(
        1,
        lambda j: x_skip.at[pl.ds(1, 2), :, j],
        lambda j: (x_skip.at[2, :, j], x_skip.at[0, :, j]),
        lambda j: (x_skip.at[1, :, j], x_skip.at[3, :, j]),
    )
    move_lab = Exchange(2, lambda j: x_lab.at[j])
    moves = (move_image, move_lab, move_skip)
    for move in moves:
        move.begin()
    @pl.when(r == 0)
    def _():
        x_one[0] = jnp.zeros_like(x_one[0])
        x_skip[0] = jnp.zeros_like(x_skip[0])
        a_one[0] = jnp.zeros_like(a_one[0])
        u_full[0] = jnp.zeros_like(u_full[0])
        dz_low[0] = jnp.zeros_like(dz_low[0])
        dz_high[0] = jnp.zeros_like(dz_high[0])

    @pl.when(r == nr - 1)
    def _():
        x_one[2] = jnp.zeros_like(x_one[2])
        x_skip[3] = jnp.zeros_like(x_skip[3])
        a_one[2] = jnp.zeros_like(a_one[2])
        u_full[3] = jnp.zeros_like(u_full[3])
        dz_low[2] = jnp.zeros_like(dz_low[2])
        dz_high[3] = jnp.zeros_like(dz_high[3])

    gather.forward(moves)
    move_image.finish()
    move_lab.finish()
    middle = max(1, nb // 2)
    for k in range(2, middle + 1):
        move_skip.hop(k)

    def arrange(number, target):
        out, width, taps, first = layers[number]
        across = width // TILE

        def body(n, _):
            ib = lax.rem(n, across)
            t = lax.rem(lax.div(n, across), taps)
            ob = lax.div(n, across * taps)
            target[
                pl.ds(pl.multiple_of(t * out + ob * TILE, TILE), TILE), lanes(ib, TILE)
            ] = grad_ref[place_ref[first + n]]
            return 0

        lax.fori_loop(0, out // TILE * taps * across, body, 0)

    arrange(0, w_one)
    def own_params(first, width):
        start = first // TILE + b * (width // TILE)
        return jnp.concatenate(
            [params_ref[pl.ds(start + n, 1), :] for n in range(width // TILE)], 1
        )

    gain_one, shift_one, gain_two, shift_two = [own_params(n * C1, wide) for n in range(4)]
    gain_three, shift_three = [own_params(4 * C1 + n * C0, slim) for n in range(2)]
    size_low, size_high = C1 // GROUPS, C0 // GROUPS

    def conv_low(z_ref, weight, source, lines=(0, 1, 2), more=False):
        def tap(dx):
            total = 0.0
            for dy in lines:
                first = (3 * dy + dx) * wide
                total = total + dot_nt(source(dy), weight[first : first + wide, :])
            return total

        if more:
            z_ref[0] += tap(1)
        else:
            z_ref[0] = tap(1)
        z_ref[0] += shift_down(tap(0))
        z_ref[0] += shift_up(tap(2))

    conv_low(z_one, w_one, lambda dy: x_one[dy].reshape(px, C0))
    reduce_one, reduce_two = reduce_wide.at[0], reduce_wide.at[1]
    norm_sums(reduce_one, z_one)
    count = 0.0
    for image in range(nb):
        for part in range(4):
            line = 4 + part // 2
            value = x_lab[image, part % 2, line : line + 1, :]
            count = count + jnp.sum(value, 1, keepdims=True)
    reduce_one[r, 2 * nb : 2 * nb + 1, :] = jnp.broadcast_to(count, (1, wide))
    reduce_start(0, reduce_one)
    arrange(1, w_two)
    total = reduce_finish(0, reduce_one)
    count = total[2 * nb : 2 * nb + 1, :1]

    def put_one(part, image, value):
        a_one[1, rows_of(image), lanes(b, wide)] = value

    norm_apply(total, z_one, inv_one, gain_one, shift_one, size_low, put_one)
    move = Exchange(
        3,
        lambda j: a_one.at[1, :, lanes(j, wide)],
        lambda j: (a_one.at[1, :, lanes(j, wide)], a_one.at[0, :, lanes(j, wide)]),
        lambda j: (a_one.at[1, :, lanes(j, wide)], a_one.at[2, :, lanes(j, wide)]),
    )
    move.begin()
    move.hop(1)
    arrange(2, w_up)
    for k in range(2, nb):
        move.hop(k)
    conv_low(z_two, w_two, lambda dy: a_one[dy], (1,))
    move.finish()
    for k in range(middle + 1, nb):
        move_skip.hop(k)
    conv_low(z_two, w_two, lambda dy: a_one[dy], (0, 2), True)
    norm_sums(reduce_two, z_two)
    reduce_start(1, reduce_two)
    arrange(3, w_three)
    total = reduce_finish(1, reduce_two)

    def put_two(part, image, value):
        a_two[rows_of(image), lanes(b, wide)] = value

    norm_apply(total, z_two, inv_two, gain_two, shift_two, size_low, put_two)
    move = Exchange(4, lambda j: a_two.at[:, lanes(j, wide)])
    move.begin()
    move.hops()
    move.finish()
    for part in range(4):
        u_full[1 + part // 2, part % 2, :, lanes(b, slim)] = dot_nt(
            a_two[...], w_up[part * slim : (part + 1) * slim, :]
        ).astype(bf16)
    move = Exchange(
        5,
        lambda j: u_full.at[pl.ds(1, 2), :, :, lanes(j, slim)],
        lambda j: (u_full.at[2, :, :, lanes(j, slim)], u_full.at[0, :, :, lanes(j, slim)]),
        lambda j: (u_full.at[1, :, :, lanes(j, slim)], u_full.at[3, :, :, lanes(j, slim)]),
    )
    def conv_high(product, more):
        for e in range(2):
            even, odd = product(e, 0), product(e, 1)
            first = even[:, slim : 2 * slim] + shift_down(odd[:, :slim]) + odd[:, 2 * slim :]
            second = odd[:, slim : 2 * slim] + even[:, :slim] + shift_up(even[:, 2 * slim :])
            if more:
                z_three[2 * e] += first
                z_three[2 * e + 1] += second
            else:
                z_three[2 * e] = first
                z_three[2 * e + 1] = second

    def high_product(source, start, lines):
        def product(e, f):
            total = 0.0
            for dy in lines[e]:
                weight = w_three[dy * taps_high : (dy + 1) * taps_high, start : start + C0]
                total = total + dot_nt(source[e + dy, f].reshape(px, C0), weight)
            return total

        return product

    every = ((0, 1, 2), (0, 1, 2))
    inner, outer = ((1, 2), (0, 1)), ((0,), (2,))
    move.begin()
    move_skip.finish()
    conv_high(high_product(x_skip, C0, every), False)
    move.hops()
    conv_high(high_product(u_full, 0, inner), True)
    move.finish()
    conv_high(high_product(u_full, 0, outer), True)
    reduce_three, reduce_four = reduce_narrow.at[0], reduce_narrow.at[1]
    norm_sums(reduce_three, z_three)
    total = all_reduce(2, reduce_three)
    a_three = send_high

    def put_three(part, image, value):
        a_three[part, 0, rows_of(image), :] = value

    norm_apply(total, z_three, inv_three, gain_three, shift_three, size_high, put_three)
    pairs = 2 * slim // TILE
    start = (4 * C1 + 2 * C0) // TILE + b * pairs
    head = []
    for number in range(2):
        total = 0.0
        for n in range(pairs):
            value = params_ref[pl.ds(start + n, 1), :].astype(bf16)
            total = total + dot_nn(value, pick((TILE, slim), 0, 2, number - TILE * n))
        head.append(total)
    head = jnp.concatenate(head + [jnp.zeros((6, slim), f32)], 0)
    head_low = head.astype(bf16)
    for part in range(4):
        for image in range(nb):
            tile = dot_nt(head_low, a_three[part, 0, rows_of(image), :])
            logit[b, part, 2 * image : 2 * image + 2, :] = tile[:2]
    spread = Spread(all_send.at[0], all_recv.at[0], lambda other: logit.at[b], lambda j: logit.at[j])
    spread.begin()
    spread.finish()
    loss = jnp.zeros((1, cols), f32)
    bias_grad = [jnp.zeros((1, cols), f32), jnp.zeros((1, cols), f32)]
    head_grad = jnp.zeros((8, slim), f32)
    level = lax.broadcasted_iota(jnp.int32, (8, cols), 0)

    def head_of(part, image):
        two = slice(2 * image, 2 * image + 2)
        tile = logit[0, part, two, :]
        for j in range(1, nb):
            tile = tile + logit[j, part, two, :]
        first = tile[0:1, :] + bias_ref[0]
        second = tile[1:2, :] + bias_ref[1]
        e, f = part // 2, part % 2
        label, level_map, counted = [
            x_lab[image, f, line : line + 1, :] for line in (e, 2 + e, 4 + e)
        ]
        scale = counted * level_map * 0.125
        largest = jnp.maximum(first, second)
        log_total = jnp.log(jnp.exp(first - largest) + jnp.exp(second - largest)) + largest
        picked = first * (1.0 - label) + second * label
        unit = scale / count
        return (
            scale * (log_total - picked),
            (jnp.exp(first - log_total) - (1.0 - label)) * unit,
            (jnp.exp(second - log_total) - label) * unit,
        )

    for part in range(4):
        for image in range(nb):
            cost, first, second = head_of(part, image)
            loss = loss + cost
            bias_grad = [bias_grad[0] + first, bias_grad[1] + second]
            tile = jnp.where(level == 0, first, jnp.where(level == 1, second, 0.0))
            grad_logit[part * nb + image] = tile
            head_grad = head_grad + jnp.dot(
                tile,
                a_three[part, 0, rows_of(image), :].astype(f32),
                preferred_element_type=f32,
                precision=highest,
            )

    def grad_three(part, image):
        return lax.dot_general(
            grad_logit[part * nb + image],
            head,
            (((0,), (0,)), ((), ())),
            preferred_element_type=f32,
            precision=highest,
        )

    reduce_four[r, 2 * nb : 2 * nb + 8, :] = head_grad
    for row, value in enumerate([loss] + bias_grad):
        reduce_four[r, 2 * nb + 2 + row : 2 * nb + 3 + row, :] = jnp.broadcast_to(
            jnp.sum(value, 1, keepdims=True), (1, slim)
        )
    back_sums(reduce_four, z_three, dy_high, gain_three, shift_three, grad_three)
    total = all_reduce(3, reduce_four)

    def put_high(part, image, value):
        dz_high[1 + part // 2, part % 2, rows_of(image), :] = value

    gain_grad, shift_grad = back_apply(
        total, z_three, dy_high, inv_three, gain_three, size_high, put_high
    )
    sums_ref[b] = jnp.zeros_like(sums_ref[b])
    sums_ref[b, 4:5, :slim] = gain_grad
    sums_ref[b, 4:5, slim : 2 * slim] = shift_grad
    sums_ref[b, 5:6, :slim] = total[2 * nb : 2 * nb + 1]
    sums_ref[b, 5:6, slim : 2 * slim] = total[2 * nb + 1 : 2 * nb + 2]
    for row in range(3):
        sums_ref[b, 6 + row : 7 + row, :slim] = total[2 * nb + 2 + row : 2 * nb + 3 + row]
    sums_ref[b, 9:10, :] = jnp.broadcast_to(count, (1, wide))

    def edges(number, source_up, target_up, source_down, target_down):
        def higher():
            return remote(
                source_up,
                target_up,
                edge_send.at[number, 0],
                edge_recv.at[number, 0],
                ring(r + 1, nr),
                b,
            )

        def lower():
            return remote(
                source_down,
                target_down,
                edge_send.at[number, 1],
                edge_recv.at[number, 1],
                ring(r - 1, nr),
                b,
            )

        def begin():
            @pl.when(r + 1 < nr)
            def _():
                higher().start()

            @pl.when(r > 0)
            def _():
                lower().start()

        def finish():
            @pl.when(r + 1 < nr)
            def _():
                higher().wait_send()
                lower().wait_recv()

            @pl.when(r > 0)
            def _():
                lower().wait_send()
                higher().wait_recv()

        return begin, finish

    def widen_high(row):
        even, odd = dz_high[row, 0], dz_high[row, 1]
        shifted_high[row, 0, :, :slim] = odd
        shifted_high[row, 0, :, slim : 2 * slim] = even
        shifted_high[row, 0, :, 2 * slim :] = shift_down(odd.astype(f32)).astype(bf16)
        shifted_high[row, 1, :, :slim] = shift_up(even.astype(f32)).astype(bf16)
        shifted_high[row, 1, :, slim : 2 * slim] = odd
        shifted_high[row, 1, :, 2 * slim :] = even

    def put_grad(first, across, value, rows, start):
        for row, number in rows:
            for k in range(value.shape[1] // TILE):
                grad_ref[first + number * across + start + k] = value[
                    row : row + TILE, k * TILE : (k + 1) * TILE
                ].astype(bf16)

    def weight_high(dy):
        out, width, taps, first = layers[3]
        rows = [(dx * slim, 3 * dy + dx) for dx in range(3)]
        for half, source in enumerate((u_full, x_skip)):
            total = 0.0
            for e in range(2):
                for f in range(2):
                    value = source[e + dy, f].reshape(px, C0)
                    total = total + dot_nn(turned_high[e, :, f * px : (f + 1) * px], value)
            put_grad(first, width // TILE, total, rows, half * (C0 // TILE))

    begin, finish = edges(0, dz_high.at[2], dz_high.at[0], dz_high.at[1], dz_high.at[3])
    begin()
    widen_high(1)
    widen_high(2)
    for e in range(2):
        for f in range(2):
            turned_high[e, :, f * px : (f + 1) * px] = shifted_high[1 + e, f].T
    weight_high(0)
    finish()
    widen_high(0)
    widen_high(3)
    spreads = []
    own_high = []
    for part in range(4):
        e, f = part // 2, part % 2
        total = 0.0
        for dy in range(3):
            total = total + dot_nn(
                shifted_high[e + 2 - dy, f], w_three[dy * taps_high : (dy + 1) * taps_high, :C0]
            )
        for j in range(nb):
            send_high[part, j] = total[:, j * slim : (j + 1) * slim].astype(bf16)

            @pl.when(b == j)
            def _():
                dy_high[part] = total[:, j * slim : (j + 1) * slim]

        spread = Spread(
            high_send.at[part],
            high_recv.at[part],
            lambda other, part=part: send_high.at[part, other],
            lambda j, part=part: recv_high.at[part, j],
        )
        spread.begin()
        spreads.append(spread)

    weight_high(1)
    weight_high(2)
    for part in range(4):
        spreads[part].finish()
        total = dy_high[part]
        for step in range(1, nb):
            total = total + recv_high[part, ring(b + step, nb)].astype(f32)
        dub[:, part * slim : (part + 1) * slim] = total.astype(bf16)

    def input_low(number, product):
        for j in range(nb):
            total = product(j)
            send_low[j] = total.astype(bf16)

            @pl.when(b == j)
            def _():
                dy_low[0] = total

        spread = Spread(
            all_send.at[number],
            all_recv.at[number],
            lambda other: send_low.at[other],
            lambda j: recv_low.at[number - 1, j],
        )
        spread.begin()

        def finish():
            spread.finish()
            total = dy_low[0]
            for step in range(1, nb):
                total = total + recv_low[number - 1, ring(b + step, nb)].astype(f32)
            dy_low[0] = total

        return finish

    finish_sum = input_low(
        1, lambda j: dot_nn(dub[...], w_up[:, j * wide : (j + 1) * wide])
    )
    out, width, taps, first = layers[2]
    turned_low[: 4 * slim, :] = dub[...].T
    for j in range(nb):
        total = dot_nn(turned_low[: 4 * slim, :], a_two[:, j * wide : (j + 1) * wide])
        rows = [(part * slim, part) for part in range(4)]
        put_grad(first, width // TILE, total, rows, j * (wide // TILE))
    finish_sum()

    def back_low(number, z_ref, inv_ref, gain, shift):
        def grad_of(part, image):
            return dy_low[0, rows_of(image), :]

        buffer = reduce_wide.at[number - 2]
        back_sums(buffer, z_ref, dy_low, gain, shift, grad_of)
        total = all_reduce(number, buffer)

        def put(part, image, value):
            dz_low[1, rows_of(image), :] = value

        return back_apply(total, z_ref, dy_low, inv_ref, gain, size_low, put)

    def widen_low(row):
        value = dz_low[row]
        wider = value.astype(f32)
        shifted_low[row, :, :wide] = shift_up(wider).astype(bf16)
        shifted_low[row, :, wide : 2 * wide] = value
        shifted_low[row, :, 2 * wide :] = shift_down(wider).astype(bf16)

    def weight_low(number, source, lines):
        out, width, taps, first = layers[number]
        chunk = 2 * TILE
        for dy in lines:
            rows = []
            for dx in range(3):
                for ob in range(wide // TILE):
                    rows.append((dx * wide + ob * TILE, ob * taps + 3 * dy + dx))
            for j in range(width // chunk):
                total = dot_nn(turned_low[...], source(dy, j * chunk, chunk))
                put_grad(first, width // TILE, total, rows, j * (chunk // TILE))

    gain_grad, shift_grad = back_low(4, z_two, inv_two, gain_two, shift_two)
    sums_ref[b, 2:3, :] = gain_grad
    sums_ref[b, 3:4, :] = shift_grad
    begin, finish = edges(1, dz_low.at[1], dz_low.at[0], dz_low.at[1], dz_low.at[2])
    begin()
    widen_low(1)
    turned_low[...] = shifted_low[1].T
    weight_low(1, lambda dy, start, size: a_one[dy, :, start : start + size], (0,))
    finish()
    widen_low(0)
    widen_low(2)

    def product_two(j):
        total = 0.0
        for dy in range(3):
            total = total + dot_nn(
                shifted_low[2 - dy],
                w_two[3 * dy * wide : 3 * (dy + 1) * wide, j * wide : (j + 1) * wide],
            )
        return total

    finish_sum = input_low(2, product_two)
    weight_low(1, lambda dy, start, size: a_one[dy, :, start : start + size], (1, 2))
    ready = pltpu.make_async_copy(
        grad_ref.at[pl.ds(layers[1][3], grad_ref.shape[0] - layers[1][3])],
        blocks_ref.at[pl.ds(layers[1][3], grad_ref.shape[0] - layers[1][3])],
        local_sem.at[0],
    )
    ready.start()
    finish_sum()
    gain_grad, shift_grad = back_low(5, z_one, inv_one, gain_one, shift_one)
    sums_ref[b, 0:1, :] = gain_grad
    sums_ref[b, 1:2, :] = shift_grad
    spread = Spread(
        all_send.at[3], all_recv.at[3], lambda other: sums_ref.at[b], lambda j: sums_ref.at[j]
    )
    spread.begin()
    widen_low(1)
    turned_low[...] = shifted_low[1].T
    weight_low(
        0, lambda dy, start, size: x_one[dy].reshape(px, C0)[:, start : start + size], (0, 1, 2)
    )
    last = pltpu.make_async_copy(
        grad_ref.at[pl.ds(0, layers[1][3])], blocks_ref.at[pl.ds(0, layers[1][3])], local_sem.at[1]
    )
    last.start()
    spread.finish()
    ready.wait()
    last.wait()


def run_step(master, place, bias, image, skip, labels, weight_map, valid, params):
    nr, nb = lax.axis_size("rows"), lax.axis_size("blk")
    cols = image.shape[0]
    px = nb * cols
    wide, slim = C1 // nb, C0 // nb
    vmem = pl.BlockSpec(memory_space=pltpu.VMEM)
    smem = pl.BlockSpec(memory_space=pltpu.SMEM)
    dma = pltpu.SemaphoreType.DMA
    scratch = [
        pltpu.VMEM((place.shape[0],) + master.shape[1:], bf16),
        dma((2,)),
        pltpu.VMEM((3, nb, cols, C0), bf16),
        pltpu.VMEM((4, 2, nb, cols, C0), bf16),
        pltpu.VMEM((nb, 2, 8, cols), f32),
        pltpu.VMEM((9 * wide, C0), bf16),
        pltpu.VMEM((9 * wide, C1), bf16),
        pltpu.VMEM((4 * slim, C1), bf16),
        pltpu.VMEM((9 * slim, 2 * C0), bf16),
        pltpu.VMEM((3, px, C1), bf16),
        pltpu.VMEM((px, C1), bf16),
        pltpu.VMEM((4, 2, px, C0), bf16),
        pltpu.VMEM((1, px, wide), f32),
        pltpu.VMEM((1, px, wide), f32),
        pltpu.VMEM((4, px, slim), f32),
        pltpu.VMEM((1, px, wide), f32),
        pltpu.VMEM((4, px, slim), f32),
        pltpu.VMEM((8, wide), f32),
        pltpu.VMEM((8, wide), f32),
        pltpu.VMEM((8, slim), f32),
        pltpu.VMEM((3, px, wide), bf16),
        pltpu.VMEM((4, 2, px, slim), bf16),
        pltpu.VMEM((3, px, 3 * wide), bf16),
        pltpu.VMEM((4, 2, px, 3 * slim), bf16),
        pltpu.VMEM((3 * wide, px), bf16),
        pltpu.VMEM((2, 3 * slim, 2 * px), bf16),
        pltpu.VMEM((px, 4 * slim), bf16),
        pltpu.VMEM((4, nb, px, slim), bf16),
        pltpu.VMEM((4, nb, px, slim), bf16),
        pltpu.VMEM((nb, px, wide), bf16),
        pltpu.VMEM((2, nb, px, wide), bf16),
        pltpu.VMEM((nb, 4, 2 * nb, cols), f32),
        pltpu.VMEM((4 * nb, 8, cols), f32),
        pltpu.VMEM((4, nr, 2 * nb + 8, wide), f32),
        pltpu.VMEM((2, nr, 2 * nb + 8, slim), f32),
        dma((3, nr, 2)),
        dma((nr, 2)),
        dma((6, nb, 2)),
        dma((6, nb)),
        dma((6, nb, 2)),
        dma((6, nb, 2)),
        dma((6, nr)),
        dma((6, nr)),
        dma((4, nb)),
        dma((4, nb)),
        dma((4, nb)),
        dma((4, nb)),
        dma((2, 2)),
        dma((2, 2)),
    ]
    return pl.pallas_call(
        functools.partial(step_kernel, nr, nb, cols),
        out_shape=(
            jax.ShapeDtypeStruct((place.shape[0],) + master.shape[1:], bf16),
            jax.ShapeDtypeStruct((nb, 16, wide), f32),
        ),
        in_specs=[vmem, smem, smem] + [vmem] * 6,
        out_specs=(pl.BlockSpec(memory_space=pl.ANY), vmem),
        scratch_shapes=scratch,
        compiler_params=pltpu.CompilerParams(
            collective_id=0, has_side_effects=True, vmem_limit_bytes=60 * 2**20
        ),
    )(master, place, bias, image, skip, labels, weight_map, valid, params)


LANES = 128


def inverse_factor_kernel(stat_ref, inverse_ref, factor_ref):
    order = stat_ref.shape[0]
    tile = (8, LANES)
    sub = lax.broadcasted_iota(jnp.int32, tile, 0)
    groups = order // 8

    def eliminate(source_ref, base, starts, first, count, accs):
        width = len(starts)

        def body(group, accs):
            top = pl.multiple_of(group * 8, 8)
            accs = [list(acc) for acc in accs]
            for unit in range(8):
                values = [source_ref[top + unit, pl.ds(start, 8), :] for start in starts]
                for c in range(8):
                    scale = jnp.broadcast_to(
                        factor_ref[top + unit, pl.ds(base + c, 1), :], tile
                    )
                    for s in range(width):
                        accs[s][c] = accs[s][c] - values[s] * scale
            return tuple(tuple(acc) for acc in accs)

        return lax.fori_loop(first, count, body, tuple(tuple(acc) for acc in accs))

    def batches(first, last, run):
        total = last - first

        def at(group):
            return pl.multiple_of(group * 8, 8)

        def two(n, _):
            run(first + 2 * n, [at(first + 2 * n), at(first + 2 * n + 1)])
            return 0

        lax.fori_loop(0, lax.div(total, 2), two, 0)

        @pl.when(lax.rem(total, 2) == 1)
        def _():
            run(last - 1, [at(last - 1)])

    def block(kb, _):
        base = pl.multiple_of(kb * 8, 8)
        accs = [stat_ref[base + c, pl.ds(base, 8), :] for c in range(8)]
        accs = list(eliminate(factor_ref, base, [base], 0, kb, [accs])[0])
        scale = []
        coef = {}
        for c in range(8):
            scale.append(jnp.broadcast_to(lax.rsqrt(accs[c][c : c + 1, :]), tile))
            accs[c] = accs[c] * scale[c]
            for d in range(c + 1, 8):
                coef[(c, d)] = jnp.broadcast_to(accs[c][d : d + 1, :], tile)
                accs[d] = accs[d] - accs[c] * coef[(c, d)]
        for c in range(8):
            factor_ref[base + c, pl.ds(base, 8), :] = jnp.where(sub >= c, accs[c], 0.0)

        def finish(accs, target_ref, start):
            accs = list(accs)
            for c in range(8):
                for e in range(c):
                    accs[c] = accs[c] - accs[e] * coef[(e, c)]
                accs[c] = accs[c] * scale[c]
                target_ref[base + c, pl.ds(start, 8), :] = accs[c]

        def below(group, starts):
            accs = [[stat_ref[base + c, pl.ds(s, 8), :] for c in range(8)] for s in starts]
            accs = eliminate(factor_ref, base, starts, 0, kb, accs)
            for acc, start in zip(accs, starts):
                finish(acc, factor_ref, start)

        def left(group, starts):
            accs = [[jnp.zeros(tile, jnp.float32) for c in range(8)] for s in starts]
            accs = eliminate(inverse_ref, base, starts, group, kb, accs)
            for acc, start in zip(accs, starts):
                finish(acc, inverse_ref, start)

        def clear(group, _):
            start = pl.multiple_of(group * 8, 8)
            for c in range(8):
                inverse_ref[base + c, pl.ds(start, 8), :] = jnp.zeros(tile, jnp.float32)
            return 0

        batches(kb + 1, groups, below)
        batches(0, kb, left)
        finish([jnp.where(sub == c, 1.0, 0.0) for c in range(8)], inverse_ref, base)
        lax.fori_loop(kb + 1, groups, clear, 0)
        return 0

    lax.fori_loop(0, groups, block, 0)


def split(value):
    high = value.astype(bf16)
    return high, (value - high.astype(f32)).astype(bf16)


def split_three(value):
    high = value.astype(bf16)
    rest = value - high.astype(f32)
    middle = rest.astype(bf16)
    return high, middle, (rest - middle.astype(f32)).astype(bf16)


def diagonal(pair):
    u, v = pair
    empty = jnp.zeros_like(u)
    return jnp.concatenate(
        [jnp.concatenate([u, empty], 1), jnp.concatenate([empty, v], 1)], 0
    )


def pair_product(packed, pair):
    a, b = split(packed)
    u, v = [split(value) for value in pair]
    c, d = diagonal((u[0], v[0])), diagonal((u[1], v[1]))
    result = dot_nn(jnp.concatenate([a, a, b], 1), jnp.concatenate([c, d, c], 0))
    order = packed.shape[1]
    return result[:, :order], result[:, order:]


def pair_cross(one, two):
    a, b = [jnp.concatenate(half, 1) for half in zip(*[split(value) for value in one])]
    c, d = [diagonal(half) for half in zip(*[split(value) for value in two])]
    return dot_nt(jnp.concatenate([a, a, b], 1), jnp.concatenate([c, d, c], 1))


def pair_square(pair):
    thirds = list(zip(*[split_three(value) for value in pair]))
    a, b, c = [jnp.concatenate(third, 1) for third in thirds]
    d, e, f = [diagonal(third) for third in thirds]
    return dot_nt(
        jnp.concatenate([a, a, b, a, b, c], 1), jnp.concatenate([d, e, d, f, e, d], 1)
    )


def product_three(left, right, right_dim):
    (a, b), (c, d) = left, right
    return lax.dot_general(
        jnp.concatenate([a, a, b], 1),
        jnp.concatenate([c, d, c], right_dim),
        (((1,), (right_dim,)), ((), ())),
        preferred_element_type=f32,
    )


def soap_blocks(indices, grads, ins, outs):
    def every(function, *lists):
        return [function(*items) for items in zip(*lists)]

    def load(ref):
        return [ref[index] for index in indices]

    def store(ref, values):
        for index, value in zip(indices, values):
            ref[index] = value

    master_ref, first_ref, second_ref, left_ref, right_ref, left_stat_ref, right_stat_ref = ins
    left = load(left_ref)
    sides, bases = every(split, grads), every(split, load(right_ref))
    lefts, turned = every(split, left), every(lambda grad: split(grad.T), grads)

    def three(dim):
        return lambda one, two: product_three(one, two, dim)

    lefts_turned = every(lambda value: split(value.T), left)
    half = every(three(0), lefts_turned, sides)
    left_outer = every(three(1), sides, sides)
    rotated = every(three(0), every(split, half), bases)
    right_outer = every(three(1), turned, turned)
    first = every(
        lambda old, new: beta_one * old + (1.0 - beta_one) * new, load(first_ref), rotated
    )
    second = every(
        lambda old, new: beta_two * old + (1.0 - beta_two) * new * new, load(second_ref), rotated
    )
    store(outs[2], first)
    store(outs[3], second)
    direction = every(
        lambda one, two: one
        * (1.0 / (1.0 - beta_one**STEP))
        / (jnp.sqrt(two * (1.0 / (1.0 - beta_two**STEP))) + adam_eps),
        first,
        second,
    )
    half = every(three(0), lefts, every(split, direction))
    stats = []
    for ref, target, outer in (
        (left_stat_ref, outs[4], left_outer),
        (right_stat_ref, outs[5], right_outer),
    ):
        stat = every(
            lambda old, new: beta_stat * old + (1.0 - beta_stat) * new, load(ref), outer
        )
        store(target, stat)
        stats.append(every(split, stat))
    moved = every(three(0), lefts_turned, stats[0])
    update = every(three(1), every(split, half), bases)
    moved_right = every(
        lambda stat, basis: product_three(stat, basis, 0).T, stats[1], bases
    )
    master = every(
        lambda old, new: old - soap_rate * (new + soap_decay * old), load(master_ref), update
    )
    store(outs[0], master)
    store(outs[1], every(lambda value: value.astype(bf16), master))
    store(outs[6], moved)
    store(outs[7], moved_right)
    middle = moved[0].shape[0] // 2
    store(
        outs[8],
        every(lambda one, two: pair_square((one[:middle], two[:middle])), moved, moved_right),
    )


def collect_kernel(nr, size, *refs):
    (owner_ref, blocks_ref), refs = refs[:2], refs[2:]
    ins, refs = refs[:7], refs[7:]
    outs, refs = refs[:9], refs[9:]
    (
        out_a,
        in_a,
        out_b,
        in_b,
        total,
        in_buffer,
        out_buffer,
        copy_buffer,
        gram_buffer,
        grad_ref,
        local_sem,
        a_send,
        a_recv,
        b_send,
        b_recv,
        in_sem,
        out_sem,
    ) = refs
    r = lax.axis_index("rows")
    b = lax.axis_index("blk")
    core = lax.rem(r, 2)
    chip = lax.div(r, 2)
    chips = nr // 2
    mate = r + 1 - 2 * core
    count = ins[0].shape[0]
    chunks = count // size
    square = in_square(chips, size)
    half = size // 2

    def device(chip, core):
        return {"rows": 2 * chip + core, "blk": b}

    stage = pltpu.make_async_copy(blocks_ref, grad_ref, local_sem)
    stage.start()
    barrier = pltpu.get_barrier_semaphore()
    pl.semaphore_signal(
        barrier, inc=1, device_id={"rows": mate, "blk": b}, device_id_type=MESH
    )

    def greet(step, _):
        pl.semaphore_signal(
            barrier,
            inc=1,
            device_id=device(lax.rem(chip + step, chips), core),
            device_id_type=MESH,
        )
        return 0

    lax.fori_loop(1, chips, greet, 0)

    def loads(chunk):
        return [
            pltpu.make_async_copy(
                ref.at[pl.ds(chunk * size, size)],
                in_buffer.at[chunk % 2, number],
                in_sem.at[chunk % 2, number],
            )
            for number, ref in enumerate(ins)
        ]

    def stores(chunk):
        copies = []
        for number, ref in enumerate(outs):
            if number in (1, 8):
                source = {1: copy_buffer, 8: gram_buffer}[number].at[chunk % 2]
            else:
                source = out_buffer.at[chunk % 2, number - (number > 1)]
            copies.append(
                pltpu.make_async_copy(
                    source, ref.at[pl.ds(chunk * size, size)], out_sem.at[chunk % 2, number]
                )
            )
        return copies

    def mine(to_chip, to_core, chunk, index):
        return grad_ref[owner_ref[(2 * to_chip + to_core) * count + chunk * size + index]]

    def joined(to_chip, chunk, index):
        value = mine(to_chip, core, chunk, index).astype(f32)
        return value + in_a[chunk, to_chip, index].astype(f32)

    def send_a(chunk):
        return pltpu.make_async_remote_copy(
            src_ref=out_a.at[chunk],
            dst_ref=in_a.at[chunk],
            send_sem=a_send.at[chunk],
            recv_sem=a_recv.at[chunk],
            device_id={"rows": mate, "blk": b},
            device_id_type=MESH,
        )

    def fill_a(chunk):
        def fill(n, _):
            to_chip, index = lax.div(n, size), lax.rem(n, size)
            out_a[chunk, to_chip, index] = mine(to_chip, 1 - core, chunk, index)
            return 0

        lax.fori_loop(0, chips * size, fill, 0)
        send_a(chunk).start()

    class Straight:
        def copy(self, chunk, step, source):
            other = lax.rem(chip + step, chips)
            return pltpu.make_async_remote_copy(
                src_ref=out_b.at[chunk, other],
                dst_ref=in_b.at[chunk, source],
                send_sem=b_send.at[chunk, step],
                recv_sem=b_recv.at[chunk, source],
                device_id=device(other, core),
                device_id_type=MESH,
            )

        def first(self, chunk):
            def join(step, _):
                other = lax.rem(chip + step, chips)

                def each(index, _):
                    out_b[chunk, other, index] = joined(other, chunk, index).astype(bf16)
                    return 0

                lax.fori_loop(0, size, each, 0)
                self.copy(chunk, step, chip).start()
                return 0

            lax.fori_loop(1, chips, join, 0)

        def second(self, chunk):
            pass

        def arrive(self, chunk):
            def wait(step, _):
                self.copy(chunk, step, lax.rem(chip + step, chips)).wait_recv()
                return 0

            lax.fori_loop(1, chips, wait, 0)

        def grad(self, chunk, index):
            return lax.fori_loop(
                1,
                chips,
                lambda step, value: value
                + in_b[chunk, lax.rem(chip + step, chips), index].astype(f32),
                total[chunk, index],
            )

        def close(self, chunk):
            def wait(step, _):
                self.copy(chunk, step, chip).wait_send()
                return 0

            lax.fori_loop(1, chips, wait, 0)

    class Square:
        def __init__(self):
            self.x = chip + 1 - 2 * lax.rem(chip, 2)
            self.y = chip + 2 - 4 * lax.div(chip, 2)
            self.corner = 3 - chip

        def one(self, chunk, way):
            return pltpu.make_async_remote_copy(
                src_ref=out_b.at[chunk, pl.ds(2 * way, 2)],
                dst_ref=in_b.at[chunk, pl.ds(2 * way, 2)],
                send_sem=b_send.at[chunk, way],
                recv_sem=b_recv.at[chunk, way],
                device_id=device((self.x, self.y)[way], core),
                device_id_type=MESH,
            )

        def two(self, chunk, way):
            return pltpu.make_async_remote_copy(
                src_ref=out_b.at[chunk, 4 + way],
                dst_ref=in_b.at[chunk, 4 + way],
                send_sem=b_send.at[chunk, 2 + way],
                recv_sem=b_recv.at[chunk, 2 + way],
                device_id=device((self.y, self.x)[way], core),
                device_id_type=MESH,
            )

        def first(self, chunk):
            for way, near in enumerate((self.x, self.y)):

                def each(index, _, way=way, near=near):
                    slot = way * half + index
                    out_b[chunk, 2 * way, index] = joined(near, chunk, slot).astype(bf16)
                    value = joined(self.corner, chunk, slot)
                    out_b[chunk, 2 * way + 1, index] = value.astype(bf16)
                    return 0

                lax.fori_loop(0, half, each, 0)
                self.one(chunk, way).start()

        def second(self, chunk):
            for way, far in enumerate((self.y, self.x)):
                self.one(chunk, way).wait_recv()

                def each(index, _, way=way, far=far):
                    value = joined(far, chunk, way * half + index)
                    value = value + in_b[chunk, 2 * way + 1, index].astype(f32)
                    out_b[chunk, 4 + way, index] = value.astype(bf16)
                    return 0

                lax.fori_loop(0, half, each, 0)
                self.two(chunk, way).start()

        def arrive(self, chunk):
            for way in range(2):
                self.two(chunk, way).wait_recv()

        def grad(self, chunk, index):
            way, place = index // half, index % half
            value = total[chunk, index] + in_b[chunk, 2 * way, place].astype(f32)
            return value + in_b[chunk, 4 + way, place].astype(f32)

        def close(self, chunk):
            for way in range(2):
                self.one(chunk, way).wait_send()
                self.two(chunk, way).wait_send()

    plan = Square() if square else Straight()

    def keep(chunk):
        def each(index, _):
            total[chunk, index] = joined(chip, chunk, index)
            return 0

        lax.fori_loop(0, size, each, 0)

    def work(chunk):
        plan.arrive(chunk)
        for copy in loads(chunk):
            copy.wait()
        if chunk >= 2:
            for copy in stores(chunk - 2):
                copy.wait()
        slot = chunk % 2
        chunk_ins = [in_buffer.at[slot, number] for number in range(7)]
        chunk_outs = [out_buffer.at[slot, number] for number in range(7)]
        chunk_outs.insert(1, copy_buffer.at[slot])
        chunk_outs.append(gram_buffer.at[slot])
        grads = [plan.grad(chunk, index) for index in range(size)]
        soap_blocks(range(size), grads, chunk_ins, chunk_outs)
        for copy in stores(chunk):
            copy.start()
        if chunk + 2 < chunks:
            for copy in loads(chunk + 2):
                copy.start()

    for chunk in range(min(2, chunks)):
        for copy in loads(chunk):
            copy.start()
    pl.semaphore_wait(barrier, chips)
    stage.wait()
    for chunk in range(chunks):
        fill_a(chunk)
    for chunk in range(chunks + 2):
        if chunk < chunks:
            send_a(chunk).wait_recv()
            plan.first(chunk)
            keep(chunk)
        if 1 <= chunk <= chunks:
            plan.second(chunk - 1)
        if chunk >= 2:
            work(chunk - 2)
    for chunk in range(chunks):
        send_a(chunk).wait_send()
        plan.close(chunk)
        if chunk >= chunks - 2:
            for copy in stores(chunk):
                copy.wait()


def in_square(chips, size):
    return chips == 4 and size % 2 == 0


def soap_update(blocks, owner, states):
    nr = lax.axis_size("rows")
    count, order = states[0].shape[0], states[0].shape[-1]
    size = 8 if count % 8 == 0 else count
    chunks = count // size
    anywhere = pl.BlockSpec(memory_space=pl.ANY)
    vmem = pl.BlockSpec(memory_space=pltpu.VMEM)
    shape = jax.ShapeDtypeStruct(states[0].shape, f32)
    dma = pltpu.SemaphoreType.DMA
    square = (order, order)
    chips = nr // 2
    parts = (6, size // 2) if in_square(chips, size) else (chips, size)
    results = pl.pallas_call(
        functools.partial(collect_kernel, nr, size),
        out_shape=(shape, jax.ShapeDtypeStruct(shape.shape, bf16)) + (shape,) * 6
        + (jax.ShapeDtypeStruct((count, order // 2, order), f32),),
        in_specs=[pl.BlockSpec(memory_space=pltpu.SMEM)] + [anywhere] * 8,
        out_specs=[anywhere] * 9,
        scratch_shapes=[
            pltpu.VMEM((chunks, chips, size) + square, bf16),
            pltpu.VMEM((chunks, chips, size) + square, bf16),
            pltpu.VMEM((chunks,) + parts + square, bf16),
            pltpu.VMEM((chunks,) + parts + square, bf16),
            pltpu.VMEM((chunks, size) + square, f32),
            pltpu.VMEM((2, 7, size) + square, f32),
            pltpu.VMEM((2, 7, size) + square, f32),
            pltpu.VMEM((2, size) + square, bf16),
            pltpu.VMEM((2, size, order // 2, order), f32),
            pltpu.VMEM(blocks.shape, bf16),
            dma(()),
            dma((chunks,)),
            dma((chunks,)),
            dma((chunks, chips)),
            dma((chunks, chips)),
            dma((2, 7)),
            dma((2, 9)),
        ],
        compiler_params=pltpu.CompilerParams(
            collective_id=1, has_side_effects=True, vmem_limit_bytes=60 * 2**20
        ),
    )(owner, blocks, *states)
    kept = list(results[:6])
    new_left, new_right, *kept = new_bases(results[6:8], results[8], kept)
    new_master, new_copy, new_first, new_second, new_left_stat, new_right_stat = kept
    return [
        new_master,
        new_copy,
        new_first,
        new_second,
        new_left,
        new_right,
        new_left_stat,
        new_right_stat,
    ]


def basis_kernel(gram_ref, left_ref, right_ref, *refs):
    number = (len(refs) - 9) // 3
    kept, new_left_ref, new_right_ref = refs[:number], refs[number], refs[number + 1]
    moved, refs = refs[number + 2 : 2 * number + 2], refs[2 * number + 2 :]
    stat_ref, inverse_ref, factor_ref, solve_ref, rest_ref, in_sem, out_sem, *halts = refs
    arriving = [
        pltpu.make_async_copy(source, halt, in_sem.at[n])
        for n, (source, halt) in enumerate(zip(kept, halts))
    ]
    leaving = [
        pltpu.make_async_copy(halt, target, out_sem.at[n])
        for n, (halt, target) in enumerate(zip(halts, moved))
    ]
    for copy in arriving:
        copy.start()
    count, order = left_ref.shape[0], left_ref.shape[1]
    half = order // 2
    width = next(size for size in (8, 5, 4, 2, 1) if count % size == 0)
    column = lax.broadcasted_iota(jnp.int32, (half, order), 1)

    def invert(source_ref):
        def enter(row, _):
            value = source_ref[pl.ds(row, count, stride=half), :]
            if count < half:
                spare = column[: half - count]
                spare = (spare == row) | (spare == row + half)
                value = jnp.concatenate([value, jnp.where(spare, 1.0, 0.0)], 0)
            value = jnp.concatenate([value, pltpu.roll(value, half, 1)], 0)
            stat_ref[row] = value.T[:half]
            return 0

        lax.fori_loop(0, half, enter, 0, unroll=8)
        inverse_factor_kernel(stat_ref, inverse_ref, factor_ref)

        def leave(row, _):
            value = inverse_ref[row]
            value = jnp.concatenate([value, value], 0).T
            solve_ref[pl.ds(row, count, stride=half), :] = jnp.where(
                column[:count] < half, value[:count], value[half : half + count]
            )
            return 0

        lax.fori_loop(0, half, leave, 0, unroll=8)

    def rows(index):
        return pl.ds(pl.multiple_of(index * half, half), half)

    def project(step, _):
        blocks = [step * width + n for n in range(width)]
        first = [(left_ref[n, :half], right_ref[n, :half]) for n in blocks]
        second = [(left_ref[n, half:], right_ref[n, half:]) for n in blocks]
        first = [pair_product(solve_ref[rows(n), :], pair) for n, pair in zip(blocks, first)]
        cross = [pair_cross(one, two) for one, two in zip(second, first)]
        shares = [pair_product(value, pair) for value, pair in zip(cross, first)]
        second = [
            (pair[0] - share[0], pair[1] - share[1]) for pair, share in zip(second, shares)
        ]
        squares = [pair_square(pair) for pair in second]
        for n, one, two, value in zip(blocks, first, second, squares):
            for side, ref in enumerate((new_left_ref, new_right_ref)):
                ref[n, :half] = one[side]
                ref[n, half:] = two[side]
            rest_ref[rows(n), :] = value
        return 0

    def complete(step, _):
        blocks = [step * width + n for n in range(width)]
        refs = (new_left_ref, new_right_ref)
        second = [
            pair_product(solve_ref[rows(n), :], [ref[n, half:] for ref in refs]) for n in blocks
        ]
        for n, pair in zip(blocks, second):
            for ref, value in zip(refs, pair):
                ref[n] = jnp.concatenate([ref[n, :half], value], 0).T
        return 0

    invert(gram_ref)
    for come, go in zip(arriving, leaving):
        come.wait()
        go.start()
    lax.fori_loop(0, count // width, project, 0)
    invert(rest_ref)
    lax.fori_loop(0, count // width, complete, 0)
    for copy in leaving:
        copy.wait()


def new_bases(products, grams, kept):
    count, order = products[0].shape[0], products[0].shape[-1]
    half = order // 2
    vmem = pl.BlockSpec(memory_space=pltpu.VMEM)
    anywhere = pl.BlockSpec(memory_space=pl.ANY)
    lanes = pltpu.VMEM((half, half, LANES), f32)
    flat = pltpu.VMEM((count * half, order), f32)
    return pl.pallas_call(
        basis_kernel,
        out_shape=[
            jax.ShapeDtypeStruct(value.shape, value.dtype) for value in list(products) + kept
        ],
        in_specs=[vmem] * 3 + [anywhere] * len(kept),
        out_specs=[vmem] * 2 + [anywhere] * len(kept),
        scratch_shapes=[lanes, lanes, lanes, flat, flat]
        + [pltpu.SemaphoreType.DMA((len(kept),))] * 2
        + [pltpu.VMEM(value.shape, value.dtype) for value in kept],
        compiler_params=pltpu.CompilerParams(vmem_limit_bytes=60 * 2**20),
    )(grams.reshape(count * half, order), *products, *kept)


def adam_small(grads, value, first, second):
    first_new = beta_one * first + (1.0 - beta_one) * grads
    second_new = beta_two * second + (1.0 - beta_two) * grads * grads
    direction = (
        first_new
        / (1.0 - beta_one**STEP)
        / (jnp.sqrt(second_new / (1.0 - beta_two**STEP)) + adam_eps)
    )
    return (first_new, second_new, value - small_rate * (direction + small_decay * value))


def local(
    image,
    skip,
    labels,
    weight_map,
    valid,
    owner,
    master,
    first_moment,
    second_moment,
    left_basis,
    right_basis,
    left_stat,
    right_stat,
    norm_params,
    norm_first,
    norm_second,
    head_bias,
    bias_first,
    bias_second,
):
    shards = lax.axis_size("blk")
    slots = jnp.arange(owner.shape[0])
    place = jnp.sum(jnp.where(owner[None, :] == slots[:, None], slots[None, :], 0), 1)
    part = C0 // shards
    blocks, sums = run_step(
        master[0],
        place.astype(jnp.int32),
        head_bias,
        image[0, 0],
        skip[0],
        labels[0],
        weight_map[0],
        valid[0],
        norm_params.reshape(-1, TILE),
    )
    loss_sum, valid_count = sums[0, 6, 0], sums[0, 9, 0]
    grad_bias = sums[0, 7:9, 0]
    grad_head = jnp.stack([sums[:, 5, :part].reshape(-1), sums[:, 5, part : 2 * part].reshape(-1)], 1)
    small = jnp.concatenate(
        [sums[:, row].reshape(-1) for row in range(4)]
        + [
            sums[:, 4, :part].reshape(-1),
            sums[:, 4, part : 2 * part].reshape(-1),
            grad_head.reshape(-1),
        ]
    )
    states = (
        master,
        first_moment,
        second_moment,
        left_basis,
        right_basis,
        left_stat,
        right_stat,
    )
    soap = soap_update(blocks, owner, [state[0] for state in states])
    soap = [value[None] for value in soap]
    norm_new = adam_small(small, norm_params, norm_first, norm_second)
    bias_new = adam_small(grad_bias, head_bias, bias_first, bias_second)
    return (
        loss_sum,
        valid_count,
        soap[0],
        soap[1],
        soap[2],
        soap[3],
        soap[4],
        soap[5],
        soap[6],
        soap[7],
        norm_new[0],
        norm_new[1],
        norm_new[2],
        bias_new[0],
        bias_new[1],
        bias_new[2],
    )


def solution(mesh):
    placed = (
        P("blk", "rows", None, None),
        P("blk", "rows", None, None),
        P("blk", "rows", None),
        P("blk", "rows", None),
        P("blk", "rows", None),
        P(),
        P("blk", "rows", None, None),
        P("blk", "rows", None, None),
        P("blk", "rows", None, None),
        P("blk", "rows", None, None),
        P("blk", "rows", None, None),
        P("blk", "rows", None, None),
        P("blk", "rows", None, None),
        P(),
        P(),
        P(),
        P(),
        P(),
        P(),
    )
    return jax.shard_map(
        local,
        mesh=mesh,
        in_specs=placed,
        out_specs=(
            P(),
            P(),
            P("blk", "rows", None, None),
            P("blk", "rows", None, None),
            P("blk", "rows", None, None),
            P("blk", "rows", None, None),
            P("blk", "rows", None, None),
            P("blk", "rows", None, None),
            P("blk", "rows", None, None),
            P("blk", "rows", None, None),
            P(),
            P(),
            P(),
            P(),
            P(),
            P(),
        ),
        check_vma=False,
    )
```
